32 devices in a mesh: dp: 16 (over z, x, core), mp: 2 (over y).
Axes of the slice: x: 2, y: 2, z: 4, core: 2. Of those that a mesh axis runs over, the one named last changes fastest.
Arguments:
- tokens: bfloat16 [2, 16, 448, 2048], P(None, 'dp'), may hold values from -6 to 6
- cotangent: bfloat16 [2, 16, 448, 2048], P(None, 'dp', None, 'mp'), may hold values from -6 to 6
- lengths: int32 [2, 16], P(None, 'dp'), may hold values from 1 to 448, as said below
- domains: int32 [2, 16, 1], P(None, 'dp'), may hold values from 0 to 7
- lower_bound: float32 [2048], replicated, may hold values from 0 to 1
- mixer_master: float32 [4, 2048, 2048], P(None, ('dp', 'mp')), may hold values from -0.125 to 0.125
- mixer_first: float32 [4, 2048, 2048], P(None, ('dp', 'mp'))
- mixer_second: float32 [4, 2048, 2048], P(None, ('dp', 'mp'))
- glu_in_master: float32 [2, 2048, 5632], P(None, 'dp', 'mp'), may hold values from -0.125 to 0.125
- glu_in_first: float32 [2, 2048, 5632], P(None, 'dp', 'mp')
- glu_in_second: float32 [2, 2048, 5632], P(None, 'dp', 'mp')
- glu_out_master: float32 [5632, 2048], P('mp', 'dp'), may hold values from -0.078125 to 0.078125
- glu_out_first: float32 [5632, 2048], P('mp', 'dp')
- glu_out_second: float32 [5632, 2048], P('mp', 'dp')
- gain_master: float32 [3, 2048], P(None, ('dp', 'mp')), may hold values from 0.5 to 1.5
- gain_first: float32 [3, 2048], P(None, ('dp', 'mp'))
- gain_second: float32 [3, 2048], P(None, ('dp', 'mp'))
Outputs:
- layer_out: bfloat16 [2, 16, 448, 2048], P(None, 'dp', None, 'mp')
- grad_tokens: bfloat16 [2, 16, 448, 2048], P(None, 'dp', None, 'mp')
- mixer_master_new: float32 [4, 2048, 2048], P(None, ('dp', 'mp'))
- mixer_first_new: float32 [4, 2048, 2048], P(None, ('dp', 'mp'))
- mixer_second_new: float32 [4, 2048, 2048], P(None, ('dp', 'mp'))
- glu_in_master_new: float32 [2, 2048, 5632], P(None, 'dp', 'mp')
- glu_in_first_new: float32 [2, 2048, 5632], P(None, 'dp', 'mp')
- glu_in_second_new: float32 [2, 2048, 5632], P(None, 'dp', 'mp')
- glu_out_master_new: float32 [5632, 2048], P('mp', 'dp')
- glu_out_first_new: float32 [5632, 2048], P('mp', 'dp')
- glu_out_second_new: float32 [5632, 2048], P('mp', 'dp')
- gain_master_new: float32 [3, 2048], P(None, ('dp', 'mp'))
- gain_first_new: float32 [3, 2048], P(None, ('dp', 'mp'))
- gain_second_new: float32 [3, 2048], P(None, ('dp', 'mp'))
The draws below stay inside these ranges and needn't reach their ends.
Inputs may be any that keep to these rules, and one draw needn't show every extreme that they name: lengths rise from about a third of 448 at the first sequence index to 448 at the last; the last sequence of each micro-batch holds all 448 tokens.
All inputs are finite; a program needn't handle non-finite values.
Results may differ from the reference program's by a relative error of at most 0.023.
Values may be sent and summed in bfloat16 or wider, within the bound.
A program may use at most 296 MiB of HBM per device.

```python
import math
import jax
import jax.numpy as jnp
from jax import lax

D = 2048
FF = 5632
LENGTH = 448
MB = 2
NDOM = 8
SEQS = 16


def grad_scale():
    return math.sqrt(0.6 * LENGTH / (MB * SEQS))


def first_moment(key, shape, factor):
    return 0.111 * factor * grad_scale() * jax.random.normal(key, shape, jnp.float32)


def second_moment(key, shape, factor):
    key_one, key_two = jax.random.split(jax.random.fold_in(key, 7))
    level = jnp.exp(jax.random.uniform(key_one, shape, jnp.float32, 0.0, math.log(4.0)))
    spread = jnp.exp(jax.random.uniform(key_two, shape, jnp.float32, math.log(0.5), math.log(2.0)))
    return 0.0526 * (factor * grad_scale()) ** 2 * level * spread


def draw_lengths(key, part):
    seq_place = jnp.arange(SEQS, dtype=jnp.int32)
    rising = LENGTH // 3 + (LENGTH - LENGTH // 3) * seq_place // max(SEQS - 1, 1)
    jitter = jax.random.randint(key, (MB, SEQS), 0, LENGTH // 8 + 1)
    drawn = jnp.maximum(rising[None, :] - jitter, 1)
    return jnp.where(seq_place[None, :] == SEQS - 1, LENGTH, drawn).astype(jnp.int32)


def draw_lower_bound(key, part):
    key_pick, key_slow, key_fast = jax.random.split(jax.random.fold_in(key, 11), 3)
    share = 0.75
    picked = jax.random.uniform(key_pick, (D,), jnp.float32) < share
    reach = jnp.exp(jax.random.uniform(key_slow, (D,), jnp.float32, math.log(2.0), math.log(8.0)))
    slow_bound = 1.0 - reach / LENGTH
    fast_bound = jax.random.uniform(key_fast, (D,), jnp.float32, 0.0, 0.6)
    return jnp.where(picked, slow_bound, fast_bound).astype(jnp.float32)


def draw_mixer_first(key, part):
    return first_moment(key, (4, D, D), 0.3)


def draw_mixer_second(key, part):
    return second_moment(key, (4, D, D), 0.3)


def draw_glu_in_first(key, part):
    return first_moment(key, (2, D, FF), 0.5)


def draw_glu_in_second(key, part):
    return second_moment(key, (2, D, FF), 0.5)


def draw_glu_out_first(key, part):
    return first_moment(key, (FF, D), 0.5)


def draw_glu_out_second(key, part):
    return second_moment(key, (FF, D), 0.5)


def draw_gain_first(key, part):
    return first_moment(key, (3, D), 0.8)


def draw_gain_second(key, part):
    return second_moment(key, (3, D), 0.8)


def block_levels(rng, extent, pieces, least, top_value):
    gain, own = 1.0, jax.random.fold_in(rng, 6)
    for axis_at, parts in pieces:
        heights = jnp.exp(jax.random.uniform(jax.random.fold_in(own, axis_at), (parts,), jnp.float32, least / len(pieces), top_value / len(pieces)))
        gain = gain * jnp.repeat(heights, extent[axis_at] // parts).reshape([-1 if axis == axis_at else 1 for axis in range(len(extent))])
    return gain


def different_ones(key, rows, count, top, lift):
    order = jax.random.permutation(jax.random.fold_in(key, 1), count)
    pull = order
    for power in range(3):
        pull = pull * pull // count
    pull = pull * lift // count
    lots = jax.random.randint(jax.random.fold_in(key, 2), (rows, count), 0, 4096) + pull
    sure = jax.random.permutation(jax.random.fold_in(key, 3), rows)[jnp.arange(count) % rows]
    lots = jnp.where(jnp.arange(rows)[:, None] == sure[None, :], 1 << 14, lots)
    merit = lots * count + jnp.arange(count)
    return lax.top_k(merit.astype(jnp.int32), top)[1].astype(jnp.int32)


def bell_draw(own_key, extent, scale, limit, cuts=(), kind=jnp.bfloat16):
    values = jax.random.normal(own_key, extent, jnp.float32) * scale
    if len(cuts) > 0:
        values = block_levels(own_key, extent, cuts, -0.22, 0.18) * values
    return jnp.clip(values, min=-limit, max=limit).astype(kind)


def setup_inputs(seed: int = 0) -> dict:
    key_list = jax.random.split(jax.random.key(seed), 18)
    return {
        "tokens": bell_draw(key_list[0], (MB, SEQS, LENGTH, D), 1.0, 6.0, ((1, 16),)),
        "cotangent": bell_draw(key_list[1], (MB, SEQS, LENGTH, D), 1.0, 6.0, ((1, 16), (3, 2))),
        "lengths": draw_lengths(jax.random.fold_in(key_list[17], 71), 0),
        "domains": different_ones(key_list[3], MB * SEQS, NDOM, 1, 2048).reshape((MB, SEQS, 1)),
        "lower_bound": draw_lower_bound(jax.random.fold_in(key_list[17], 71), 0),
        "mixer_master": bell_draw(key_list[5], (4, D, D), D ** -0.5, 0.125, ((1, 32),), jnp.float32),
        "mixer_first": draw_mixer_first(jax.random.fold_in(key_list[17], 71), 0),
        "mixer_second": draw_mixer_second(jax.random.fold_in(key_list[17], 71), 0),
        "glu_in_master": bell_draw(key_list[8], (2, D, FF), D ** -0.5, 0.125, ((1, 16), (2, 2)), jnp.float32),
        "glu_in_first": draw_glu_in_first(jax.random.fold_in(key_list[17], 71), 0),
        "glu_in_second": draw_glu_in_second(jax.random.fold_in(key_list[17], 71), 0),
        "glu_out_master": bell_draw(key_list[11], (FF, D), FF ** -0.5, 0.078125, ((0, 2), (1, 16)), jnp.float32),
        "glu_out_first": draw_glu_out_first(jax.random.fold_in(key_list[17], 71), 0),
        "glu_out_second": draw_glu_out_second(jax.random.fold_in(key_list[17], 71), 0),
        "gain_master": jnp.clip(1.0 + 0.1 * jax.random.normal(key_list[14], (3, D), jnp.float32), 0.5, 1.5),
        "gain_first": draw_gain_first(jax.random.fold_in(key_list[17], 71), 0),
        "gain_second": draw_gain_second(jax.random.fold_in(key_list[17], 71), 0),
    }


EPSILON = 1e-06
BETA_ONE = 0.9
BETA_TWO = 0.95
ADAM_EPSILON = 1e-08
DECAY_RATE = 0.1
MATRIX_RATE = 0.06
GAIN_RATE = 0.5
STEP_NUMBER = 3.0

@jax.custom_vjp
def low(v):
    return lax.optimization_barrier(v.astype(jnp.bfloat16)).astype(jnp.float32)

@jax.custom_vjp
def low_back(v):
    return v

def low_keep(v):
    return (low(v), None)

def low_pass(kept, grad):
    return (grad,)

def back_keep(v):
    return (v, None)

def back_low(kept, grad):
    return (low(grad),)
low.defvjp(low_keep, low_pass)
low_back.defvjp(back_keep, back_low)

def normed(values):
    return values * lax.rsqrt(lax.optimization_barrier(jnp.mean(values * values, axis=-1, keepdims=True)) + EPSILON)

def product(left_side, right_side):
    return jnp.dot(left_side, right_side, precision=lax.Precision.HIGHEST, preferred_element_type=jnp.float32)

def recurrence(forget, fresh_input):

    def advance(carried, forget_fresh):
        carried = forget_fresh[0] * carried + (1.0 - forget_fresh[0]) * forget_fresh[1]
        return (carried, carried)
    initial = jnp.zeros(forget.shape[1:], jnp.float32)
    return lax.scan(advance, initial, (forget, fresh_input))[1]

def block_forward(sequence, mixer, glu_in, glu_out, gain_rows, lower_bound):
    normed_in = low(normed(sequence) * gain_rows[0])
    pre_input = low_back(product(normed_in, mixer[0]))
    pre_forget = low_back(product(normed_in, mixer[1]))
    pre_gate = low_back(product(normed_in, mixer[2]))
    fresh_input = jax.nn.silu(pre_input)
    forget = lower_bound + (1.0 - lower_bound) * jax.nn.sigmoid(pre_forget)
    states = recurrence(forget, fresh_input)
    gated_out = low(normed(states) * gain_rows[1] * jax.nn.silu(pre_gate))
    middle = sequence + low_back(product(gated_out, mixer[3]))
    normed_mid = low(normed(middle) * gain_rows[2])
    pre_act = low_back(product(normed_mid, glu_in[0]))
    pre_up = low_back(product(normed_mid, glu_in[1]))
    hidden = low(jax.nn.silu(pre_act) * pre_up)
    return middle + low_back(product(hidden, glu_out))

def token_weights(lengths, domains):
    domain_tags = domains[..., 0]
    member = (domain_tags[..., None] == jnp.arange(NDOM, dtype=jnp.int32)).astype(jnp.float32)
    live_counts = lengths.astype(jnp.float32)
    counts = lax.optimization_barrier(jnp.sum(member * live_counts[..., None], axis=(0, 1)))
    token_total = jnp.sum(live_counts)
    seq_weight = token_total / (NDOM * lax.optimization_barrier(jnp.sum(member * counts, axis=-1)))
    positions = jnp.arange(LENGTH, dtype=jnp.int32)
    live_mask = (positions[None, None, :] < lengths[..., None]).astype(jnp.float32)
    return seq_weight[..., None] * live_mask

def adamw_update(master, first, second, gradient, count, rate, decay):
    first_new = BETA_ONE * first + (1.0 - BETA_ONE) * gradient
    second_new = BETA_TWO * second + (1.0 - BETA_TWO) * gradient * gradient
    first_hat = first_new / (1.0 - BETA_ONE ** count)
    second_hat = second_new / (1.0 - BETA_TWO ** count)
    master_new = master - rate * (first_hat / (jnp.sqrt(second_hat) + ADAM_EPSILON) + decay * master)
    return (master_new, first_new, second_new)

def reference(tokens, cotangent, lengths, domains, lower_bound, mixer_master, mixer_first, mixer_second, glu_in_master, glu_in_first, glu_in_second, glu_out_master, glu_out_first, glu_out_second, gain_master, gain_first, gain_second):
    weights = token_weights(lengths, domains)
    flat_tokens = tokens.astype(jnp.float32).reshape(MB * SEQS, LENGTH, D)
    flat_back = (cotangent.astype(jnp.float32) * weights[..., None]).reshape(MB * SEQS, LENGTH, D)
    copies = (low(mixer_master), low(glu_in_master), low(glu_out_master), low(gain_master))

    def forward(seq_in, mixer, glu_in, glu_out, gain_rows):
        return block_forward(seq_in, mixer, glu_in, glu_out, gain_rows, lower_bound)

    def one_sequence(totals, seq_pair):
        result, pullback = jax.vjp(forward, seq_pair[0], copies[0], copies[1], copies[2], copies[3])
        grads = pullback(seq_pair[1])
        totals = tuple((total_now + grad_now for total_now, grad_now in zip(totals, grads[1:])))
        return (totals, (result.astype(jnp.bfloat16), grads[0].astype(jnp.bfloat16)))
    initial = tuple((jnp.zeros_like(member_now) for member_now in copies))
    totals, (outputs, grad_rows) = lax.scan(one_sequence, initial, (flat_tokens, flat_back))
    scale_factor = 1.0 / (MB * SEQS)
    count = STEP_NUMBER
    mixer_new = adamw_update(mixer_master, mixer_first, mixer_second, totals[0] * scale_factor, count, MATRIX_RATE, DECAY_RATE)
    glu_in_new = adamw_update(glu_in_master, glu_in_first, glu_in_second, totals[1] * scale_factor, count, MATRIX_RATE, DECAY_RATE)
    glu_out_new = adamw_update(glu_out_master, glu_out_first, glu_out_second, totals[2] * scale_factor, count, MATRIX_RATE, DECAY_RATE)
    gain_new = adamw_update(gain_master, gain_first, gain_second, totals[3] * scale_factor, count, GAIN_RATE, 0.0)
    return (outputs.reshape(MB, SEQS, LENGTH, D), grad_rows.reshape(MB, SEQS, LENGTH, D), mixer_new[0], mixer_new[1], mixer_new[2], glu_in_new[0], glu_in_new[1], glu_in_new[2], glu_out_new[0], glu_out_new[1], glu_out_new[2], gain_new[0], gain_new[1], gain_new[2])
```

```python
import functools

import jax
import jax.numpy as jnp
from jax import lax
from jax.experimental import pallas as pl
from jax.experimental.pallas import tpu as pltpu
from jax.sharding import PartitionSpec as P

NDOM = 8

EPSILON = 1e-06
BETA_ONE = 0.9
BETA_TWO = 0.95
ADAM_EPSILON = 1e-08
DECAY_RATE = 0.1
MATRIX_RATE = 0.06
GAIN_RATE = 0.5
STEP_NUMBER = 3.0

BF = jnp.bfloat16
F32 = jnp.float32
VMEM_LIMIT = 56 * 1024 * 1024


def inverse_rms(values):
    return lax.rsqrt(jnp.mean(values * values, axis=-1, keepdims=True) + EPSILON)


def silu_slope(values):
    sigma = jax.nn.sigmoid(values)
    return sigma * (1.0 + values * (1.0 - sigma))


def adamw_update(master, first, second, gradient, count, rate, decay):
    first_new = BETA_ONE * first + (1.0 - BETA_ONE) * gradient
    second_new = BETA_TWO * second + (1.0 - BETA_TWO) * gradient * gradient
    first_hat = first_new / (1.0 - BETA_ONE**count)
    second_hat = second_new / (1.0 - BETA_TWO**count)
    master_new = master - rate * (
        first_hat / (jnp.sqrt(second_hat) + ADAM_EPSILON) + decay * master
    )
    return (master_new, first_new, second_new)


def partner_swap(value):
    return lax.ppermute(value, "mp", [(0, 1), (1, 0)])


def mp_sum(part):
    low = part.astype(BF)
    if lax.axis_size("mp") == 2:
        return low.astype(F32) + partner_swap(low).astype(F32)
    return lax.psum(low.astype(F32), "mp")


def mp_sum_wide(part):
    if lax.axis_size("mp") == 2:
        return part + partner_swap(part)
    return lax.psum(part, "mp")


def mp_scatter(part):
    if lax.axis_size("mp") == 2:
        half = part.shape[1] // 2
        place = lax.axis_index("mp")
        own = lax.dynamic_slice_in_dim(part, place * half, half, 1)
        other = lax.dynamic_slice_in_dim(part, (1 - place) * half, half, 1)
        return own.astype(BF).astype(F32) + partner_swap(other.astype(BF)).astype(F32)
    return lax.psum_scatter(part.astype(BF), "mp", scatter_dimension=1, tiled=True).astype(F32)


def mp_swap(pieces):
    if lax.axis_size("mp") == 2:
        place = lax.axis_index("mp")
        own = lax.dynamic_index_in_dim(pieces, place, 0, keepdims=False)
        came = partner_swap(lax.dynamic_index_in_dim(pieces, 1 - place, 0, keepdims=False))
        first = place == 0
        return jnp.stack([jnp.where(first, own, came), jnp.where(first, came, own)])
    return lax.all_to_all(pieces, "mp", 0, 0, tiled=False)


def mp_gather(part):
    if lax.axis_size("mp") == 2:
        place = lax.axis_index("mp")
        came = partner_swap(part)
        first = place == 0
        return jnp.concatenate([jnp.where(first, part, came), jnp.where(first, came, part)], axis=1)
    return lax.all_gather(part, "mp", axis=1, tiled=True)


SUB_ROWS = 8
TILE_ROWS = 16


def channel_block(width):
    return 256 if width % 256 == 0 else width


def scan_rows(total, decay, carry):
    row = lax.broadcasted_iota(jnp.int32, total.shape, 0)
    shift = 1
    while shift < SUB_ROWS:
        keep = row >= shift
        total = total + decay * jnp.where(keep, pltpu.roll(total, shift, 0), 0.0)
        decay = decay * jnp.where(keep, pltpu.roll(decay, shift, 0), 1.0)
        shift *= 2
    return total + decay * carry


def scan_rows_back(total, decay, carry):
    row = lax.broadcasted_iota(jnp.int32, total.shape, 0)
    shift = 1
    while shift < SUB_ROWS:
        keep = row < SUB_ROWS - shift
        total = total + decay * jnp.where(keep, pltpu.roll(total, SUB_ROWS - shift, 0), 0.0)
        decay = decay * jnp.where(keep, pltpu.roll(decay, SUB_ROWS - shift, 0), 1.0)
        shift *= 2
    return total + decay * carry


def scan_forward_kernel(pre_ref, bound_ref, gain_ref, states_ref, raw_ref, square_ref):
    length, width = states_ref.shape[1], states_ref.shape[2]
    bound = bound_ref[...]
    gain = gain_ref[...]
    first_block = pl.program_id(1) == 0

    def step(index, carry):
        rows = pl.ds(pl.multiple_of(index * TILE_ROWS, TILE_ROWS), TILE_ROWS)
        forget = bound + (1.0 - bound) * jax.nn.sigmoid(pre_ref[1, 0, rows, :])
        total = (1.0 - forget) * jax.nn.silu(pre_ref[0, 0, rows, :])
        parts = []
        for low in range(0, TILE_ROWS, SUB_ROWS):
            part = scan_rows(total[low : low + SUB_ROWS], forget[low : low + SUB_ROWS], carry)
            carry = part[SUB_ROWS - 1 : SUB_ROWS]
            parts.append(part)
        states = jnp.concatenate(parts)
        states_ref[0, rows, :] = states
        raw = states * gain * jax.nn.silu(pre_ref[2, 0, rows, :])
        raw_ref[0, rows, :] = raw.astype(raw_ref.dtype)
        square = jnp.sum(states * states, axis=-1, keepdims=True)
        square_ref[0, rows, :] = square + jnp.where(first_block, 0.0, square_ref[0, rows, :])
        return carry

    lax.fori_loop(0, length // TILE_ROWS, step, jnp.zeros((1, width), F32))


def scan_forward(pre, bound, gain):
    _, batches, length, width = pre.shape
    block = channel_block(width)
    return pl.pallas_call(
        scan_forward_kernel,
        grid=(batches, width // block),
        in_specs=[
            pl.BlockSpec((3, 1, length, block), lambda b, c: (0, b, 0, c)),
            pl.BlockSpec((1, block), lambda b, c: (0, c)),
            pl.BlockSpec((1, block), lambda b, c: (0, c)),
        ],
        out_specs=[
            pl.BlockSpec((1, length, block), lambda b, c: (b, 0, c)),
            pl.BlockSpec((1, length, block), lambda b, c: (b, 0, c)),
            pl.BlockSpec((1, length, 1), lambda b, c: (b, 0, 0)),
        ],
        out_shape=[
            jax.ShapeDtypeStruct((batches, length, width), F32),
            jax.ShapeDtypeStruct((batches, length, width), BF),
            jax.ShapeDtypeStruct((batches, length, 1), F32),
        ],
        compiler_params=pltpu.CompilerParams(vmem_limit_bytes=VMEM_LIMIT),
        cost_estimate=pl.CostEstimate(
            flops=batches * length * width * 40,
            bytes_accessed=batches * length * width * 18,
            transcendentals=batches * length * width * 3,
        ),
    )(pre, bound[None], gain[None])


def scan_backward_kernel(
    pre_ref, states_ref, gated_ref, inverse_ref, mean_ref, bound_ref, gain_ref,
    grad_ref, out_ref, gain_grad_ref, dot_ref,
):
    length, width = states_ref.shape[1], states_ref.shape[2]
    bound = bound_ref[...]
    gain = gain_ref[...]
    first_block = pl.program_id(1) == 0
    row = lax.broadcasted_iota(jnp.int32, (TILE_ROWS, width), 0)
    tiles = length // TILE_ROWS

    def step(index, carry):
        carried_next, forget_next, gain_sum = carry
        place = tiles - 1 - index
        rows = pl.ds(pl.multiple_of(place * TILE_ROWS, TILE_ROWS), TILE_ROWS)
        pre_input = pre_ref[0, 0, rows, :]
        pre_forget = pre_ref[1, 0, rows, :]
        pre_gate = pre_ref[2, 0, rows, :]
        states = states_ref[0, rows, :]
        inverse = inverse_ref[0, rows, :]
        grad_gated = gated_ref[0, rows, :]
        unit = states * inverse
        gate_sig = jax.nn.sigmoid(pre_gate)
        gate = pre_gate * gate_sig
        out_ref[0, rows, :] = (unit * gain * gate).astype(out_ref.dtype)
        gain_sum = gain_sum + grad_gated * unit * gate
        scaled = grad_gated * gain
        grad_gate = (scaled * unit * (gate_sig * (1.0 + pre_gate * (1.0 - gate_sig)))).astype(BF)
        grad_ref[2, 0, rows, :] = grad_gate
        total = inverse * (scaled * gate - unit * mean_ref[0, rows, :])
        sigma = jax.nn.sigmoid(pre_forget)
        forget = bound + (1.0 - bound) * sigma
        decay = jnp.where(row == TILE_ROWS - 1, forget_next, pltpu.roll(forget, TILE_ROWS - 1, 0))
        parts = []
        for low in range(TILE_ROWS - SUB_ROWS, -1, -SUB_ROWS):
            part = scan_rows_back(
                total[low : low + SUB_ROWS], decay[low : low + SUB_ROWS], carried_next
            )
            carried_next = part[0:1]
            parts.insert(0, part)
        carried = jnp.concatenate(parts)
        before_rows = pl.ds(
            pl.multiple_of(jnp.maximum(place - 1, 0) * TILE_ROWS, TILE_ROWS), TILE_ROWS
        )
        before = states_ref[0, before_rows, :][TILE_ROWS - 1 : TILE_ROWS, :]
        before = jnp.where(place == 0, 0.0, before)
        earlier = jnp.where(row == 0, before, pltpu.roll(states, 1, 0))
        input_sig = jax.nn.sigmoid(pre_input)
        fresh = pre_input * input_sig
        slope = input_sig * (1.0 + pre_input * (1.0 - input_sig))
        grad_input = (carried * (1.0 - forget) * slope).astype(BF)
        grad_forget = (
            carried * (earlier - fresh) * (1.0 - bound) * sigma * (1.0 - sigma)
        ).astype(BF)
        grad_ref[0, 0, rows, :] = grad_input
        grad_ref[1, 0, rows, :] = grad_forget
        dots = (
            grad_input.astype(F32) * pre_input
            + grad_forget.astype(F32) * pre_forget
            + grad_gate.astype(F32) * pre_gate
        )
        dot = jnp.sum(dots, axis=-1, keepdims=True)
        dot_ref[0, rows, :] = dot + jnp.where(first_block, 0.0, dot_ref[0, rows, :])
        return carried_next, forget[0:1, :], gain_sum

    zero = jnp.zeros((1, width), F32)
    _, _, gain_sum = lax.fori_loop(
        0, tiles, step, (zero, zero, jnp.zeros((TILE_ROWS, width), F32))
    )
    gain_grad_ref[0] = jnp.sum(gain_sum, axis=0, keepdims=True)


def scan_backward(pre, states, grad_gated, inverse, mean, bound, gain):
    _, batches, length, width = pre.shape
    block = channel_block(width)
    whole = pl.BlockSpec((1, length, block), lambda b, c: (b, 0, c))
    column = pl.BlockSpec((1, length, 1), lambda b, c: (b, 0, 0))
    line = pl.BlockSpec((1, block), lambda b, c: (0, c))
    three = pl.BlockSpec((3, 1, length, block), lambda b, c: (0, b, 0, c))
    return pl.pallas_call(
        scan_backward_kernel,
        grid=(batches, width // block),
        in_specs=[three, whole, whole, column, column, line, line],
        out_specs=[
            three,
            whole,
            pl.BlockSpec((1, 1, block), lambda b, c: (b, 0, c)),
            column,
        ],
        out_shape=[
            jax.ShapeDtypeStruct((3, batches, length, width), BF),
            jax.ShapeDtypeStruct((batches, length, width), BF),
            jax.ShapeDtypeStruct((batches, 1, width), F32),
            jax.ShapeDtypeStruct((batches, length, 1), F32),
        ],
        compiler_params=pltpu.CompilerParams(vmem_limit_bytes=VMEM_LIMIT),
        cost_estimate=pl.CostEstimate(
            flops=batches * length * width * 80,
            bytes_accessed=batches * length * width * 28,
            transcendentals=batches * length * width * 3,
        ),
    )(pre, states, grad_gated, inverse, mean, bound[None], gain[None])


def shards(
    tokens,
    cotangent,
    lengths,
    domains,
    lower_bound,
    mixer_master,
    mixer_first,
    mixer_second,
    glu_in_master,
    glu_in_first,
    glu_in_second,
    glu_out_master,
    glu_out_first,
    glu_out_second,
    gain_master,
    gain_first,
    gain_second,
):
    batches, _, length, full = tokens.shape
    rows = batches * length
    groups = lax.axis_size("dp")
    narrow = lax.axis_size("mp")
    place = lax.axis_index("mp")
    own_rows = mixer_master.shape[1]
    channels = groups * own_rows
    part = full // narrow

    domain_ids = jnp.arange(NDOM, dtype=jnp.int32)
    member = (domains[..., 0][..., None] == domain_ids).astype(F32)
    live_counts = lengths.astype(F32)
    counts = lax.psum(jnp.sum(member * live_counts[..., None], axis=(0, 1)), "dp")
    seq_weight = jnp.sum(counts) / (NDOM * jnp.sum(member * counts, axis=-1))
    positions = jnp.arange(length, dtype=jnp.int32)
    token_weight = jnp.where(positions[None, :] < lengths[:, :1], seq_weight[:, :1], 0.0)
    token_weight = token_weight.reshape(rows, 1)

    gain_full = lax.all_gather(gain_master.astype(BF), ("dp", "mp"), axis=1, tiled=True).astype(F32)
    mixer_low = mixer_master.astype(BF)
    in_blocks = mixer_low[:3].reshape(3, own_rows, groups, narrow, own_rows)
    in_blocks = in_blocks.transpose(3, 0, 1, 2, 4).reshape(narrow, 3, own_rows, channels)
    in_rows = mp_swap(in_blocks).transpose(1, 0, 2, 3).reshape(3, narrow * own_rows, channels)
    mixer_in = lax.all_gather(in_rows, "dp", axis=1, tiled=True)
    mixer_out = lax.all_gather(mixer_low[3], "dp", axis=0, tiled=True)
    glu_low = jnp.concatenate([glu_in_master.astype(BF), glu_out_master.astype(BF).T[None]])
    glu_low, _ = lax.optimization_barrier((glu_low, mixer_in))
    glu = lax.all_gather(glu_low, "dp", axis=1, tiled=True)

    own_channels = lambda v: lax.dynamic_index_in_dim(
        v.reshape(groups, narrow, own_rows), place, 1, keepdims=False
    ).reshape(channels)
    bound = own_channels(lower_bound)
    state_gain = own_channels(gain_full[1])

    seq_in = tokens.reshape(rows, full).astype(F32)
    inverse_in = inverse_rms(seq_in)
    unit_in = seq_in * inverse_in
    normed_in = (unit_in * gain_full[0]).astype(BF)
    pre = jnp.einsum("td,kde->kte", normed_in, mixer_in, preferred_element_type=F32)
    pre = pre.reshape(3, batches, length, channels)
    states, raw, square = scan_forward(pre, bound, state_gain)
    square = mp_sum_wide(square.reshape(rows, 1))
    inverse_state = lax.rsqrt(square / full + EPSILON)
    mixed = jnp.dot(raw.reshape(rows, channels), mixer_out, preferred_element_type=F32)
    branch_mix = inverse_state * mp_sum(mixed)
    middle = seq_in + branch_mix
    inverse_mid = inverse_rms(middle)
    unit_mid = middle * inverse_mid
    normed_mid = (unit_mid * gain_full[2]).astype(BF)

    cot_full = mp_gather(cotangent.reshape(rows, part))
    back = cot_full.astype(F32) * token_weight
    back_low = back.astype(BF)
    pre_act = jnp.dot(normed_mid, glu[0], preferred_element_type=F32)
    pre_up = jnp.dot(normed_mid, glu[1], preferred_element_type=F32)
    grad_hidden = jnp.dot(back_low, glu[2], preferred_element_type=F32)
    act_sig = jax.nn.sigmoid(pre_act)
    act_part = pre_act * act_sig
    hidden = (act_part * pre_up).astype(BF)
    grad_act = (grad_hidden * pre_up * silu_slope(pre_act)).astype(BF)
    grad_up = (grad_hidden * act_part).astype(BF)
    across = (((1,), (1,)), ((), ()))
    down = (((0,), (0,)), ((), ()))
    dot = functools.partial(lax.dot_general, preferred_element_type=F32)
    grad_normed_part = dot(grad_act, glu[0], across) + dot(grad_up, glu[1], across)
    grad_normed = mp_sum(grad_normed_part)
    partial_out = dot(hidden, glu[2], across)
    glu_grad = jnp.stack(
        [
            dot(normed_mid, grad_act, down).astype(BF),
            dot(normed_mid, grad_up, down).astype(BF),
            dot(back_low, hidden, down).astype(BF),
        ]
    )
    glu_own = lax.psum_scatter(glu_grad, "dp", scatter_dimension=1, tiled=True).astype(F32)
    middle_own = lax.dynamic_slice_in_dim(middle, place * part, part, 1)
    layer_out = (middle_own + mp_scatter(partial_out)).astype(BF)

    gain_mid = jnp.sum(grad_normed * unit_mid, axis=0)
    scaled_mid = grad_normed * gain_full[2]
    grad_middle = back + inverse_mid * (
        scaled_mid - unit_mid * jnp.mean(scaled_mid * unit_mid, axis=-1, keepdims=True)
    )
    middle_low = grad_middle.astype(BF)
    state_mean = jnp.mean(middle_low.astype(F32) * branch_mix, axis=-1, keepdims=True)
    grad_gated = dot(middle_low, mixer_out, across)
    by_batch = lambda v: v.reshape(batches, length, v.shape[-1])
    grad_pre, gated_out, gain_state, pre_dot = scan_backward(
        pre, states, by_batch(grad_gated), by_batch(inverse_state), by_batch(state_mean), bound, state_gain
    )
    grad_pre = grad_pre.reshape(3, rows, channels)
    grad_mix_out = dot(gated_out.reshape(rows, channels), middle_low, down).astype(BF)
    grad_mix_in = jnp.einsum("td,kte->kde", normed_in, grad_pre, preferred_element_type=F32).astype(BF)
    in_own = lax.psum_scatter(grad_mix_in, "dp", scatter_dimension=1, tiled=True)
    out_own = lax.psum_scatter(grad_mix_out, "dp", scatter_dimension=0, tiled=True)
    in_own = mp_swap(in_own.reshape(3, narrow, own_rows, channels).transpose(1, 0, 2, 3))
    in_own = in_own.reshape(narrow, 3, own_rows, groups, own_rows).transpose(1, 2, 3, 0, 4)
    mixer_own = jnp.concatenate([in_own.reshape(3, own_rows, full), out_own[None]]).astype(F32)

    grad_normed_in = jnp.einsum("kte,kde->td", grad_pre, mixer_in, preferred_element_type=F32)
    grad_normed_in = mp_scatter(grad_normed_in)
    in_mean = mp_sum_wide(pre_dot.reshape(rows, 1)) / full
    own_features = lambda v: lax.dynamic_slice_in_dim(v, place * part, part, v.ndim - 1)
    unit_in_own = own_features(unit_in)
    gain_in = jnp.sum(grad_normed_in * unit_in_own, axis=0)
    grad_seq = own_features(grad_middle) + inverse_in * (
        grad_normed_in * own_features(gain_full[0]) - unit_in_own * in_mean
    )
    grad_tokens = grad_seq.astype(BF)

    zeros = jnp.zeros((full,), F32)
    gain_rows = jnp.stack(
        [
            lax.dynamic_update_slice_in_dim(zeros, gain_in, place * part, 0),
            lax.dynamic_update_slice_in_dim(
                zeros.reshape(groups, narrow, own_rows),
                jnp.sum(gain_state, axis=0).reshape(groups, 1, own_rows),
                place,
                1,
            ).reshape(full),
            lax.dynamic_update_slice_in_dim(zeros, own_features(gain_mid), place * part, 0),
        ]
    )
    gain_total = lax.psum(gain_rows, ("dp", "mp"))
    device = lax.axis_index("dp") * narrow + place
    gain_own = lax.dynamic_slice_in_dim(gain_total, device * own_rows, own_rows, 1)

    scale = 1.0 / (batches * groups * tokens.shape[1])
    count = STEP_NUMBER
    update = functools.partial(adamw_update, count=count)
    mixer_new = update(
        mixer_master, mixer_first, mixer_second, mixer_own * scale, rate=MATRIX_RATE, decay=DECAY_RATE
    )
    gain_new = update(
        gain_master, gain_first, gain_second, gain_own * scale, rate=GAIN_RATE, decay=0.0
    )
    glu_in_new = update(
        glu_in_master, glu_in_first, glu_in_second, glu_own[:2] * scale, rate=MATRIX_RATE, decay=DECAY_RATE
    )
    glu_out_new = update(
        glu_out_master, glu_out_first, glu_out_second, glu_own[2].T * scale, rate=MATRIX_RATE, decay=DECAY_RATE
    )
    return (
        layer_out.reshape(batches, 1, length, part),
        grad_tokens.reshape(batches, 1, length, part),
        *mixer_new,
        *glu_in_new,
        *glu_out_new,
        *gain_new,
    )


def solution(mesh):
    weights = (
        [P(None, ("dp", "mp"), None)] * 3
        + [P(None, "dp", "mp")] * 3
        + [P("mp", "dp")] * 3
        + [P(None, ("dp", "mp"))] * 3
    )
    in_specs = (
        P(None, "dp", None, None),
        P(None, "dp", None, "mp"),
        P(None, "dp"),
        P(None, "dp", None),
        P(),
        *weights,
    )
    out_specs = (P(None, "dp", None, "mp"), P(None, "dp", None, "mp"), *weights)
    return jax.shard_map(shards, mesh=mesh, in_specs=in_specs, out_specs=out_specs, check_vma=False)
```

```python
import functools

import jax
import jax.numpy as jnp
from jax import lax
from jax.experimental import pallas as pl
from jax.experimental.pallas import tpu as pltpu
from jax.sharding import PartitionSpec as P

NDOM = 8

EPSILON = 1e-06
BETA_ONE = 0.9
BETA_TWO = 0.95
ADAM_EPSILON = 1e-08
DECAY_RATE = 0.1
MATRIX_RATE = 0.06
GAIN_RATE = 0.5
STEP_NUMBER = 3.0

BF = jnp.bfloat16
F32 = jnp.float32
VMEM_LIMIT = 56 * 1024 * 1024


def inverse_rms(values):
    return lax.rsqrt(jnp.mean(values * values, axis=-1, keepdims=True) + EPSILON)


def silu_slope(values):
    sigma = jax.nn.sigmoid(values)
    return sigma * (1.0 + values * (1.0 - sigma))


def adamw_update(master, first, second, gradient, count, rate, decay):
    first_new = BETA_ONE * first + (1.0 - BETA_ONE) * gradient
    second_new = BETA_TWO * second + (1.0 - BETA_TWO) * gradient * gradient
    first_hat = first_new / (1.0 - BETA_ONE**count)
    second_hat = second_new / (1.0 - BETA_TWO**count)
    master_new = master - rate * (
        first_hat / (jnp.sqrt(second_hat) + ADAM_EPSILON) + decay * master
    )
    return (master_new, first_new, second_new)


def partner_swap(value):
    return lax.ppermute(value, "mp", [(0, 1), (1, 0)])


def mp_sum(part):
    low = part.astype(BF)
    if lax.axis_size("mp") == 2:
        return low.astype(F32) + partner_swap(low).astype(F32)
    return lax.psum(low.astype(F32), "mp")


def mp_sum_wide(part):
    if lax.axis_size("mp") == 2:
        return part + partner_swap(part)
    return lax.psum(part, "mp")


def mp_scatter(part):
    if lax.axis_size("mp") == 2:
        half = part.shape[1] // 2
        place = lax.axis_index("mp")
        own = lax.dynamic_slice_in_dim(part, place * half, half, 1)
        other = lax.dynamic_slice_in_dim(part, (1 - place) * half, half, 1)
        return own.astype(BF).astype(F32) + partner_swap(other.astype(BF)).astype(F32)
    return lax.psum_scatter(part.astype(BF), "mp", scatter_dimension=1, tiled=True).astype(F32)


def mp_swap(pieces):
    if lax.axis_size("mp") == 2:
        place = lax.axis_index("mp")
        own = lax.dynamic_index_in_dim(pieces, place, 0, keepdims=False)
        came = partner_swap(lax.dynamic_index_in_dim(pieces, 1 - place, 0, keepdims=False))
        first = place == 0
        return jnp.stack([jnp.where(first, own, came), jnp.where(first, came, own)])
    return lax.all_to_all(pieces, "mp", 0, 0, tiled=False)


def mp_gather(part):
    if lax.axis_size("mp") == 2:
        place = lax.axis_index("mp")
        came = partner_swap(part)
        first = place == 0
        return jnp.concatenate([jnp.where(first, part, came), jnp.where(first, came, part)], axis=1)
    return lax.all_gather(part, "mp", axis=1, tiled=True)


SUB_ROWS = 8
TILE_ROWS = 64


def channel_block(width):
    return 512 if width % 512 == 0 else width


def scan_rows(total, decay, carry):
    row = lax.broadcasted_iota(jnp.int32, total.shape, 0)
    shift = 1
    while shift < SUB_ROWS:
        keep = row >= shift
        total = total + decay * jnp.where(keep, pltpu.roll(total, shift, 0), 0.0)
        decay = decay * jnp.where(keep, pltpu.roll(decay, shift, 0), 1.0)
        shift *= 2
    return total + decay * carry


def scan_rows_back(total, decay, carry):
    row = lax.broadcasted_iota(jnp.int32, total.shape, 0)
    shift = 1
    while shift < SUB_ROWS:
        keep = row < SUB_ROWS - shift
        total = total + decay * jnp.where(keep, pltpu.roll(total, SUB_ROWS - shift, 0), 0.0)
        decay = decay * jnp.where(keep, pltpu.roll(decay, SUB_ROWS - shift, 0), 1.0)
        shift *= 2
    return total + decay * carry


def scan_forward_kernel(pre_ref, bound_ref, gain_ref, states_ref, raw_ref, square_ref):
    length, width = states_ref.shape[1], states_ref.shape[2]
    bound = bound_ref[...]
    gain = gain_ref[...]
    first_block = pl.program_id(1) == 0

    def step(index, carry):
        rows = pl.ds(pl.multiple_of(index * TILE_ROWS, TILE_ROWS), TILE_ROWS)
        forget = bound + (1.0 - bound) * jax.nn.sigmoid(pre_ref[1, 0, rows, :])
        total = (1.0 - forget) * jax.nn.silu(pre_ref[0, 0, rows, :])
        parts = []
        for low in range(0, TILE_ROWS, SUB_ROWS):
            part = scan_rows(total[low : low + SUB_ROWS], forget[low : low + SUB_ROWS], carry)
            carry = part[SUB_ROWS - 1 : SUB_ROWS]
            parts.append(part)
        states = jnp.concatenate(parts)
        states_ref[0, rows, :] = states
        raw = states * gain * jax.nn.silu(pre_ref[2, 0, rows, :])
        raw_ref[0, rows, :] = raw.astype(raw_ref.dtype)
        square = jnp.sum(states * states, axis=-1, keepdims=True)
        square_ref[0, rows, :] = square + jnp.where(first_block, 0.0, square_ref[0, rows, :])
        return carry

    lax.fori_loop(0, length // TILE_ROWS, step, jnp.zeros((1, width), F32))


def scan_forward(pre, bound, gain):
    _, batches, length, width = pre.shape
    block = channel_block(width)
    return pl.pallas_call(
        scan_forward_kernel,
        grid=(batches, width // block),
        in_specs=[
            pl.BlockSpec((3, 1, length, block), lambda b, c: (0, b, 0, c)),
            pl.BlockSpec((1, block), lambda b, c: (0, c)),
            pl.BlockSpec((1, block), lambda b, c: (0, c)),
        ],
        out_specs=[
            pl.BlockSpec((1, length, block), lambda b, c: (b, 0, c)),
            pl.BlockSpec((1, length, block), lambda b, c: (b, 0, c)),
            pl.BlockSpec((1, length, 1), lambda b, c: (b, 0, 0)),
        ],
        out_shape=[
            jax.ShapeDtypeStruct((batches, length, width), F32),
            jax.ShapeDtypeStruct((batches, length, width), BF),
            jax.ShapeDtypeStruct((batches, length, 1), F32),
        ],
        compiler_params=pltpu.CompilerParams(vmem_limit_bytes=VMEM_LIMIT),
        cost_estimate=pl.CostEstimate(
            flops=batches * length * width * 40,
            bytes_accessed=batches * length * width * 18,
            transcendentals=batches * length * width * 3,
        ),
    )(pre, bound[None], gain[None])


def scan_backward_kernel(
    pre_ref, states_ref, gated_ref, inverse_ref, mean_ref, bound_ref, gain_ref,
    grad_ref, out_ref, gain_grad_ref, dot_ref,
):
    length, width = states_ref.shape[1], states_ref.shape[2]
    bound = bound_ref[...]
    gain = gain_ref[...]
    first_block = pl.program_id(1) == 0
    row = lax.broadcasted_iota(jnp.int32, (TILE_ROWS, width), 0)
    tiles = length // TILE_ROWS

    def step(index, carry):
        carried_next, forget_next, gain_sum = carry
        place = tiles - 1 - index
        rows = pl.ds(pl.multiple_of(place * TILE_ROWS, TILE_ROWS), TILE_ROWS)
        pre_input = pre_ref[0, 0, rows, :]
        pre_forget = pre_ref[1, 0, rows, :]
        pre_gate = pre_ref[2, 0, rows, :]
        states = states_ref[0, rows, :]
        inverse = inverse_ref[0, rows, :]
        grad_gated = gated_ref[0, rows, :]
        unit = states * inverse
        gate_sig = jax.nn.sigmoid(pre_gate)
        gate = pre_gate * gate_sig
        out_ref[0, rows, :] = (unit * gain * gate).astype(out_ref.dtype)
        gain_sum = gain_sum + grad_gated * unit * gate
        scaled = grad_gated * gain
        grad_gate = (scaled * unit * (gate_sig * (1.0 + pre_gate * (1.0 - gate_sig)))).astype(BF)
        grad_ref[2, 0, rows, :] = grad_gate
        total = inverse * (scaled * gate - unit * mean_ref[0, rows, :])
        sigma = jax.nn.sigmoid(pre_forget)
        forget = bound + (1.0 - bound) * sigma
        decay = jnp.where(row == TILE_ROWS - 1, forget_next, pltpu.roll(forget, TILE_ROWS - 1, 0))
        parts = []
        for low in range(TILE_ROWS - SUB_ROWS, -1, -SUB_ROWS):
            part = scan_rows_back(
                total[low : low + SUB_ROWS], decay[low : low + SUB_ROWS], carried_next
            )
            carried_next = part[0:1]
            parts.insert(0, part)
        carried = jnp.concatenate(parts)
        before_rows = pl.ds(
            pl.multiple_of(jnp.maximum(place - 1, 0) * TILE_ROWS, TILE_ROWS), TILE_ROWS
        )
        before = states_ref[0, before_rows, :][TILE_ROWS - 1 : TILE_ROWS, :]
        before = jnp.where(place == 0, 0.0, before)
        earlier = jnp.where(row == 0, before, pltpu.roll(states, 1, 0))
        input_sig = jax.nn.sigmoid(pre_input)
        fresh = pre_input * input_sig
        slope = input_sig * (1.0 + pre_input * (1.0 - input_sig))
        grad_input = (carried * (1.0 - forget) * slope).astype(BF)
        grad_forget = (
            carried * (earlier - fresh) * (1.0 - bound) * sigma * (1.0 - sigma)
        ).astype(BF)
        grad_ref[0, 0, rows, :] = grad_input
        grad_ref[1, 0, rows, :] = grad_forget
        dots = (
            grad_input.astype(F32) * pre_input
            + grad_forget.astype(F32) * pre_forget
            + grad_gate.astype(F32) * pre_gate
        )
        dot = jnp.sum(dots, axis=-1, keepdims=True)
        dot_ref[0, rows, :] = dot + jnp.where(first_block, 0.0, dot_ref[0, rows, :])
        return carried_next, forget[0:1, :], gain_sum

    zero = jnp.zeros((1, width), F32)
    _, _, gain_sum = lax.fori_loop(
        0, tiles, step, (zero, zero, jnp.zeros((TILE_ROWS, width), F32))
    )
    gain_grad_ref[0] = jnp.sum(gain_sum, axis=0, keepdims=True)


def scan_backward(pre, states, grad_gated, inverse, mean, bound, gain):
    _, batches, length, width = pre.shape
    block = channel_block(width)
    whole = pl.BlockSpec((1, length, block), lambda b, c: (b, 0, c))
    column = pl.BlockSpec((1, length, 1), lambda b, c: (b, 0, 0))
    line = pl.BlockSpec((1, block), lambda b, c: (0, c))
    three = pl.BlockSpec((3, 1, length, block), lambda b, c: (0, b, 0, c))
    return pl.pallas_call(
        scan_backward_kernel,
        grid=(batches, width // block),
        in_specs=[three, whole, whole, column, column, line, line],
        out_specs=[
            three,
            whole,
            pl.BlockSpec((1, 1, block), lambda b, c: (b, 0, c)),
            column,
        ],
        out_shape=[
            jax.ShapeDtypeStruct((3, batches, length, width), BF),
            jax.ShapeDtypeStruct((batches, length, width), BF),
            jax.ShapeDtypeStruct((batches, 1, width), F32),
            jax.ShapeDtypeStruct((batches, length, 1), F32),
        ],
        compiler_params=pltpu.CompilerParams(vmem_limit_bytes=VMEM_LIMIT),
        cost_estimate=pl.CostEstimate(
            flops=batches * length * width * 80,
            bytes_accessed=batches * length * width * 28,
            transcendentals=batches * length * width * 3,
        ),
    )(pre, states, grad_gated, inverse, mean, bound[None], gain[None])


MESH_ID = pl.DeviceIdType.MESH
DEPTH = 4
LANES = 256
Z_LAG = 4


def device_place():
    dp = lax.axis_index("dp")
    return dp // 4, lax.rem(dp // 2, 2), lax.rem(dp, 2)


def device_at(z, x, core):
    return (z * 4 + x * 2 + core, lax.axis_index("mp"))


def scatter_kernel(compute, chunks, n_in, *refs):
    ins, out_ref = refs[:n_in], refs[n_in]
    (own, core_out, core_in, keep, x_out, x_in, sums, mine, z_out, z_in,
     core_send, core_recv, x_send, x_recv, z_send, z_recv) = refs[n_in + 1 :]
    z, x, core = device_place()
    step = pl.program_id(0)

    def core_copy(p):
        return pltpu.make_async_remote_copy(
            core_out.at[lax.rem(p, 2)], core_in.at[lax.rem(p, 4)],
            core_send.at[lax.rem(p, 2)], core_recv.at[lax.rem(p, 4)],
            device_id=device_at(z, x, 1 - core), device_id_type=MESH_ID)

    def x_copy(p):
        return pltpu.make_async_remote_copy(
            x_out.at[lax.rem(p, 2)], x_in.at[lax.rem(p, 4)],
            x_send.at[lax.rem(p, 2)], x_recv.at[lax.rem(p, 4)],
            device_id=device_at(z, 1 - x, core), device_id_type=MESH_ID)

    def z_copy(p, hop):
        return pltpu.make_async_remote_copy(
            z_out.at[lax.rem(p, 4), hop - 1], z_in.at[lax.rem(p, 8), hop - 1],
            z_send.at[lax.rem(p, 4), hop - 1], z_recv.at[lax.rem(p, 8), hop - 1],
            device_id=device_at(lax.rem(z + hop, DEPTH), x, core), device_id_type=MESH_ID)

    @pl.when(step == 0)
    def _():
        barrier = pltpu.get_barrier_semaphore()
        pl.semaphore_signal(barrier, 1, device_id=device_at(z, x, 1 - core), device_id_type=MESH_ID)
        pl.semaphore_signal(barrier, 1, device_id=device_at(z, 1 - x, core), device_id_type=MESH_ID)
        for hop in range(1, DEPTH):
            pl.semaphore_signal(
                barrier, 1, device_id=device_at(lax.rem(z + hop, DEPTH), x, core), device_id_type=MESH_ID)
        pl.semaphore_wait(barrier, DEPTH + 1)

    @pl.when(step < chunks)
    def _():
        @pl.when(step >= 2)
        def _():
            core_copy(step - 2).wait_send()

        core_out[lax.rem(step, 2)] = compute(step, 1 - core, *ins).astype(BF)
        core_copy(step).start()
        own[lax.rem(step, 2)] = compute(step, core, *ins)

    @pl.when((step >= 1) & (step < chunks + 1))
    def _():
        p = step - 1
        core_copy(p).wait_recv()

        @pl.when(p >= 2)
        def _():
            x_copy(p - 2).wait_send()

        two, four = lax.rem(p, 2), lax.rem(p, 4)
        x_out[two] = (own[two, :, 1 - x] + core_in[four, :, 1 - x].astype(F32)).astype(BF)
        x_copy(p).start()
        keep[two] = own[two, :, x] + core_in[four, :, x].astype(F32)

    @pl.when((step >= 2) & (step < chunks + 2))
    def _():
        p = step - 2
        x_copy(p).wait_recv()
        two, four = lax.rem(p, 2), lax.rem(p, 4)
        sums[...] = keep[two] + x_in[four].astype(F32)
        for hop in range(1, DEPTH):
            @pl.when(p >= 4)
            def _():
                z_copy(p - 4, hop).wait_send()

            z_out[four, hop - 1] = sums[lax.rem(z + hop, DEPTH)].astype(BF)
            z_copy(p, hop).start()
        mine[four] = sums[z]

    @pl.when(step >= Z_LAG)
    def _():
        p = step - Z_LAG
        for hop in range(1, DEPTH):
            z_copy(p, hop).wait_recv()
        got = z_in.at[lax.rem(p, 8)]
        total = mine[lax.rem(p, 4)] + got[0].astype(F32) + got[1].astype(F32) + got[2].astype(F32)
        out_ref[0] = total

    @pl.when(step == chunks + Z_LAG - 1)
    def _():
        for p in range(max(chunks - 2, 0), chunks):
            core_copy(p).wait_send()
            x_copy(p).wait_send()
        for p in range(max(chunks - 4, 0), chunks):
            for hop in range(1, DEPTH):
                z_copy(p, hop).wait_send()


def scatter_call(compute, chunks, block, operands, in_specs, collective, flops):
    rows, lanes = block
    quad = (DEPTH, 2, rows, lanes)
    line = (DEPTH, rows, lanes)
    return pl.pallas_call(
        functools.partial(scatter_kernel, compute, chunks, len(operands)),
        grid=(chunks + Z_LAG,),
        in_specs=in_specs,
        out_specs=pl.BlockSpec((1, rows, lanes), lambda q: (jnp.maximum(q - Z_LAG, 0), 0, 0)),
        out_shape=jax.ShapeDtypeStruct((chunks, rows, lanes), F32),
        scratch_shapes=[
            pltpu.VMEM((2, *quad), F32),
            pltpu.VMEM((2, *quad), BF),
            pltpu.VMEM((4, *quad), BF),
            pltpu.VMEM((2, *line), F32),
            pltpu.VMEM((2, *line), BF),
            pltpu.VMEM((4, *line), BF),
            pltpu.VMEM(line, F32),
            pltpu.VMEM((4, rows, lanes), F32),
            pltpu.VMEM((4, DEPTH - 1, rows, lanes), BF),
            pltpu.VMEM((8, DEPTH - 1, rows, lanes), BF),
            pltpu.SemaphoreType.DMA((2,)),
            pltpu.SemaphoreType.DMA((4,)),
            pltpu.SemaphoreType.DMA((2,)),
            pltpu.SemaphoreType.DMA((4,)),
            pltpu.SemaphoreType.DMA((4, DEPTH - 1)),
            pltpu.SemaphoreType.DMA((8, DEPTH - 1)),
        ],
        compiler_params=pltpu.CompilerParams(
            collective_id=collective, has_side_effects=True, vmem_limit_bytes=VMEM_LIMIT),
        cost_estimate=pl.CostEstimate(flops=flops, bytes_accessed=flops // 500, transcendentals=0),
    )(*operands)


def glu_scatter(left, right, collective):
    _, full, tokens = left.shape
    hidden = right.shape[2]
    across = hidden // LANES
    rows = full // 16

    def compute(q, core, left_ref, right_ref):
        side = left_ref[jnp.minimum(q, 3 * across - 1) // (2 * across), :, :, core]
        product = jnp.dot(side.reshape(full // 2, tokens), right_ref[0], preferred_element_type=F32)
        return product.reshape(DEPTH, 2, rows, LANES)

    chunks = 3 * across
    spot = lambda q: jnp.minimum(q, chunks - 1)
    out = scatter_call(
        compute, chunks, (rows, LANES),
        (left.reshape(2, DEPTH, 2, 2, rows, tokens), right),
        [
            pl.BlockSpec((2, DEPTH, 2, 2, rows, tokens), lambda q: (0, 0, 0, 0, 0, 0), pipeline_mode=pl.Buffered(1)),
            pl.BlockSpec((1, tokens, LANES), lambda q: (spot(q) // across, 0, lax.rem(spot(q), across))),
        ],
        collective, 2 * 3 * full * tokens * hidden)
    return out.reshape(3, across, rows, LANES).transpose(0, 2, 1, 3).reshape(3, rows, hidden)


def mixer_scatter(left_in, right_in, left_out, right_out, collective):
    full, tokens = left_in.shape
    channels = right_in.shape[2]
    rows = full // 16
    half = channels // 16
    across = channels // LANES
    across_out = full // (2 * LANES)
    inside = 3 * across
    chunks = inside + across_out

    def compute(q, core, left_ref, right_ref, left_out_ref, right_out_ref):
        def first():
            side = left_ref[:, :, core].reshape(full // 2, tokens)
            product = jnp.dot(side, right_ref[0], preferred_element_type=F32)
            return product.reshape(DEPTH, 2, rows, LANES)

        def second():
            side = left_out_ref[:, :, core].reshape(channels // 2, tokens)
            parts = [
                jnp.dot(side, right_out_ref[:, at : at + LANES], preferred_element_type=F32).reshape(
                    DEPTH, 2, half, LANES)
                for at in (0, LANES)
            ]
            return jnp.concatenate(parts, axis=2)

        return lax.cond(q < inside, first, second)

    spot = lambda q: jnp.minimum(q, inside - 1)
    spot_out = lambda q: jnp.clip(q - inside, 0, across_out - 1)
    out = scatter_call(
        compute, chunks, (rows, LANES),
        (left_in.reshape(DEPTH, 2, 2, rows, tokens), right_in,
         left_out.reshape(DEPTH, 2, 2, half, tokens), right_out),
        [
            pl.BlockSpec((DEPTH, 2, 2, rows, tokens), lambda q: (0, 0, 0, 0, 0), pipeline_mode=pl.Buffered(1)),
            pl.BlockSpec((1, tokens, LANES), lambda q: (spot(q) // across, 0, lax.rem(spot(q), across))),
            pl.BlockSpec((DEPTH, 2, 2, half, tokens), lambda q: (0, 0, 0, 0, 0), pipeline_mode=pl.Buffered(1)),
            pl.BlockSpec((tokens, 2 * LANES), lambda q: (0, spot_out(q))),
        ],
        collective, 2 * tokens * (3 * full * channels + channels * full))
    first = out[:inside].reshape(3, across, rows, LANES).transpose(0, 2, 1, 3).reshape(3, rows, channels)
    second = out[inside:].reshape(across_out, 2, half, LANES).transpose(2, 0, 1, 3).reshape(half, full)
    return first, second


ITEMS = 4


def gather_kernel(in_ref, out_ref, small_ref, all_in, all_out, all_small, right_send, left_send,
                  z_recv, x_send, x_recv, core_send, core_recv, y_send, y_recv, local_sem):
    z, x, core = device_place()
    mp = lax.axis_index("mp")
    barrier = pltpu.get_barrier_semaphore()
    right, left = lax.rem(z + 1, DEPTH), lax.rem(z + DEPTH - 1, DEPTH)
    dp = lax.axis_index("dp")
    for target in (
        device_at(right, x, core), device_at(left, x, core), device_at(z, 1 - x, core),
        device_at(z, x, 1 - core), (dp, 1 - mp),
    ):
        pl.semaphore_signal(barrier, 1, device_id=target, device_id_type=MESH_ID)
    pl.semaphore_wait(barrier, 5)

    def spot(item, zs, xs, cs, side=None):
        if item == 0:
            return all_in.at[:, zs, xs, cs, mp if side is None else side]
        if item == 1:
            return all_out.at[zs, xs, cs]
        if item == 2:
            return all_in.at[:, zs, xs, cs, 1 - mp]
        return all_small.at[zs, xs, cs]

    def own(item):
        if item == 0:
            return in_ref.at[mp]
        if item == 1:
            return out_ref
        return spot(item, z, x, core)

    def copy(item, zs, xs, target, send, recv, source=None):
        return pltpu.make_async_remote_copy(
            spot(item, zs, xs, core) if source is None else source, spot(item, zs, xs, core),
            send, recv, device_id=target, device_id_type=MESH_ID)

    def right_copy(item, zs, source=None):
        return copy(item, zs, x, device_at(right, x, core), right_send.at[zs, item], z_recv.at[zs, item], source)

    def left_copy(item, zs, source=None):
        return copy(item, zs, x, device_at(left, x, core), left_send.at[zs, item], z_recv.at[zs, item], source)

    def x_copy(item, zs, source=None):
        return copy(item, zs, x, device_at(z, 1 - x, core), x_send.at[zs, item], x_recv.at[zs, item], source)

    def core_copy(item, zs, xs, source=None):
        return copy(item, zs, xs, device_at(z, x, 1 - core), core_send.at[zs, xs, item], core_recv.at[zs, xs, item], source)

    y_copies = [
        pltpu.make_async_remote_copy(
            in_ref.at[1 - mp], all_in.at[:, z, x, core, mp], y_send.at[0], y_recv.at[0],
            device_id=(dp, 1 - mp), device_id_type=MESH_ID),
        pltpu.make_async_remote_copy(
            small_ref, all_small.at[z, x, core, mp], y_send.at[1], y_recv.at[1],
            device_id=(dp, 1 - mp), device_id_type=MESH_ID),
    ]
    locals_ = [
        pltpu.make_async_copy(in_ref.at[mp], spot(0, z, x, core), local_sem.at[0]),
        pltpu.make_async_copy(out_ref, spot(1, z, x, core), local_sem.at[1]),
        pltpu.make_async_copy(small_ref, all_small.at[z, x, core, mp], local_sem.at[2]),
    ]
    for one in y_copies:
        one.start()
    locals_[2].start()

    for item in range(ITEMS):
        if item == 2:
            y_copies[0].wait_recv()
        if item == 3:
            y_copies[1].wait_recv()
            locals_[2].wait()
        source = own(item)

        @pl.when(z < DEPTH - 1)
        def _():
            right_copy(item, z, source).start()

        @pl.when(z > 0)
        def _():
            left_copy(item, z, source).start()

        x_copy(item, z, source).start()
        core_copy(item, z, x, source).start()
    locals_[0].start()
    locals_[1].start()

    def from_x(item, zs):
        pltpu.make_async_remote_copy(
            spot(item, zs, 1 - x, core), spot(item, zs, 1 - x, core), x_send.at[zs, item],
            x_recv.at[zs, item], device_id=device_at(z, 1 - x, core), device_id_type=MESH_ID).wait_recv()
        core_copy(item, zs, 1 - x).start()

    for hop in range(1, DEPTH + 1):
        for item in range(ITEMS):
            if hop < DEPTH:
                @pl.when(z >= hop)
                def _():
                    zs = z - hop
                    right_copy(item, zs).wait_recv()

                    @pl.when(z < DEPTH - 1)
                    def _():
                        right_copy(item, zs).start()

                    x_copy(item, zs).start()
                    core_copy(item, zs, x).start()

                @pl.when(z + hop < DEPTH)
                def _():
                    zs = z + hop
                    left_copy(item, zs).wait_recv()

                    @pl.when(z > 0)
                    def _():
                        left_copy(item, zs).start()

                    x_copy(item, zs).start()
                    core_copy(item, zs, x).start()
            if hop == 1:
                from_x(item, z)
            else:
                @pl.when(z >= hop - 1)
                def _():
                    from_x(item, z - (hop - 1))

                @pl.when(z + hop - 1 < DEPTH)
                def _():
                    from_x(item, z + (hop - 1))

    for item in range(ITEMS):
        for zs in range(DEPTH):
            @pl.when((z >= zs) & (z < DEPTH - 1))
            def _():
                right_copy(item, zs).wait_send()

            @pl.when((z <= zs) & (z > 0))
            def _():
                left_copy(item, zs).wait_send()

            x_copy(item, zs).wait_send()
            for xs in range(2):
                core_copy(item, zs, xs).wait()
    for one in y_copies:
        one.wait_send()
    locals_[0].wait()
    locals_[1].wait()


def gather_call(in_blocks, out_rows, small, collective):
    _, three, own_rows, channels = in_blocks.shape
    full = out_rows.shape[1]
    dma = pltpu.SemaphoreType.DMA
    any_space = pl.BlockSpec(memory_space=pl.ANY)
    return pl.pallas_call(
        gather_kernel,
        in_specs=[any_space] * 3,
        out_specs=[any_space] * 3,
        out_shape=[
            jax.ShapeDtypeStruct((three, DEPTH, 2, 2, 2, own_rows, channels), BF),
            jax.ShapeDtypeStruct((DEPTH, 2, 2, own_rows, full), BF),
            jax.ShapeDtypeStruct((DEPTH, 2, 2, 2, *small.shape), F32),
        ],
        scratch_shapes=[
            dma((DEPTH, ITEMS)), dma((DEPTH, ITEMS)), dma((DEPTH, ITEMS)), dma((DEPTH, ITEMS)),
            dma((DEPTH, ITEMS)), dma((DEPTH, 2, ITEMS)), dma((DEPTH, 2, ITEMS)), dma((2,)), dma((2,)), dma((3,)),
        ],
        compiler_params=pltpu.CompilerParams(collective_id=collective, has_side_effects=True),
        cost_estimate=pl.CostEstimate(flops=0, bytes_accessed=300_000_000, transcendentals=0),
    )(in_blocks, out_rows, small)


def shards(
    tokens,
    cotangent,
    lengths,
    domains,
    lower_bound,
    mixer_master,
    mixer_first,
    mixer_second,
    glu_in_master,
    glu_in_first,
    glu_in_second,
    glu_out_master,
    glu_out_first,
    glu_out_second,
    gain_master,
    gain_first,
    gain_second,
):
    batches, _, length, full = tokens.shape
    rows = batches * length
    groups = lax.axis_size("dp")
    narrow = lax.axis_size("mp")
    place = lax.axis_index("mp")
    own_rows = mixer_master.shape[1]
    channels = groups * own_rows
    part = full // narrow
    quick = groups == 16 and narrow == 2

    domain_ids = jnp.arange(NDOM, dtype=jnp.int32)
    member = (domains[..., 0][..., None] == domain_ids).astype(F32)
    live_counts = lengths.astype(F32)
    counts = jnp.sum(member * live_counts[..., None], axis=(0, 1))
    gain_low = gain_master.astype(BF)
    mixer_low = mixer_master.astype(BF)
    in_blocks = mixer_low[:3].reshape(3, own_rows, groups, narrow, own_rows)
    in_blocks = in_blocks.transpose(3, 0, 1, 2, 4).reshape(narrow, 3, own_rows, channels)
    if quick:
        small = jnp.zeros((8, 128), F32)
        small = small.at[:3, :own_rows].set(gain_low.astype(F32)).at[3, :NDOM].set(counts)
        mixer_in, mixer_out, small = gather_call(in_blocks, mixer_low[3], small, 2)
        mixer_in = mixer_in.reshape(3, full, channels)
        mixer_out = mixer_out.reshape(channels, full)
        small = small.reshape(groups, narrow, 8, 128)
        gain_full = small[:, :, :3, :own_rows].transpose(2, 0, 1, 3).reshape(3, full)
        counts = jnp.sum(small[:, 0, 3, :NDOM], axis=0)
    else:
        gain_full = lax.all_gather(gain_low, ("dp", "mp"), axis=1, tiled=True).astype(F32)
        in_rows = mp_swap(in_blocks).transpose(1, 0, 2, 3).reshape(3, narrow * own_rows, channels)
        mixer_in = lax.all_gather(in_rows, "dp", axis=1, tiled=True)
        mixer_out = lax.all_gather(mixer_low[3], "dp", axis=0, tiled=True)
        counts = lax.psum(counts, "dp")
    glu_low = jnp.concatenate([glu_in_master.astype(BF), glu_out_master.astype(BF).T[None]])
    glu_low, mixer_in = lax.optimization_barrier((glu_low, mixer_in))
    glu = lax.all_gather(glu_low, "dp", axis=1, tiled=True)

    seq_weight = jnp.sum(counts) / (NDOM * jnp.sum(member * counts, axis=-1))
    positions = jnp.arange(length, dtype=jnp.int32)
    token_weight = jnp.where(positions[None, :] < lengths[:, :1], seq_weight[:, :1], 0.0)
    token_weight = token_weight.reshape(rows, 1)

    own_channels = lambda v: lax.dynamic_index_in_dim(
        v.reshape(groups, narrow, own_rows), place, 1, keepdims=False
    ).reshape(channels)
    bound = own_channels(lower_bound)
    state_gain = own_channels(gain_full[1])

    seq_in = tokens.reshape(rows, full).astype(F32)
    inverse_in = inverse_rms(seq_in)
    unit_in = seq_in * inverse_in
    normed_in = (unit_in * gain_full[0]).astype(BF)
    pre = jnp.einsum("td,kde->kte", normed_in, mixer_in, preferred_element_type=F32)
    pre = pre.reshape(3, batches, length, channels)
    states, raw, square = scan_forward(pre, bound, state_gain)
    square = mp_sum_wide(square.reshape(rows, 1))
    inverse_state = lax.rsqrt(square / full + EPSILON)
    mixed = jnp.dot(raw.reshape(rows, channels), mixer_out, preferred_element_type=F32)
    branch_mix = inverse_state * mp_sum(mixed)
    middle = seq_in + branch_mix
    inverse_mid = inverse_rms(middle)
    unit_mid = middle * inverse_mid
    normed_mid = (unit_mid * gain_full[2]).astype(BF)

    cot_full = mp_gather(cotangent.reshape(rows, part))
    back = cot_full.astype(F32) * token_weight
    back_low = back.astype(BF)
    pre_act = jnp.dot(normed_mid, glu[0], preferred_element_type=F32)
    pre_up = jnp.dot(normed_mid, glu[1], preferred_element_type=F32)
    grad_hidden = jnp.dot(back_low, glu[2], preferred_element_type=F32)
    act_sig = jax.nn.sigmoid(pre_act)
    act_part = pre_act * act_sig
    hidden = (act_part * pre_up).astype(BF)
    grad_act = (grad_hidden * pre_up * silu_slope(pre_act)).astype(BF)
    grad_up = (grad_hidden * act_part).astype(BF)
    across = (((1,), (1,)), ((), ()))
    down = (((0,), (0,)), ((), ()))
    dot = functools.partial(lax.dot_general, preferred_element_type=F32)
    grad_normed_part = dot(grad_act, glu[0], across) + dot(grad_up, glu[1], across)
    grad_normed_low = grad_normed_part.astype(BF)
    grad_normed_came = partner_swap(grad_normed_low) if quick else None
    partial_out = dot(hidden, glu[2], across)
    rights = jnp.stack([grad_act, grad_up, hidden])
    if quick:
        lefts = jnp.stack([normed_mid.T, back_low.T])
        lefts, rights, grad_normed_low = lax.optimization_barrier((lefts, rights, grad_normed_low))
        glu_own = glu_scatter(lefts, rights, 0)
        glu_own, grad_normed_came = lax.optimization_barrier((glu_own, grad_normed_came))
        grad_normed = grad_normed_low.astype(F32) + grad_normed_came.astype(F32)
    else:
        grad_normed = mp_sum(grad_normed_part)
        glu_grad = jnp.stack(
            [dot(normed_mid, grad_act, down), dot(normed_mid, grad_up, down), dot(back_low, hidden, down)]
        ).astype(BF)
        glu_own = lax.psum_scatter(glu_grad, "dp", scatter_dimension=1, tiled=True).astype(F32)
    middle_own = lax.dynamic_slice_in_dim(middle, place * part, part, 1)
    layer_out = (middle_own + mp_scatter(partial_out)).astype(BF)

    gain_mid = jnp.sum(grad_normed * unit_mid, axis=0)
    scaled_mid = grad_normed * gain_full[2]
    grad_middle = back + inverse_mid * (
        scaled_mid - unit_mid * jnp.mean(scaled_mid * unit_mid, axis=-1, keepdims=True)
    )
    middle_low = grad_middle.astype(BF)
    state_mean = jnp.mean(middle_low.astype(F32) * branch_mix, axis=-1, keepdims=True)
    grad_gated = dot(middle_low, mixer_out, across)
    by_batch = lambda v: v.reshape(batches, length, v.shape[-1])
    grad_pre, gated_out, gain_state, pre_dot = scan_backward(
        pre, states, by_batch(grad_gated), by_batch(inverse_state), by_batch(state_mean), bound, state_gain
    )
    grad_pre = grad_pre.reshape(3, rows, channels)
    gated_out = gated_out.reshape(rows, channels)
    if quick:
        in_own, out_own = mixer_scatter(normed_in.T, grad_pre, gated_out.T, middle_low, 1)
        in_own = in_own.astype(BF)
    else:
        grad_mix_out = dot(gated_out, middle_low, down).astype(BF)
        grad_mix_in = jnp.einsum("td,kte->kde", normed_in, grad_pre, preferred_element_type=F32)
        in_own = lax.psum_scatter(grad_mix_in.astype(BF), "dp", scatter_dimension=1, tiled=True)
        out_own = lax.psum_scatter(grad_mix_out, "dp", scatter_dimension=0, tiled=True)
    in_own = mp_swap(in_own.reshape(3, narrow, own_rows, channels).transpose(1, 0, 2, 3))
    in_own = in_own.reshape(narrow, 3, own_rows, groups, own_rows).transpose(1, 2, 3, 0, 4)
    mixer_own = jnp.concatenate(
        [in_own.reshape(3, own_rows, full).astype(F32), out_own[None].astype(F32)]
    )

    grad_normed_in = jnp.einsum("kte,kde->td", grad_pre, mixer_in, preferred_element_type=F32)
    grad_normed_in = mp_scatter(grad_normed_in)
    in_mean = mp_sum_wide(pre_dot.reshape(rows, 1)) / full
    own_features = lambda v: lax.dynamic_slice_in_dim(v, place * part, part, v.ndim - 1)
    unit_in_own = own_features(unit_in)
    gain_in = jnp.sum(grad_normed_in * unit_in_own, axis=0)
    grad_seq = own_features(grad_middle) + inverse_in * (
        grad_normed_in * own_features(gain_full[0]) - unit_in_own * in_mean
    )
    grad_tokens = grad_seq.astype(BF)

    zeros = jnp.zeros((full,), F32)
    gain_rows = jnp.stack(
        [
            lax.dynamic_update_slice_in_dim(zeros, gain_in, place * part, 0),
            lax.dynamic_update_slice_in_dim(
                zeros.reshape(groups, narrow, own_rows),
                jnp.sum(gain_state, axis=0).reshape(groups, 1, own_rows),
                place,
                1,
            ).reshape(full),
            lax.dynamic_update_slice_in_dim(zeros, own_features(gain_mid), place * part, 0),
        ]
    )
    gain_total = lax.psum(gain_rows, ("dp", "mp"))
    device = lax.axis_index("dp") * narrow + place
    gain_own = lax.dynamic_slice_in_dim(gain_total, device * own_rows, own_rows, 1)

    scale = 1.0 / (batches * groups * tokens.shape[1])
    count = STEP_NUMBER
    update = functools.partial(adamw_update, count=count)
    mixer_new = update(
        mixer_master, mixer_first, mixer_second, mixer_own * scale, rate=MATRIX_RATE, decay=DECAY_RATE
    )
    gain_new = update(
        gain_master, gain_first, gain_second, gain_own * scale, rate=GAIN_RATE, decay=0.0
    )
    glu_in_new = update(
        glu_in_master, glu_in_first, glu_in_second, glu_own[:2] * scale, rate=MATRIX_RATE, decay=DECAY_RATE
    )
    glu_out_new = update(
        glu_out_master, glu_out_first, glu_out_second, glu_own[2].T * scale, rate=MATRIX_RATE, decay=DECAY_RATE
    )
    return (
        layer_out.reshape(batches, 1, length, part),
        grad_tokens.reshape(batches, 1, length, part),
        *mixer_new,
        *glu_in_new,
        *glu_out_new,
        *gain_new,
    )


def solution(mesh):
    weights = (
        [P(None, ("dp", "mp"), None)] * 3
        + [P(None, "dp", "mp")] * 3
        + [P("mp", "dp")] * 3
        + [P(None, ("dp", "mp"))] * 3
    )
    in_specs = (
        P(None, "dp", None, None),
        P(None, "dp", None, "mp"),
        P(None, "dp"),
        P(None, "dp", None),
        P(),
        *weights,
    )
    out_specs = (P(None, "dp", None, "mp"), P(None, "dp", None, "mp"), *weights)
    return jax.shard_map(shards, mesh=mesh, in_specs=in_specs, out_specs=out_specs, check_vma=False)
```

```python
import functools

import jax
import jax.numpy as jnp
from jax import lax
from jax.experimental import pallas as pl
from jax.experimental.pallas import tpu as pltpu
from jax.sharding import PartitionSpec as P

NDOM = 8

EPSILON = 1e-06
BETA_ONE = 0.9
BETA_TWO = 0.95
ADAM_EPSILON = 1e-08
DECAY_RATE = 0.1
MATRIX_RATE = 0.06
GAIN_RATE = 0.5
STEP_NUMBER = 3.0

BF = jnp.bfloat16
F32 = jnp.float32
VMEM_LIMIT = 56 * 1024 * 1024


def inverse_rms(values):
    return lax.rsqrt(jnp.mean(values * values, axis=-1, keepdims=True) + EPSILON)


def silu_slope(values):
    sigma = jax.nn.sigmoid(values)
    return sigma * (1.0 + values * (1.0 - sigma))


def adamw_update(master, first, second, gradient, count, rate, decay):
    first_new = BETA_ONE * first + (1.0 - BETA_ONE) * gradient
    second_new = BETA_TWO * second + (1.0 - BETA_TWO) * gradient * gradient
    first_hat = first_new / (1.0 - BETA_ONE**count)
    second_hat = second_new / (1.0 - BETA_TWO**count)
    master_new = master - rate * (
        first_hat / (jnp.sqrt(second_hat) + ADAM_EPSILON) + decay * master
    )
    return (master_new, first_new, second_new)


def partner_swap(value):
    return lax.ppermute(value, "mp", [(0, 1), (1, 0)])


def mp_sum(part):
    low = part.astype(BF)
    if lax.axis_size("mp") == 2:
        return low.astype(F32) + partner_swap(low).astype(F32)
    return lax.psum(low.astype(F32), "mp")


def mp_sum_wide(part):
    if lax.axis_size("mp") == 2:
        return part + partner_swap(part)
    return lax.psum(part, "mp")


def mp_scatter(part):
    if lax.axis_size("mp") == 2:
        half = part.shape[1] // 2
        place = lax.axis_index("mp")
        own = lax.dynamic_slice_in_dim(part, place * half, half, 1)
        other = lax.dynamic_slice_in_dim(part, (1 - place) * half, half, 1)
        return own.astype(BF).astype(F32) + partner_swap(other.astype(BF)).astype(F32)
    return lax.psum_scatter(part.astype(BF), "mp", scatter_dimension=1, tiled=True).astype(F32)


def mp_swap(pieces):
    if lax.axis_size("mp") == 2:
        place = lax.axis_index("mp")
        own = lax.dynamic_index_in_dim(pieces, place, 0, keepdims=False)
        came = partner_swap(lax.dynamic_index_in_dim(pieces, 1 - place, 0, keepdims=False))
        first = place == 0
        return jnp.stack([jnp.where(first, own, came), jnp.where(first, came, own)])
    return lax.all_to_all(pieces, "mp", 0, 0, tiled=False)


def mp_gather(part):
    if lax.axis_size("mp") == 2:
        place = lax.axis_index("mp")
        came = partner_swap(part)
        first = place == 0
        return jnp.concatenate([jnp.where(first, part, came), jnp.where(first, came, part)], axis=1)
    return lax.all_gather(part, "mp", axis=1, tiled=True)


SUB_ROWS = 8
TILE_ROWS = 64


def channel_block(width):
    return 512 if width % 512 == 0 else width


def scan_rows(total, decay, carry):
    row = lax.broadcasted_iota(jnp.int32, total.shape, 0)
    shift = 1
    while shift < SUB_ROWS:
        keep = row >= shift
        total = total + decay * jnp.where(keep, pltpu.roll(total, shift, 0), 0.0)
        decay = decay * jnp.where(keep, pltpu.roll(decay, shift, 0), 1.0)
        shift *= 2
    return total + decay * carry


def scan_rows_back(total, decay, carry):
    row = lax.broadcasted_iota(jnp.int32, total.shape, 0)
    shift = 1
    while shift < SUB_ROWS:
        keep = row < SUB_ROWS - shift
        total = total + decay * jnp.where(keep, pltpu.roll(total, SUB_ROWS - shift, 0), 0.0)
        decay = decay * jnp.where(keep, pltpu.roll(decay, SUB_ROWS - shift, 0), 1.0)
        shift *= 2
    return total + decay * carry


def scan_forward_kernel(pre_ref, bound_ref, gain_ref, states_ref, raw_ref, square_ref):
    length, width = states_ref.shape[1], states_ref.shape[2]
    bound = bound_ref[...]
    gain = gain_ref[...]
    first_block = pl.program_id(1) == 0

    def step(index, carry):
        rows = pl.ds(pl.multiple_of(index * TILE_ROWS, TILE_ROWS), TILE_ROWS)
        forget = bound + (1.0 - bound) * jax.nn.sigmoid(pre_ref[1, 0, rows, :])
        total = (1.0 - forget) * jax.nn.silu(pre_ref[0, 0, rows, :])
        parts = []
        for low in range(0, TILE_ROWS, SUB_ROWS):
            part = scan_rows(total[low : low + SUB_ROWS], forget[low : low + SUB_ROWS], carry)
            carry = part[SUB_ROWS - 1 : SUB_ROWS]
            parts.append(part)
        states = jnp.concatenate(parts)
        states_ref[0, rows, :] = states
        raw = states * gain * jax.nn.silu(pre_ref[2, 0, rows, :])
        raw_ref[0, rows, :] = raw.astype(raw_ref.dtype)
        square = jnp.sum(states * states, axis=-1, keepdims=True)
        square_ref[0, rows, :] = square + jnp.where(first_block, 0.0, square_ref[0, rows, :])
        return carry

    lax.fori_loop(0, length // TILE_ROWS, step, jnp.zeros((1, width), F32))


def scan_forward(pre, bound, gain):
    _, batches, length, width = pre.shape
    block = channel_block(width)
    return pl.pallas_call(
        scan_forward_kernel,
        grid=(batches, width // block),
        in_specs=[
            pl.BlockSpec((3, 1, length, block), lambda b, c: (0, b, 0, c)),
            pl.BlockSpec((1, block), lambda b, c: (0, c)),
            pl.BlockSpec((1, block), lambda b, c: (0, c)),
        ],
        out_specs=[
            pl.BlockSpec((1, length, block), lambda b, c: (b, 0, c)),
            pl.BlockSpec((1, length, block), lambda b, c: (b, 0, c)),
            pl.BlockSpec((1, length, 1), lambda b, c: (b, 0, 0)),
        ],
        out_shape=[
            jax.ShapeDtypeStruct((batches, length, width), F32),
            jax.ShapeDtypeStruct((batches, length, width), BF),
            jax.ShapeDtypeStruct((batches, length, 1), F32),
        ],
        compiler_params=pltpu.CompilerParams(vmem_limit_bytes=VMEM_LIMIT),
        cost_estimate=pl.CostEstimate(
            flops=batches * length * width * 40,
            bytes_accessed=batches * length * width * 18,
            transcendentals=batches * length * width * 3,
        ),
    )(pre, bound[None], gain[None])


def scan_backward_kernel(
    pre_ref, states_ref, gated_ref, inverse_ref, mean_ref, bound_ref, gain_ref,
    grad_ref, out_ref, gain_grad_ref, dot_ref,
):
    length, width = states_ref.shape[1], states_ref.shape[2]
    bound = bound_ref[...]
    gain = gain_ref[...]
    first_block = pl.program_id(1) == 0
    row = lax.broadcasted_iota(jnp.int32, (TILE_ROWS, width), 0)
    tiles = length // TILE_ROWS

    def step(index, carry):
        carried_next, forget_next, gain_sum = carry
        place = tiles - 1 - index
        rows = pl.ds(pl.multiple_of(place * TILE_ROWS, TILE_ROWS), TILE_ROWS)
        pre_input = pre_ref[0, 0, rows, :]
        pre_forget = pre_ref[1, 0, rows, :]
        pre_gate = pre_ref[2, 0, rows, :]
        states = states_ref[0, rows, :]
        inverse = inverse_ref[0, rows, :]
        grad_gated = gated_ref[0, rows, :]
        unit = states * inverse
        gate_sig = jax.nn.sigmoid(pre_gate)
        gate = pre_gate * gate_sig
        out_ref[0, rows, :] = (unit * gain * gate).astype(out_ref.dtype)
        gain_sum = gain_sum + grad_gated * unit * gate
        scaled = grad_gated * gain
        grad_gate = (scaled * unit * (gate_sig * (1.0 + pre_gate * (1.0 - gate_sig)))).astype(BF)
        grad_ref[2, 0, rows, :] = grad_gate
        total = inverse * (scaled * gate - unit * mean_ref[0, rows, :])
        sigma = jax.nn.sigmoid(pre_forget)
        forget = bound + (1.0 - bound) * sigma
        decay = jnp.where(row == TILE_ROWS - 1, forget_next, pltpu.roll(forget, TILE_ROWS - 1, 0))
        parts = []
        for low in range(TILE_ROWS - SUB_ROWS, -1, -SUB_ROWS):
            part = scan_rows_back(
                total[low : low + SUB_ROWS], decay[low : low + SUB_ROWS], carried_next
            )
            carried_next = part[0:1]
            parts.insert(0, part)
        carried = jnp.concatenate(parts)
        before_rows = pl.ds(
            pl.multiple_of(jnp.maximum(place - 1, 0) * TILE_ROWS, TILE_ROWS), TILE_ROWS
        )
        before = states_ref[0, before_rows, :][TILE_ROWS - 1 : TILE_ROWS, :]
        before = jnp.where(place == 0, 0.0, before)
        earlier = jnp.where(row == 0, before, pltpu.roll(states, 1, 0))
        input_sig = jax.nn.sigmoid(pre_input)
        fresh = pre_input * input_sig
        slope = input_sig * (1.0 + pre_input * (1.0 - input_sig))
        grad_input = (carried * (1.0 - forget) * slope).astype(BF)
        grad_forget = (
            carried * (earlier - fresh) * (1.0 - bound) * sigma * (1.0 - sigma)
        ).astype(BF)
        grad_ref[0, 0, rows, :] = grad_input
        grad_ref[1, 0, rows, :] = grad_forget
        dots = (
            grad_input.astype(F32) * pre_input
            + grad_forget.astype(F32) * pre_forget
            + grad_gate.astype(F32) * pre_gate
        )
        dot = jnp.sum(dots, axis=-1, keepdims=True)
        dot_ref[0, rows, :] = dot + jnp.where(first_block, 0.0, dot_ref[0, rows, :])
        return carried_next, forget[0:1, :], gain_sum

    zero = jnp.zeros((1, width), F32)
    _, _, gain_sum = lax.fori_loop(
        0, tiles, step, (zero, zero, jnp.zeros((TILE_ROWS, width), F32))
    )
    gain_grad_ref[0] = jnp.sum(gain_sum, axis=0, keepdims=True)


def scan_backward(pre, states, grad_gated, inverse, mean, bound, gain):
    _, batches, length, width = pre.shape
    block = channel_block(width)
    whole = pl.BlockSpec((1, length, block), lambda b, c: (b, 0, c))
    column = pl.BlockSpec((1, length, 1), lambda b, c: (b, 0, 0))
    line = pl.BlockSpec((1, block), lambda b, c: (0, c))
    three = pl.BlockSpec((3, 1, length, block), lambda b, c: (0, b, 0, c))
    return pl.pallas_call(
        scan_backward_kernel,
        grid=(batches, width // block),
        in_specs=[three, whole, whole, column, column, line, line],
        out_specs=[
            three,
            whole,
            pl.BlockSpec((1, 1, block), lambda b, c: (b, 0, c)),
            column,
        ],
        out_shape=[
            jax.ShapeDtypeStruct((3, batches, length, width), BF),
            jax.ShapeDtypeStruct((batches, length, width), BF),
            jax.ShapeDtypeStruct((batches, 1, width), F32),
            jax.ShapeDtypeStruct((batches, length, 1), F32),
        ],
        compiler_params=pltpu.CompilerParams(vmem_limit_bytes=VMEM_LIMIT),
        cost_estimate=pl.CostEstimate(
            flops=batches * length * width * 80,
            bytes_accessed=batches * length * width * 28,
            transcendentals=batches * length * width * 3,
        ),
    )(pre, states, grad_gated, inverse, mean, bound[None], gain[None])


MESH_ID = pl.DeviceIdType.MESH
DEPTH = 4
LANES = 256
Z_LAG = 4


def device_place():
    dp = lax.axis_index("dp")
    return dp // 4, lax.rem(dp // 2, 2), lax.rem(dp, 2)


def device_at(z, x, core):
    return (z * 4 + x * 2 + core, lax.axis_index("mp"))


def scatter_barrier(z, x, core, with_mp=False):
    barrier = pltpu.get_barrier_semaphore()
    targets = [device_at(z, x, 1 - core), device_at(z, 1 - x, core)]
    targets += [device_at(lax.rem(z + hop, DEPTH), x, core) for hop in range(1, DEPTH)]
    if with_mp:
        targets.append((lax.axis_index("dp"), 1 - lax.axis_index("mp")))
    for target in targets:
        pl.semaphore_signal(barrier, 1, device_id=target, device_id_type=MESH_ID)
    pl.semaphore_wait(barrier, len(targets))


def scatter_step(step, chunks, compute, out_ref, scratch):
    (own, core_out, core_in, keep, x_out, x_in, sums, mine, z_out, z_in,
     core_send, core_recv, x_send, x_recv, z_send, z_recv) = scratch
    z, x, core = device_place()

    def core_copy(p):
        return pltpu.make_async_remote_copy(
            core_out.at[lax.rem(p, 2)], core_in.at[lax.rem(p, 4)],
            core_send.at[lax.rem(p, 2)], core_recv.at[lax.rem(p, 4)],
            device_id=device_at(z, x, 1 - core), device_id_type=MESH_ID)

    def x_copy(p):
        return pltpu.make_async_remote_copy(
            x_out.at[lax.rem(p, 2)], x_in.at[lax.rem(p, 4)],
            x_send.at[lax.rem(p, 2)], x_recv.at[lax.rem(p, 4)],
            device_id=device_at(z, 1 - x, core), device_id_type=MESH_ID)

    def z_copy(p, hop):
        return pltpu.make_async_remote_copy(
            z_out.at[lax.rem(p, 4), hop - 1], z_in.at[lax.rem(p, 8), hop - 1],
            z_send.at[lax.rem(p, 4), hop - 1], z_recv.at[lax.rem(p, 8), hop - 1],
            device_id=device_at(lax.rem(z + hop, DEPTH), x, core), device_id_type=MESH_ID)

    @pl.when(step < chunks)
    def _():
        @pl.when(step >= 2)
        def _():
            core_copy(step - 2).wait_send()

        core_out[lax.rem(step, 2)] = compute(step, 1 - core).astype(BF)
        core_copy(step).start()
        own[lax.rem(step, 2)] = compute(step, core)

    @pl.when((step >= 1) & (step < chunks + 1))
    def _():
        p = step - 1
        core_copy(p).wait_recv()

        @pl.when(p >= 2)
        def _():
            x_copy(p - 2).wait_send()

        two, four = lax.rem(p, 2), lax.rem(p, 4)
        x_out[two] = (own[two, :, 1 - x] + core_in[four, :, 1 - x].astype(F32)).astype(BF)
        x_copy(p).start()
        keep[two] = own[two, :, x] + core_in[four, :, x].astype(F32)

    @pl.when((step >= 2) & (step < chunks + 2))
    def _():
        p = step - 2
        x_copy(p).wait_recv()
        two, four = lax.rem(p, 2), lax.rem(p, 4)
        sums[...] = keep[two] + x_in[four].astype(F32)
        for hop in range(1, DEPTH):
            @pl.when(p >= 4)
            def _():
                z_copy(p - 4, hop).wait_send()

            z_out[four, hop - 1] = sums[lax.rem(z + hop, DEPTH)].astype(BF)
            z_copy(p, hop).start()
        mine[four] = sums[z]

    @pl.when(step >= Z_LAG)
    def _():
        p = step - Z_LAG
        for hop in range(1, DEPTH):
            z_copy(p, hop).wait_recv()
        got = z_in.at[lax.rem(p, 8)]
        total = mine[lax.rem(p, 4)] + got[0].astype(F32) + got[1].astype(F32) + got[2].astype(F32)
        out_ref[0] = total

    @pl.when(step == chunks + Z_LAG - 1)
    def _():
        for p in range(max(chunks - 2, 0), chunks):
            core_copy(p).wait_send()
            x_copy(p).wait_send()
        for p in range(max(chunks - 4, 0), chunks):
            for hop in range(1, DEPTH):
                z_copy(p, hop).wait_send()


def scatter_scratch(rows, lanes):
    quad = (DEPTH, 2, rows, lanes)
    line = (DEPTH, rows, lanes)
    dma = pltpu.SemaphoreType.DMA
    return [
        pltpu.VMEM((2, *quad), F32),
        pltpu.VMEM((2, *quad), BF),
        pltpu.VMEM((4, *quad), BF),
        pltpu.VMEM((2, *line), F32),
        pltpu.VMEM((2, *line), BF),
        pltpu.VMEM((4, *line), BF),
        pltpu.VMEM(line, F32),
        pltpu.VMEM((4, rows, lanes), F32),
        pltpu.VMEM((4, DEPTH - 1, rows, lanes), BF),
        pltpu.VMEM((8, DEPTH - 1, rows, lanes), BF),
        dma((2,)), dma((4,)), dma((2,)), dma((4,)), dma((4, DEPTH - 1)), dma((8, DEPTH - 1)),
    ]


def scatter_out(chunks, rows, lanes):
    spec = pl.BlockSpec((1, rows, lanes), lambda q: (jnp.maximum(q - Z_LAG, 0), 0, 0))
    return spec, jax.ShapeDtypeStruct((chunks, rows, lanes), F32)


def fixed(shape):
    return pl.BlockSpec(shape, lambda q: (0,) * len(shape), pipeline_mode=pl.Buffered(1))


def glu_kernel(
    hidden_blocks, full_blocks, normed_ref, back_ref, left_ref, glu_ref,
    out_ref, sum_own, sum_came, half_own, half_send, half_came,
    acts, weights_in, weights_back, sum_stage, half_stage,
    in_sem, back_sem, stage_sem, sum_send, sum_recv, half_send_sem, half_recv, *scratch,
):
    z, x, core = device_place()
    dp, mp = lax.axis_index("dp"), lax.axis_index("mp")
    step = pl.program_id(0)
    chunks = 3 * hidden_blocks
    rows = normed_ref.shape[0]
    row_block = rows // 2
    half_blocks = full_blocks // 2
    across = (((1,), (1,)), ((), ()))

    def lane_block(index):
        return pl.ds(pl.multiple_of(index * LANES, LANES), LANES)

    def load_in(index):
        return pltpu.make_async_copy(glu_ref.at[:, :, lane_block(index)], weights_in, in_sem)

    def load_back(index):
        return pltpu.make_async_copy(glu_ref.at[:, lane_block(index), :], weights_back, back_sem)

    def stage(index, kind, target):
        source = (sum_stage, half_stage)[kind].at[lax.rem(index, 2)]
        return pltpu.make_async_copy(source, target, stage_sem.at[lax.rem(index, 2), kind])

    def half_spot(index):
        return lax.rem(index, half_blocks)

    def sum_copy(index):
        return pltpu.make_async_remote_copy(
            sum_own.at[:, lane_block(index)], sum_came.at[:, lane_block(index)],
            sum_send.at[index], sum_recv.at[index], device_id=(dp, 1 - mp), device_id_type=MESH_ID)

    def half_copy(spot):
        return pltpu.make_async_remote_copy(
            half_send.at[:, lane_block(spot)], half_came.at[:, lane_block(spot)],
            half_send_sem.at[spot], half_recv.at[spot], device_id=(dp, 1 - mp), device_id_type=MESH_ID)

    @pl.when(step == 0)
    def _():
        load_in(0).start()
        load_back(0).start()
        scatter_barrier(z, x, core, with_mp=True)

    @pl.when(step < hidden_blocks)
    def _():
        load_in(step).wait()
        lanes = lane_block(step)

        def part(index, _):
            part_rows = pl.ds(pl.multiple_of(index * row_block, row_block), row_block)
            normed = normed_ref[part_rows, :]
            pre_act = jnp.dot(normed, weights_in[0], preferred_element_type=F32)
            pre_up = jnp.dot(normed, weights_in[1], preferred_element_type=F32)
            grad_hidden = jnp.dot(back_ref[part_rows, :], weights_in[2], preferred_element_type=F32)
            sigma = jax.nn.sigmoid(pre_act)
            act_part = pre_act * sigma
            acts[0, part_rows, lanes] = (
                grad_hidden * pre_up * (sigma * (1.0 + pre_act * (1.0 - sigma)))).astype(BF)
            acts[1, part_rows, lanes] = (grad_hidden * act_part).astype(BF)
            acts[2, part_rows, lanes] = (act_part * pre_up).astype(BF)
            return 0

        lax.fori_loop(0, rows // row_block, part, 0)

        @pl.when(step + 1 < hidden_blocks)
        def _():
            load_in(step + 1).start()

    @pl.when((step > hidden_blocks) & (step <= hidden_blocks + full_blocks))
    def _():
        index = step - hidden_blocks - 1
        stage(index, 0, sum_own.at[:, lane_block(index)]).wait()
        sum_copy(index).start()
        spot = half_spot(index)
        stage(index, 1, half_own.at[:, lane_block(spot)]).wait()

        @pl.when(index // half_blocks != mp)
        def _():
            half_copy(spot).start()

    @pl.when((step >= hidden_blocks) & (step < hidden_blocks + full_blocks))
    def _():
        index = step - hidden_blocks
        load_back(index).wait()
        slot = lax.rem(index, 2)

        def part(at, _):
            part_rows = pl.ds(pl.multiple_of(at * row_block, row_block), row_block)
            dot = functools.partial(
                lax.dot_general, dimension_numbers=across, preferred_element_type=F32)
            grad_normed = dot(acts[0, part_rows, :], weights_back[0])
            grad_normed += dot(acts[1, part_rows, :], weights_back[1])
            sum_stage[slot, part_rows, :] = grad_normed.astype(BF)
            half_stage[slot, part_rows, :] = dot(acts[2, part_rows, :], weights_back[2]).astype(BF)
            return 0

        lax.fori_loop(0, rows // row_block, part, 0)

        @pl.when(index + 1 < full_blocks)
        def _():
            load_back(index + 1).start()

        stage(index, 0, sum_own.at[:, lane_block(index)]).start()
        spot = half_spot(index)

        @pl.when(index // half_blocks == mp)
        def _():
            stage(index, 1, half_own.at[:, lane_block(spot)]).start()

        @pl.when(index // half_blocks != mp)
        def _():
            stage(index, 1, half_send.at[:, lane_block(spot)]).start()

    def compute(q, core_side):
        kind = lax.rem(q, 3)
        side = left_ref[kind // 2, :, :, core_side]
        side_rows = side.shape[2]
        product = jnp.dot(
            side.reshape(DEPTH * 2 * side_rows, rows), acts[kind, :, lane_block(q // 3)],
            preferred_element_type=F32)
        return product.reshape(DEPTH, 2, side_rows, LANES)

    scatter_step(step, chunks, compute, out_ref, scratch)

    @pl.when(step == chunks + Z_LAG - 1)
    def _():
        for index in range(full_blocks):
            sum_copy(index).wait()
        for spot in range(half_blocks):
            half_copy(spot).wait()


def glu_call(normed, back_low, glu, collective):
    rows, full = normed.shape
    hidden = glu.shape[2]
    hidden_blocks, full_blocks = hidden // LANES, full // LANES
    block = full // 16
    chunks = 3 * hidden_blocks
    left = jnp.stack([normed.T, back_low.T]).reshape(2, DEPTH, 2, 2, block, rows)
    any_space = pl.BlockSpec(memory_space=pl.ANY)
    out_spec, out_shape = scatter_out(chunks, block, LANES)
    dma = pltpu.SemaphoreType.DMA
    wide = jax.ShapeDtypeStruct((rows, full), BF)
    half = jax.ShapeDtypeStruct((rows, full // 2), BF)
    out, sum_own, sum_came, half_own, _, half_came = pl.pallas_call(
        functools.partial(glu_kernel, hidden_blocks, full_blocks),
        grid=(chunks + Z_LAG,),
        in_specs=[fixed(normed.shape), fixed(back_low.shape), fixed(left.shape), any_space],
        out_specs=[out_spec] + [any_space] * 5,
        out_shape=[out_shape, wide, wide, half, half, half],
        scratch_shapes=[
            pltpu.VMEM((3, rows, hidden), BF),
            pltpu.VMEM((3, full, LANES), BF),
            pltpu.VMEM((3, LANES, hidden), BF),
            pltpu.VMEM((2, rows, LANES), BF),
            pltpu.VMEM((2, rows, LANES), BF),
            dma(()), dma(()), dma((2, 2)),
            dma((full_blocks,)), dma((full_blocks,)), dma((full_blocks // 2,)), dma((full_blocks // 2,)),
            *scatter_scratch(block, LANES),
        ],
        compiler_params=pltpu.CompilerParams(
            collective_id=collective, has_side_effects=True, vmem_limit_bytes=62 * 1024 * 1024),
        cost_estimate=pl.CostEstimate(
            flops=18 * rows * full * hidden, bytes_accessed=6 * full * hidden * 2,
            transcendentals=rows * hidden),
    )(normed, back_low, left, glu)
    return out, sum_own, sum_came, half_own, half_came


def mixer_kernel(
    full_blocks, left_ref, grad_ref, left_out_ref, right_out_ref, gain_ref, tokens_ref, inverse_ref,
    weights_ref, out_ref, half_own, half_send, half_came, swap_came,
    weights, token_block, gain_sum, gain_chunk, total, swap_out, half_stage,
    load_sem, stage_sem, half_send_sem, half_recv, swap_send, swap_recv, *scratch,
):
    z, x, core = device_place()
    dp, mp = lax.axis_index("dp"), lax.axis_index("mp")
    step = pl.program_id(0)
    tokens, channels = grad_ref.shape[1], grad_ref.shape[2]
    block, half = left_ref.shape[3], left_out_ref.shape[3]
    outer = full_blocks // 2
    across = channels // LANES
    gains = outer + 3 * across
    chunks = gains + 1
    half_blocks = full_blocks // 2
    row_block = tokens // 2
    partner = (dp, 1 - mp)

    def lane_block(index):
        return pl.ds(pl.multiple_of(index * LANES, LANES), LANES)

    def loads(index):
        return (
            pltpu.make_async_copy(weights_ref.at[:, lane_block(index), :], weights, load_sem.at[0]),
            pltpu.make_async_copy(tokens_ref.at[:, lane_block(index)], token_block, load_sem.at[1]),
        )

    def stage(index, target):
        return pltpu.make_async_copy(
            half_stage.at[lax.rem(index, 2)], target, stage_sem.at[lax.rem(index, 2)])

    def half_copy(spot):
        return pltpu.make_async_remote_copy(
            half_send.at[:, lane_block(spot)], half_came.at[:, lane_block(spot)],
            half_send_sem.at[spot], half_recv.at[spot], device_id=partner, device_id_type=MESH_ID)

    def swap_copy(index):
        return pltpu.make_async_remote_copy(
            swap_out.at[lax.rem(index, 2)], swap_came.at[index],
            swap_send.at[lax.rem(index, 2)], swap_recv.at[index],
            device_id=partner, device_id_type=MESH_ID)

    @pl.when(step == 0)
    def _():
        for one in loads(0):
            one.start()
        gain_chunk[...] = jnp.zeros_like(gain_chunk)
        gain_sum[...] = jnp.zeros_like(gain_sum)
        scatter_barrier(z, x, core, with_mp=True)

    @pl.when((step > 0) & (step <= full_blocks))
    def _():
        index = step - 1
        spot = lax.rem(index, half_blocks)
        stage(index, half_own.at[:, lane_block(spot)]).wait()

        @pl.when(index // half_blocks != mp)
        def _():
            half_copy(spot).start()

    @pl.when(step < full_blocks)
    def _():
        for one in loads(step):
            one.wait()
        slot = lax.rem(step, 2)
        spot = lax.rem(step, half_blocks)

        def part(at, gain_in):
            part_rows = pl.ds(pl.multiple_of(at * row_block, row_block), row_block)
            dot = functools.partial(
                lax.dot_general, dimension_numbers=(((1,), (1,)), ((), ())), preferred_element_type=F32)
            grad = dot(grad_ref[0, part_rows, :], weights[0])
            grad += dot(grad_ref[1, part_rows, :], weights[1])
            grad += dot(grad_ref[2, part_rows, :], weights[2])
            half_stage[slot, part_rows, :] = grad.astype(BF)
            unit = token_block[part_rows, :].astype(F32) * inverse_ref[part_rows, :]
            return gain_in + jnp.sum(grad * unit, axis=0, keepdims=True)

        gain_in = lax.fori_loop(0, tokens // row_block, part, jnp.zeros((1, LANES), F32))
        gain_sum[2 * step, 0:1, :] = gain_in[:, :128]
        gain_sum[2 * step + 1, 0:1, :] = gain_in[:, 128:]

        @pl.when(step + 1 < full_blocks)
        def _():
            for one in loads(step + 1):
                one.start()

        @pl.when(step // half_blocks == mp)
        def _():
            stage(step, half_own.at[:, lane_block(spot)]).start()

        @pl.when(step // half_blocks != mp)
        def _():
            stage(step, half_send.at[:, lane_block(spot)]).start()

    def compute(q, core_side):
        def outer_chunk():
            side = left_out_ref[:, :, core_side].reshape(channels // 2, tokens)
            parts = [
                jnp.dot(side, right_out_ref[:, lane_block(2 * q + at)], preferred_element_type=F32)
                for at in (0, 1)
            ]
            parts = [part.reshape(DEPTH, 2, half, LANES) for part in parts]
            return jnp.concatenate(parts, axis=2)

        def inner_chunk():
            at = q - outer
            side = left_ref[:, :, core_side].reshape(DEPTH * 2 * block, tokens)
            right = grad_ref[at // across, :, lane_block(lax.rem(at, across))]
            return jnp.dot(side, right, preferred_element_type=F32).reshape(DEPTH, 2, block, LANES)

        def gain_block():
            for owner in range(2 * DEPTH):
                line = 2 * owner + core_side
                gain_chunk[owner // 2, owner % 2, 0:8, 0:128] = gain_ref[line] + gain_sum[line]
            return gain_chunk[...]

        return lax.cond(
            q < outer, outer_chunk, lambda: lax.cond(q < gains, inner_chunk, gain_block))

    scatter_step(step, chunks, compute, out_ref, scratch)

    @pl.when(step >= Z_LAG + outer)
    def _():
        index = step - Z_LAG - outer

        @pl.when(index >= 2)
        def _():
            swap_copy(index - 2).wait_send()

        total[...] = out_ref[0]
        first = jnp.where(index == gains - outer, 0, 1 - mp) * half
        swap_out[lax.rem(index, 2)] = total[pl.ds(pl.multiple_of(first, half), half), :].astype(BF)
        swap_copy(index).start()

    @pl.when(step == chunks + Z_LAG - 1)
    def _():
        for spot in range(half_blocks):
            half_copy(spot).wait()
        for index in range(gains - outer + 1):
            swap_copy(index).wait_recv()
        for index in range(gains - outer - 1, gains - outer + 1):
            swap_copy(index).wait_send()


def mixer_call(left_in, grad_pre, left_out, right_out, gain_parts, tokens, inverse, weights, collective):
    _, rows, channels = grad_pre.shape
    full = left_in.shape[0]
    block, half = full // 16, channels // 16
    full_blocks, across = full // LANES, channels // LANES
    outer, inner = full_blocks // 2, 3 * across
    chunks = outer + inner + 1
    any_space = pl.BlockSpec(memory_space=pl.ANY)
    dma = pltpu.SemaphoreType.DMA
    out_spec, out_shape = scatter_out(chunks, block, LANES)
    part = jax.ShapeDtypeStruct((rows, full // 2), BF)
    out, half_own, _, half_came, swap_came = pl.pallas_call(
        functools.partial(mixer_kernel, full_blocks),
        grid=(chunks + Z_LAG,),
        in_specs=[
            fixed((DEPTH, 2, 2, block, rows)), fixed(grad_pre.shape),
            fixed((DEPTH, 2, 2, half, rows)), fixed(right_out.shape), fixed(gain_parts.shape),
            any_space, fixed(inverse.shape), any_space,
        ],
        out_specs=[out_spec] + [any_space] * 4,
        out_shape=[
            out_shape, part, part, part, jax.ShapeDtypeStruct((inner + 1, half, LANES), BF),
        ],
        scratch_shapes=[
            pltpu.VMEM((3, LANES, channels), BF),
            pltpu.VMEM((rows, LANES), BF),
            pltpu.VMEM((16, 8, 128), F32),
            pltpu.VMEM((DEPTH, 2, block, LANES), F32),
            pltpu.VMEM((block, LANES), F32),
            pltpu.VMEM((2, half, LANES), BF),
            pltpu.VMEM((2, rows, LANES), BF),
            dma((2,)), dma((2,)), dma((full_blocks // 2,)), dma((full_blocks // 2,)),
            dma((2,)), dma((inner + 1,)),
            *scatter_scratch(block, LANES),
        ],
        compiler_params=pltpu.CompilerParams(
            collective_id=collective, has_side_effects=True, vmem_limit_bytes=VMEM_LIMIT),
        cost_estimate=pl.CostEstimate(
            flops=14 * full * rows * channels, bytes_accessed=16 * full * channels, transcendentals=0),
    )(
        left_in.reshape(DEPTH, 2, 2, block, rows), grad_pre,
        left_out.reshape(DEPTH, 2, 2, half, rows), right_out, gain_parts, tokens, inverse, weights,
    )
    place = lax.axis_index("mp")
    out_own = out[:outer].reshape(outer, 2, half, LANES).transpose(2, 0, 1, 3).reshape(half, full)
    own = lax.dynamic_slice_in_dim(out[outer : outer + inner], place * half, half, 1)
    came = swap_came[:inner].astype(F32)
    first = place == 0
    in_own = jnp.stack([jnp.where(first, own, came), jnp.where(first, came, own)])
    in_own = in_own.reshape(2, 3, across, half, LANES).transpose(1, 3, 0, 2, 4)
    in_own = in_own.reshape(3, half, 2, channels)
    gains = out[chunks - 1, :3, :128] + swap_came[inner, :3, :128].astype(F32)
    return in_own, out_own, gains, half_own.astype(F32) + half_came.astype(F32)


def middle_back_kernel(
    sum_own_ref, sum_came_ref, middle_ref, cot_ref, tokens_ref, weight_ref, gain_ref, mixer_ref,
    grad_own_ref, low_ref, mean_ref, gated_ref, gain_grad_ref,
):
    rows, full = middle_ref.shape
    part = full // 2
    middle = middle_ref[...]
    inverse = lax.rsqrt(jnp.mean(middle * middle, axis=-1, keepdims=True) + EPSILON)
    unit = middle * inverse
    grad_normed = sum_own_ref[...].astype(F32) + sum_came_ref[...].astype(F32)
    gain_grad = jnp.sum(grad_normed * unit, axis=0, keepdims=True)
    before = jnp.where(pl.program_id(0) == 0, 0.0, gain_grad_ref[...])
    gain_grad_ref[...] = before + gain_grad
    scaled = grad_normed * gain_ref[...]
    dots = jnp.mean(scaled * unit, axis=-1, keepdims=True)
    back = cot_ref[...].astype(F32) * weight_ref[...]
    grad = back + inverse * (scaled - unit * dots)
    first = lax.axis_index("mp") == 0
    grad_own_ref[...] = jnp.where(first, grad[:, :part], grad[:, part:])
    low = grad.astype(BF)
    low_ref[...] = low
    branch = middle - tokens_ref[...].astype(F32)
    mean_ref[...] = jnp.mean(low.astype(F32) * branch, axis=-1, keepdims=True)
    gated_ref[...] = lax.dot_general(
        low, mixer_ref[...], (((1,), (1,)), ((), ())), preferred_element_type=F32)


def middle_back(sum_own, sum_came, middle, cot, tokens, weight, gain, mixer_out):
    rows, full = middle.shape
    channels = mixer_out.shape[0]
    step = 128 if rows % 128 == 0 else rows
    line = lambda width: pl.BlockSpec((step, width), lambda r: (r, 0))
    shape = jax.ShapeDtypeStruct
    return pl.pallas_call(
        middle_back_kernel,
        grid=(rows // step,),
        in_specs=[line(full)] * 5 + [line(1), fixed((1, full)), fixed(mixer_out.shape)],
        out_specs=[
            line(full // 2), line(full), line(1), line(channels),
            pl.BlockSpec((1, full), lambda r: (0, 0)),
        ],
        out_shape=[
            shape((rows, full // 2), F32), shape((rows, full), BF), shape((rows, 1), F32),
            shape((rows, channels), F32), shape((1, full), F32),
        ],
        compiler_params=pltpu.CompilerParams(vmem_limit_bytes=VMEM_LIMIT),
        cost_estimate=pl.CostEstimate(
            flops=2 * rows * full * channels, bytes_accessed=rows * full * 20, transcendentals=0),
    )(sum_own, sum_came, middle, cot, tokens, weight, gain[None], mixer_out)


def glu_update_kernel(scale, act_ref, up_ref, out_ref, *refs):
    in_refs, down_refs, in_new, down_new = refs[:3], refs[3:6], refs[6:9], refs[9:12]
    count = STEP_NUMBER
    for at, grad_ref in ((0, act_ref), (1, up_ref)):
        new = adamw_update(
            *(ref[at] for ref in in_refs), grad_ref[0] * scale, count, MATRIX_RATE, DECAY_RATE)
        for ref, value in zip(in_new, new):
            ref[at] = value
    new = adamw_update(
        *(ref[...] for ref in down_refs), out_ref[0].T * scale, count, MATRIX_RATE, DECAY_RATE)
    for ref, value in zip(down_new, new):
        ref[...] = value


def glu_update(sums, ins, downs, scale):
    _, rows, lanes = sums.shape
    blocks = ins[0].shape[2] // lanes
    sum_spec = lambda kind: pl.BlockSpec((1, rows, lanes), lambda q: (3 * q + kind, 0, 0))
    in_spec = pl.BlockSpec((2, rows, lanes), lambda q: (0, 0, q))
    down_spec = pl.BlockSpec((lanes, rows), lambda q: (q, 0))
    new = pl.pallas_call(
        functools.partial(glu_update_kernel, scale),
        grid=(blocks,),
        in_specs=[sum_spec(0), sum_spec(1), sum_spec(2)] + [in_spec] * 3 + [down_spec] * 3,
        out_specs=[in_spec] * 3 + [down_spec] * 3,
        out_shape=[jax.ShapeDtypeStruct(ins[0].shape, F32)] * 3 + [jax.ShapeDtypeStruct(downs[0].shape, F32)] * 3,
        compiler_params=pltpu.CompilerParams(vmem_limit_bytes=VMEM_LIMIT),
        cost_estimate=pl.CostEstimate(
            flops=60 * rows * lanes * blocks, bytes_accessed=84 * rows * lanes * blocks,
            transcendentals=6 * rows * lanes * blocks),
    )(sums, sums, sums, *ins, *downs)
    return tuple(new[:3]), tuple(new[3:])


ITEMS = 4


def gather_kernel(in_ref, out_ref, small_ref, all_in, all_out, all_small, right_send, left_send,
                  z_recv, x_send, x_recv, core_send, core_recv, y_send, y_recv, local_sem):
    z, x, core = device_place()
    mp = lax.axis_index("mp")
    barrier = pltpu.get_barrier_semaphore()
    right, left = lax.rem(z + 1, DEPTH), lax.rem(z + DEPTH - 1, DEPTH)
    dp = lax.axis_index("dp")
    for target in (
        device_at(right, x, core), device_at(left, x, core), device_at(z, 1 - x, core),
        device_at(z, x, 1 - core), (dp, 1 - mp),
    ):
        pl.semaphore_signal(barrier, 1, device_id=target, device_id_type=MESH_ID)
    pl.semaphore_wait(barrier, 5)

    def spot(item, zs, xs, cs, side=None):
        if item == 0:
            return all_in.at[:, zs, xs, cs, mp if side is None else side]
        if item == 1:
            return all_out.at[zs, xs, cs]
        if item == 2:
            return all_in.at[:, zs, xs, cs, 1 - mp]
        return all_small.at[zs, xs, cs]

    def own(item):
        if item == 0:
            return in_ref.at[mp]
        if item == 1:
            return out_ref
        return spot(item, z, x, core)

    def copy(item, zs, xs, target, send, recv, source=None):
        return pltpu.make_async_remote_copy(
            spot(item, zs, xs, core) if source is None else source, spot(item, zs, xs, core),
            send, recv, device_id=target, device_id_type=MESH_ID)

    def right_copy(item, zs, source=None):
        return copy(item, zs, x, device_at(right, x, core), right_send.at[zs, item], z_recv.at[zs, item], source)

    def left_copy(item, zs, source=None):
        return copy(item, zs, x, device_at(left, x, core), left_send.at[zs, item], z_recv.at[zs, item], source)

    def x_copy(item, zs, source=None):
        return copy(item, zs, x, device_at(z, 1 - x, core), x_send.at[zs, item], x_recv.at[zs, item], source)

    def core_copy(item, zs, xs, source=None):
        return copy(item, zs, xs, device_at(z, x, 1 - core), core_send.at[zs, xs, item], core_recv.at[zs, xs, item], source)

    y_copies = [
        pltpu.make_async_remote_copy(
            in_ref.at[1 - mp], all_in.at[:, z, x, core, mp], y_send.at[0], y_recv.at[0],
            device_id=(dp, 1 - mp), device_id_type=MESH_ID),
        pltpu.make_async_remote_copy(
            small_ref, all_small.at[z, x, core, mp], y_send.at[1], y_recv.at[1],
            device_id=(dp, 1 - mp), device_id_type=MESH_ID),
    ]
    locals_ = [
        pltpu.make_async_copy(in_ref.at[mp], spot(0, z, x, core), local_sem.at[0]),
        pltpu.make_async_copy(out_ref, spot(1, z, x, core), local_sem.at[1]),
        pltpu.make_async_copy(small_ref, all_small.at[z, x, core, mp], local_sem.at[2]),
    ]
    for one in y_copies:
        one.start()
    locals_[2].start()

    for item in range(ITEMS):
        if item == 2:
            y_copies[0].wait_recv()
        if item == 3:
            y_copies[1].wait_recv()
            locals_[2].wait()
        source = own(item)

        @pl.when(z < DEPTH - 1)
        def _():
            right_copy(item, z, source).start()

        @pl.when(z > 0)
        def _():
            left_copy(item, z, source).start()

        x_copy(item, z, source).start()
        core_copy(item, z, x, source).start()
    locals_[0].start()
    locals_[1].start()

    def from_x(item, zs):
        pltpu.make_async_remote_copy(
            spot(item, zs, 1 - x, core), spot(item, zs, 1 - x, core), x_send.at[zs, item],
            x_recv.at[zs, item], device_id=device_at(z, 1 - x, core), device_id_type=MESH_ID).wait_recv()
        core_copy(item, zs, 1 - x).start()

    for hop in range(1, DEPTH + 1):
        for item in range(ITEMS):
            if hop < DEPTH:
                @pl.when(z >= hop)
                def _():
                    zs = z - hop
                    right_copy(item, zs).wait_recv()

                    @pl.when(z < DEPTH - 1)
                    def _():
                        right_copy(item, zs).start()

                    x_copy(item, zs).start()
                    core_copy(item, zs, x).start()

                @pl.when(z + hop < DEPTH)
                def _():
                    zs = z + hop
                    left_copy(item, zs).wait_recv()

                    @pl.when(z > 0)
                    def _():
                        left_copy(item, zs).start()

                    x_copy(item, zs).start()
                    core_copy(item, zs, x).start()
            if hop == 1:
                from_x(item, z)
            else:
                @pl.when(z >= hop - 1)
                def _():
                    from_x(item, z - (hop - 1))

                @pl.when(z + hop - 1 < DEPTH)
                def _():
                    from_x(item, z + (hop - 1))

    for item in range(ITEMS):
        for zs in range(DEPTH):
            @pl.when((z >= zs) & (z < DEPTH - 1))
            def _():
                right_copy(item, zs).wait_send()

            @pl.when((z <= zs) & (z > 0))
            def _():
                left_copy(item, zs).wait_send()

            x_copy(item, zs).wait_send()
            for xs in range(2):
                core_copy(item, zs, xs).wait()
    for one in y_copies:
        one.wait_send()
    locals_[0].wait()
    locals_[1].wait()


def gather_call(in_blocks, out_rows, small, collective):
    _, three, own_rows, channels = in_blocks.shape
    full = out_rows.shape[1]
    dma = pltpu.SemaphoreType.DMA
    any_space = pl.BlockSpec(memory_space=pl.ANY)
    return pl.pallas_call(
        gather_kernel,
        in_specs=[any_space] * 3,
        out_specs=[any_space] * 3,
        out_shape=[
            jax.ShapeDtypeStruct((three, DEPTH, 2, 2, 2, own_rows, channels), BF),
            jax.ShapeDtypeStruct((DEPTH, 2, 2, own_rows, full), BF),
            jax.ShapeDtypeStruct((DEPTH, 2, 2, 2, *small.shape), F32),
        ],
        scratch_shapes=[
            dma((DEPTH, ITEMS)), dma((DEPTH, ITEMS)), dma((DEPTH, ITEMS)), dma((DEPTH, ITEMS)),
            dma((DEPTH, ITEMS)), dma((DEPTH, 2, ITEMS)), dma((DEPTH, 2, ITEMS)), dma((2,)), dma((2,)), dma((3,)),
        ],
        compiler_params=pltpu.CompilerParams(collective_id=collective, has_side_effects=True),
        cost_estimate=pl.CostEstimate(flops=0, bytes_accessed=300_000_000, transcendentals=0),
    )(in_blocks, out_rows, small)


def shards(
    tokens,
    cotangent,
    lengths,
    domains,
    lower_bound,
    mixer_master,
    mixer_first,
    mixer_second,
    glu_in_master,
    glu_in_first,
    glu_in_second,
    glu_out_master,
    glu_out_first,
    glu_out_second,
    gain_master,
    gain_first,
    gain_second,
):
    batches, _, length, full = tokens.shape
    rows = batches * length
    groups = lax.axis_size("dp")
    narrow = lax.axis_size("mp")
    place = lax.axis_index("mp")
    own_rows = mixer_master.shape[1]
    channels = groups * own_rows
    part = full // narrow
    quick = groups == 16 and narrow == 2

    cot_full = mp_gather(cotangent.reshape(rows, part))

    domain_ids = jnp.arange(NDOM, dtype=jnp.int32)
    member = (domains[..., 0][..., None] == domain_ids).astype(F32)
    live_counts = lengths.astype(F32)
    counts = jnp.sum(member * live_counts[..., None], axis=(0, 1))
    gain_low = gain_master.astype(BF)
    mixer_low = mixer_master.astype(BF)
    in_blocks = mixer_low[:3].reshape(3, own_rows, groups, narrow, own_rows)
    in_blocks = in_blocks.transpose(3, 0, 1, 2, 4).reshape(narrow, 3, own_rows, channels)
    if quick:
        small = jnp.zeros((8, 128), F32)
        small = small.at[:3, :own_rows].set(gain_low.astype(F32)).at[3, :NDOM].set(counts)
        mixer_in, mixer_out, small = gather_call(in_blocks, mixer_low[3], small, 2)
        mixer_in = mixer_in.reshape(3, full, channels)
        mixer_out = mixer_out.reshape(channels, full)
        small = small.reshape(groups, narrow, 8, 128)
        gain_full = small[:, :, :3, :own_rows].transpose(2, 0, 1, 3).reshape(3, full)
        counts = jnp.sum(small[:, 0, 3, :NDOM], axis=0)
    else:
        gain_full = lax.all_gather(gain_low, ("dp", "mp"), axis=1, tiled=True).astype(F32)
        in_rows = mp_swap(in_blocks).transpose(1, 0, 2, 3).reshape(3, narrow * own_rows, channels)
        mixer_in = lax.all_gather(in_rows, "dp", axis=1, tiled=True)
        mixer_out = lax.all_gather(mixer_low[3], "dp", axis=0, tiled=True)
        counts = lax.psum(counts, "dp")
    glu_low = jnp.concatenate([glu_in_master.astype(BF), glu_out_master.astype(BF).T[None]])
    glu_low, mixer_in, cot_full = lax.optimization_barrier((glu_low, mixer_in, cot_full))
    glu = lax.all_gather(glu_low, "dp", axis=1, tiled=True)

    seq_weight = jnp.sum(counts) / (NDOM * jnp.sum(member * counts, axis=-1))
    positions = jnp.arange(length, dtype=jnp.int32)
    token_weight = jnp.where(positions[None, :] < lengths[:, :1], seq_weight[:, :1], 0.0)
    token_weight = token_weight.reshape(rows, 1)

    own_channels = lambda v: lax.dynamic_index_in_dim(
        v.reshape(groups, narrow, own_rows), place, 1, keepdims=False
    ).reshape(channels)
    bound = own_channels(lower_bound)
    state_gain = own_channels(gain_full[1])

    token_rows = tokens.reshape(rows, full)
    seq_in = token_rows.astype(F32)
    inverse_in = inverse_rms(seq_in)
    unit_in = seq_in * inverse_in
    normed_in = (unit_in * gain_full[0]).astype(BF)
    pre = jnp.einsum("td,kde->kte", normed_in, mixer_in, preferred_element_type=F32)
    pre = pre.reshape(3, batches, length, channels)
    states, raw, square = scan_forward(pre, bound, state_gain)
    square = mp_sum_wide(square.reshape(rows, 1))
    inverse_state = lax.rsqrt(square / full + EPSILON)
    mixed = jnp.dot(raw.reshape(rows, channels), mixer_out, preferred_element_type=F32)
    branch_mix = inverse_state * mp_sum(mixed)
    middle = seq_in + branch_mix
    inverse_mid = inverse_rms(middle)
    unit_mid = middle * inverse_mid
    normed_mid = (unit_mid * gain_full[2]).astype(BF)

    back = cot_full.astype(F32) * token_weight
    back_low = back.astype(BF)
    across = (((1,), (1,)), ((), ()))
    down = (((0,), (0,)), ((), ()))
    dot = functools.partial(lax.dot_general, preferred_element_type=F32)
    if quick:
        glu_sums, sum_own, sum_came, half_own, half_came = glu_call(normed_mid, back_low, glu, 0)
        branch = half_own.astype(F32) + half_came.astype(F32)
    else:
        pre_act = jnp.dot(normed_mid, glu[0], preferred_element_type=F32)
        pre_up = jnp.dot(normed_mid, glu[1], preferred_element_type=F32)
        grad_hidden = jnp.dot(back_low, glu[2], preferred_element_type=F32)
        act_part = jax.nn.silu(pre_act)
        hidden = (act_part * pre_up).astype(BF)
        grad_act = (grad_hidden * pre_up * silu_slope(pre_act)).astype(BF)
        grad_up = (grad_hidden * act_part).astype(BF)
        grad_normed = mp_sum(dot(grad_act, glu[0], across) + dot(grad_up, glu[1], across))
        glu_grad = jnp.stack(
            [dot(normed_mid, grad_act, down), dot(normed_mid, grad_up, down), dot(back_low, hidden, down)]
        ).astype(BF)
        glu_own = lax.psum_scatter(glu_grad, "dp", scatter_dimension=1, tiled=True).astype(F32)
        branch = mp_scatter(dot(hidden, glu[2], across))
    own_features = lambda v: lax.dynamic_slice_in_dim(v, place * part, part, v.ndim - 1)
    layer_out = (own_features(middle) + branch).astype(BF)

    if quick:
        grad_middle_own, middle_low, state_mean, grad_gated, gain_mid = middle_back(
            sum_own, sum_came, middle, cot_full, token_rows, token_weight, gain_full[2], mixer_out
        )
        gain_mid = gain_mid[0]
    else:
        inverse_mid = inverse_rms(middle)
        unit_mid = middle * inverse_mid
        gain_mid = jnp.sum(grad_normed * unit_mid, axis=0)
        scaled_mid = grad_normed * gain_full[2]
        grad_middle = back + inverse_mid * (
            scaled_mid - unit_mid * jnp.mean(scaled_mid * unit_mid, axis=-1, keepdims=True)
        )
        grad_middle_own = own_features(grad_middle)
        middle_low = grad_middle.astype(BF)
        state_mean = jnp.mean(middle_low.astype(F32) * branch_mix, axis=-1, keepdims=True)
        grad_gated = dot(middle_low, mixer_out, across)
    by_batch = lambda v: v.reshape(batches, length, v.shape[-1])
    grad_pre, gated_out, gain_state, pre_dot = scan_backward(
        pre, states, by_batch(grad_gated), by_batch(inverse_state), by_batch(state_mean), bound, state_gain
    )
    grad_pre = grad_pre.reshape(3, rows, channels)
    gated_out = gated_out.reshape(rows, channels)
    in_mean = mp_sum_wide(pre_dot.reshape(rows, 1)) / full
    gain_state = jnp.sum(gain_state, axis=0).reshape(groups, 1, own_rows)
    gain_state = lax.dynamic_update_slice_in_dim(
        jnp.zeros((groups, narrow, own_rows), F32), gain_state, place, 1
    )
    device = lax.axis_index("dp") * narrow + place
    if quick:
        gain_parts = jnp.stack(
            [
                jnp.zeros((groups, narrow * own_rows), F32),
                gain_state.reshape(groups, narrow * own_rows),
                0.5 * gain_mid.reshape(groups, narrow * own_rows),
            ],
            axis=1,
        )
        gain_parts = jnp.pad(gain_parts, ((0, 0), (0, 5), (0, 0)))
        in_own, out_own, gain_own, grad_normed_in = mixer_call(
            normed_in.T, grad_pre, gated_out.T, middle_low, gain_parts, token_rows, inverse_in, mixer_in, 1
        )
        gain_own = lax.dynamic_slice_in_dim(gain_own, place * own_rows, own_rows, 1)
        in_own = in_own.reshape(3, own_rows, narrow, groups, own_rows).transpose(0, 1, 3, 2, 4)
    else:
        grad_mix_out = dot(gated_out, middle_low, down).astype(BF)
        grad_mix_in = jnp.einsum("td,kte->kde", normed_in, grad_pre, preferred_element_type=F32)
        in_own = lax.psum_scatter(grad_mix_in.astype(BF), "dp", scatter_dimension=1, tiled=True)
        out_own = lax.psum_scatter(grad_mix_out, "dp", scatter_dimension=0, tiled=True)
        in_own = mp_swap(in_own.reshape(3, narrow, own_rows, channels).transpose(1, 0, 2, 3))
        in_own = in_own.reshape(narrow, 3, own_rows, groups, own_rows).transpose(1, 2, 3, 0, 4)
        grad_normed_in = jnp.einsum("kte,kde->td", grad_pre, mixer_in, preferred_element_type=F32)
        gain_in = jnp.sum(grad_normed_in * unit_in, axis=0)
        grad_normed_in = mp_scatter(grad_normed_in)
        gain_rows = jnp.stack([gain_in, gain_state.reshape(full), gain_mid / narrow])
        gain_total = lax.psum(gain_rows, ("dp", "mp"))
        gain_own = lax.dynamic_slice_in_dim(gain_total, device * own_rows, own_rows, 1)
    in_own = in_own.reshape(3, own_rows, full).astype(F32)
    out_own = out_own.astype(F32)
    unit_in_own = own_features(token_rows).astype(F32) * inverse_in
    grad_seq = grad_middle_own + inverse_in * (
        grad_normed_in * own_features(gain_full[0]) - unit_in_own * in_mean
    )
    grad_tokens = grad_seq.astype(BF)

    scale = 1.0 / (batches * groups * tokens.shape[1])
    update = functools.partial(adamw_update, count=STEP_NUMBER)
    mixer_own = jnp.concatenate([in_own, out_own[None]])
    mixer_new = update(
        mixer_master, mixer_first, mixer_second, mixer_own * scale, rate=MATRIX_RATE, decay=DECAY_RATE
    )
    gain_new = update(
        gain_master, gain_first, gain_second, gain_own * scale, rate=GAIN_RATE, decay=0.0
    )
    glu_ins = (glu_in_master, glu_in_first, glu_in_second)
    glu_downs = (glu_out_master, glu_out_first, glu_out_second)
    if quick:
        glu_in_new, glu_out_new = glu_update(glu_sums, glu_ins, glu_downs, scale)
    else:
        glu_in_new = update(*glu_ins, glu_own[:2] * scale, rate=MATRIX_RATE, decay=DECAY_RATE)
        glu_out_new = update(*glu_downs, glu_own[2].T * scale, rate=MATRIX_RATE, decay=DECAY_RATE)
    return (
        layer_out.reshape(batches, 1, length, part),
        grad_tokens.reshape(batches, 1, length, part),
        *mixer_new,
        *glu_in_new,
        *glu_out_new,
        *gain_new,
    )


def solution(mesh):
    weights = (
        [P(None, ("dp", "mp"), None)] * 3
        + [P(None, "dp", "mp")] * 3
        + [P("mp", "dp")] * 3
        + [P(None, ("dp", "mp"))] * 3
    )
    in_specs = (
        P(None, "dp", None, None),
        P(None, "dp", None, "mp"),
        P(None, "dp"),
        P(None, "dp", None),
        P(),
        *weights,
    )
    out_specs = (P(None, "dp", None, "mp"), P(None, "dp", None, "mp"), *weights)
    return jax.shard_map(shards, mesh=mesh, in_specs=in_specs, out_specs=out_specs, check_vma=False)
```

```python
import functools

import jax
import jax.numpy as jnp
from jax import lax
from jax.experimental import pallas as pl
from jax.experimental.pallas import tpu as pltpu
from jax.sharding import PartitionSpec as P

NDOM = 8

EPSILON = 1e-06
BETA_ONE = 0.9
BETA_TWO = 0.95
ADAM_EPSILON = 1e-08
DECAY_RATE = 0.1
MATRIX_RATE = 0.06
GAIN_RATE = 0.5
STEP_NUMBER = 3.0

BF = jnp.bfloat16
F32 = jnp.float32
VMEM_LIMIT = 56 * 1024 * 1024


def inverse_rms(values):
    return lax.rsqrt(jnp.mean(values * values, axis=-1, keepdims=True) + EPSILON)


def silu_slope(values):
    sigma = jax.nn.sigmoid(values)
    return sigma * (1.0 + values * (1.0 - sigma))


def adamw_update(master, first, second, gradient, count, rate, decay):
    first_new = BETA_ONE * first + (1.0 - BETA_ONE) * gradient
    second_new = BETA_TWO * second + (1.0 - BETA_TWO) * gradient * gradient
    first_hat = first_new / (1.0 - BETA_ONE**count)
    second_hat = second_new / (1.0 - BETA_TWO**count)
    master_new = master - rate * (
        first_hat / (jnp.sqrt(second_hat) + ADAM_EPSILON) + decay * master
    )
    return (master_new, first_new, second_new)


def partner_swap(value):
    return lax.ppermute(value, "mp", [(0, 1), (1, 0)])


def mp_sum(part):
    low = part.astype(BF)
    if lax.axis_size("mp") == 2:
        return low.astype(F32) + partner_swap(low).astype(F32)
    return lax.psum(low.astype(F32), "mp")


def mp_sum_wide(part):
    if lax.axis_size("mp") == 2:
        return part + partner_swap(part)
    return lax.psum(part, "mp")


def mp_scatter(part):
    if lax.axis_size("mp") == 2:
        half = part.shape[1] // 2
        place = lax.axis_index("mp")
        own = lax.dynamic_slice_in_dim(part, place * half, half, 1)
        other = lax.dynamic_slice_in_dim(part, (1 - place) * half, half, 1)
        return own.astype(BF).astype(F32) + partner_swap(other.astype(BF)).astype(F32)
    return lax.psum_scatter(part.astype(BF), "mp", scatter_dimension=1, tiled=True).astype(F32)


def mp_swap(pieces):
    if lax.axis_size("mp") == 2:
        place = lax.axis_index("mp")
        own = lax.dynamic_index_in_dim(pieces, place, 0, keepdims=False)
        came = partner_swap(lax.dynamic_index_in_dim(pieces, 1 - place, 0, keepdims=False))
        first = place == 0
        return jnp.stack([jnp.where(first, own, came), jnp.where(first, came, own)])
    return lax.all_to_all(pieces, "mp", 0, 0, tiled=False)


def mp_gather(part):
    if lax.axis_size("mp") == 2:
        place = lax.axis_index("mp")
        came = partner_swap(part)
        first = place == 0
        return jnp.concatenate([jnp.where(first, part, came), jnp.where(first, came, part)], axis=1)
    return lax.all_gather(part, "mp", axis=1, tiled=True)


SUB_ROWS = 8
TILE_ROWS = 64


def channel_block(width):
    return 512 if width % 512 == 0 else width


def scan_rows(total, decay, carry):
    row = lax.broadcasted_iota(jnp.int32, total.shape, 0)
    shift = 1
    while shift < SUB_ROWS:
        keep = row >= shift
        total = total + decay * jnp.where(keep, pltpu.roll(total, shift, 0), 0.0)
        decay = decay * jnp.where(keep, pltpu.roll(decay, shift, 0), 1.0)
        shift *= 2
    return total + decay * carry


def scan_rows_back(total, decay, carry):
    row = lax.broadcasted_iota(jnp.int32, total.shape, 0)
    shift = 1
    while shift < SUB_ROWS:
        keep = row < SUB_ROWS - shift
        total = total + decay * jnp.where(keep, pltpu.roll(total, SUB_ROWS - shift, 0), 0.0)
        decay = decay * jnp.where(keep, pltpu.roll(decay, SUB_ROWS - shift, 0), 1.0)
        shift *= 2
    return total + decay * carry


def scan_forward_kernel(pre_ref, bound_ref, gain_ref, states_ref, raw_ref, square_ref):
    length, width = states_ref.shape[1], states_ref.shape[2]
    bound = bound_ref[...]
    gain = gain_ref[...]
    first_block = pl.program_id(1) == 0

    def step(index, carry):
        rows = pl.ds(pl.multiple_of(index * TILE_ROWS, TILE_ROWS), TILE_ROWS)
        forget = bound + (1.0 - bound) * jax.nn.sigmoid(pre_ref[1, 0, rows, :])
        total = (1.0 - forget) * jax.nn.silu(pre_ref[0, 0, rows, :])
        parts = []
        for low in range(0, TILE_ROWS, SUB_ROWS):
            part = scan_rows(total[low : low + SUB_ROWS], forget[low : low + SUB_ROWS], carry)
            carry = part[SUB_ROWS - 1 : SUB_ROWS]
            parts.append(part)
        states = jnp.concatenate(parts)
        states_ref[0, rows, :] = states
        raw = states * gain * jax.nn.silu(pre_ref[2, 0, rows, :])
        raw_ref[0, rows, :] = raw.astype(raw_ref.dtype)
        square = jnp.sum(states * states, axis=-1, keepdims=True)
        square_ref[0, rows, :] = square + jnp.where(first_block, 0.0, square_ref[0, rows, :])
        return carry

    lax.fori_loop(0, length // TILE_ROWS, step, jnp.zeros((1, width), F32))


def scan_forward(pre, bound, gain):
    _, batches, length, width = pre.shape
    block = channel_block(width)
    return pl.pallas_call(
        scan_forward_kernel,
        grid=(batches, width // block),
        in_specs=[
            pl.BlockSpec((3, 1, length, block), lambda b, c: (0, b, 0, c)),
            pl.BlockSpec((1, block), lambda b, c: (0, c)),
            pl.BlockSpec((1, block), lambda b, c: (0, c)),
        ],
        out_specs=[
            pl.BlockSpec((1, length, block), lambda b, c: (b, 0, c)),
            pl.BlockSpec((1, length, block), lambda b, c: (b, 0, c)),
            pl.BlockSpec((1, length, 1), lambda b, c: (b, 0, 0)),
        ],
        out_shape=[
            jax.ShapeDtypeStruct((batches, length, width), F32),
            jax.ShapeDtypeStruct((batches, length, width), BF),
            jax.ShapeDtypeStruct((batches, length, 1), F32),
        ],
        compiler_params=pltpu.CompilerParams(vmem_limit_bytes=VMEM_LIMIT),
        cost_estimate=pl.CostEstimate(
            flops=batches * length * width * 40,
            bytes_accessed=batches * length * width * 18,
            transcendentals=batches * length * width * 3,
        ),
    )(pre, bound[None], gain[None])


def scan_backward_kernel(
    pre_ref, states_ref, gated_ref, inverse_ref, mean_ref, bound_ref, gain_ref,
    grad_ref, out_ref, gain_grad_ref, dot_ref,
):
    length, width = states_ref.shape[1], states_ref.shape[2]
    bound = bound_ref[...]
    gain = gain_ref[...]
    first_block = pl.program_id(1) == 0
    row = lax.broadcasted_iota(jnp.int32, (TILE_ROWS, width), 0)
    tiles = length // TILE_ROWS

    def step(index, carry):
        carried_next, forget_next, gain_sum = carry
        place = tiles - 1 - index
        rows = pl.ds(pl.multiple_of(place * TILE_ROWS, TILE_ROWS), TILE_ROWS)
        pre_input = pre_ref[0, 0, rows, :]
        pre_forget = pre_ref[1, 0, rows, :]
        pre_gate = pre_ref[2, 0, rows, :]
        states = states_ref[0, rows, :]
        inverse = inverse_ref[0, rows, :]
        grad_gated = gated_ref[0, rows, :]
        unit = states * inverse
        gate_sig = jax.nn.sigmoid(pre_gate)
        gate = pre_gate * gate_sig
        out_ref[0, rows, :] = (unit * gain * gate).astype(out_ref.dtype)
        gain_sum = gain_sum + grad_gated * unit * gate
        scaled = grad_gated * gain
        grad_gate = (scaled * unit * (gate_sig * (1.0 + pre_gate * (1.0 - gate_sig)))).astype(BF)
        grad_ref[2, 0, rows, :] = grad_gate
        total = inverse * (scaled * gate - unit * mean_ref[0, rows, :])
        sigma = jax.nn.sigmoid(pre_forget)
        forget = bound + (1.0 - bound) * sigma
        decay = jnp.where(row == TILE_ROWS - 1, forget_next, pltpu.roll(forget, TILE_ROWS - 1, 0))
        parts = []
        for low in range(TILE_ROWS - SUB_ROWS, -1, -SUB_ROWS):
            part = scan_rows_back(
                total[low : low + SUB_ROWS], decay[low : low + SUB_ROWS], carried_next
            )
            carried_next = part[0:1]
            parts.insert(0, part)
        carried = jnp.concatenate(parts)
        before_rows = pl.ds(
            pl.multiple_of(jnp.maximum(place - 1, 0) * TILE_ROWS, TILE_ROWS), TILE_ROWS
        )
        before = states_ref[0, before_rows, :][TILE_ROWS - 1 : TILE_ROWS, :]
        before = jnp.where(place == 0, 0.0, before)
        earlier = jnp.where(row == 0, before, pltpu.roll(states, 1, 0))
        input_sig = jax.nn.sigmoid(pre_input)
        fresh = pre_input * input_sig
        slope = input_sig * (1.0 + pre_input * (1.0 - input_sig))
        grad_input = (carried * (1.0 - forget) * slope).astype(BF)
        grad_forget = (
            carried * (earlier - fresh) * (1.0 - bound) * sigma * (1.0 - sigma)
        ).astype(BF)
        grad_ref[0, 0, rows, :] = grad_input
        grad_ref[1, 0, rows, :] = grad_forget
        dots = (
            grad_input.astype(F32) * pre_input
            + grad_forget.astype(F32) * pre_forget
            + grad_gate.astype(F32) * pre_gate
        )
        dot = jnp.sum(dots, axis=-1, keepdims=True)
        dot_ref[0, rows, :] = dot + jnp.where(first_block, 0.0, dot_ref[0, rows, :])
        return carried_next, forget[0:1, :], gain_sum

    zero = jnp.zeros((1, width), F32)
    _, _, gain_sum = lax.fori_loop(
        0, tiles, step, (zero, zero, jnp.zeros((TILE_ROWS, width), F32))
    )
    gain_grad_ref[0] = jnp.sum(gain_sum, axis=0, keepdims=True)


def scan_backward(pre, states, grad_gated, inverse, mean, bound, gain):
    _, batches, length, width = pre.shape
    block = channel_block(width)
    whole = pl.BlockSpec((1, length, block), lambda b, c: (b, 0, c))
    column = pl.BlockSpec((1, length, 1), lambda b, c: (b, 0, 0))
    line = pl.BlockSpec((1, block), lambda b, c: (0, c))
    three = pl.BlockSpec((3, 1, length, block), lambda b, c: (0, b, 0, c))
    return pl.pallas_call(
        scan_backward_kernel,
        grid=(batches, width // block),
        in_specs=[three, whole, whole, column, column, line, line],
        out_specs=[
            three,
            whole,
            pl.BlockSpec((1, 1, block), lambda b, c: (b, 0, c)),
            column,
        ],
        out_shape=[
            jax.ShapeDtypeStruct((3, batches, length, width), BF),
            jax.ShapeDtypeStruct((batches, length, width), BF),
            jax.ShapeDtypeStruct((batches, 1, width), F32),
            jax.ShapeDtypeStruct((batches, length, 1), F32),
        ],
        compiler_params=pltpu.CompilerParams(vmem_limit_bytes=VMEM_LIMIT),
        cost_estimate=pl.CostEstimate(
            flops=batches * length * width * 80,
            bytes_accessed=batches * length * width * 28,
            transcendentals=batches * length * width * 3,
        ),
    )(pre, states, grad_gated, inverse, mean, bound[None], gain[None])


MESH_ID = pl.DeviceIdType.MESH
DEPTH = 4
LANES = 256
X_LAG = 4
Z_LAG = X_LAG + 2
SWAP_LAG = 2


def device_place():
    dp = lax.axis_index("dp")
    return dp // 4, lax.rem(dp // 2, 2), lax.rem(dp, 2)


def device_at(z, x, core):
    return (z * 4 + x * 2 + core, lax.axis_index("mp"))


def scatter_barrier(z, x, core, with_mp=False):
    barrier = pltpu.get_barrier_semaphore()
    targets = [device_at(z, x, 1 - core), device_at(z, 1 - x, core)]
    targets += [device_at(lax.rem(z + hop, DEPTH), x, core) for hop in range(1, DEPTH)]
    if with_mp:
        targets.append((lax.axis_index("dp"), 1 - lax.axis_index("mp")))
    for target in targets:
        pl.semaphore_signal(barrier, 1, device_id=target, device_id_type=MESH_ID)
    pl.semaphore_wait(barrier, len(targets))


def scatter_step(step, chunks, compute, finish, scratch):
    (own, core_out, core_in, keep, x_out, x_in, sums, mine, z_out, z_in,
     core_send, core_recv, x_send, x_recv, z_send, z_recv) = scratch
    z, x, core = device_place()

    def core_copy(p):
        return pltpu.make_async_remote_copy(
            core_out.at[lax.rem(p, 2)], core_in.at[lax.rem(p, 4)],
            core_send.at[lax.rem(p, 2)], core_recv.at[lax.rem(p, 4)],
            device_id=device_at(z, x, 1 - core), device_id_type=MESH_ID)

    def x_copy(p):
        return pltpu.make_async_remote_copy(
            x_out.at[lax.rem(p, X_LAG)], x_in.at[lax.rem(p, 2 * X_LAG)],
            x_send.at[lax.rem(p, X_LAG)], x_recv.at[lax.rem(p, 2 * X_LAG)],
            device_id=device_at(z, 1 - x, core), device_id_type=MESH_ID)

    def z_copy(p, hop):
        return pltpu.make_async_remote_copy(
            z_out.at[lax.rem(p, 4), hop - 1], z_in.at[lax.rem(p, 8), hop - 1],
            z_send.at[lax.rem(p, 4), hop - 1], z_recv.at[lax.rem(p, 8), hop - 1],
            device_id=device_at(lax.rem(z + hop, DEPTH), x, core), device_id_type=MESH_ID)

    @pl.when(step < chunks)
    def _():
        @pl.when(step >= 2)
        def _():
            core_copy(step - 2).wait_send()

        def to_partner(value):
            core_out[lax.rem(step, 2)] = value.astype(BF)

        def to_own(value):
            own[lax.rem(step, 2)] = value

        compute(step, 1 - core, to_partner)
        core_copy(step).start()
        compute(step, core, to_own)

    @pl.when((step >= 1) & (step < chunks + 1))
    def _():
        p = step - 1
        core_copy(p).wait_recv()

        @pl.when(p >= X_LAG)
        def _():
            x_copy(p - X_LAG).wait_send()

        two, four, slot = lax.rem(p, 2), lax.rem(p, 4), lax.rem(p, X_LAG)
        x_out[slot] = (own[two, :, 1 - x] + core_in[four, :, 1 - x].astype(F32)).astype(BF)
        x_copy(p).start()
        keep[slot] = own[two, :, x] + core_in[four, :, x].astype(F32)

    @pl.when((step >= X_LAG) & (step < chunks + X_LAG))
    def _():
        p = step - X_LAG
        x_copy(p).wait_recv()
        four = lax.rem(p, 4)
        sums[...] = keep[lax.rem(p, X_LAG)] + x_in[lax.rem(p, 2 * X_LAG)].astype(F32)
        for hop in range(1, DEPTH):
            @pl.when(p >= 4)
            def _():
                z_copy(p - 4, hop).wait_send()

            z_out[four, hop - 1] = sums[lax.rem(z + hop, DEPTH)].astype(BF)
            z_copy(p, hop).start()
        mine[four] = sums[z]

    @pl.when((step >= Z_LAG) & (step < chunks + Z_LAG))
    def _():
        p = step - Z_LAG
        for hop in range(1, DEPTH):
            z_copy(p, hop).wait_recv()
        got = z_in.at[lax.rem(p, 8)]
        finish(p, mine[lax.rem(p, 4)] + got[0].astype(F32) + got[1].astype(F32) + got[2].astype(F32))

    @pl.when(step == chunks + Z_LAG - 1)
    def _():
        for p in range(chunks - 2, chunks):
            core_copy(p).wait_send()
        for p in range(chunks - X_LAG, chunks):
            x_copy(p).wait_send()
        for p in range(chunks - 4, chunks):
            for hop in range(1, DEPTH):
                z_copy(p, hop).wait_send()


def scatter_scratch(rows, lanes):
    quad = (DEPTH, 2, rows, lanes)
    line = (DEPTH, rows, lanes)
    dma = pltpu.SemaphoreType.DMA
    return [
        pltpu.VMEM((2, *quad), F32),
        pltpu.VMEM((2, *quad), BF),
        pltpu.VMEM((4, *quad), BF),
        pltpu.VMEM((X_LAG, *line), F32),
        pltpu.VMEM((X_LAG, *line), BF),
        pltpu.VMEM((2 * X_LAG, *line), BF),
        pltpu.VMEM(line, F32),
        pltpu.VMEM((4, rows, lanes), F32),
        pltpu.VMEM((4, DEPTH - 1, rows, lanes), BF),
        pltpu.VMEM((8, DEPTH - 1, rows, lanes), BF),
        dma((2,)), dma((4,)), dma((X_LAG,)), dma((2 * X_LAG,)), dma((4, DEPTH - 1)), dma((8, DEPTH - 1)),
    ]


def scatter_out(chunks, rows, lanes):
    spec = pl.BlockSpec((1, rows, lanes), lambda q: (jnp.maximum(q - Z_LAG, 0), 0, 0))
    return spec, jax.ShapeDtypeStruct((chunks, rows, lanes), F32)


def fixed(shape):
    return pl.BlockSpec(shape, lambda q: (0,) * len(shape), pipeline_mode=pl.Buffered(1))


def glu_kernel(
    hidden_blocks, full_blocks, normed_ref, back_ref, left_ref, left_back_ref, glu_ref,
    out_ref, sum_own, sum_came, half_own, half_send, half_came,
    acts, weights_in, weights_back, sum_stage, half_stage,
    in_sem, back_sem, stage_sem, sum_send, sum_recv, half_send_sem, half_recv, *scratch,
):
    z, x, core = device_place()
    dp, mp = lax.axis_index("dp"), lax.axis_index("mp")
    step = pl.program_id(0)
    chunks = 3 * hidden_blocks
    rows = normed_ref.shape[0]
    row_block = rows // 2
    half_blocks = full_blocks // 2
    across = (((1,), (1,)), ((), ()))
    spread = min(hidden_blocks + hidden_blocks // 2, 16)
    second = step - spread

    def first_tasks(at):
        return at * hidden_blocks // spread

    unit_block = first_tasks(step)
    in_second = (second >= 0) & (second < 2 * full_blocks)

    def lane_block(index):
        return pl.ds(pl.multiple_of(index * LANES, LANES), LANES)

    def load_in(index):
        return pltpu.make_async_copy(glu_ref.at[:, :, lane_block(index)], weights_in, in_sem)

    def load_back(index):
        return pltpu.make_async_copy(glu_ref.at[:, lane_block(index), :], weights_back, back_sem)

    def stage(index, kind, target):
        source = (sum_stage, half_stage)[kind].at[lax.rem(index, 2)]
        return pltpu.make_async_copy(source, target, stage_sem.at[lax.rem(index, 2), kind])

    def half_spot(index):
        return lax.rem(index, half_blocks)

    def sum_copy(index):
        return pltpu.make_async_remote_copy(
            sum_own.at[:, lane_block(index)], sum_came.at[:, lane_block(index)],
            sum_send.at[index], sum_recv.at[index], device_id=(dp, 1 - mp), device_id_type=MESH_ID)

    def half_copy(spot):
        return pltpu.make_async_remote_copy(
            half_send.at[:, lane_block(spot)], half_came.at[:, lane_block(spot)],
            half_send_sem.at[spot], half_recv.at[spot], device_id=(dp, 1 - mp), device_id_type=MESH_ID)

    @pl.when(step == 0)
    def _():
        load_in(0).start()
        load_back(0).start()
        scatter_barrier(z, x, core, with_mp=True)

    @pl.when((step < spread) & ((step == 0) | (unit_block > first_tasks(step - 1))))
    def _():
        load_in(unit_block).wait()
        lanes = lane_block(unit_block)

        def part(index, _):
            part_rows = pl.ds(pl.multiple_of(index * row_block, row_block), row_block)
            normed = normed_ref[part_rows, :]
            pre_act = jnp.dot(normed, weights_in[0], preferred_element_type=F32)
            pre_up = jnp.dot(normed, weights_in[1], preferred_element_type=F32)
            grad_hidden = jnp.dot(back_ref[part_rows, :], weights_in[2], preferred_element_type=F32)
            sigma = jax.nn.sigmoid(pre_act)
            act_part = pre_act * sigma
            acts[0, part_rows, lanes] = (
                grad_hidden * pre_up * (sigma * (1.0 + pre_act * (1.0 - sigma)))).astype(BF)
            acts[1, part_rows, lanes] = (grad_hidden * act_part).astype(BF)
            acts[2, part_rows, lanes] = (act_part * pre_up).astype(BF)
            return 0

        lax.fori_loop(0, rows // row_block, part, 0)

        @pl.when(unit_block + 1 < hidden_blocks)
        def _():
            load_in(unit_block + 1).start()

    @pl.when(in_second & (lax.rem(second, 2) == 1))
    def _():
        index = second // 2
        stage(index, 0, sum_own.at[:, lane_block(index)]).wait()
        sum_copy(index).start()
        spot = half_spot(index)
        stage(index, 1, half_own.at[:, lane_block(spot)]).wait()

        @pl.when(index // half_blocks != mp)
        def _():
            half_copy(spot).start()

    @pl.when(in_second & (lax.rem(second, 2) == 0))
    def _():
        index = second // 2
        load_back(index).wait()
        slot = lax.rem(index, 2)

        def part(at, _):
            part_rows = pl.ds(pl.multiple_of(at * row_block, row_block), row_block)
            dot = functools.partial(
                lax.dot_general, dimension_numbers=across, preferred_element_type=F32)
            grad_normed = dot(acts[0, part_rows, :], weights_back[0])
            grad_normed += dot(acts[1, part_rows, :], weights_back[1])
            sum_stage[slot, part_rows, :] = grad_normed.astype(BF)
            half_stage[slot, part_rows, :] = dot(acts[2, part_rows, :], weights_back[2]).astype(BF)
            return 0

        lax.fori_loop(0, rows // row_block, part, 0)

        @pl.when(index + 1 < full_blocks)
        def _():
            load_back(index + 1).start()

        stage(index, 0, sum_own.at[:, lane_block(index)]).start()
        spot = half_spot(index)

        @pl.when(index // half_blocks == mp)
        def _():
            stage(index, 1, half_own.at[:, lane_block(spot)]).start()

        @pl.when(index // half_blocks != mp)
        def _():
            stage(index, 1, half_send.at[:, lane_block(spot)]).start()

    def compute(q, core_side, store):
        kind = lax.rem(q, 3)
        side_rows = left_ref.shape[3]

        def product(side_ref):
            side = side_ref[:, :, core_side].reshape(DEPTH * 2 * side_rows, rows)
            right = acts[kind, :, lane_block(q // 3)]
            store(jnp.dot(side, right, preferred_element_type=F32).reshape(
                DEPTH, 2, side_rows, LANES))

        pl.when(kind < 2)(lambda: product(left_ref))
        pl.when(kind == 2)(lambda: product(left_back_ref))

    def finish(p, value):
        out_ref[0] = value

    scatter_step(step, chunks, compute, finish, scratch)

    @pl.when(step == chunks + Z_LAG - 1)
    def _():
        for index in range(full_blocks):
            sum_copy(index).wait()
        for spot in range(half_blocks):
            half_copy(spot).wait()


def glu_call(normed, back_low, left_back, glu, collective):
    rows, full = normed.shape
    hidden = glu.shape[2]
    hidden_blocks, full_blocks = hidden // LANES, full // LANES
    block = full // 16
    chunks = 3 * hidden_blocks
    left_shape = (DEPTH, 2, 2, block, rows)
    any_space = pl.BlockSpec(memory_space=pl.ANY)
    out_spec, out_shape = scatter_out(chunks, block, LANES)
    dma = pltpu.SemaphoreType.DMA
    wide = jax.ShapeDtypeStruct((rows, full), BF)
    half = jax.ShapeDtypeStruct((rows, full // 2), BF)
    out, sum_own, sum_came, half_own, _, half_came = pl.pallas_call(
        functools.partial(glu_kernel, hidden_blocks, full_blocks),
        grid=(chunks + Z_LAG,),
        in_specs=[fixed(normed.shape), fixed(back_low.shape), fixed(left_shape), fixed(left_shape), any_space],
        out_specs=[out_spec] + [any_space] * 5,
        out_shape=[out_shape, wide, wide, half, half, half],
        scratch_shapes=[
            pltpu.VMEM((3, rows, hidden), BF),
            pltpu.VMEM((3, full, LANES), BF),
            pltpu.VMEM((3, LANES, hidden), BF),
            pltpu.VMEM((2, rows, LANES), BF),
            pltpu.VMEM((2, rows, LANES), BF),
            dma(()), dma(()), dma((2, 2)),
            dma((full_blocks,)), dma((full_blocks,)), dma((full_blocks // 2,)), dma((full_blocks // 2,)),
            *scatter_scratch(block, LANES),
        ],
        compiler_params=pltpu.CompilerParams(
            collective_id=collective, has_side_effects=True, vmem_limit_bytes=62 * 1024 * 1024),
        cost_estimate=pl.CostEstimate(
            flops=18 * rows * full * hidden, bytes_accessed=6 * full * hidden * 2,
            transcendentals=rows * hidden),
    )(normed, back_low, normed.T.reshape(left_shape), left_back.reshape(left_shape), glu)
    return out, sum_own, sum_came, half_own, half_came


def mixer_kernel(
    full_blocks, left_ref, grad_ref, left_out_ref, right_out_ref, gain_ref, tokens_ref, inverse_ref,
    weights_ref, dot_ref, out_ref, gain_out, half_own, half_send, half_came, dot_came,
    weights, token_block, gain_sum, gain_chunk, total, swap_out, swap_in, half_stage,
    load_sem, stage_sem, half_send_sem, half_recv, swap_send, swap_recv, dot_sem, *scratch,
):
    z, x, core = device_place()
    dp, mp = lax.axis_index("dp"), lax.axis_index("mp")
    step = pl.program_id(0)
    tokens, channels = grad_ref.shape[1], grad_ref.shape[2]
    block, half = left_ref.shape[3], left_out_ref.shape[3]
    outer = full_blocks // 2
    across = channels // LANES
    gains = outer + 3 * across
    chunks = gains + 1
    half_blocks = full_blocks // 2
    row_block = tokens // 2
    partner = (dp, 1 - mp)

    def lane_block(index):
        return pl.ds(pl.multiple_of(index * LANES, LANES), LANES)

    def loads(index):
        return (
            pltpu.make_async_copy(weights_ref.at[:, lane_block(index), :], weights, load_sem.at[0]),
            pltpu.make_async_copy(tokens_ref.at[:, lane_block(index)], token_block, load_sem.at[1]),
        )

    def stage(index, target):
        return pltpu.make_async_copy(
            half_stage.at[lax.rem(index, 2)], target, stage_sem.at[lax.rem(index, 2)])

    def half_copy(spot):
        return pltpu.make_async_remote_copy(
            half_send.at[:, lane_block(spot)], half_came.at[:, lane_block(spot)],
            half_send_sem.at[spot], half_recv.at[spot], device_id=partner, device_id_type=MESH_ID)

    def swap_copy(index):
        return pltpu.make_async_remote_copy(
            swap_out.at[lax.rem(index, 2)], swap_in.at[lax.rem(index, 8)],
            swap_send.at[lax.rem(index, 2)], swap_recv.at[lax.rem(index, 8)],
            device_id=partner, device_id_type=MESH_ID)

    dot_copy = pltpu.make_async_remote_copy(
        dot_ref, dot_came, dot_sem.at[0], dot_sem.at[1], device_id=partner, device_id_type=MESH_ID)

    @pl.when(step == 0)
    def _():
        for one in loads(0):
            one.start()
        gain_chunk[...] = jnp.zeros_like(gain_chunk)
        gain_sum[...] = jnp.zeros_like(gain_sum)
        scatter_barrier(z, x, core, with_mp=True)
        dot_copy.start()

    @pl.when((step > 0) & (step <= full_blocks))
    def _():
        index = step - 1
        spot = lax.rem(index, half_blocks)
        stage(index, half_own.at[:, lane_block(spot)]).wait()

        @pl.when(index // half_blocks != mp)
        def _():
            half_copy(spot).start()

    @pl.when(step < full_blocks)
    def _():
        for one in loads(step):
            one.wait()
        slot = lax.rem(step, 2)
        spot = lax.rem(step, half_blocks)

        def part(at, gain_in):
            part_rows = pl.ds(pl.multiple_of(at * row_block, row_block), row_block)
            dot = functools.partial(
                lax.dot_general, dimension_numbers=(((1,), (1,)), ((), ())), preferred_element_type=F32)
            grad = dot(grad_ref[0, part_rows, :], weights[0])
            grad += dot(grad_ref[1, part_rows, :], weights[1])
            grad += dot(grad_ref[2, part_rows, :], weights[2])
            half_stage[slot, part_rows, :] = grad.astype(BF)
            unit = token_block[part_rows, :].astype(F32) * inverse_ref[part_rows, :]
            return gain_in + jnp.sum(grad * unit, axis=0, keepdims=True)

        gain_in = lax.fori_loop(0, tokens // row_block, part, jnp.zeros((1, LANES), F32))
        gain_sum[2 * step, 0:1, :] = gain_in[:, :128]
        gain_sum[2 * step + 1, 0:1, :] = gain_in[:, 128:]

        @pl.when(step + 1 < full_blocks)
        def _():
            for one in loads(step + 1):
                one.start()

        @pl.when(step // half_blocks == mp)
        def _():
            stage(step, half_own.at[:, lane_block(spot)]).start()

        @pl.when(step // half_blocks != mp)
        def _():
            stage(step, half_send.at[:, lane_block(spot)]).start()

    def compute(q, core_side, store):
        @pl.when(q < outer)
        def _():
            side = left_out_ref[:, :, core_side].reshape(channels // 2, tokens)
            parts = [
                jnp.dot(side, right_out_ref[:, lane_block(2 * q + at)], preferred_element_type=F32)
                for at in (0, 1)
            ]
            parts = [part.reshape(DEPTH, 2, half, LANES) for part in parts]
            store(jnp.concatenate(parts, axis=2))

        @pl.when((q >= outer) & (q < gains))
        def _():
            at = q - outer
            side = left_ref[:, :, core_side].reshape(DEPTH * 2 * block, tokens)
            right = grad_ref[at // across, :, lane_block(lax.rem(at, across))]
            store(jnp.dot(side, right, preferred_element_type=F32).reshape(DEPTH, 2, block, LANES))

        @pl.when(q == gains)
        def _():
            for owner in range(2 * DEPTH):
                line = 2 * owner + core_side
                gain_chunk[owner // 2, owner % 2, 0:8, 0:128] = gain_ref[line] + gain_sum[line]
            store(gain_chunk[...])

    def finish(p, value):
        total[lax.rem(p, 4)] = value

        @pl.when(p >= outer)
        def _():
            index = p - outer

            @pl.when(index >= 2)
            def _():
                swap_copy(index - 2).wait_send()

            first = jnp.where(p == gains, 0, 1 - mp) * half
            rows = pl.ds(pl.multiple_of(first, half), half)
            swap_out[lax.rem(index, 2)] = total[lax.rem(p, 4), rows, :].astype(BF)
            swap_copy(index).start()

    scatter_step(step, chunks, compute, finish, scratch)

    @pl.when((step >= Z_LAG + SWAP_LAG) & (step < chunks + Z_LAG + SWAP_LAG))
    def _():
        p = step - Z_LAG - SWAP_LAG
        slot = lax.rem(p, 4)

        @pl.when(p < outer)
        def _():
            out_ref[0, :, :LANES] = total[slot, :half, :]
            out_ref[0, :, LANES:] = total[slot, half:, :]

        @pl.when(p >= outer)
        def _():
            swap_copy(p - outer).wait_recv()
            came = swap_in[lax.rem(p - outer, 8)].astype(F32)

            @pl.when(p < gains)
            def _():
                own = total[slot, pl.ds(pl.multiple_of(mp * half, half), half), :]
                first = jnp.where(mp == 0, own, came)
                second = jnp.where(mp == 0, came, own)
                for tile in (0, 1):
                    lanes = slice(128 * tile, 128 * tile + 128)
                    left, right = split_lanes(first[:, lanes], second[:, lanes])
                    out_ref[0, :, 256 * tile : 256 * tile + 128] = left
                    out_ref[0, :, 256 * tile + 128 : 256 * tile + 256] = right

            @pl.when(p == gains)
            def _():
                gain_out[...] = total[slot, 0:8, 0:128] + came[0:8, 0:128]

    @pl.when(step == chunks + Z_LAG + SWAP_LAG - 1)
    def _():
        for spot in range(half_blocks):
            half_copy(spot).wait()
        for index in range(gains - outer - 1, gains - outer + 1):
            swap_copy(index).wait_send()
        dot_copy.wait()


def mixer_call(
    left_in, grad_pre, left_out, right_out, gain_parts, tokens, inverse, weights, dots, collective
):
    _, rows, channels = grad_pre.shape
    full = left_in.shape[0]
    block, half = full // 16, channels // 16
    full_blocks, across = full // LANES, channels // LANES
    outer, inner = full_blocks // 2, 3 * across
    chunks = outer + inner + 1
    any_space = pl.BlockSpec(memory_space=pl.ANY)
    dma = pltpu.SemaphoreType.DMA
    part = jax.ShapeDtypeStruct((rows, full // 2), BF)

    def out_place(q):
        p = jnp.clip(q - Z_LAG - SWAP_LAG, 0, outer + inner - 1)
        inside = jnp.maximum(p - outer, 0)
        return (
            jnp.where(p < outer, 3, inside // across), 0, jnp.where(p < outer, p, lax.rem(inside, across)))

    out, gains, half_own, _, half_came, dot_came = pl.pallas_call(
        functools.partial(mixer_kernel, full_blocks),
        grid=(chunks + Z_LAG + SWAP_LAG,),
        in_specs=[
            fixed((DEPTH, 2, 2, block, rows)), fixed(grad_pre.shape),
            fixed((DEPTH, 2, 2, half, rows)), fixed(right_out.shape), fixed(gain_parts.shape),
            any_space, fixed(inverse.shape), any_space, any_space,
        ],
        out_specs=[
            pl.BlockSpec((1, half, 2 * LANES), out_place),
            pl.BlockSpec((8, 128), lambda q: (0, 0)),
        ] + [any_space] * 4,
        out_shape=[
            jax.ShapeDtypeStruct((4, half, full), F32), jax.ShapeDtypeStruct((8, 128), F32),
            part, part, part, jax.ShapeDtypeStruct(dots.shape, F32),
        ],
        scratch_shapes=[
            pltpu.VMEM((3, LANES, channels), BF),
            pltpu.VMEM((rows, LANES), BF),
            pltpu.VMEM((16, 8, 128), F32),
            pltpu.VMEM((DEPTH, 2, block, LANES), F32),
            pltpu.VMEM((4, block, LANES), F32),
            pltpu.VMEM((2, half, LANES), BF),
            pltpu.VMEM((8, half, LANES), BF),
            pltpu.VMEM((2, rows, LANES), BF),
            dma((2,)), dma((2,)), dma((full_blocks // 2,)), dma((full_blocks // 2,)),
            dma((2,)), dma((8,)), dma((2,)),
            *scatter_scratch(block, LANES),
        ],
        compiler_params=pltpu.CompilerParams(
            collective_id=collective, has_side_effects=True, vmem_limit_bytes=VMEM_LIMIT),
        cost_estimate=pl.CostEstimate(
            flops=14 * full * rows * channels, bytes_accessed=16 * full * channels, transcendentals=0),
    )(
        left_in.reshape(DEPTH, 2, 2, block, rows), grad_pre,
        left_out.reshape(DEPTH, 2, 2, half, rows), right_out, gain_parts, tokens, inverse, weights, dots,
    )
    return out, gains, half_own.astype(F32) + half_came.astype(F32), dot_came


def middle_back_kernel(
    sum_own_ref, sum_came_ref, middle_ref, cot_ref, tokens_ref, weight_ref, gain_ref, mixer_ref,
    grad_own_ref, low_ref, mean_ref, gated_ref, gain_grad_ref,
):
    rows, full = middle_ref.shape
    part = full // 2
    middle = middle_ref[...]
    inverse = lax.rsqrt(jnp.mean(middle * middle, axis=-1, keepdims=True) + EPSILON)
    unit = middle * inverse
    grad_normed = sum_own_ref[...].astype(F32) + sum_came_ref[...].astype(F32)
    product = grad_normed * unit
    before = jnp.where(pl.program_id(0) == 0, 0.0, gain_grad_ref[...])
    gain_grad_ref[...] = before + jnp.sum(product, axis=0, keepdims=True)
    dots = jnp.mean(product * gain_ref[...], axis=-1, keepdims=True)
    back = cot_ref[...].astype(F32) * weight_ref[...]
    grad = back + inverse * (grad_normed * gain_ref[...] - unit * dots)
    first = lax.axis_index("mp") == 0
    grad_own_ref[...] = jnp.where(first, grad[:, :part], grad[:, part:])
    low = grad.astype(BF)
    low_ref[...] = low
    branch = middle - tokens_ref[...].astype(F32)
    mean_ref[...] = jnp.mean(low.astype(F32) * branch, axis=-1, keepdims=True)
    gated_ref[...] = lax.dot_general(
        low, mixer_ref[...], (((1,), (1,)), ((), ())), preferred_element_type=F32)


def middle_back(sum_own, sum_came, middle, cot, tokens, weight, gain, mixer_out):
    rows, full = middle.shape
    channels = mixer_out.shape[0]
    step = 224 if rows % 224 == 0 else rows
    line = lambda width: pl.BlockSpec((step, width), lambda r: (r, 0))
    shape = jax.ShapeDtypeStruct
    return pl.pallas_call(
        middle_back_kernel,
        grid=(rows // step,),
        in_specs=[line(full)] * 5 + [line(1), fixed((1, full)), fixed(mixer_out.shape)],
        out_specs=[
            line(full // 2), line(full), line(1), line(channels),
            pl.BlockSpec((1, full), lambda r: (0, 0)),
        ],
        out_shape=[
            shape((rows, full // 2), F32), shape((rows, full), BF), shape((rows, 1), F32),
            shape((rows, channels), F32), shape((1, full), F32),
        ],
        compiler_params=pltpu.CompilerParams(vmem_limit_bytes=VMEM_LIMIT),
        cost_estimate=pl.CostEstimate(
            flops=2 * rows * full * channels, bytes_accessed=rows * full * 20, transcendentals=0),
    )(sum_own, sum_came, middle, cot, tokens, weight, gain[None], mixer_out)


def glu_update_kernel(scale, act_ref, up_ref, out_ref, *refs):
    in_refs, down_refs, in_new, down_new = refs[:3], refs[3:6], refs[6:9], refs[9:12]
    count = STEP_NUMBER
    for at, grad_ref in ((0, act_ref), (1, up_ref)):
        new = adamw_update(
            *(ref[at] for ref in in_refs), grad_ref[0] * scale, count, MATRIX_RATE, DECAY_RATE)
        for ref, value in zip(in_new, new):
            ref[at] = value
    new = adamw_update(
        *(ref[...] for ref in down_refs), out_ref[0].T * scale, count, MATRIX_RATE, DECAY_RATE)
    for ref, value in zip(down_new, new):
        ref[...] = value


def glu_update(sums, ins, downs, scale):
    _, rows, lanes = sums.shape
    blocks = ins[0].shape[2] // lanes
    sum_spec = lambda kind: pl.BlockSpec((1, rows, lanes), lambda q: (3 * q + kind, 0, 0))
    in_spec = pl.BlockSpec((2, rows, lanes), lambda q: (0, 0, q))
    down_spec = pl.BlockSpec((lanes, rows), lambda q: (q, 0))
    new = pl.pallas_call(
        functools.partial(glu_update_kernel, scale),
        grid=(blocks,),
        in_specs=[sum_spec(0), sum_spec(1), sum_spec(2)] + [in_spec] * 3 + [down_spec] * 3,
        out_specs=[in_spec] * 3 + [down_spec] * 3,
        out_shape=[jax.ShapeDtypeStruct(ins[0].shape, F32)] * 3 + [jax.ShapeDtypeStruct(downs[0].shape, F32)] * 3,
        compiler_params=pltpu.CompilerParams(vmem_limit_bytes=VMEM_LIMIT),
        cost_estimate=pl.CostEstimate(
            flops=60 * rows * lanes * blocks, bytes_accessed=84 * rows * lanes * blocks,
            transcendentals=6 * rows * lanes * blocks),
    )(sums, sums, sums, *ins, *downs)
    return tuple(new[:3]), tuple(new[3:])


ITEMS = 4


def split_lanes(first, second):
    low = lax.broadcasted_iota(jnp.int32, first.shape, 1) < 64
    return (
        jnp.where(low, first, pltpu.roll(second, 64, 1)),
        jnp.where(low, pltpu.roll(first, 64, 1), second),
    )


def gather_kernel(mixer_ref, gain_ref, lengths_ref, domains_ref, glu_in_ref, glu_out_ref, cot_ref,
                  all_in, all_out, all_small, cot_full, glu_low,
                  in_ref, out_ref, small_ref, right_send, left_send,
                  z_recv, x_send, x_recv, core_send, core_recv, y_send, y_recv, local_sem):
    z, x, core = device_place()
    mp = lax.axis_index("mp")
    barrier = pltpu.get_barrier_semaphore()
    for kind in range(3):
        for tile in range(in_ref.shape[3] // 128):
            first = mixer_ref[kind, :, 256 * tile : 256 * tile + 128]
            second = mixer_ref[kind, :, 256 * tile + 128 : 256 * tile + 256]
            for side, value in enumerate(split_lanes(first, second)):
                in_ref[side, kind, :, 128 * tile : 128 * tile + 128] = value.astype(BF)
    out_ref[...] = mixer_ref[3].astype(BF)
    lane = lax.broadcasted_iota(jnp.int32, (1, 128), 1)
    live = jnp.zeros((1, 128), F32)
    for batch in range(lengths_ref.shape[0]):
        count = lengths_ref[batch : batch + 1, :].astype(F32)
        live = live + jnp.where(lane == domains_ref[batch : batch + 1, :], count, 0.0)
    small_ref[...] = jnp.zeros_like(small_ref)
    small_ref[0:3, 0:64] = gain_ref[...].astype(BF).astype(F32)
    small_ref[3:4, :] = live
    right, left = lax.rem(z + 1, DEPTH), lax.rem(z + DEPTH - 1, DEPTH)
    dp = lax.axis_index("dp")
    for target in (
        device_at(right, x, core), device_at(left, x, core), device_at(z, 1 - x, core),
        device_at(z, x, 1 - core), (dp, 1 - mp),
    ):
        pl.semaphore_signal(barrier, 1, device_id=target, device_id_type=MESH_ID)
    pl.semaphore_wait(barrier, 5)

    def spot(item, zs, xs, cs, side=None):
        if item == 0:
            return all_in.at[:, zs, xs, cs, mp if side is None else side]
        if item == 1:
            return all_out.at[zs, xs, cs]
        if item == 2:
            return all_in.at[:, zs, xs, cs, 1 - mp]
        return all_small.at[zs, xs, cs]

    def own(item):
        if item == 0:
            return in_ref.at[mp]
        if item == 1:
            return out_ref
        return spot(item, z, x, core)

    def copy(item, zs, xs, target, send, recv, source=None):
        return pltpu.make_async_remote_copy(
            spot(item, zs, xs, core) if source is None else source, spot(item, zs, xs, core),
            send, recv, device_id=target, device_id_type=MESH_ID)

    def right_copy(item, zs, source=None):
        return copy(item, zs, x, device_at(right, x, core), right_send.at[zs, item], z_recv.at[zs, item], source)

    def left_copy(item, zs, source=None):
        return copy(item, zs, x, device_at(left, x, core), left_send.at[zs, item], z_recv.at[zs, item], source)

    def x_copy(item, zs, source=None):
        return copy(item, zs, x, device_at(z, 1 - x, core), x_send.at[zs, item], x_recv.at[zs, item], source)

    def core_copy(item, zs, xs, source=None):
        return copy(item, zs, xs, device_at(z, x, 1 - core), core_send.at[zs, xs, item], core_recv.at[zs, xs, item], source)

    y_copies = [
        pltpu.make_async_remote_copy(
            in_ref.at[1 - mp], all_in.at[:, z, x, core, mp], y_send.at[0], y_recv.at[0],
            device_id=(dp, 1 - mp), device_id_type=MESH_ID),
        pltpu.make_async_remote_copy(
            small_ref, all_small.at[z, x, core, mp], y_send.at[1], y_recv.at[1],
            device_id=(dp, 1 - mp), device_id_type=MESH_ID),
    ]
    locals_ = [
        pltpu.make_async_copy(in_ref.at[mp], spot(0, z, x, core), local_sem.at[0]),
        pltpu.make_async_copy(out_ref, spot(1, z, x, core), local_sem.at[1]),
        pltpu.make_async_copy(small_ref, all_small.at[z, x, core, mp], local_sem.at[2]),
    ]
    cot_lanes = pl.ds(pl.multiple_of(mp * cot_ref.shape[1], 128), cot_ref.shape[1])
    cot_local = pltpu.make_async_copy(cot_ref, cot_full.at[:, cot_lanes], local_sem.at[3])
    cot_copy = pltpu.make_async_remote_copy(
        cot_ref, cot_full.at[:, cot_lanes], y_send.at[2], y_recv.at[2],
        device_id=(dp, 1 - mp), device_id_type=MESH_ID)
    for one in y_copies:
        one.start()
    locals_[2].start()

    for item in range(ITEMS):
        if item == 2:
            y_copies[0].wait_recv()
        if item == 3:
            y_copies[1].wait_recv()
            locals_[2].wait()
        source = own(item)

        @pl.when(z < DEPTH - 1)
        def _():
            right_copy(item, z, source).start()

        @pl.when(z > 0)
        def _():
            left_copy(item, z, source).start()

        x_copy(item, z, source).start()
        core_copy(item, z, x, source).start()
    locals_[0].start()
    locals_[1].start()
    cot_copy.start()
    cot_local.start()
    glu_low[0:2] = glu_in_ref[...].astype(BF)
    for tile in range(glu_out_ref.shape[0] // 128):
        lanes = slice(128 * tile, 128 * tile + 128)
        glu_low[2, :, lanes] = glu_out_ref[lanes, :].T.astype(BF)

    def from_x(item, zs):
        pltpu.make_async_remote_copy(
            spot(item, zs, 1 - x, core), spot(item, zs, 1 - x, core), x_send.at[zs, item],
            x_recv.at[zs, item], device_id=device_at(z, 1 - x, core), device_id_type=MESH_ID).wait_recv()
        core_copy(item, zs, 1 - x).start()

    for hop in range(1, DEPTH + 1):
        for item in range(ITEMS):
            if hop < DEPTH:
                @pl.when(z >= hop)
                def _():
                    zs = z - hop
                    right_copy(item, zs).wait_recv()

                    @pl.when(z < DEPTH - 1)
                    def _():
                        right_copy(item, zs).start()

                    x_copy(item, zs).start()
                    core_copy(item, zs, x).start()

                @pl.when(z + hop < DEPTH)
                def _():
                    zs = z + hop
                    left_copy(item, zs).wait_recv()

                    @pl.when(z > 0)
                    def _():
                        left_copy(item, zs).start()

                    x_copy(item, zs).start()
                    core_copy(item, zs, x).start()
            if hop == 1:
                from_x(item, z)
            else:
                @pl.when(z >= hop - 1)
                def _():
                    from_x(item, z - (hop - 1))

                @pl.when(z + hop - 1 < DEPTH)
                def _():
                    from_x(item, z + (hop - 1))

    for item in range(ITEMS):
        for zs in range(DEPTH):
            @pl.when((z >= zs) & (z < DEPTH - 1))
            def _():
                right_copy(item, zs).wait_send()

            @pl.when((z <= zs) & (z > 0))
            def _():
                left_copy(item, zs).wait_send()

            x_copy(item, zs).wait_send()
            for xs in range(2):
                core_copy(item, zs, xs).wait()
    for one in y_copies:
        one.wait_send()
    locals_[0].wait()
    locals_[1].wait()
    cot_local.wait()
    cot_copy.wait_send()
    pltpu.make_async_remote_copy(
        cot_ref, cot_full.at[:, pl.ds(pl.multiple_of((1 - mp) * cot_ref.shape[1], 128), cot_ref.shape[1])],
        y_send.at[2], y_recv.at[2], device_id=(dp, 1 - mp), device_id_type=MESH_ID).wait_recv()


def gather_call(mixer, gain, lengths, domains, glu_in, glu_out, cot, collective):
    _, own_rows, full = mixer.shape
    channels = full // 2
    dma = pltpu.SemaphoreType.DMA
    any_space = pl.BlockSpec(memory_space=pl.ANY)
    in_vmem = pl.BlockSpec(memory_space=pltpu.VMEM)
    _, glu_rows, hidden = glu_in.shape
    return pl.pallas_call(
        gather_kernel,
        in_specs=[in_vmem] * 6 + [any_space],
        out_specs=[any_space] * 4 + [in_vmem],
        out_shape=[
            jax.ShapeDtypeStruct((3, DEPTH, 2, 2, 2, own_rows, channels), BF),
            jax.ShapeDtypeStruct((DEPTH, 2, 2, own_rows, full), BF),
            jax.ShapeDtypeStruct((DEPTH, 2, 2, 2, 8, 128), F32),
            jax.ShapeDtypeStruct((cot.shape[0], 2 * cot.shape[1]), BF),
            jax.ShapeDtypeStruct((3, glu_rows, hidden), BF),
        ],
        scratch_shapes=[
            pltpu.VMEM((2, 3, own_rows, channels), BF),
            pltpu.VMEM((own_rows, full), BF),
            pltpu.VMEM((8, 128), F32),
            dma((DEPTH, ITEMS)), dma((DEPTH, ITEMS)), dma((DEPTH, ITEMS)), dma((DEPTH, ITEMS)),
            dma((DEPTH, ITEMS)), dma((DEPTH, 2, ITEMS)), dma((DEPTH, 2, ITEMS)), dma((3,)), dma((3,)), dma((4,)),
        ],
        compiler_params=pltpu.CompilerParams(
            collective_id=collective, has_side_effects=True, vmem_limit_bytes=VMEM_LIMIT),
        cost_estimate=pl.CostEstimate(flops=0, bytes_accessed=300_000_000, transcendentals=0),
    )(mixer, gain, lengths, domains, glu_in, glu_out, cot)


def shards(
    tokens,
    cotangent,
    lengths,
    domains,
    lower_bound,
    mixer_master,
    mixer_first,
    mixer_second,
    glu_in_master,
    glu_in_first,
    glu_in_second,
    glu_out_master,
    glu_out_first,
    glu_out_second,
    gain_master,
    gain_first,
    gain_second,
):
    batches, _, length, full = tokens.shape
    rows = batches * length
    groups = lax.axis_size("dp")
    narrow = lax.axis_size("mp")
    place = lax.axis_index("mp")
    own_rows = mixer_master.shape[1]
    channels = groups * own_rows
    part = full // narrow
    quick = groups == 16 and narrow == 2 and own_rows == 64

    domain_ids = jnp.arange(NDOM, dtype=jnp.int32)
    member = (domains[..., 0][..., None] == domain_ids).astype(F32)
    cot_part = cotangent.reshape(rows, part)
    if quick:
        mixer_in, mixer_out, small, cot_full, glu_low = gather_call(
            mixer_master, gain_master, lengths, domains[..., 0], glu_in_master, glu_out_master, cot_part, 2
        )
        mixer_in = mixer_in.reshape(3, full, channels)
        mixer_out = mixer_out.reshape(channels, full)
        small = small.reshape(groups, narrow, 8, 128)
        gain_full = small[:, :, :3, :own_rows].transpose(2, 0, 1, 3).reshape(3, full)
        counts = jnp.sum(small[:, 0, 3, :NDOM], axis=0)
    else:
        gain_full = lax.all_gather(
            gain_master.astype(BF), ("dp", "mp"), axis=1, tiled=True
        ).astype(F32)
        mixer_low = mixer_master.astype(BF)
        in_blocks = mixer_low[:3].reshape(3, own_rows, groups, narrow, own_rows)
        in_blocks = in_blocks.transpose(3, 0, 1, 2, 4).reshape(narrow, 3, own_rows, channels)
        in_rows = mp_swap(in_blocks).transpose(1, 0, 2, 3).reshape(3, narrow * own_rows, channels)
        mixer_in = lax.all_gather(in_rows, "dp", axis=1, tiled=True)
        mixer_out = lax.all_gather(mixer_low[3], "dp", axis=0, tiled=True)
        counts = lax.psum(jnp.sum(member * lengths.astype(F32)[..., None], axis=(0, 1)), "dp")
        cot_full = mp_gather(cot_part)
        glu_low = jnp.concatenate([glu_in_master.astype(BF), glu_out_master.astype(BF).T[None]])
    glu = lax.all_gather(glu_low, "dp", axis=1, tiled=True)

    seq_weight = jnp.sum(counts) / (NDOM * jnp.sum(member * counts, axis=-1))
    positions = jnp.arange(length, dtype=jnp.int32)
    token_weight = jnp.where(positions[None, :] < lengths[:, :1], seq_weight[:, :1], 0.0)
    token_weight = token_weight.reshape(rows, 1)

    own_channels = lambda v: lax.dynamic_index_in_dim(
        v.reshape(groups, narrow, own_rows), place, 1, keepdims=False
    ).reshape(channels)
    bound = own_channels(lower_bound)
    state_gain = own_channels(gain_full[1])

    token_rows = tokens.reshape(rows, full)
    seq_in = token_rows.astype(F32)
    inverse_in = inverse_rms(seq_in)
    unit_in = seq_in * inverse_in
    normed_in = (unit_in * gain_full[0]).astype(BF)
    pre = jnp.einsum("td,kde->kte", normed_in, mixer_in, preferred_element_type=F32)
    pre = pre.reshape(3, batches, length, channels)
    states, raw, square = scan_forward(pre, bound, state_gain)
    square = mp_sum_wide(square.reshape(rows, 1))
    inverse_state = lax.rsqrt(square / full + EPSILON)
    mixed = jnp.dot(raw.reshape(rows, channels), mixer_out, preferred_element_type=F32)
    back_low = (cot_full.astype(F32) * token_weight).astype(BF)
    if quick:
        mixed = mixed.astype(BF)
        came, left_back, left_in = lax.optimization_barrier(
            (partner_swap(mixed), back_low.T, normed_in.T)
        )
        mixed = mixed.astype(F32) + came.astype(F32)
    else:
        mixed = mp_sum(mixed)
    branch_mix = inverse_state * mixed
    middle = seq_in + branch_mix
    inverse_mid = inverse_rms(middle)
    unit_mid = middle * inverse_mid
    normed_mid = (unit_mid * gain_full[2]).astype(BF)

    across = (((1,), (1,)), ((), ()))
    down = (((0,), (0,)), ((), ()))
    dot = functools.partial(lax.dot_general, preferred_element_type=F32)
    if quick:
        glu_sums, sum_own, sum_came, half_own, half_came = glu_call(normed_mid, back_low, left_back, glu, 0)
        branch = half_own.astype(F32) + half_came.astype(F32)
    else:
        pre_act = jnp.dot(normed_mid, glu[0], preferred_element_type=F32)
        pre_up = jnp.dot(normed_mid, glu[1], preferred_element_type=F32)
        grad_hidden = jnp.dot(back_low, glu[2], preferred_element_type=F32)
        act_part = jax.nn.silu(pre_act)
        hidden = (act_part * pre_up).astype(BF)
        grad_act = (grad_hidden * pre_up * silu_slope(pre_act)).astype(BF)
        grad_up = (grad_hidden * act_part).astype(BF)
        grad_normed = mp_sum(dot(grad_act, glu[0], across) + dot(grad_up, glu[1], across))
        glu_grad = jnp.stack(
            [dot(normed_mid, grad_act, down), dot(normed_mid, grad_up, down), dot(back_low, hidden, down)]
        ).astype(BF)
        glu_own = lax.psum_scatter(glu_grad, "dp", scatter_dimension=1, tiled=True).astype(F32)
        branch = mp_scatter(dot(hidden, glu[2], across))
    own_features = lambda v: lax.dynamic_slice_in_dim(v, place * part, part, v.ndim - 1)
    layer_out = (own_features(middle) + branch).astype(BF)

    if quick:
        grad_middle_own, middle_low, state_mean, grad_gated, gain_mid = middle_back(
            sum_own, sum_came, middle, cot_full, token_rows, token_weight, gain_full[2], mixer_out
        )
        gain_mid = gain_mid[0]
    else:
        inverse_mid = inverse_rms(middle)
        unit_mid = middle * inverse_mid
        gain_mid = jnp.sum(grad_normed * unit_mid, axis=0)
        scaled_mid = grad_normed * gain_full[2]
        back = cot_full.astype(F32) * token_weight
        grad_middle = back + inverse_mid * (
            scaled_mid - unit_mid * jnp.mean(scaled_mid * unit_mid, axis=-1, keepdims=True)
        )
        grad_middle_own = own_features(grad_middle)
        middle_low = grad_middle.astype(BF)
        state_mean = jnp.mean(middle_low.astype(F32) * branch_mix, axis=-1, keepdims=True)
        grad_gated = dot(middle_low, mixer_out, across)
    by_batch = lambda v: v.reshape(batches, length, v.shape[-1])
    grad_pre, gated_out, gain_state, pre_dot = scan_backward(
        pre, states, by_batch(grad_gated), by_batch(inverse_state), by_batch(state_mean), bound, state_gain
    )
    grad_pre = grad_pre.reshape(3, rows, channels)
    gated_out = gated_out.reshape(rows, channels)
    gain_state = jnp.sum(gain_state, axis=0).reshape(groups, 1, own_rows)
    gain_state = lax.dynamic_update_slice_in_dim(
        jnp.zeros((groups, narrow, own_rows), F32), gain_state, place, 1
    )
    device = lax.axis_index("dp") * narrow + place
    if quick:
        gain_parts = jnp.stack(
            [
                jnp.zeros((groups, narrow * own_rows), F32),
                gain_state.reshape(groups, narrow * own_rows),
                0.5 * gain_mid.reshape(groups, narrow * own_rows),
            ],
            axis=1,
        )
        gain_parts = jnp.pad(gain_parts, ((0, 0), (0, 5), (0, 0)))
        pre_dot = pre_dot.reshape(-1, 128)
        mixer_own, gain_own, grad_normed_in, dot_came = mixer_call(
            left_in, grad_pre, gated_out.T, middle_low, gain_parts, token_rows, inverse_in, mixer_in, pre_dot, 1
        )
        in_mean = (pre_dot + dot_came).reshape(rows, 1) / full
        gain_own = lax.dynamic_slice_in_dim(gain_own[:3], place * own_rows, own_rows, 1)
    else:
        grad_mix_out = dot(gated_out, middle_low, down).astype(BF)
        grad_mix_in = jnp.einsum("td,kte->kde", normed_in, grad_pre, preferred_element_type=F32)
        in_own = lax.psum_scatter(grad_mix_in.astype(BF), "dp", scatter_dimension=1, tiled=True)
        out_own = lax.psum_scatter(grad_mix_out, "dp", scatter_dimension=0, tiled=True)
        in_own = mp_swap(in_own.reshape(3, narrow, own_rows, channels).transpose(1, 0, 2, 3))
        in_own = in_own.reshape(narrow, 3, own_rows, groups, own_rows).transpose(1, 2, 3, 0, 4)
        grad_normed_in = jnp.einsum("kte,kde->td", grad_pre, mixer_in, preferred_element_type=F32)
        gain_in = jnp.sum(grad_normed_in * unit_in, axis=0)
        grad_normed_in = mp_scatter(grad_normed_in)
        gain_rows = jnp.stack([gain_in, gain_state.reshape(full), gain_mid / narrow])
        gain_total = lax.psum(gain_rows, ("dp", "mp"))
        gain_own = lax.dynamic_slice_in_dim(gain_total, device * own_rows, own_rows, 1)
        in_mean = mp_sum_wide(pre_dot.reshape(rows, 1)) / full
        in_own = in_own.reshape(3, own_rows, full)
        mixer_own = jnp.concatenate([in_own, out_own[None]]).astype(F32)
    unit_in_own = own_features(token_rows).astype(F32) * inverse_in
    grad_seq = grad_middle_own + inverse_in * (
        grad_normed_in * own_features(gain_full[0]) - unit_in_own * in_mean
    )
    grad_tokens = grad_seq.astype(BF)

    scale = 1.0 / (batches * groups * tokens.shape[1])
    update = functools.partial(adamw_update, count=STEP_NUMBER)
    mixer_new = update(
        mixer_master, mixer_first, mixer_second, mixer_own * scale, rate=MATRIX_RATE, decay=DECAY_RATE
    )
    gain_new = update(
        gain_master, gain_first, gain_second, gain_own * scale, rate=GAIN_RATE, decay=0.0
    )
    glu_ins = (glu_in_master, glu_in_first, glu_in_second)
    glu_downs = (glu_out_master, glu_out_first, glu_out_second)
    if quick:
        glu_in_new, glu_out_new = glu_update(glu_sums, glu_ins, glu_downs, scale)
    else:
        glu_in_new = update(*glu_ins, glu_own[:2] * scale, rate=MATRIX_RATE, decay=DECAY_RATE)
        glu_out_new = update(*glu_downs, glu_own[2].T * scale, rate=MATRIX_RATE, decay=DECAY_RATE)
    return (
        layer_out.reshape(batches, 1, length, part),
        grad_tokens.reshape(batches, 1, length, part),
        *mixer_new,
        *glu_in_new,
        *glu_out_new,
        *gain_new,
    )


def solution(mesh):
    weights = (
        [P(None, ("dp", "mp"), None)] * 3
        + [P(None, "dp", "mp")] * 3
        + [P("mp", "dp")] * 3
        + [P(None, ("dp", "mp"))] * 3
    )
    in_specs = (
        P(None, "dp", None, None),
        P(None, "dp", None, "mp"),
        P(None, "dp"),
        P(None, "dp", None),
        P(),
        *weights,
    )
    out_specs = (P(None, "dp", None, "mp"), P(None, "dp", None, "mp"), *weights)
    return jax.shard_map(shards, mesh=mesh, in_specs=in_specs, out_specs=out_specs, check_vma=False)
```

```python
import functools

import jax
import jax.numpy as jnp
from jax import lax
from jax.experimental import pallas as pl
from jax.experimental.pallas import tpu as pltpu
from jax.sharding import PartitionSpec as P

NDOM = 8

EPSILON = 1e-06
BETA_ONE = 0.9
BETA_TWO = 0.95
ADAM_EPSILON = 1e-08
DECAY_RATE = 0.1
MATRIX_RATE = 0.06
GAIN_RATE = 0.5
STEP_NUMBER = 3.0

BF = jnp.bfloat16
F32 = jnp.float32
VMEM_LIMIT = 56 * 1024 * 1024


def inverse_rms(values):
    return lax.rsqrt(jnp.mean(values * values, axis=-1, keepdims=True) + EPSILON)


def silu_slope(values):
    sigma = jax.nn.sigmoid(values)
    return sigma * (1.0 + values * (1.0 - sigma))


def adamw_update(master, first, second, gradient, count, rate, decay):
    first_new = BETA_ONE * first + (1.0 - BETA_ONE) * gradient
    second_new = BETA_TWO * second + (1.0 - BETA_TWO) * gradient * gradient
    first_hat = first_new / (1.0 - BETA_ONE**count)
    second_hat = second_new / (1.0 - BETA_TWO**count)
    master_new = master - rate * (
        first_hat / (jnp.sqrt(second_hat) + ADAM_EPSILON) + decay * master
    )
    return (master_new, first_new, second_new)


def partner_swap(value):
    return lax.ppermute(value, "mp", [(0, 1), (1, 0)])


def mp_sum(part):
    low = part.astype(BF)
    if lax.axis_size("mp") == 2:
        return low.astype(F32) + partner_swap(low).astype(F32)
    return lax.psum(low.astype(F32), "mp")


def mp_sum_wide(part):
    if lax.axis_size("mp") == 2:
        return part + partner_swap(part)
    return lax.psum(part, "mp")


def mp_scatter(part):
    if lax.axis_size("mp") == 2:
        half = part.shape[1] // 2
        place = lax.axis_index("mp")
        own = lax.dynamic_slice_in_dim(part, place * half, half, 1)
        other = lax.dynamic_slice_in_dim(part, (1 - place) * half, half, 1)
        return own.astype(BF).astype(F32) + partner_swap(other.astype(BF)).astype(F32)
    return lax.psum_scatter(part.astype(BF), "mp", scatter_dimension=1, tiled=True).astype(F32)


def mp_swap(pieces):
    if lax.axis_size("mp") == 2:
        place = lax.axis_index("mp")
        own = lax.dynamic_index_in_dim(pieces, place, 0, keepdims=False)
        came = partner_swap(lax.dynamic_index_in_dim(pieces, 1 - place, 0, keepdims=False))
        first = place == 0
        return jnp.stack([jnp.where(first, own, came), jnp.where(first, came, own)])
    return lax.all_to_all(pieces, "mp", 0, 0, tiled=False)


def mp_gather(part):
    if lax.axis_size("mp") == 2:
        place = lax.axis_index("mp")
        came = partner_swap(part)
        first = place == 0
        return jnp.concatenate([jnp.where(first, part, came), jnp.where(first, came, part)], axis=1)
    return lax.all_gather(part, "mp", axis=1, tiled=True)


SUB_ROWS = 8
TILE_ROWS = 64


def channel_block(width):
    return 512 if width % 512 == 0 else width


def scan_rows(total, decay, carry):
    row = lax.broadcasted_iota(jnp.int32, total.shape, 0)
    shift = 1
    while shift < SUB_ROWS:
        keep = row >= shift
        total = total + decay * jnp.where(keep, pltpu.roll(total, shift, 0), 0.0)
        decay = decay * jnp.where(keep, pltpu.roll(decay, shift, 0), 1.0)
        shift *= 2
    return total + decay * carry


def scan_rows_back(total, decay, carry):
    row = lax.broadcasted_iota(jnp.int32, total.shape, 0)
    shift = 1
    while shift < SUB_ROWS:
        keep = row < SUB_ROWS - shift
        total = total + decay * jnp.where(keep, pltpu.roll(total, SUB_ROWS - shift, 0), 0.0)
        decay = decay * jnp.where(keep, pltpu.roll(decay, SUB_ROWS - shift, 0), 1.0)
        shift *= 2
    return total + decay * carry


def scan_forward_kernel(pre_ref, bound_ref, gain_ref, states_ref, raw_ref, square_ref):
    length, width = states_ref.shape[1], states_ref.shape[2]
    bound = bound_ref[...]
    gain = gain_ref[...]
    first_block = pl.program_id(1) == 0

    def step(index, carry):
        rows = pl.ds(pl.multiple_of(index * TILE_ROWS, TILE_ROWS), TILE_ROWS)
        forget = bound + (1.0 - bound) * jax.nn.sigmoid(pre_ref[1, 0, rows, :])
        total = (1.0 - forget) * jax.nn.silu(pre_ref[0, 0, rows, :])
        parts = []
        for low in range(0, TILE_ROWS, SUB_ROWS):
            part = scan_rows(total[low : low + SUB_ROWS], forget[low : low + SUB_ROWS], carry)
            carry = part[SUB_ROWS - 1 : SUB_ROWS]
            parts.append(part)
        states = jnp.concatenate(parts)
        states_ref[0, rows, :] = states
        raw = states * gain * jax.nn.silu(pre_ref[2, 0, rows, :])
        raw_ref[0, rows, :] = raw.astype(raw_ref.dtype)
        square = jnp.sum(states * states, axis=-1, keepdims=True)
        square_ref[0, rows, :] = square + jnp.where(first_block, 0.0, square_ref[0, rows, :])
        return carry

    lax.fori_loop(0, length // TILE_ROWS, step, jnp.zeros((1, width), F32))


def scan_forward(pre, bound, gain):
    _, batches, length, width = pre.shape
    block = channel_block(width)
    return pl.pallas_call(
        scan_forward_kernel,
        grid=(batches, width // block),
        in_specs=[
            pl.BlockSpec((3, 1, length, block), lambda b, c: (0, b, 0, c)),
            pl.BlockSpec((1, block), lambda b, c: (0, c)),
            pl.BlockSpec((1, block), lambda b, c: (0, c)),
        ],
        out_specs=[
            pl.BlockSpec((1, length, block), lambda b, c: (b, 0, c)),
            pl.BlockSpec((1, length, block), lambda b, c: (b, 0, c)),
            pl.BlockSpec((1, length, 1), lambda b, c: (b, 0, 0)),
        ],
        out_shape=[
            jax.ShapeDtypeStruct((batches, length, width), F32),
            jax.ShapeDtypeStruct((batches, length, width), BF),
            jax.ShapeDtypeStruct((batches, length, 1), F32),
        ],
        compiler_params=pltpu.CompilerParams(vmem_limit_bytes=VMEM_LIMIT),
        cost_estimate=pl.CostEstimate(
            flops=batches * length * width * 40,
            bytes_accessed=batches * length * width * 18,
            transcendentals=batches * length * width * 3,
        ),
    )(pre, bound[None], gain[None])


def scan_backward_kernel(
    pre_ref, states_ref, gated_ref, inverse_ref, mean_ref, bound_ref, gain_ref,
    grad_ref, out_ref, gain_grad_ref, dot_ref,
):
    length, width = states_ref.shape[1], states_ref.shape[2]
    bound = bound_ref[...]
    gain = gain_ref[...]
    first_block = pl.program_id(1) == 0
    row = lax.broadcasted_iota(jnp.int32, (TILE_ROWS, width), 0)
    tiles = length // TILE_ROWS

    def step(index, carry):
        carried_next, forget_next, gain_sum = carry
        place = tiles - 1 - index
        rows = pl.ds(pl.multiple_of(place * TILE_ROWS, TILE_ROWS), TILE_ROWS)
        pre_input = pre_ref[0, 0, rows, :]
        pre_forget = pre_ref[1, 0, rows, :]
        pre_gate = pre_ref[2, 0, rows, :]
        states = states_ref[0, rows, :]
        inverse = inverse_ref[0, rows, :]
        grad_gated = gated_ref[0, rows, :]
        unit = states * inverse
        gate_sig = jax.nn.sigmoid(pre_gate)
        gate = pre_gate * gate_sig
        out_ref[0, rows, :] = (unit * gain * gate).astype(out_ref.dtype)
        gain_sum = gain_sum + grad_gated * unit * gate
        scaled = grad_gated * gain
        grad_gate = (scaled * unit * (gate_sig * (1.0 + pre_gate * (1.0 - gate_sig)))).astype(BF)
        grad_ref[2, 0, rows, :] = grad_gate
        total = inverse * (scaled * gate - unit * mean_ref[0, rows, :])
        sigma = jax.nn.sigmoid(pre_forget)
        forget = bound + (1.0 - bound) * sigma
        decay = jnp.where(row == TILE_ROWS - 1, forget_next, pltpu.roll(forget, TILE_ROWS - 1, 0))
        parts = []
        for low in range(TILE_ROWS - SUB_ROWS, -1, -SUB_ROWS):
            part = scan_rows_back(
                total[low : low + SUB_ROWS], decay[low : low + SUB_ROWS], carried_next
            )
            carried_next = part[0:1]
            parts.insert(0, part)
        carried = jnp.concatenate(parts)
        before_rows = pl.ds(
            pl.multiple_of(jnp.maximum(place - 1, 0) * TILE_ROWS, TILE_ROWS), TILE_ROWS
        )
        before = states_ref[0, before_rows, :][TILE_ROWS - 1 : TILE_ROWS, :]
        before = jnp.where(place == 0, 0.0, before)
        earlier = jnp.where(row == 0, before, pltpu.roll(states, 1, 0))
        input_sig = jax.nn.sigmoid(pre_input)
        fresh = pre_input * input_sig
        slope = input_sig * (1.0 + pre_input * (1.0 - input_sig))
        grad_input = (carried * (1.0 - forget) * slope).astype(BF)
        grad_forget = (
            carried * (earlier - fresh) * (1.0 - bound) * sigma * (1.0 - sigma)
        ).astype(BF)
        grad_ref[0, 0, rows, :] = grad_input
        grad_ref[1, 0, rows, :] = grad_forget
        dots = (
            grad_input.astype(F32) * pre_input
            + grad_forget.astype(F32) * pre_forget
            + grad_gate.astype(F32) * pre_gate
        )
        dot = jnp.sum(dots, axis=-1, keepdims=True)
        dot_ref[0, rows, :] = dot + jnp.where(first_block, 0.0, dot_ref[0, rows, :])
        return carried_next, forget[0:1, :], gain_sum

    zero = jnp.zeros((1, width), F32)
    _, _, gain_sum = lax.fori_loop(
        0, tiles, step, (zero, zero, jnp.zeros((TILE_ROWS, width), F32))
    )
    gain_grad_ref[0] = jnp.sum(gain_sum, axis=0, keepdims=True)


def scan_backward(pre, states, grad_gated, inverse, mean, bound, gain):
    _, batches, length, width = pre.shape
    block = channel_block(width)
    whole = pl.BlockSpec((1, length, block), lambda b, c: (b, 0, c))
    column = pl.BlockSpec((1, length, 1), lambda b, c: (b, 0, 0))
    line = pl.BlockSpec((1, block), lambda b, c: (0, c))
    three = pl.BlockSpec((3, 1, length, block), lambda b, c: (0, b, 0, c))
    return pl.pallas_call(
        scan_backward_kernel,
        grid=(batches, width // block),
        in_specs=[three, whole, whole, column, column, line, line],
        out_specs=[
            three,
            whole,
            pl.BlockSpec((1, 1, block), lambda b, c: (b, 0, c)),
            column,
        ],
        out_shape=[
            jax.ShapeDtypeStruct((3, batches, length, width), BF),
            jax.ShapeDtypeStruct((batches, length, width), BF),
            jax.ShapeDtypeStruct((batches, 1, width), F32),
            jax.ShapeDtypeStruct((batches, length, 1), F32),
        ],
        compiler_params=pltpu.CompilerParams(vmem_limit_bytes=VMEM_LIMIT),
        cost_estimate=pl.CostEstimate(
            flops=batches * length * width * 80,
            bytes_accessed=batches * length * width * 28,
            transcendentals=batches * length * width * 3,
        ),
    )(pre, states, grad_gated, inverse, mean, bound[None], gain[None])


MESH_ID = pl.DeviceIdType.MESH
DEPTH = 4
LANES = 256
X_LAG = 4
Z_LAG = X_LAG + 2
SWAP_LAG = 2


def device_place():
    dp = lax.axis_index("dp")
    return dp // 4, lax.rem(dp // 2, 2), lax.rem(dp, 2)


def device_at(z, x, core):
    return (z * 4 + x * 2 + core, lax.axis_index("mp"))


def scatter_barrier(z, x, core, with_mp=False):
    barrier = pltpu.get_barrier_semaphore()
    targets = [device_at(z, x, 1 - core), device_at(z, 1 - x, core)]
    targets += [device_at(lax.rem(z + hop, DEPTH), x, core) for hop in range(1, DEPTH)]
    if with_mp:
        targets.append((lax.axis_index("dp"), 1 - lax.axis_index("mp")))
    for target in targets:
        pl.semaphore_signal(barrier, 1, device_id=target, device_id_type=MESH_ID)
    pl.semaphore_wait(barrier, len(targets))


def scatter_step(step, chunks, compute, finish, scratch, small_last=False):
    (own, core_out, core_in, keep, x_out, x_in, sums, mine, z_out, z_in,
     core_send, core_recv, x_send, x_recv, z_send, z_recv) = scratch
    z, x, core = device_place()

    def core_copy(p, cut=()):
        return pltpu.make_async_remote_copy(
            core_out.at[(lax.rem(p, 2), *cut)], core_in.at[(lax.rem(p, 4), *cut)],
            core_send.at[lax.rem(p, 2)], core_recv.at[lax.rem(p, 4)],
            device_id=device_at(z, x, 1 - core), device_id_type=MESH_ID)

    def x_copy(p, cut=()):
        return pltpu.make_async_remote_copy(
            x_out.at[(lax.rem(p, X_LAG), *cut)], x_in.at[(lax.rem(p, 2 * X_LAG), *cut)],
            x_send.at[lax.rem(p, X_LAG)], x_recv.at[lax.rem(p, 2 * X_LAG)],
            device_id=device_at(z, 1 - x, core), device_id_type=MESH_ID)

    def z_copy(p, hop, cut=()):
        return pltpu.make_async_remote_copy(
            z_out.at[(lax.rem(p, 4), hop - 1, *cut)], z_in.at[(lax.rem(p, 8), hop - 1, *cut)],
            z_send.at[lax.rem(p, 4), hop - 1], z_recv.at[lax.rem(p, 8), hop - 1],
            device_id=device_at(lax.rem(z + hop, DEPTH), x, core), device_id_type=MESH_ID)

    corner = (slice(0, 16), slice(0, 128))
    every = slice(None)

    def go(copy, lead, p, act):
        if not small_last:
            act(copy(p))
            return
        pl.when(p < chunks - 1)(lambda: act(copy(p)))
        pl.when(p == chunks - 1)(lambda: act(copy(p, (*(every,) * lead, *corner))))

    def core_go(p, act):
        go(core_copy, 2, p, act)

    def x_go(p, act):
        go(x_copy, 1, p, act)

    def z_go(p, hop, act):
        go(lambda p, cut=(): z_copy(p, hop, cut), 0, p, act)

    start, wait_recv, wait_send = (
        lambda copy: copy.start(), lambda copy: copy.wait_recv(), lambda copy: copy.wait_send())

    @pl.when(step < chunks)
    def _():
        @pl.when(step >= 2)
        def _():
            core_go(step - 2, wait_send)

        def to_partner(value):
            core_out[lax.rem(step, 2)] = value.astype(BF)

        def to_own(value):
            own[lax.rem(step, 2)] = value

        compute(step, 1 - core, to_partner)
        core_go(step, start)
        compute(step, core, to_own)

    @pl.when((step >= 1) & (step < chunks + 1))
    def _():
        p = step - 1
        core_go(p, wait_recv)

        @pl.when(p >= X_LAG)
        def _():
            x_go(p - X_LAG, wait_send)

        two, four, slot = lax.rem(p, 2), lax.rem(p, 4), lax.rem(p, X_LAG)
        x_out[slot] = (own[two, :, 1 - x] + core_in[four, :, 1 - x].astype(F32)).astype(BF)
        x_go(p, start)
        keep[slot] = own[two, :, x] + core_in[four, :, x].astype(F32)

    @pl.when((step >= X_LAG) & (step < chunks + X_LAG))
    def _():
        p = step - X_LAG
        x_go(p, wait_recv)
        four = lax.rem(p, 4)
        sums[...] = keep[lax.rem(p, X_LAG)] + x_in[lax.rem(p, 2 * X_LAG)].astype(F32)
        for hop in range(1, DEPTH):
            @pl.when(p >= 4)
            def _():
                z_go(p - 4, hop, wait_send)

            z_out[four, hop - 1] = sums[lax.rem(z + hop, DEPTH)].astype(BF)
            z_go(p, hop, start)
        mine[four] = sums[z]

    @pl.when((step >= Z_LAG) & (step < chunks + Z_LAG))
    def _():
        p = step - Z_LAG
        for hop in range(1, DEPTH):
            z_go(p, hop, wait_recv)
        got = z_in.at[lax.rem(p, 8)]
        finish(p, mine[lax.rem(p, 4)] + got[0].astype(F32) + got[1].astype(F32) + got[2].astype(F32))

    @pl.when(step == chunks + Z_LAG - 1)
    def _():
        for p in range(chunks - 2, chunks):
            core_go(jnp.int32(p), wait_send)
        for p in range(chunks - X_LAG, chunks):
            x_go(jnp.int32(p), wait_send)
        for p in range(chunks - 4, chunks):
            for hop in range(1, DEPTH):
                z_go(jnp.int32(p), hop, wait_send)


def scatter_scratch(rows, lanes):
    quad = (DEPTH, 2, rows, lanes)
    line = (DEPTH, rows, lanes)
    dma = pltpu.SemaphoreType.DMA
    return [
        pltpu.VMEM((2, *quad), F32),
        pltpu.VMEM((2, *quad), BF),
        pltpu.VMEM((4, *quad), BF),
        pltpu.VMEM((X_LAG, *line), F32),
        pltpu.VMEM((X_LAG, *line), BF),
        pltpu.VMEM((2 * X_LAG, *line), BF),
        pltpu.VMEM(line, F32),
        pltpu.VMEM((4, rows, lanes), F32),
        pltpu.VMEM((4, DEPTH - 1, rows, lanes), BF),
        pltpu.VMEM((8, DEPTH - 1, rows, lanes), BF),
        dma((2,)), dma((4,)), dma((X_LAG,)), dma((2 * X_LAG,)), dma((4, DEPTH - 1)), dma((8, DEPTH - 1)),
    ]


def scatter_out(chunks, rows, lanes):
    spec = pl.BlockSpec((1, rows, lanes), lambda q: (jnp.maximum(q - Z_LAG, 0), 0, 0))
    return spec, jax.ShapeDtypeStruct((chunks, rows, lanes), F32)


def fixed(shape):
    return pl.BlockSpec(shape, lambda q: (0,) * len(shape), pipeline_mode=pl.Buffered(1))


def glu_kernel(
    hidden_blocks, full_blocks, normed_ref, back_ref, left_ref, left_back_ref, glu_ref,
    out_ref, sum_own, sum_came, half_own, half_send,
    left, left_back, left_sem, acts, weights_in, weights_back, sum_stage, half_stage,
    in_sem, back_sem, stage_sem, sum_send, sum_recv, *scratch,
):
    z, x, core = device_place()
    dp, mp = lax.axis_index("dp"), lax.axis_index("mp")
    step = pl.program_id(0)
    chunks = 3 * hidden_blocks
    rows = normed_ref.shape[0]
    row_block = rows // 2
    half_blocks = full_blocks // 2
    across = (((1,), (1,)), ((), ()))
    spread = min(hidden_blocks + hidden_blocks // 2, 16)
    second = step - spread

    def first_tasks(at):
        return at * hidden_blocks // spread

    unit_block = first_tasks(step)
    in_second = (second >= 0) & (second < 2 * full_blocks)

    def lane_block(index):
        return pl.ds(pl.multiple_of(index * LANES, LANES), LANES)

    def load_in(index):
        return pltpu.make_async_copy(glu_ref.at[:, :, lane_block(index)], weights_in, in_sem)

    def load_back(index):
        return pltpu.make_async_copy(glu_ref.at[:, lane_block(index), :], weights_back, back_sem)

    def stage(index, kind, target):
        source = (sum_stage, half_stage)[kind].at[lax.rem(index, 2)]
        return pltpu.make_async_copy(source, target, stage_sem.at[lax.rem(index, 2), kind])

    def half_spot(index):
        return lax.rem(index, half_blocks)

    def sum_copy(index):
        return pltpu.make_async_remote_copy(
            sum_own.at[:, lane_block(index)], sum_came.at[:, lane_block(index)],
            sum_send.at[index], sum_recv.at[index], device_id=(dp, 1 - mp), device_id_type=MESH_ID)

    left_loads = (
        pltpu.make_async_copy(left_ref, left, left_sem.at[0]),
        pltpu.make_async_copy(left_back_ref, left_back, left_sem.at[1]),
    )

    @pl.when(step == 0)
    def _():
        for one in (load_in(0), *left_loads, load_back(0)):
            one.start()
        scatter_barrier(z, x, core, with_mp=True)

    @pl.when((step < spread) & ((step == 0) | (unit_block > first_tasks(step - 1))))
    def _():
        load_in(unit_block).wait()
        lanes = lane_block(unit_block)

        def part(index, _):
            part_rows = pl.ds(pl.multiple_of(index * row_block, row_block), row_block)
            normed = normed_ref[part_rows, :]
            pre_act = jnp.dot(normed, weights_in[0], preferred_element_type=F32)
            pre_up = jnp.dot(normed, weights_in[1], preferred_element_type=F32)
            grad_hidden = jnp.dot(back_ref[part_rows, :], weights_in[2], preferred_element_type=F32)
            sigma = jax.nn.sigmoid(pre_act)
            act_part = pre_act * sigma
            acts[0, part_rows, lanes] = (
                grad_hidden * pre_up * (sigma * (1.0 + pre_act * (1.0 - sigma)))).astype(BF)
            acts[1, part_rows, lanes] = (grad_hidden * act_part).astype(BF)
            acts[2, part_rows, lanes] = (act_part * pre_up).astype(BF)
            return 0

        lax.fori_loop(0, rows // row_block, part, 0)

        @pl.when(unit_block + 1 < hidden_blocks)
        def _():
            load_in(unit_block + 1).start()

    @pl.when(in_second & (lax.rem(second, 2) == 1))
    def _():
        index = second // 2
        stage(index, 0, sum_own.at[:, lane_block(index)]).wait()
        sum_copy(index).start()
        spot = half_spot(index)
        stage(index, 1, half_own.at[:, lane_block(spot)]).wait()

    @pl.when(in_second & (lax.rem(second, 2) == 0))
    def _():
        index = second // 2
        load_back(index).wait()
        slot = lax.rem(index, 2)

        def part(at, _):
            part_rows = pl.ds(pl.multiple_of(at * row_block, row_block), row_block)
            dot = functools.partial(
                lax.dot_general, dimension_numbers=across, preferred_element_type=F32)
            grad_normed = dot(acts[0, part_rows, :], weights_back[0])
            grad_normed += dot(acts[1, part_rows, :], weights_back[1])
            sum_stage[slot, part_rows, :] = grad_normed.astype(BF)
            half_stage[slot, part_rows, :] = dot(acts[2, part_rows, :], weights_back[2]).astype(BF)
            return 0

        lax.fori_loop(0, rows // row_block, part, 0)

        @pl.when(index + 1 < full_blocks)
        def _():
            load_back(index + 1).start()

        stage(index, 0, sum_own.at[:, lane_block(index)]).start()
        spot = half_spot(index)

        @pl.when(index // half_blocks == mp)
        def _():
            stage(index, 1, half_own.at[:, lane_block(spot)]).start()

        @pl.when(index // half_blocks != mp)
        def _():
            stage(index, 1, half_send.at[:, lane_block(spot)]).start()

    def compute(q, core_side, store):
        kind = lax.rem(q, 3)
        side_rows = left.shape[3]

        def product(side_ref):
            side = side_ref[:, :, core_side].reshape(DEPTH * 2 * side_rows, rows)
            right = acts[kind, :, lane_block(q // 3)]
            store(jnp.dot(side, right, preferred_element_type=F32).reshape(
                DEPTH, 2, side_rows, LANES))

        pl.when(kind < 2)(lambda: product(left))
        pl.when(kind == 2)(lambda: product(left_back))

    @pl.when(step == 0)
    def _():
        for one in left_loads:
            one.wait()

    def finish(p, value):
        out_ref[0] = value

    scatter_step(step, chunks, compute, finish, scratch)

    @pl.when(step == chunks + Z_LAG - 1)
    def _():
        for index in range(full_blocks):
            sum_copy(index).wait()


def glu_call(normed, back_low, left_back, glu, collective):
    rows, full = normed.shape
    hidden = glu.shape[2]
    hidden_blocks, full_blocks = hidden // LANES, full // LANES
    block = full // 16
    chunks = 3 * hidden_blocks
    left_shape = (DEPTH, 2, 2, block, rows)
    any_space = pl.BlockSpec(memory_space=pl.ANY)
    out_spec, out_shape = scatter_out(chunks, block, LANES)
    dma = pltpu.SemaphoreType.DMA
    wide = jax.ShapeDtypeStruct((rows, full), BF)
    half = jax.ShapeDtypeStruct((rows, full // 2), BF)
    out, sum_own, sum_came, half_own, half_send = pl.pallas_call(
        functools.partial(glu_kernel, hidden_blocks, full_blocks),
        grid=(chunks + Z_LAG,),
        in_specs=[fixed(normed.shape), fixed(back_low.shape)] + [any_space] * 3,
        out_specs=[out_spec] + [any_space] * 4,
        out_shape=[out_shape, wide, wide, half, half],
        scratch_shapes=[
            pltpu.VMEM(left_shape, BF),
            pltpu.VMEM(left_shape, BF),
            dma((2,)),
            pltpu.VMEM((3, rows, hidden), BF),
            pltpu.VMEM((3, full, LANES), BF),
            pltpu.VMEM((3, LANES, hidden), BF),
            pltpu.VMEM((2, rows, LANES), BF),
            pltpu.VMEM((2, rows, LANES), BF),
            dma(()), dma(()), dma((2, 2)),
            dma((full_blocks,)), dma((full_blocks,)),
            *scatter_scratch(block, LANES),
        ],
        compiler_params=pltpu.CompilerParams(
            collective_id=collective, has_side_effects=True, vmem_limit_bytes=62 * 1024 * 1024),
        cost_estimate=pl.CostEstimate(
            flops=18 * rows * full * hidden, bytes_accessed=6 * full * hidden * 2,
            transcendentals=rows * hidden),
    )(normed, back_low, normed.T.reshape(left_shape), left_back.reshape(left_shape), glu)
    return out, sum_own, sum_came, half_own, half_send


def mixer_kernel(
    full_blocks, left_hbm, grad_hbm, left_out_ref, right_out_ref, gain_ref, tokens_ref, inverse_ref,
    weights_ref, dot_ref, out_ref, gain_out, half_own, half_send, half_came, dot_came,
    left_ref, grad_ref, big_sem, weights, token_block, gain_sum, gain_chunk, total, swap_out, swap_in, half_stage,
    load_sem, stage_sem, half_send_sem, half_recv, swap_send, swap_recv, dot_sem, *scratch,
):
    z, x, core = device_place()
    dp, mp = lax.axis_index("dp"), lax.axis_index("mp")
    step = pl.program_id(0)
    tokens, channels = grad_ref.shape[1], grad_ref.shape[2]
    block, half = left_ref.shape[3], left_out_ref.shape[3]
    outer = full_blocks // 2
    across = channels // LANES
    gains = outer + 3 * across
    chunks = gains + 1
    half_blocks = full_blocks // 2
    row_block = tokens // 2
    partner = (dp, 1 - mp)

    def lane_block(index):
        return pl.ds(pl.multiple_of(index * LANES, LANES), LANES)

    def loads(index):
        return (
            pltpu.make_async_copy(weights_ref.at[:, lane_block(index), :], weights, load_sem.at[0]),
            pltpu.make_async_copy(tokens_ref.at[:, lane_block(index)], token_block, load_sem.at[1]),
        )

    def stage(index, target):
        return pltpu.make_async_copy(
            half_stage.at[lax.rem(index, 2)], target, stage_sem.at[lax.rem(index, 2)])

    def half_copy(spot):
        return pltpu.make_async_remote_copy(
            half_send.at[:, lane_block(spot)], half_came.at[:, lane_block(spot)],
            half_send_sem.at[spot], half_recv.at[spot], device_id=partner, device_id_type=MESH_ID)

    def swap_copy(index):
        return pltpu.make_async_remote_copy(
            swap_out.at[lax.rem(index, 2)], swap_in.at[lax.rem(index, 8)],
            swap_send.at[lax.rem(index, 2)], swap_recv.at[lax.rem(index, 8)],
            device_id=partner, device_id_type=MESH_ID)

    big_loads = (
        pltpu.make_async_copy(grad_hbm, grad_ref, big_sem.at[0]),
        pltpu.make_async_copy(left_hbm, left_ref, big_sem.at[1]),
    )
    dot_copy = pltpu.make_async_remote_copy(
        dot_ref, dot_came, dot_sem.at[0], dot_sem.at[1], device_id=partner, device_id_type=MESH_ID)

    @pl.when(step == 0)
    def _():
        for one in (*big_loads, *loads(0)):
            one.start()
        gain_chunk[...] = jnp.zeros_like(gain_chunk)
        gain_sum[...] = jnp.zeros_like(gain_sum)
        scatter_barrier(z, x, core, with_mp=True)
        dot_copy.start()

    @pl.when(step == 1)
    def _():
        for one in big_loads:
            one.wait()

    task = (step - 1) // 2

    @pl.when((step >= 2) & (step <= 2 * full_blocks) & (lax.rem(step, 2) == 0))
    def _():
        index = task
        spot = lax.rem(index, half_blocks)
        stage(index, half_own.at[:, lane_block(spot)]).wait()

        @pl.when(index // half_blocks != mp)
        def _():
            half_copy(spot).start()

    @pl.when((step < 2 * full_blocks) & (lax.rem(step, 2) == 1))
    def _():
        for one in loads(task):
            one.wait()
        slot = lax.rem(task, 2)
        spot = lax.rem(task, half_blocks)

        def part(at, gain_in):
            part_rows = pl.ds(pl.multiple_of(at * row_block, row_block), row_block)
            dot = functools.partial(
                lax.dot_general, dimension_numbers=(((1,), (1,)), ((), ())), preferred_element_type=F32)
            grad = dot(grad_ref[0, part_rows, :], weights[0])
            grad += dot(grad_ref[1, part_rows, :], weights[1])
            grad += dot(grad_ref[2, part_rows, :], weights[2])
            half_stage[slot, part_rows, :] = grad.astype(BF)
            unit = token_block[part_rows, :].astype(F32) * inverse_ref[part_rows, :]
            return gain_in + jnp.sum(grad * unit, axis=0, keepdims=True)

        gain_in = lax.fori_loop(0, tokens // row_block, part, jnp.zeros((1, LANES), F32))
        gain_sum[2 * task, 0:1, :] = gain_in[:, :128]
        gain_sum[2 * task + 1, 0:1, :] = gain_in[:, 128:]

        @pl.when(task + 1 < full_blocks)
        def _():
            for one in loads(task + 1):
                one.start()

        @pl.when(task // half_blocks == mp)
        def _():
            stage(task, half_own.at[:, lane_block(spot)]).start()

        @pl.when(task // half_blocks != mp)
        def _():
            stage(task, half_send.at[:, lane_block(spot)]).start()

    def compute(q, core_side, store):
        @pl.when(q < outer)
        def _():
            side = left_out_ref[:, :, core_side].reshape(channels // 2, tokens)
            parts = [
                jnp.dot(side, right_out_ref[:, lane_block(2 * q + at)], preferred_element_type=F32)
                for at in (0, 1)
            ]
            parts = [part.reshape(DEPTH, 2, half, LANES) for part in parts]
            store(jnp.concatenate(parts, axis=2))

        @pl.when((q >= outer) & (q < gains))
        def _():
            at = q - outer
            side = left_ref[:, :, core_side].reshape(DEPTH * 2 * block, tokens)
            right = grad_ref[at // across, :, lane_block(lax.rem(at, across))]
            store(jnp.dot(side, right, preferred_element_type=F32).reshape(DEPTH, 2, block, LANES))

        @pl.when(q == gains)
        def _():
            for owner in range(2 * DEPTH):
                line = 2 * owner + core_side
                gain_chunk[owner // 2, owner % 2, 0:8, 0:128] = gain_ref[line] + gain_sum[line]
            store(gain_chunk[...])

    def finish(p, value):
        total[lax.rem(p, 4)] = value

        @pl.when(p >= outer)
        def _():
            index = p - outer

            @pl.when(index >= 2)
            def _():
                swap_copy(index - 2).wait_send()

            first = jnp.where(p == gains, 0, 1 - mp) * half
            rows = pl.ds(pl.multiple_of(first, half), half)
            swap_out[lax.rem(index, 2)] = total[lax.rem(p, 4), rows, :].astype(BF)
            swap_copy(index).start()

    scatter_step(step, chunks, compute, finish, scratch, small_last=True)

    @pl.when((step >= Z_LAG + SWAP_LAG) & (step < chunks + Z_LAG + SWAP_LAG))
    def _():
        p = step - Z_LAG - SWAP_LAG
        slot = lax.rem(p, 4)

        @pl.when(p < outer)
        def _():
            out_ref[0, :, :LANES] = total[slot, :half, :]
            out_ref[0, :, LANES:] = total[slot, half:, :]

        @pl.when(p >= outer)
        def _():
            swap_copy(p - outer).wait_recv()
            came = swap_in[lax.rem(p - outer, 8)].astype(F32)

            @pl.when(p < gains)
            def _():
                own = total[slot, pl.ds(pl.multiple_of(mp * half, half), half), :]
                first = jnp.where(mp == 0, own, came)
                second = jnp.where(mp == 0, came, own)
                for tile in (0, 1):
                    lanes = slice(128 * tile, 128 * tile + 128)
                    left, right = split_lanes(first[:, lanes], second[:, lanes])
                    out_ref[0, :, 256 * tile : 256 * tile + 128] = left
                    out_ref[0, :, 256 * tile + 128 : 256 * tile + 256] = right

            @pl.when(p == gains)
            def _():
                gain_out[...] = total[slot, 0:8, 0:128] + came[0:8, 0:128]

    @pl.when(step == chunks + Z_LAG + SWAP_LAG - 1)
    def _():
        for spot in range(half_blocks):
            half_copy(spot).wait()
        for index in range(gains - outer - 1, gains - outer + 1):
            swap_copy(index).wait_send()
        dot_copy.wait()


def mixer_call(
    left_in, grad_pre, left_out, right_out, gain_parts, tokens, inverse, weights, dots, collective
):
    _, rows, channels = grad_pre.shape
    full = left_in.shape[0]
    block, half = full // 16, channels // 16
    full_blocks, across = full // LANES, channels // LANES
    outer, inner = full_blocks // 2, 3 * across
    chunks = outer + inner + 1
    any_space = pl.BlockSpec(memory_space=pl.ANY)
    dma = pltpu.SemaphoreType.DMA
    part = jax.ShapeDtypeStruct((rows, full // 2), BF)

    def out_place(q):
        p = jnp.clip(q - Z_LAG - SWAP_LAG, 0, outer + inner - 1)
        inside = jnp.maximum(p - outer, 0)
        return (
            jnp.where(p < outer, 3, inside // across), 0, jnp.where(p < outer, p, lax.rem(inside, across)))

    out, gains, half_own, _, half_came, dot_came = pl.pallas_call(
        functools.partial(mixer_kernel, full_blocks),
        grid=(chunks + Z_LAG + SWAP_LAG,),
        in_specs=[
            any_space, any_space,
            fixed((DEPTH, 2, 2, half, rows)), fixed(right_out.shape), fixed(gain_parts.shape),
            any_space, fixed(inverse.shape), any_space, any_space,
        ],
        out_specs=[
            pl.BlockSpec((1, half, 2 * LANES), out_place),
            pl.BlockSpec((8, 128), lambda q: (0, 0)),
        ] + [any_space] * 4,
        out_shape=[
            jax.ShapeDtypeStruct((4, half, full), F32), jax.ShapeDtypeStruct((8, 128), F32),
            part, part, part, jax.ShapeDtypeStruct(dots.shape, F32),
        ],
        scratch_shapes=[
            pltpu.VMEM((DEPTH, 2, 2, block, rows), BF),
            pltpu.VMEM(grad_pre.shape, BF),
            dma((2,)),
            pltpu.VMEM((3, LANES, channels), BF),
            pltpu.VMEM((rows, LANES), BF),
            pltpu.VMEM((16, 8, 128), F32),
            pltpu.VMEM((DEPTH, 2, block, LANES), F32),
            pltpu.VMEM((4, block, LANES), F32),
            pltpu.VMEM((2, half, LANES), BF),
            pltpu.VMEM((8, half, LANES), BF),
            pltpu.VMEM((2, rows, LANES), BF),
            dma((2,)), dma((2,)), dma((full_blocks // 2,)), dma((full_blocks // 2,)),
            dma((2,)), dma((8,)), dma((2,)),
            *scatter_scratch(block, LANES),
        ],
        compiler_params=pltpu.CompilerParams(
            collective_id=collective, has_side_effects=True, vmem_limit_bytes=VMEM_LIMIT),
        cost_estimate=pl.CostEstimate(
            flops=14 * full * rows * channels, bytes_accessed=16 * full * channels, transcendentals=0),
    )(
        left_in.reshape(DEPTH, 2, 2, block, rows), grad_pre,
        left_out.reshape(DEPTH, 2, 2, half, rows), right_out, gain_parts, tokens, inverse, weights, dots,
    )
    return out, gains, half_own.astype(F32) + half_came.astype(F32), dot_came


def middle_back_kernel(
    sum_own_ref, sum_came_ref, middle_ref, cot_ref, tokens_ref, weight_ref, gain_ref, mixer_ref,
    grad_own_ref, low_ref, mean_ref, gated_ref, gain_grad_ref,
):
    rows, full = middle_ref.shape
    part = full // 2
    middle = middle_ref[...]
    inverse = lax.rsqrt(jnp.mean(middle * middle, axis=-1, keepdims=True) + EPSILON)
    unit = middle * inverse
    grad_normed = sum_own_ref[...].astype(F32) + sum_came_ref[...].astype(F32)
    product = grad_normed * unit
    before = jnp.where(pl.program_id(0) == 0, 0.0, gain_grad_ref[...])
    gain_grad_ref[...] = before + jnp.sum(product, axis=0, keepdims=True)
    dots = jnp.mean(product * gain_ref[...], axis=-1, keepdims=True)
    back = cot_ref[...].astype(F32) * weight_ref[...]
    grad = back + inverse * (grad_normed * gain_ref[...] - unit * dots)
    first = lax.axis_index("mp") == 0
    grad_own_ref[...] = jnp.where(first, grad[:, :part], grad[:, part:])
    low = grad.astype(BF)
    low_ref[...] = low
    branch = middle - tokens_ref[...].astype(F32)
    mean_ref[...] = jnp.mean(low.astype(F32) * branch, axis=-1, keepdims=True)
    gated_ref[...] = lax.dot_general(
        low, mixer_ref[...], (((1,), (1,)), ((), ())), preferred_element_type=F32)


def middle_back(sum_own, sum_came, middle, cot, tokens, weight, gain, mixer_out):
    rows, full = middle.shape
    channels = mixer_out.shape[0]
    step = 224 if rows % 224 == 0 else rows
    line = lambda width: pl.BlockSpec((step, width), lambda r: (r, 0))
    shape = jax.ShapeDtypeStruct
    return pl.pallas_call(
        middle_back_kernel,
        grid=(rows // step,),
        in_specs=[line(full)] * 5 + [line(1), fixed((1, full)), fixed(mixer_out.shape)],
        out_specs=[
            line(full // 2), line(full), line(1), line(channels),
            pl.BlockSpec((1, full), lambda r: (0, 0)),
        ],
        out_shape=[
            shape((rows, full // 2), F32), shape((rows, full), BF), shape((rows, 1), F32),
            shape((rows, channels), F32), shape((1, full), F32),
        ],
        compiler_params=pltpu.CompilerParams(vmem_limit_bytes=VMEM_LIMIT),
        cost_estimate=pl.CostEstimate(
            flops=2 * rows * full * channels, bytes_accessed=rows * full * 20, transcendentals=0),
    )(sum_own, sum_came, middle, cot, tokens, weight, gain[None], mixer_out)


def glu_update_kernel(scale, act_ref, up_ref, out_ref, *refs):
    in_refs, down_refs, in_new, down_new = refs[:3], refs[3:6], refs[6:9], refs[9:12]
    count = STEP_NUMBER
    for at, grad_ref in ((0, act_ref), (1, up_ref)):
        new = adamw_update(
            *(ref[at] for ref in in_refs), grad_ref[0] * scale, count, MATRIX_RATE, DECAY_RATE)
        for ref, value in zip(in_new, new):
            ref[at] = value
    new = adamw_update(
        *(ref[...] for ref in down_refs), out_ref[0].T * scale, count, MATRIX_RATE, DECAY_RATE)
    for ref, value in zip(down_new, new):
        ref[...] = value


def glu_update(sums, ins, downs, scale):
    _, rows, lanes = sums.shape
    blocks = ins[0].shape[2] // lanes
    sum_spec = lambda kind: pl.BlockSpec((1, rows, lanes), lambda q: (3 * q + kind, 0, 0))
    in_spec = pl.BlockSpec((2, rows, lanes), lambda q: (0, 0, q))
    down_spec = pl.BlockSpec((lanes, rows), lambda q: (q, 0))
    new = pl.pallas_call(
        functools.partial(glu_update_kernel, scale),
        grid=(blocks,),
        in_specs=[sum_spec(0), sum_spec(1), sum_spec(2)] + [in_spec] * 3 + [down_spec] * 3,
        out_specs=[in_spec] * 3 + [down_spec] * 3,
        out_shape=[jax.ShapeDtypeStruct(ins[0].shape, F32)] * 3 + [jax.ShapeDtypeStruct(downs[0].shape, F32)] * 3,
        compiler_params=pltpu.CompilerParams(vmem_limit_bytes=VMEM_LIMIT),
        cost_estimate=pl.CostEstimate(
            flops=60 * rows * lanes * blocks, bytes_accessed=84 * rows * lanes * blocks,
            transcendentals=6 * rows * lanes * blocks),
    )(sums, sums, sums, *ins, *downs)
    return tuple(new[:3]), tuple(new[3:])


ITEMS = 4


def split_lanes(first, second):
    low = lax.broadcasted_iota(jnp.int32, first.shape, 1) < 64
    return (
        jnp.where(low, first, pltpu.roll(second, 64, 1)),
        jnp.where(low, pltpu.roll(first, 64, 1), second),
    )


def gather_kernel(mixer_ref, gain_ref, lengths_ref, domains_ref, glu_in_ref, glu_out_ref, cot_ref,
                  all_in, all_out, all_small, cot_full, glu_low,
                  in_ref, out_ref, small_ref, right_send, left_send,
                  z_recv, x_send, x_recv, core_send, core_recv, y_send, y_recv, local_sem):
    z, x, core = device_place()
    mp = lax.axis_index("mp")
    barrier = pltpu.get_barrier_semaphore()
    for kind in range(3):
        for tile in range(in_ref.shape[3] // 128):
            first = mixer_ref[kind, :, 256 * tile : 256 * tile + 128]
            second = mixer_ref[kind, :, 256 * tile + 128 : 256 * tile + 256]
            for side, value in enumerate(split_lanes(first, second)):
                in_ref[side, kind, :, 128 * tile : 128 * tile + 128] = value.astype(BF)
    out_ref[...] = mixer_ref[3].astype(BF)
    lane = lax.broadcasted_iota(jnp.int32, (1, 128), 1)
    live = jnp.zeros((1, 128), F32)
    for batch in range(lengths_ref.shape[0]):
        count = lengths_ref[batch : batch + 1, :].astype(F32)
        live = live + jnp.where(lane == domains_ref[batch : batch + 1, :], count, 0.0)
    small_ref[...] = jnp.zeros_like(small_ref)
    small_ref[0:3, 0:64] = gain_ref[...].astype(BF).astype(F32)
    small_ref[3:4, :] = live
    right, left = lax.rem(z + 1, DEPTH), lax.rem(z + DEPTH - 1, DEPTH)
    dp = lax.axis_index("dp")
    for target in (
        device_at(right, x, core), device_at(left, x, core), device_at(z, 1 - x, core),
        device_at(z, x, 1 - core), (dp, 1 - mp),
    ):
        pl.semaphore_signal(barrier, 1, device_id=target, device_id_type=MESH_ID)
    pl.semaphore_wait(barrier, 5)

    def spot(item, zs, xs, cs, side=None):
        if item == 0:
            return all_in.at[:, zs, xs, cs, mp if side is None else side]
        if item == 1:
            return all_out.at[zs, xs, cs]
        if item == 2:
            return all_in.at[:, zs, xs, cs, 1 - mp]
        return all_small.at[zs, xs, cs]

    def own(item):
        if item == 0:
            return in_ref.at[mp]
        if item == 1:
            return out_ref
        return spot(item, z, x, core)

    def copy(item, zs, xs, target, send, recv, source=None):
        return pltpu.make_async_remote_copy(
            spot(item, zs, xs, core) if source is None else source, spot(item, zs, xs, core),
            send, recv, device_id=target, device_id_type=MESH_ID)

    def right_copy(item, zs, source=None):
        return copy(item, zs, x, device_at(right, x, core), right_send.at[zs, item], z_recv.at[zs, item], source)

    def left_copy(item, zs, source=None):
        return copy(item, zs, x, device_at(left, x, core), left_send.at[zs, item], z_recv.at[zs, item], source)

    def x_copy(item, zs, source=None):
        return copy(item, zs, x, device_at(z, 1 - x, core), x_send.at[zs, item], x_recv.at[zs, item], source)

    def core_copy(item, zs, xs, source=None):
        return copy(item, zs, xs, device_at(z, x, 1 - core), core_send.at[zs, xs, item], core_recv.at[zs, xs, item], source)

    y_copies = [
        pltpu.make_async_remote_copy(
            in_ref.at[1 - mp], all_in.at[:, z, x, core, mp], y_send.at[0], y_recv.at[0],
            device_id=(dp, 1 - mp), device_id_type=MESH_ID),
        pltpu.make_async_remote_copy(
            small_ref, all_small.at[z, x, core, mp], y_send.at[1], y_recv.at[1],
            device_id=(dp, 1 - mp), device_id_type=MESH_ID),
    ]
    locals_ = [
        pltpu.make_async_copy(in_ref.at[mp], spot(0, z, x, core), local_sem.at[0]),
        pltpu.make_async_copy(out_ref, spot(1, z, x, core), local_sem.at[1]),
        pltpu.make_async_copy(small_ref, all_small.at[z, x, core, mp], local_sem.at[2]),
    ]
    cot_lanes = pl.ds(pl.multiple_of(mp * cot_ref.shape[1], 128), cot_ref.shape[1])
    cot_local = pltpu.make_async_copy(cot_ref, cot_full.at[:, cot_lanes], local_sem.at[3])
    cot_copy = pltpu.make_async_remote_copy(
        cot_ref, cot_full.at[:, cot_lanes], y_send.at[2], y_recv.at[2],
        device_id=(dp, 1 - mp), device_id_type=MESH_ID)
    for one in y_copies:
        one.start()
    locals_[2].start()

    for item in range(ITEMS):
        if item == 2:
            y_copies[0].wait_recv()
        if item == 3:
            y_copies[1].wait_recv()
            locals_[2].wait()
        source = own(item)

        @pl.when(z < DEPTH - 1)
        def _():
            right_copy(item, z, source).start()

        @pl.when(z > 0)
        def _():
            left_copy(item, z, source).start()

        x_copy(item, z, source).start()
        core_copy(item, z, x, source).start()
    locals_[0].start()
    locals_[1].start()
    cot_copy.start()
    cot_local.start()
    glu_low[0:2] = glu_in_ref[...].astype(BF)
    for tile in range(glu_out_ref.shape[0] // 128):
        lanes = slice(128 * tile, 128 * tile + 128)
        glu_low[2, :, lanes] = glu_out_ref[lanes, :].T.astype(BF)

    def from_x(item, zs):
        pltpu.make_async_remote_copy(
            spot(item, zs, 1 - x, core), spot(item, zs, 1 - x, core), x_send.at[zs, item],
            x_recv.at[zs, item], device_id=device_at(z, 1 - x, core), device_id_type=MESH_ID).wait_recv()
        core_copy(item, zs, 1 - x).start()

    for hop in range(1, DEPTH + 1):
        for item in range(ITEMS):
            if hop < DEPTH:
                @pl.when(z >= hop)
                def _():
                    zs = z - hop
                    right_copy(item, zs).wait_recv()

                    @pl.when(z < DEPTH - 1)
                    def _():
                        right_copy(item, zs).start()

                    x_copy(item, zs).start()
                    core_copy(item, zs, x).start()

                @pl.when(z + hop < DEPTH)
                def _():
                    zs = z + hop
                    left_copy(item, zs).wait_recv()

                    @pl.when(z > 0)
                    def _():
                        left_copy(item, zs).start()

                    x_copy(item, zs).start()
                    core_copy(item, zs, x).start()
            if hop == 1:
                from_x(item, z)
            else:
                @pl.when(z >= hop - 1)
                def _():
                    from_x(item, z - (hop - 1))

                @pl.when(z + hop - 1 < DEPTH)
                def _():
                    from_x(item, z + (hop - 1))

    for item in range(ITEMS):
        for zs in range(DEPTH):
            @pl.when((z >= zs) & (z < DEPTH - 1))
            def _():
                right_copy(item, zs).wait_send()

            @pl.when((z <= zs) & (z > 0))
            def _():
                left_copy(item, zs).wait_send()

            x_copy(item, zs).wait_send()
            for xs in range(2):
                core_copy(item, zs, xs).wait()
    for one in y_copies:
        one.wait_send()
    locals_[0].wait()
    locals_[1].wait()
    cot_local.wait()
    cot_copy.wait_send()
    pltpu.make_async_remote_copy(
        cot_ref, cot_full.at[:, pl.ds(pl.multiple_of((1 - mp) * cot_ref.shape[1], 128), cot_ref.shape[1])],
        y_send.at[2], y_recv.at[2], device_id=(dp, 1 - mp), device_id_type=MESH_ID).wait_recv()


def gather_call(mixer, gain, lengths, domains, glu_in, glu_out, cot, collective):
    _, own_rows, full = mixer.shape
    channels = full // 2
    dma = pltpu.SemaphoreType.DMA
    any_space = pl.BlockSpec(memory_space=pl.ANY)
    in_vmem = pl.BlockSpec(memory_space=pltpu.VMEM)
    _, glu_rows, hidden = glu_in.shape
    return pl.pallas_call(
        gather_kernel,
        in_specs=[in_vmem] * 6 + [any_space],
        out_specs=[any_space] * 4 + [in_vmem],
        out_shape=[
            jax.ShapeDtypeStruct((3, DEPTH, 2, 2, 2, own_rows, channels), BF),
            jax.ShapeDtypeStruct((DEPTH, 2, 2, own_rows, full), BF),
            jax.ShapeDtypeStruct((DEPTH, 2, 2, 2, 8, 128), F32),
            jax.ShapeDtypeStruct((cot.shape[0], 2 * cot.shape[1]), BF),
            jax.ShapeDtypeStruct((3, glu_rows, hidden), BF),
        ],
        scratch_shapes=[
            pltpu.VMEM((2, 3, own_rows, channels), BF),
            pltpu.VMEM((own_rows, full), BF),
            pltpu.VMEM((8, 128), F32),
            dma((DEPTH, ITEMS)), dma((DEPTH, ITEMS)), dma((DEPTH, ITEMS)), dma((DEPTH, ITEMS)),
            dma((DEPTH, ITEMS)), dma((DEPTH, 2, ITEMS)), dma((DEPTH, 2, ITEMS)), dma((3,)), dma((3,)), dma((4,)),
        ],
        compiler_params=pltpu.CompilerParams(
            collective_id=collective, has_side_effects=True, vmem_limit_bytes=VMEM_LIMIT),
        cost_estimate=pl.CostEstimate(flops=0, bytes_accessed=300_000_000, transcendentals=0),
    )(mixer, gain, lengths, domains, glu_in, glu_out, cot)


def shards(
    tokens,
    cotangent,
    lengths,
    domains,
    lower_bound,
    mixer_master,
    mixer_first,
    mixer_second,
    glu_in_master,
    glu_in_first,
    glu_in_second,
    glu_out_master,
    glu_out_first,
    glu_out_second,
    gain_master,
    gain_first,
    gain_second,
):
    batches, _, length, full = tokens.shape
    rows = batches * length
    groups = lax.axis_size("dp")
    narrow = lax.axis_size("mp")
    place = lax.axis_index("mp")
    own_rows = mixer_master.shape[1]
    channels = groups * own_rows
    part = full // narrow
    quick = groups == 16 and narrow == 2 and own_rows == 64

    domain_ids = jnp.arange(NDOM, dtype=jnp.int32)
    member = (domains[..., 0][..., None] == domain_ids).astype(F32)
    cot_part = cotangent.reshape(rows, part)
    if quick:
        mixer_in, mixer_out, small, cot_full, glu_low = gather_call(
            mixer_master, gain_master, lengths, domains[..., 0], glu_in_master, glu_out_master, cot_part, 2
        )
        mixer_in = mixer_in.reshape(3, full, channels)
        mixer_out = mixer_out.reshape(channels, full)
        small = small.reshape(groups, narrow, 8, 128)
        gain_full = small[:, :, :3, :own_rows].transpose(2, 0, 1, 3).reshape(3, full)
        counts = jnp.sum(small[:, 0, 3, :NDOM], axis=0)
    else:
        gain_full = lax.all_gather(
            gain_master.astype(BF), ("dp", "mp"), axis=1, tiled=True
        ).astype(F32)
        mixer_low = mixer_master.astype(BF)
        in_blocks = mixer_low[:3].reshape(3, own_rows, groups, narrow, own_rows)
        in_blocks = in_blocks.transpose(3, 0, 1, 2, 4).reshape(narrow, 3, own_rows, channels)
        in_rows = mp_swap(in_blocks).transpose(1, 0, 2, 3).reshape(3, narrow * own_rows, channels)
        mixer_in = lax.all_gather(in_rows, "dp", axis=1, tiled=True)
        mixer_out = lax.all_gather(mixer_low[3], "dp", axis=0, tiled=True)
        counts = lax.psum(jnp.sum(member * lengths.astype(F32)[..., None], axis=(0, 1)), "dp")
        cot_full = mp_gather(cot_part)
        glu_low = jnp.concatenate([glu_in_master.astype(BF), glu_out_master.astype(BF).T[None]])
    glu = lax.all_gather(glu_low, "dp", axis=1, tiled=True)

    seq_weight = jnp.sum(counts) / (NDOM * jnp.sum(member * counts, axis=-1))
    positions = jnp.arange(length, dtype=jnp.int32)
    token_weight = jnp.where(positions[None, :] < lengths[:, :1], seq_weight[:, :1], 0.0)
    token_weight = token_weight.reshape(rows, 1)

    own_channels = lambda v: lax.dynamic_index_in_dim(
        v.reshape(groups, narrow, own_rows), place, 1, keepdims=False
    ).reshape(channels)
    bound = own_channels(lower_bound)
    state_gain = own_channels(gain_full[1])

    token_rows = tokens.reshape(rows, full)
    seq_in = token_rows.astype(F32)
    inverse_in = inverse_rms(seq_in)
    unit_in = seq_in * inverse_in
    normed_in = (unit_in * gain_full[0]).astype(BF)
    pre = jnp.einsum("td,kde->kte", normed_in, mixer_in, preferred_element_type=F32)
    pre = pre.reshape(3, batches, length, channels)
    states, raw, square = scan_forward(pre, bound, state_gain)
    square = mp_sum_wide(square.reshape(rows, 1))
    inverse_state = lax.rsqrt(square / full + EPSILON)
    mixed = jnp.dot(raw.reshape(rows, channels), mixer_out, preferred_element_type=F32)
    back_low = (cot_full.astype(F32) * token_weight).astype(BF)
    if quick:
        mixed = mixed.astype(BF)
        came, left_back, left_in = lax.optimization_barrier(
            (partner_swap(mixed), back_low.T, normed_in.T)
        )
        mixed = mixed.astype(F32) + came.astype(F32)
    else:
        mixed = mp_sum(mixed)
    branch_mix = inverse_state * mixed
    middle = seq_in + branch_mix
    inverse_mid = inverse_rms(middle)
    unit_mid = middle * inverse_mid
    normed_mid = (unit_mid * gain_full[2]).astype(BF)

    across = (((1,), (1,)), ((), ()))
    down = (((0,), (0,)), ((), ()))
    dot = functools.partial(lax.dot_general, preferred_element_type=F32)
    if quick:
        glu_sums, sum_own, sum_came, half_own, half_send = glu_call(normed_mid, back_low, left_back, glu, 0)
        branch = half_own.astype(F32) + partner_swap(half_send).astype(F32)
    else:
        pre_act = jnp.dot(normed_mid, glu[0], preferred_element_type=F32)
        pre_up = jnp.dot(normed_mid, glu[1], preferred_element_type=F32)
        grad_hidden = jnp.dot(back_low, glu[2], preferred_element_type=F32)
        act_part = jax.nn.silu(pre_act)
        hidden = (act_part * pre_up).astype(BF)
        grad_act = (grad_hidden * pre_up * silu_slope(pre_act)).astype(BF)
        grad_up = (grad_hidden * act_part).astype(BF)
        grad_normed = mp_sum(dot(grad_act, glu[0], across) + dot(grad_up, glu[1], across))
        glu_grad = jnp.stack(
            [dot(normed_mid, grad_act, down), dot(normed_mid, grad_up, down), dot(back_low, hidden, down)]
        ).astype(BF)
        glu_own = lax.psum_scatter(glu_grad, "dp", scatter_dimension=1, tiled=True).astype(F32)
        branch = mp_scatter(dot(hidden, glu[2], across))
    own_features = lambda v: lax.dynamic_slice_in_dim(v, place * part, part, v.ndim - 1)
    if quick:
        grad_middle_own, middle_low, state_mean, grad_gated, gain_mid = middle_back(
            sum_own, sum_came, middle, cot_full, token_rows, token_weight, gain_full[2], mixer_out
        )
        gain_mid = gain_mid[0]
    else:
        inverse_mid = inverse_rms(middle)
        unit_mid = middle * inverse_mid
        gain_mid = jnp.sum(grad_normed * unit_mid, axis=0)
        scaled_mid = grad_normed * gain_full[2]
        back = cot_full.astype(F32) * token_weight
        grad_middle = back + inverse_mid * (
            scaled_mid - unit_mid * jnp.mean(scaled_mid * unit_mid, axis=-1, keepdims=True)
        )
        grad_middle_own = own_features(grad_middle)
        middle_low = grad_middle.astype(BF)
        state_mean = jnp.mean(middle_low.astype(F32) * branch_mix, axis=-1, keepdims=True)
        grad_gated = dot(middle_low, mixer_out, across)
    by_batch = lambda v: v.reshape(batches, length, v.shape[-1])
    grad_pre, gated_out, gain_state, pre_dot = scan_backward(
        pre, states, by_batch(grad_gated), by_batch(inverse_state), by_batch(state_mean), bound, state_gain
    )
    grad_pre = grad_pre.reshape(3, rows, channels)
    gated_out = gated_out.reshape(rows, channels)
    gain_state = jnp.sum(gain_state, axis=0).reshape(groups, 1, own_rows)
    gain_state = lax.dynamic_update_slice_in_dim(
        jnp.zeros((groups, narrow, own_rows), F32), gain_state, place, 1
    )
    device = lax.axis_index("dp") * narrow + place
    if quick:
        gain_parts = jnp.stack(
            [
                jnp.zeros((groups, narrow * own_rows), F32),
                gain_state.reshape(groups, narrow * own_rows),
                0.5 * gain_mid.reshape(groups, narrow * own_rows),
            ],
            axis=1,
        )
        gain_parts = jnp.pad(gain_parts, ((0, 0), (0, 5), (0, 0)))
        pre_dot = pre_dot.reshape(-1, 128)
        mixer_own, gain_own, grad_normed_in, dot_came = mixer_call(
            left_in, grad_pre, gated_out.T, middle_low, gain_parts, token_rows, inverse_in, mixer_in, pre_dot, 1
        )
        in_mean = (pre_dot + dot_came).reshape(rows, 1) / full
        gain_own = lax.dynamic_slice_in_dim(gain_own[:3], place * own_rows, own_rows, 1)
    else:
        grad_mix_out = dot(gated_out, middle_low, down).astype(BF)
        grad_mix_in = jnp.einsum("td,kte->kde", normed_in, grad_pre, preferred_element_type=F32)
        in_own = lax.psum_scatter(grad_mix_in.astype(BF), "dp", scatter_dimension=1, tiled=True)
        out_own = lax.psum_scatter(grad_mix_out, "dp", scatter_dimension=0, tiled=True)
        in_own = mp_swap(in_own.reshape(3, narrow, own_rows, channels).transpose(1, 0, 2, 3))
        in_own = in_own.reshape(narrow, 3, own_rows, groups, own_rows).transpose(1, 2, 3, 0, 4)
        grad_normed_in = jnp.einsum("kte,kde->td", grad_pre, mixer_in, preferred_element_type=F32)
        gain_in = jnp.sum(grad_normed_in * unit_in, axis=0)
        grad_normed_in = mp_scatter(grad_normed_in)
        gain_rows = jnp.stack([gain_in, gain_state.reshape(full), gain_mid / narrow])
        gain_total = lax.psum(gain_rows, ("dp", "mp"))
        gain_own = lax.dynamic_slice_in_dim(gain_total, device * own_rows, own_rows, 1)
        in_mean = mp_sum_wide(pre_dot.reshape(rows, 1)) / full
        in_own = in_own.reshape(3, own_rows, full)
        mixer_own = jnp.concatenate([in_own, out_own[None]]).astype(F32)
    unit_in_own = own_features(token_rows).astype(F32) * inverse_in
    grad_seq = grad_middle_own + inverse_in * (
        grad_normed_in * own_features(gain_full[0]) - unit_in_own * in_mean
    )
    grad_tokens = grad_seq.astype(BF)
    layer_out = (own_features(middle) + branch).astype(BF)

    scale = 1.0 / (batches * groups * tokens.shape[1])
    update = functools.partial(adamw_update, count=STEP_NUMBER)
    mixer_new = update(
        mixer_master, mixer_first, mixer_second, mixer_own * scale, rate=MATRIX_RATE, decay=DECAY_RATE
    )
    gain_new = update(
        gain_master, gain_first, gain_second, gain_own * scale, rate=GAIN_RATE, decay=0.0
    )
    glu_ins = (glu_in_master, glu_in_first, glu_in_second)
    glu_downs = (glu_out_master, glu_out_first, glu_out_second)
    if quick:
        glu_in_new, glu_out_new = glu_update(glu_sums, glu_ins, glu_downs, scale)
    else:
        glu_in_new = update(*glu_ins, glu_own[:2] * scale, rate=MATRIX_RATE, decay=DECAY_RATE)
        glu_out_new = update(*glu_downs, glu_own[2].T * scale, rate=MATRIX_RATE, decay=DECAY_RATE)
    return (
        layer_out.reshape(batches, 1, length, part),
        grad_tokens.reshape(batches, 1, length, part),
        *mixer_new,
        *glu_in_new,
        *glu_out_new,
        *gain_new,
    )


def solution(mesh):
    weights = (
        [P(None, ("dp", "mp"), None)] * 3
        + [P(None, "dp", "mp")] * 3
        + [P("mp", "dp")] * 3
        + [P(None, ("dp", "mp"))] * 3
    )
    in_specs = (
        P(None, "dp", None, None),
        P(None, "dp", None, "mp"),
        P(None, "dp"),
        P(None, "dp", None),
        P(),
        *weights,
    )
    out_specs = (P(None, "dp", None, "mp"), P(None, "dp", None, "mp"), *weights)
    return jax.shard_map(shards, mesh=mesh, in_specs=in_specs, out_specs=out_specs, check_vma=False)
```

```python
import functools

import jax
import jax.numpy as jnp
from jax import lax
from jax.experimental import pallas as pl
from jax.experimental.pallas import tpu as pltpu
from jax.sharding import PartitionSpec as P

NDOM = 8

EPSILON = 1e-06
BETA_ONE = 0.9
BETA_TWO = 0.95
ADAM_EPSILON = 1e-08
DECAY_RATE = 0.1
MATRIX_RATE = 0.06
GAIN_RATE = 0.5
STEP_NUMBER = 3.0

BF = jnp.bfloat16
F32 = jnp.float32
VMEM_LIMIT = 56 * 1024 * 1024


def inverse_rms(values):
    return lax.rsqrt(jnp.mean(values * values, axis=-1, keepdims=True) + EPSILON)


def silu_slope(values):
    sigma = jax.nn.sigmoid(values)
    return sigma * (1.0 + values * (1.0 - sigma))


def adamw_update(master, first, second, gradient, count, rate, decay):
    first_new = BETA_ONE * first + (1.0 - BETA_ONE) * gradient
    second_new = BETA_TWO * second + (1.0 - BETA_TWO) * gradient * gradient
    first_hat = first_new / (1.0 - BETA_ONE**count)
    second_hat = second_new / (1.0 - BETA_TWO**count)
    master_new = master - rate * (
        first_hat / (jnp.sqrt(second_hat) + ADAM_EPSILON) + decay * master
    )
    return (master_new, first_new, second_new)


def partner_swap(value):
    return lax.ppermute(value, "mp", [(0, 1), (1, 0)])


def mp_sum(part):
    low = part.astype(BF)
    if lax.axis_size("mp") == 2:
        return low.astype(F32) + partner_swap(low).astype(F32)
    return lax.psum(low.astype(F32), "mp")


def mp_sum_wide(part):
    if lax.axis_size("mp") == 2:
        return part + partner_swap(part)
    return lax.psum(part, "mp")


def mp_scatter(part):
    if lax.axis_size("mp") == 2:
        half = part.shape[1] // 2
        place = lax.axis_index("mp")
        own = lax.dynamic_slice_in_dim(part, place * half, half, 1)
        other = lax.dynamic_slice_in_dim(part, (1 - place) * half, half, 1)
        return own.astype(BF).astype(F32) + partner_swap(other.astype(BF)).astype(F32)
    return lax.psum_scatter(part.astype(BF), "mp", scatter_dimension=1, tiled=True).astype(F32)


def mp_swap(pieces):
    if lax.axis_size("mp") == 2:
        place = lax.axis_index("mp")
        own = lax.dynamic_index_in_dim(pieces, place, 0, keepdims=False)
        came = partner_swap(lax.dynamic_index_in_dim(pieces, 1 - place, 0, keepdims=False))
        first = place == 0
        return jnp.stack([jnp.where(first, own, came), jnp.where(first, came, own)])
    return lax.all_to_all(pieces, "mp", 0, 0, tiled=False)


def mp_gather(part):
    if lax.axis_size("mp") == 2:
        place = lax.axis_index("mp")
        came = partner_swap(part)
        first = place == 0
        return jnp.concatenate([jnp.where(first, part, came), jnp.where(first, came, part)], axis=1)
    return lax.all_gather(part, "mp", axis=1, tiled=True)


SUB_ROWS = 8
TILE_ROWS = 64


def channel_block(width):
    return 512 if width % 512 == 0 else width


def scan_rows(total, decay, carry):
    row = lax.broadcasted_iota(jnp.int32, total.shape, 0)
    shift = 1
    while shift < SUB_ROWS:
        keep = row >= shift
        total = total + decay * jnp.where(keep, pltpu.roll(total, shift, 0), 0.0)
        decay = decay * jnp.where(keep, pltpu.roll(decay, shift, 0), 1.0)
        shift *= 2
    return total + decay * carry


def scan_rows_back(total, decay, carry):
    row = lax.broadcasted_iota(jnp.int32, total.shape, 0)
    shift = 1
    while shift < SUB_ROWS:
        keep = row < SUB_ROWS - shift
        total = total + decay * jnp.where(keep, pltpu.roll(total, SUB_ROWS - shift, 0), 0.0)
        decay = decay * jnp.where(keep, pltpu.roll(decay, SUB_ROWS - shift, 0), 1.0)
        shift *= 2
    return total + decay * carry


def scan_forward_kernel(pre_ref, bound_ref, gain_ref, states_ref, raw_ref, square_ref):
    length, width = states_ref.shape[1], states_ref.shape[2]
    bound = bound_ref[...]
    gain = gain_ref[...]
    first_block = pl.program_id(1) == 0

    def step(index, carry):
        rows = pl.ds(pl.multiple_of(index * TILE_ROWS, TILE_ROWS), TILE_ROWS)
        forget = bound + (1.0 - bound) * jax.nn.sigmoid(pre_ref[1, 0, rows, :])
        total = (1.0 - forget) * jax.nn.silu(pre_ref[0, 0, rows, :])
        parts = []
        for low in range(0, TILE_ROWS, SUB_ROWS):
            part = scan_rows(total[low : low + SUB_ROWS], forget[low : low + SUB_ROWS], carry)
            carry = part[SUB_ROWS - 1 : SUB_ROWS]
            parts.append(part)
        states = jnp.concatenate(parts)
        states_ref[0, rows, :] = states
        raw = states * gain * jax.nn.silu(pre_ref[2, 0, rows, :])
        raw_ref[0, rows, :] = raw.astype(raw_ref.dtype)
        square = jnp.sum(states * states, axis=-1, keepdims=True)
        square_ref[0, rows, :] = square + jnp.where(first_block, 0.0, square_ref[0, rows, :])
        return carry

    lax.fori_loop(0, length // TILE_ROWS, step, jnp.zeros((1, width), F32))


def scan_forward(pre, bound, gain):
    _, batches, length, width = pre.shape
    block = channel_block(width)
    return pl.pallas_call(
        scan_forward_kernel,
        grid=(batches, width // block),
        in_specs=[
            pl.BlockSpec((3, 1, length, block), lambda b, c: (0, b, 0, c)),
            pl.BlockSpec((1, block), lambda b, c: (0, c)),
            pl.BlockSpec((1, block), lambda b, c: (0, c)),
        ],
        out_specs=[
            pl.BlockSpec((1, length, block), lambda b, c: (b, 0, c)),
            pl.BlockSpec((1, length, block), lambda b, c: (b, 0, c)),
            pl.BlockSpec((1, length, 1), lambda b, c: (b, 0, 0)),
        ],
        out_shape=[
            jax.ShapeDtypeStruct((batches, length, width), F32),
            jax.ShapeDtypeStruct((batches, length, width), BF),
            jax.ShapeDtypeStruct((batches, length, 1), F32),
        ],
        compiler_params=pltpu.CompilerParams(vmem_limit_bytes=VMEM_LIMIT),
        cost_estimate=pl.CostEstimate(
            flops=batches * length * width * 40,
            bytes_accessed=batches * length * width * 18,
            transcendentals=batches * length * width * 3,
        ),
    )(pre, bound[None], gain[None])


def scan_backward_kernel(
    pre_ref, states_ref, gated_ref, inverse_ref, mean_ref, bound_ref, gain_ref,
    grad_ref, out_ref, gain_grad_ref, dot_ref,
):
    length, width = states_ref.shape[1], states_ref.shape[2]
    bound = bound_ref[...]
    gain = gain_ref[...]
    first_block = pl.program_id(1) == 0
    row = lax.broadcasted_iota(jnp.int32, (TILE_ROWS, width), 0)
    tiles = length // TILE_ROWS

    def step(index, carry):
        carried_next, forget_next, gain_sum = carry
        place = tiles - 1 - index
        rows = pl.ds(pl.multiple_of(place * TILE_ROWS, TILE_ROWS), TILE_ROWS)
        pre_input = pre_ref[0, 0, rows, :]
        pre_forget = pre_ref[1, 0, rows, :]
        pre_gate = pre_ref[2, 0, rows, :]
        states = states_ref[0, rows, :]
        inverse = inverse_ref[0, rows, :]
        grad_gated = gated_ref[0, rows, :]
        unit = states * inverse
        gate_sig = jax.nn.sigmoid(pre_gate)
        gate = pre_gate * gate_sig
        out_ref[0, rows, :] = (unit * gain * gate).astype(out_ref.dtype)
        gain_sum = gain_sum + grad_gated * unit * gate
        scaled = grad_gated * gain
        grad_gate = (scaled * unit * (gate_sig * (1.0 + pre_gate * (1.0 - gate_sig)))).astype(BF)
        grad_ref[2, 0, rows, :] = grad_gate
        total = inverse * (scaled * gate - unit * mean_ref[0, rows, :])
        sigma = jax.nn.sigmoid(pre_forget)
        forget = bound + (1.0 - bound) * sigma
        decay = jnp.where(row == TILE_ROWS - 1, forget_next, pltpu.roll(forget, TILE_ROWS - 1, 0))
        parts = []
        for low in range(TILE_ROWS - SUB_ROWS, -1, -SUB_ROWS):
            part = scan_rows_back(
                total[low : low + SUB_ROWS], decay[low : low + SUB_ROWS], carried_next
            )
            carried_next = part[0:1]
            parts.insert(0, part)
        carried = jnp.concatenate(parts)
        before_rows = pl.ds(
            pl.multiple_of(jnp.maximum(place - 1, 0) * TILE_ROWS, TILE_ROWS), TILE_ROWS
        )
        before = states_ref[0, before_rows, :][TILE_ROWS - 1 : TILE_ROWS, :]
        before = jnp.where(place == 0, 0.0, before)
        earlier = jnp.where(row == 0, before, pltpu.roll(states, 1, 0))
        input_sig = jax.nn.sigmoid(pre_input)
        fresh = pre_input * input_sig
        slope = input_sig * (1.0 + pre_input * (1.0 - input_sig))
        grad_input = (carried * (1.0 - forget) * slope).astype(BF)
        grad_forget = (
            carried * (earlier - fresh) * (1.0 - bound) * sigma * (1.0 - sigma)
        ).astype(BF)
        grad_ref[0, 0, rows, :] = grad_input
        grad_ref[1, 0, rows, :] = grad_forget
        dots = (
            grad_input.astype(F32) * pre_input
            + grad_forget.astype(F32) * pre_forget
            + grad_gate.astype(F32) * pre_gate
        )
        dot = jnp.sum(dots, axis=-1, keepdims=True)
        dot_ref[0, rows, :] = dot + jnp.where(first_block, 0.0, dot_ref[0, rows, :])
        return carried_next, forget[0:1, :], gain_sum

    zero = jnp.zeros((1, width), F32)
    _, _, gain_sum = lax.fori_loop(
        0, tiles, step, (zero, zero, jnp.zeros((TILE_ROWS, width), F32))
    )
    gain_grad_ref[0] = jnp.sum(gain_sum, axis=0, keepdims=True)


def scan_backward(pre, states, grad_gated, inverse, mean, bound, gain):
    _, batches, length, width = pre.shape
    block = channel_block(width)
    whole = pl.BlockSpec((1, length, block), lambda b, c: (b, 0, c))
    column = pl.BlockSpec((1, length, 1), lambda b, c: (b, 0, 0))
    line = pl.BlockSpec((1, block), lambda b, c: (0, c))
    three = pl.BlockSpec((3, 1, length, block), lambda b, c: (0, b, 0, c))
    return pl.pallas_call(
        scan_backward_kernel,
        grid=(batches, width // block),
        in_specs=[three, whole, whole, column, column, line, line],
        out_specs=[
            three,
            whole,
            pl.BlockSpec((1, 1, block), lambda b, c: (b, 0, c)),
            column,
        ],
        out_shape=[
            jax.ShapeDtypeStruct((3, batches, length, width), BF),
            jax.ShapeDtypeStruct((batches, length, width), BF),
            jax.ShapeDtypeStruct((batches, 1, width), F32),
            jax.ShapeDtypeStruct((batches, length, 1), F32),
        ],
        compiler_params=pltpu.CompilerParams(vmem_limit_bytes=VMEM_LIMIT),
        cost_estimate=pl.CostEstimate(
            flops=batches * length * width * 80,
            bytes_accessed=batches * length * width * 28,
            transcendentals=batches * length * width * 3,
        ),
    )(pre, states, grad_gated, inverse, mean, bound[None], gain[None])


MESH_ID = pl.DeviceIdType.MESH
DEPTH = 4
LANES = 256
X_LAG = 4
Z_LAG = X_LAG + 2
SWAP_LAG = 2
TAIL = 2


def device_place():
    dp = lax.axis_index("dp")
    return dp // 4, lax.rem(dp // 2, 2), lax.rem(dp, 2)


def device_at(z, x, core):
    return (z * 4 + x * 2 + core, lax.axis_index("mp"))


def scatter_barrier(z, x, core, with_mp=False):
    barrier = pltpu.get_barrier_semaphore()
    targets = [device_at(z, x, 1 - core), device_at(z, 1 - x, core)]
    targets += [device_at(lax.rem(z + hop, DEPTH), x, core) for hop in range(1, DEPTH)]
    if with_mp:
        targets.append((lax.axis_index("dp"), 1 - lax.axis_index("mp")))
    for target in targets:
        pl.semaphore_signal(barrier, 1, device_id=target, device_id_type=MESH_ID)
    pl.semaphore_wait(barrier, len(targets))


def scatter_step(step, chunks, compute, finish, scratch, small_last=False):
    (own, core_out, core_in, keep, x_out, x_in, sums, mine, z_out, z_in,
     core_send, core_recv, x_send, x_recv, z_send, z_recv) = scratch
    z, x, core = device_place()

    def core_copy(p, cut=()):
        return pltpu.make_async_remote_copy(
            core_out.at[(lax.rem(p, 2), *cut)], core_in.at[(lax.rem(p, 4), *cut)],
            core_send.at[lax.rem(p, 2)], core_recv.at[lax.rem(p, 4)],
            device_id=device_at(z, x, 1 - core), device_id_type=MESH_ID)

    def x_copy(p, cut=()):
        return pltpu.make_async_remote_copy(
            x_out.at[(lax.rem(p, X_LAG), *cut)], x_in.at[(lax.rem(p, 2 * X_LAG), *cut)],
            x_send.at[lax.rem(p, X_LAG)], x_recv.at[lax.rem(p, 2 * X_LAG)],
            device_id=device_at(z, 1 - x, core), device_id_type=MESH_ID)

    def z_copy(p, hop, cut=()):
        return pltpu.make_async_remote_copy(
            z_out.at[(lax.rem(p, 4), hop - 1, *cut)], z_in.at[(lax.rem(p, 8), hop - 1, *cut)],
            z_send.at[lax.rem(p, 4), hop - 1], z_recv.at[lax.rem(p, 8), hop - 1],
            device_id=device_at(lax.rem(z + hop, DEPTH), x, core), device_id_type=MESH_ID)

    corner = (slice(0, 16), slice(0, 128))
    every = slice(None)

    def go(copy, lead, p, act):
        if not small_last:
            act(copy(p))
            return
        pl.when(p < chunks - 1)(lambda: act(copy(p)))
        pl.when(p == chunks - 1)(lambda: act(copy(p, (*(every,) * lead, *corner))))

    def core_go(p, act):
        go(core_copy, 2, p, act)

    def x_go(p, act):
        go(x_copy, 1, p, act)

    def z_go(p, hop, act):
        go(lambda p, cut=(): z_copy(p, hop, cut), 0, p, act)

    start, wait_recv, wait_send = (
        lambda copy: copy.start(), lambda copy: copy.wait_recv(), lambda copy: copy.wait_send())

    @pl.when(step < chunks)
    def _():
        @pl.when(step >= 2)
        def _():
            core_go(step - 2, wait_send)

        def to_partner(value):
            core_out[lax.rem(step, 2)] = value.astype(BF)

        def to_own(value):
            own[lax.rem(step, 2)] = value

        compute(step, 1 - core, to_partner)
        core_go(step, start)
        compute(step, core, to_own)

    @pl.when((step >= 1) & (step < chunks + 1))
    def _():
        p = step - 1
        core_go(p, wait_recv)

        @pl.when(p >= X_LAG)
        def _():
            x_go(p - X_LAG, wait_send)

        two, four, slot = lax.rem(p, 2), lax.rem(p, 4), lax.rem(p, X_LAG)
        x_out[slot] = (own[two, :, 1 - x] + core_in[four, :, 1 - x].astype(F32)).astype(BF)
        x_go(p, start)
        keep[slot] = own[two, :, x] + core_in[four, :, x].astype(F32)

    @pl.when((step >= X_LAG) & (step < chunks + X_LAG))
    def _():
        p = step - X_LAG
        x_go(p, wait_recv)
        four = lax.rem(p, 4)
        sums[...] = keep[lax.rem(p, X_LAG)] + x_in[lax.rem(p, 2 * X_LAG)].astype(F32)
        for hop in range(1, DEPTH):
            @pl.when(p >= 4)
            def _():
                z_go(p - 4, hop, wait_send)

            z_out[four, hop - 1] = sums[lax.rem(z + hop, DEPTH)].astype(BF)
            z_go(p, hop, start)
        mine[four] = sums[z]

    @pl.when((step >= Z_LAG) & (step < chunks + Z_LAG))
    def _():
        p = step - Z_LAG
        for hop in range(1, DEPTH):
            z_go(p, hop, wait_recv)
        got = z_in.at[lax.rem(p, 8)]
        finish(p, mine[lax.rem(p, 4)] + got[0].astype(F32) + got[1].astype(F32) + got[2].astype(F32))

    @pl.when(step == chunks + Z_LAG - 1)
    def _():
        for p in range(chunks - 2, chunks):
            core_go(jnp.int32(p), wait_send)
        for p in range(chunks - X_LAG, chunks):
            x_go(jnp.int32(p), wait_send)
        for p in range(chunks - 4, chunks):
            for hop in range(1, DEPTH):
                z_go(jnp.int32(p), hop, wait_send)


def scatter_scratch(rows, lanes):
    quad = (DEPTH, 2, rows, lanes)
    line = (DEPTH, rows, lanes)
    dma = pltpu.SemaphoreType.DMA
    return [
        pltpu.VMEM((2, *quad), F32),
        pltpu.VMEM((2, *quad), BF),
        pltpu.VMEM((4, *quad), BF),
        pltpu.VMEM((X_LAG, *line), F32),
        pltpu.VMEM((X_LAG, *line), BF),
        pltpu.VMEM((2 * X_LAG, *line), BF),
        pltpu.VMEM(line, F32),
        pltpu.VMEM((4, rows, lanes), F32),
        pltpu.VMEM((4, DEPTH - 1, rows, lanes), BF),
        pltpu.VMEM((8, DEPTH - 1, rows, lanes), BF),
        dma((2,)), dma((4,)), dma((X_LAG,)), dma((2 * X_LAG,)), dma((4, DEPTH - 1)), dma((8, DEPTH - 1)),
    ]


def scatter_out(chunks, rows, lanes):
    spec = pl.BlockSpec((1, rows, lanes), lambda q: (jnp.maximum(q - Z_LAG, 0), 0, 0))
    return spec, jax.ShapeDtypeStruct((chunks, rows, lanes), F32)


def fixed(shape):
    return pl.BlockSpec(shape, lambda q: (0,) * len(shape), pipeline_mode=pl.Buffered(1))


def glu_kernel(
    hidden_blocks, full_blocks, normed_ref, back_ref, left_ref, left_back_ref, glu_ref,
    out_ref, sum_own, sum_came, half_own, half_send, tail_ref,
    tail_stage, tail_sem, left, left_back, left_sem, acts, weights_in, weights_back, sum_stage, half_stage,
    in_sem, back_sem, stage_sem, sum_send, sum_recv, *scratch,
):
    z, x, core = device_place()
    dp, mp = lax.axis_index("dp"), lax.axis_index("mp")
    step = pl.program_id(0)
    scattered = hidden_blocks - TAIL
    chunks = 3 * scattered
    rows = normed_ref.shape[0]
    row_block = rows // 2
    half_blocks = full_blocks // 2
    across = (((1,), (1,)), ((), ()))
    spread = min(hidden_blocks + hidden_blocks // 2, 16)
    second = step - spread

    def first_tasks(at):
        return at * hidden_blocks // spread

    def second_task(at):
        return 2 * at // 3

    def has_second(at):
        return (at == 0) | (
            (at > 0) & (second_task(at) > second_task(at - 1)) & (second_task(at) < full_blocks))

    unit_block = first_tasks(step)

    def lane_block(index):
        return pl.ds(pl.multiple_of(index * LANES, LANES), LANES)

    def load_in(index):
        return pltpu.make_async_copy(glu_ref.at[:, :, lane_block(index)], weights_in, in_sem)

    def load_back(index):
        return pltpu.make_async_copy(glu_ref.at[:, lane_block(index), :], weights_back, back_sem)

    def stage(index, kind, target):
        source = (sum_stage, half_stage)[kind].at[lax.rem(index, 2)]
        return pltpu.make_async_copy(source, target, stage_sem.at[lax.rem(index, 2), kind])

    def half_spot(index):
        return lax.rem(index, half_blocks)

    def sum_copy(index):
        return pltpu.make_async_remote_copy(
            sum_own.at[:, lane_block(index)], sum_came.at[:, lane_block(index)],
            sum_send.at[index], sum_recv.at[index], device_id=(dp, 1 - mp), device_id_type=MESH_ID)

    left_loads = (
        pltpu.make_async_copy(left_ref, left, left_sem.at[0]),
        pltpu.make_async_copy(left_back_ref, left_back, left_sem.at[1]),
    )

    @pl.when(step == 0)
    def _():
        for one in (load_in(0), *left_loads, load_back(0)):
            one.start()
        scatter_barrier(z, x, core, with_mp=True)

    @pl.when((step < spread) & ((step == 0) | (unit_block > first_tasks(step - 1))))
    def _():
        load_in(unit_block).wait()
        lanes = lane_block(unit_block)

        def part(index, _):
            part_rows = pl.ds(pl.multiple_of(index * row_block, row_block), row_block)
            normed = normed_ref[part_rows, :]
            pre_act = jnp.dot(normed, weights_in[0], preferred_element_type=F32)
            pre_up = jnp.dot(normed, weights_in[1], preferred_element_type=F32)
            grad_hidden = jnp.dot(back_ref[part_rows, :], weights_in[2], preferred_element_type=F32)
            sigma = jax.nn.sigmoid(pre_act)
            act_part = pre_act * sigma
            acts[0, part_rows, lanes] = (
                grad_hidden * pre_up * (sigma * (1.0 + pre_act * (1.0 - sigma)))).astype(BF)
            acts[1, part_rows, lanes] = (grad_hidden * act_part).astype(BF)
            acts[2, part_rows, lanes] = (act_part * pre_up).astype(BF)
            return 0

        lax.fori_loop(0, rows // row_block, part, 0)

        @pl.when(unit_block + 1 < hidden_blocks)
        def _():
            load_in(unit_block + 1).start()

    @pl.when(has_second(second - 1))
    def _():
        index = second_task(second - 1)
        stage(index, 0, sum_own.at[:, lane_block(index)]).wait()
        sum_copy(index).start()
        spot = half_spot(index)
        stage(index, 1, half_own.at[:, lane_block(spot)]).wait()

    @pl.when(has_second(second))
    def _():
        index = second_task(second)
        load_back(index).wait()
        slot = lax.rem(index, 2)

        def part(at, _):
            part_rows = pl.ds(pl.multiple_of(at * row_block, row_block), row_block)
            dot = functools.partial(
                lax.dot_general, dimension_numbers=across, preferred_element_type=F32)
            grad_normed = dot(acts[0, part_rows, :], weights_back[0])
            grad_normed += dot(acts[1, part_rows, :], weights_back[1])
            sum_stage[slot, part_rows, :] = grad_normed.astype(BF)
            half_stage[slot, part_rows, :] = dot(acts[2, part_rows, :], weights_back[2]).astype(BF)
            return 0

        lax.fori_loop(0, rows // row_block, part, 0)

        @pl.when(index + 1 < full_blocks)
        def _():
            load_back(index + 1).start()

        stage(index, 0, sum_own.at[:, lane_block(index)]).start()
        spot = half_spot(index)

        @pl.when(index // half_blocks == mp)
        def _():
            stage(index, 1, half_own.at[:, lane_block(spot)]).start()

        @pl.when(index // half_blocks != mp)
        def _():
            stage(index, 1, half_send.at[:, lane_block(spot)]).start()

    def compute(q, core_side, store):
        kind = lax.rem(q, 3)
        side_rows = left.shape[3]

        def product(side_ref):
            side = side_ref[:, :, core_side].reshape(DEPTH * 2 * side_rows, rows)
            right = acts[kind, :, lane_block(q // 3)]
            store(jnp.dot(side, right, preferred_element_type=F32).reshape(
                DEPTH, 2, side_rows, LANES))

        pl.when(kind < 2)(lambda: product(left))
        pl.when(kind == 2)(lambda: product(left_back))

    @pl.when(step == 0)
    def _():
        for one in left_loads:
            one.wait()

    def finish(p, value):
        out_ref[0] = value

    scatter_step(step, chunks, compute, finish, scratch)

    def tail_copy(index):
        spot = tail_ref.at[lax.rem(index, 3), :, :, :, :, lane_block(index // 3)]
        return pltpu.make_async_copy(
            tail_stage.at[lax.rem(index, 2)], spot, tail_sem.at[lax.rem(index, 2)])

    @pl.when((step >= chunks) & (step < chunks + 3 * TAIL))
    def _():
        index = step - chunks

        @pl.when(index >= 2)
        def _():
            tail_copy(index - 2).wait()

        for side in (0, 1):
            def to_stage(value):
                tail_stage[lax.rem(index, 2), :, :, side] = value.astype(BF)

            compute(step, side, to_stage)
        tail_copy(index).start()

    @pl.when(step == chunks + Z_LAG - 1)
    def _():
        for index in range(3 * TAIL - 2, 3 * TAIL):
            tail_copy(jnp.int32(index)).wait()
        for index in range(full_blocks):
            sum_copy(index).wait()


def glu_call(normed, back_low, left_back, glu, collective):
    rows, full = normed.shape
    hidden = glu.shape[2]
    hidden_blocks, full_blocks = hidden // LANES, full // LANES
    block = full // 16
    chunks = 3 * (hidden_blocks - TAIL)
    left_shape = (DEPTH, 2, 2, block, rows)
    any_space = pl.BlockSpec(memory_space=pl.ANY)
    out_spec, out_shape = scatter_out(chunks, block, LANES)
    dma = pltpu.SemaphoreType.DMA
    wide = jax.ShapeDtypeStruct((rows, full), BF)
    half = jax.ShapeDtypeStruct((rows, full // 2), BF)
    out, sum_own, sum_came, half_own, half_send, tail = pl.pallas_call(
        functools.partial(glu_kernel, hidden_blocks, full_blocks),
        grid=(chunks + Z_LAG,),
        in_specs=[fixed(normed.shape), fixed(back_low.shape)] + [any_space] * 3,
        out_specs=[out_spec] + [any_space] * 5,
        out_shape=[
            out_shape, wide, wide, half, half,
            jax.ShapeDtypeStruct((3, DEPTH, 2, 2, block, TAIL * LANES), BF),
        ],
        scratch_shapes=[
            pltpu.VMEM((2, DEPTH, 2, 2, block, LANES), BF),
            dma((2,)),
            pltpu.VMEM(left_shape, BF),
            pltpu.VMEM(left_shape, BF),
            dma((2,)),
            pltpu.VMEM((3, rows, hidden), BF),
            pltpu.VMEM((3, full, LANES), BF),
            pltpu.VMEM((3, LANES, hidden), BF),
            pltpu.VMEM((2, rows, LANES), BF),
            pltpu.VMEM((2, rows, LANES), BF),
            dma(()), dma(()), dma((2, 2)),
            dma((full_blocks,)), dma((full_blocks,)),
            *scatter_scratch(block, LANES),
        ],
        compiler_params=pltpu.CompilerParams(
            collective_id=collective, has_side_effects=True, vmem_limit_bytes=62 * 1024 * 1024),
        cost_estimate=pl.CostEstimate(
            flops=18 * rows * full * hidden, bytes_accessed=6 * full * hidden * 2,
            transcendentals=rows * hidden),
    )(normed, back_low, normed.T.reshape(left_shape), left_back.reshape(left_shape), glu)
    return out, tail.reshape(3, full, TAIL * LANES), sum_own, sum_came, half_own, half_send


def mixer_kernel(
    full_blocks, left_hbm, grad_hbm, left_out_ref, right_out_ref, gain_ref, tokens_ref, inverse_ref,
    weights_ref, dot_ref, out_ref, gain_out, half_own, half_send, half_came, dot_came,
    left_ref, grad_ref, big_sem, weights, token_block, gain_sum, gain_chunk, total, swap_out, swap_in, half_stage,
    load_sem, stage_sem, half_send_sem, half_recv, swap_send, swap_recv, dot_sem, *scratch,
):
    z, x, core = device_place()
    dp, mp = lax.axis_index("dp"), lax.axis_index("mp")
    step = pl.program_id(0)
    tokens, channels = grad_ref.shape[1], grad_ref.shape[2]
    block, half = left_ref.shape[3], left_out_ref.shape[3]
    outer = full_blocks // 2
    across = channels // LANES
    gains = outer + 3 * across
    chunks = gains + 1
    half_blocks = full_blocks // 2
    row_block = tokens // 2
    partner = (dp, 1 - mp)

    def lane_block(index):
        return pl.ds(pl.multiple_of(index * LANES, LANES), LANES)

    def loads(index):
        return (
            pltpu.make_async_copy(weights_ref.at[:, lane_block(index), :], weights, load_sem.at[0]),
            pltpu.make_async_copy(tokens_ref.at[:, lane_block(index)], token_block, load_sem.at[1]),
        )

    def stage(index, target):
        return pltpu.make_async_copy(
            half_stage.at[lax.rem(index, 2)], target, stage_sem.at[lax.rem(index, 2)])

    def half_copy(spot):
        return pltpu.make_async_remote_copy(
            half_send.at[:, lane_block(spot)], half_came.at[:, lane_block(spot)],
            half_send_sem.at[spot], half_recv.at[spot], device_id=partner, device_id_type=MESH_ID)

    def swap_copy(index):
        return pltpu.make_async_remote_copy(
            swap_out.at[lax.rem(index, 2)], swap_in.at[lax.rem(index, 8)],
            swap_send.at[lax.rem(index, 2)], swap_recv.at[lax.rem(index, 8)],
            device_id=partner, device_id_type=MESH_ID)

    big_loads = (
        pltpu.make_async_copy(grad_hbm, grad_ref, big_sem.at[0]),
        pltpu.make_async_copy(left_hbm, left_ref, big_sem.at[1]),
    )
    dot_copy = pltpu.make_async_remote_copy(
        dot_ref, dot_came, dot_sem.at[0], dot_sem.at[1], device_id=partner, device_id_type=MESH_ID)

    @pl.when(step == 0)
    def _():
        for one in (*big_loads, *loads(0)):
            one.start()
        gain_chunk[...] = jnp.zeros_like(gain_chunk)
        gain_sum[...] = jnp.zeros_like(gain_sum)
        scatter_barrier(z, x, core, with_mp=True)
        dot_copy.start()

    @pl.when(step == 1)
    def _():
        for one in big_loads:
            one.wait()

    task = (step - 1) // 2

    @pl.when((step >= 2) & (step <= 2 * full_blocks) & (lax.rem(step, 2) == 0))
    def _():
        index = task
        spot = lax.rem(index, half_blocks)
        stage(index, half_own.at[:, lane_block(spot)]).wait()

        @pl.when(index // half_blocks != mp)
        def _():
            half_copy(spot).start()

    @pl.when((step < 2 * full_blocks) & (lax.rem(step, 2) == 1))
    def _():
        for one in loads(task):
            one.wait()
        slot = lax.rem(task, 2)
        spot = lax.rem(task, half_blocks)

        def part(at, gain_in):
            part_rows = pl.ds(pl.multiple_of(at * row_block, row_block), row_block)
            dot = functools.partial(
                lax.dot_general, dimension_numbers=(((1,), (1,)), ((), ())), preferred_element_type=F32)
            grad = dot(grad_ref[0, part_rows, :], weights[0])
            grad += dot(grad_ref[1, part_rows, :], weights[1])
            grad += dot(grad_ref[2, part_rows, :], weights[2])
            half_stage[slot, part_rows, :] = grad.astype(BF)
            unit = token_block[part_rows, :].astype(F32) * inverse_ref[part_rows, :]
            return gain_in + jnp.sum(grad * unit, axis=0, keepdims=True)

        gain_in = lax.fori_loop(0, tokens // row_block, part, jnp.zeros((1, LANES), F32))
        gain_sum[2 * task, 0:1, :] = gain_in[:, :128]
        gain_sum[2 * task + 1, 0:1, :] = gain_in[:, 128:]

        @pl.when(task + 1 < full_blocks)
        def _():
            for one in loads(task + 1):
                one.start()

        @pl.when(task // half_blocks == mp)
        def _():
            stage(task, half_own.at[:, lane_block(spot)]).start()

        @pl.when(task // half_blocks != mp)
        def _():
            stage(task, half_send.at[:, lane_block(spot)]).start()

    def compute(q, core_side, store):
        @pl.when(q < outer)
        def _():
            side = left_out_ref[:, :, core_side].reshape(channels // 2, tokens)
            parts = [
                jnp.dot(side, right_out_ref[:, lane_block(2 * q + at)], preferred_element_type=F32)
                for at in (0, 1)
            ]
            parts = [part.reshape(DEPTH, 2, half, LANES) for part in parts]
            store(jnp.concatenate(parts, axis=2))

        @pl.when((q >= outer) & (q < gains))
        def _():
            at = q - outer
            side = left_ref[:, :, core_side].reshape(DEPTH * 2 * block, tokens)
            right = grad_ref[at // across, :, lane_block(lax.rem(at, across))]
            store(jnp.dot(side, right, preferred_element_type=F32).reshape(DEPTH, 2, block, LANES))

        @pl.when(q == gains)
        def _():
            for owner in range(2 * DEPTH):
                line = 2 * owner + core_side
                gain_chunk[owner // 2, owner % 2, 0:8, 0:128] = gain_ref[line] + gain_sum[line]
            store(gain_chunk[...])

    def finish(p, value):
        total[lax.rem(p, 4)] = value

        @pl.when(p >= outer)
        def _():
            index = p - outer

            @pl.when(index >= 2)
            def _():
                swap_copy(index - 2).wait_send()

            first = jnp.where(p == gains, 0, 1 - mp) * half
            rows = pl.ds(pl.multiple_of(first, half), half)
            swap_out[lax.rem(index, 2)] = total[lax.rem(p, 4), rows, :].astype(BF)
            swap_copy(index).start()

    scatter_step(step, chunks, compute, finish, scratch, small_last=True)

    @pl.when((step >= Z_LAG + SWAP_LAG) & (step < chunks + Z_LAG + SWAP_LAG))
    def _():
        p = step - Z_LAG - SWAP_LAG
        slot = lax.rem(p, 4)

        @pl.when(p < outer)
        def _():
            out_ref[0, :, :LANES] = total[slot, :half, :]
            out_ref[0, :, LANES:] = total[slot, half:, :]

        @pl.when(p >= outer)
        def _():
            swap_copy(p - outer).wait_recv()
            came = swap_in[lax.rem(p - outer, 8)].astype(F32)

            @pl.when(p < gains)
            def _():
                own = total[slot, pl.ds(pl.multiple_of(mp * half, half), half), :]
                first = jnp.where(mp == 0, own, came)
                second = jnp.where(mp == 0, came, own)
                for tile in (0, 1):
                    lanes = slice(128 * tile, 128 * tile + 128)
                    left, right = split_lanes(first[:, lanes], second[:, lanes])
                    out_ref[0, :, 256 * tile : 256 * tile + 128] = left
                    out_ref[0, :, 256 * tile + 128 : 256 * tile + 256] = right

            @pl.when(p == gains)
            def _():
                gain_out[...] = total[slot, 0:8, 0:128] + came[0:8, 0:128]

    @pl.when(step == chunks + Z_LAG + SWAP_LAG - 1)
    def _():
        for spot in range(half_blocks):
            half_copy(spot).wait()
        for index in range(gains - outer - 1, gains - outer + 1):
            swap_copy(index).wait_send()
        dot_copy.wait()


def mixer_call(
    left_in, grad_pre, left_out, right_out, gain_parts, tokens, inverse, weights, dots, collective
):
    _, rows, channels = grad_pre.shape
    full = left_in.shape[0]
    block, half = full // 16, channels // 16
    full_blocks, across = full // LANES, channels // LANES
    outer, inner = full_blocks // 2, 3 * across
    chunks = outer + inner + 1
    any_space = pl.BlockSpec(memory_space=pl.ANY)
    dma = pltpu.SemaphoreType.DMA
    part = jax.ShapeDtypeStruct((rows, full // 2), BF)

    def out_place(q):
        p = jnp.clip(q - Z_LAG - SWAP_LAG, 0, outer + inner - 1)
        inside = jnp.maximum(p - outer, 0)
        return (
            jnp.where(p < outer, 3, inside // across), 0, jnp.where(p < outer, p, lax.rem(inside, across)))

    out, gains, half_own, _, half_came, dot_came = pl.pallas_call(
        functools.partial(mixer_kernel, full_blocks),
        grid=(chunks + Z_LAG + SWAP_LAG,),
        in_specs=[
            any_space, any_space,
            fixed((DEPTH, 2, 2, half, rows)), fixed(right_out.shape), fixed(gain_parts.shape),
            any_space, fixed(inverse.shape), any_space, any_space,
        ],
        out_specs=[
            pl.BlockSpec((1, half, 2 * LANES), out_place),
            pl.BlockSpec((8, 128), lambda q: (0, 0)),
        ] + [any_space] * 4,
        out_shape=[
            jax.ShapeDtypeStruct((4, half, full), F32), jax.ShapeDtypeStruct((8, 128), F32),
            part, part, part, jax.ShapeDtypeStruct(dots.shape, F32),
        ],
        scratch_shapes=[
            pltpu.VMEM((DEPTH, 2, 2, block, rows), BF),
            pltpu.VMEM(grad_pre.shape, BF),
            dma((2,)),
            pltpu.VMEM((3, LANES, channels), BF),
            pltpu.VMEM((rows, LANES), BF),
            pltpu.VMEM((16, 8, 128), F32),
            pltpu.VMEM((DEPTH, 2, block, LANES), F32),
            pltpu.VMEM((4, block, LANES), F32),
            pltpu.VMEM((2, half, LANES), BF),
            pltpu.VMEM((8, half, LANES), BF),
            pltpu.VMEM((2, rows, LANES), BF),
            dma((2,)), dma((2,)), dma((full_blocks // 2,)), dma((full_blocks // 2,)),
            dma((2,)), dma((8,)), dma((2,)),
            *scatter_scratch(block, LANES),
        ],
        compiler_params=pltpu.CompilerParams(
            collective_id=collective, has_side_effects=True, vmem_limit_bytes=VMEM_LIMIT),
        cost_estimate=pl.CostEstimate(
            flops=14 * full * rows * channels, bytes_accessed=16 * full * channels, transcendentals=0),
    )(
        left_in.reshape(DEPTH, 2, 2, block, rows), grad_pre,
        left_out.reshape(DEPTH, 2, 2, half, rows), right_out, gain_parts, tokens, inverse, weights, dots,
    )
    return out, gains, half_own.astype(F32) + half_came.astype(F32), dot_came


def middle_back_kernel(
    sum_own_ref, sum_came_ref, middle_ref, cot_ref, tokens_ref, weight_ref, gain_ref, mixer_ref,
    grad_own_ref, low_ref, mean_ref, gated_ref, gain_grad_ref,
):
    rows, full = middle_ref.shape
    part = full // 2
    middle = middle_ref[...]
    inverse = lax.rsqrt(jnp.mean(middle * middle, axis=-1, keepdims=True) + EPSILON)
    unit = middle * inverse
    grad_normed = sum_own_ref[...].astype(F32) + sum_came_ref[...].astype(F32)
    product = grad_normed * unit
    before = jnp.where(pl.program_id(0) == 0, 0.0, gain_grad_ref[...])
    gain_grad_ref[...] = before + jnp.sum(product, axis=0, keepdims=True)
    dots = jnp.mean(product * gain_ref[...], axis=-1, keepdims=True)
    back = cot_ref[...].astype(F32) * weight_ref[...]
    grad = back + inverse * (grad_normed * gain_ref[...] - unit * dots)
    first = lax.axis_index("mp") == 0
    grad_own_ref[...] = jnp.where(first, grad[:, :part], grad[:, part:])
    low = grad.astype(BF)
    low_ref[...] = low
    branch = middle - tokens_ref[...].astype(F32)
    mean_ref[...] = jnp.mean(low.astype(F32) * branch, axis=-1, keepdims=True)
    gated_ref[...] = lax.dot_general(
        low, mixer_ref[...], (((1,), (1,)), ((), ())), preferred_element_type=F32)


def middle_back(sum_own, sum_came, middle, cot, tokens, weight, gain, mixer_out):
    rows, full = middle.shape
    channels = mixer_out.shape[0]
    step = 224 if rows % 224 == 0 else rows
    line = lambda width: pl.BlockSpec((step, width), lambda r: (r, 0))
    shape = jax.ShapeDtypeStruct
    return pl.pallas_call(
        middle_back_kernel,
        grid=(rows // step,),
        in_specs=[line(full)] * 5 + [line(1), fixed((1, full)), fixed(mixer_out.shape)],
        out_specs=[
            line(full // 2), line(full), line(1), line(channels),
            pl.BlockSpec((1, full), lambda r: (0, 0)),
        ],
        out_shape=[
            shape((rows, full // 2), F32), shape((rows, full), BF), shape((rows, 1), F32),
            shape((rows, channels), F32), shape((1, full), F32),
        ],
        compiler_params=pltpu.CompilerParams(vmem_limit_bytes=VMEM_LIMIT),
        cost_estimate=pl.CostEstimate(
            flops=2 * rows * full * channels, bytes_accessed=rows * full * 20, transcendentals=0),
    )(sum_own, sum_came, middle, cot, tokens, weight, gain[None], mixer_out)


def glu_update_kernel(scale, act_ref, up_ref, out_ref, *refs):
    in_refs, down_refs, in_new, down_new = refs[:3], refs[3:6], refs[-6:-3], refs[-3:]
    count = STEP_NUMBER
    for at, grad_ref in ((0, act_ref), (1, up_ref)):
        new = adamw_update(
            *(ref[at] for ref in in_refs), grad_ref[0].astype(F32) * scale, count, MATRIX_RATE, DECAY_RATE)
        for ref, value in zip(in_new, new):
            ref[at] = value
    new = adamw_update(
        *(ref[...] for ref in down_refs), out_ref[0].astype(F32).T * scale, count, MATRIX_RATE, DECAY_RATE)
    for ref, value in zip(down_new, new):
        ref[...] = value


def glu_update(sums, sum_place, first, blocks, ins, downs, scale, earlier=()):
    rows, lanes = ins[0].shape[1], LANES
    sum_spec = lambda kind: pl.BlockSpec((1, rows, lanes), lambda q: sum_place(kind, q))
    in_spec = pl.BlockSpec((2, rows, lanes), lambda q: (0, 0, q + first))
    down_spec = pl.BlockSpec((lanes, rows), lambda q: (q + first, 0))
    new = pl.pallas_call(
        functools.partial(glu_update_kernel, scale),
        grid=(blocks,),
        in_specs=[sum_spec(0), sum_spec(1), sum_spec(2)] + [in_spec] * 3 + [down_spec] * 3
        + [pl.BlockSpec(memory_space=pl.ANY)] * len(earlier),
        out_specs=[in_spec] * 3 + [down_spec] * 3,
        out_shape=[jax.ShapeDtypeStruct(ins[0].shape, F32)] * 3 + [jax.ShapeDtypeStruct(downs[0].shape, F32)] * 3,
        input_output_aliases={9 + at: at for at in range(len(earlier))},
        compiler_params=pltpu.CompilerParams(vmem_limit_bytes=VMEM_LIMIT),
        cost_estimate=pl.CostEstimate(
            flops=60 * rows * lanes * blocks, bytes_accessed=84 * rows * lanes * blocks,
            transcendentals=6 * rows * lanes * blocks),
    )(sums, sums, sums, *ins, *downs, *earlier)
    return tuple(new)


ITEMS = 4


def split_lanes(first, second):
    low = lax.broadcasted_iota(jnp.int32, first.shape, 1) < 64
    return (
        jnp.where(low, first, pltpu.roll(second, 64, 1)),
        jnp.where(low, pltpu.roll(first, 64, 1), second),
    )


def gather_kernel(mixer_ref, gain_ref, lengths_ref, domains_ref, glu_in_ref, glu_out_ref, cot_ref,
                  all_in, all_out, all_small, cot_full, glu_low,
                  in_ref, out_ref, small_ref, right_send, left_send,
                  z_recv, x_send, x_recv, core_send, core_recv, y_send, y_recv, local_sem):
    z, x, core = device_place()
    mp = lax.axis_index("mp")
    barrier = pltpu.get_barrier_semaphore()
    for kind in range(3):
        for tile in range(in_ref.shape[3] // 128):
            first = mixer_ref[kind, :, 256 * tile : 256 * tile + 128]
            second = mixer_ref[kind, :, 256 * tile + 128 : 256 * tile + 256]
            for side, value in enumerate(split_lanes(first, second)):
                in_ref[side, kind, :, 128 * tile : 128 * tile + 128] = value.astype(BF)
    out_ref[...] = mixer_ref[3].astype(BF)
    lane = lax.broadcasted_iota(jnp.int32, (1, 128), 1)
    live = jnp.zeros((1, 128), F32)
    for batch in range(lengths_ref.shape[0]):
        count = lengths_ref[batch : batch + 1, :].astype(F32)
        live = live + jnp.where(lane == domains_ref[batch : batch + 1, :], count, 0.0)
    small_ref[...] = jnp.zeros_like(small_ref)
    small_ref[0:3, 0:64] = gain_ref[...].astype(BF).astype(F32)
    small_ref[3:4, :] = live
    right, left = lax.rem(z + 1, DEPTH), lax.rem(z + DEPTH - 1, DEPTH)
    dp = lax.axis_index("dp")
    for target in (
        device_at(right, x, core), device_at(left, x, core), device_at(z, 1 - x, core),
        device_at(z, x, 1 - core), (dp, 1 - mp),
    ):
        pl.semaphore_signal(barrier, 1, device_id=target, device_id_type=MESH_ID)
    pl.semaphore_wait(barrier, 5)

    def spot(item, zs, xs, cs, side=None):
        if item == 0:
            return all_in.at[:, zs, xs, cs, mp if side is None else side]
        if item == 1:
            return all_out.at[zs, xs, cs]
        if item == 2:
            return all_in.at[:, zs, xs, cs, 1 - mp]
        return all_small.at[zs, xs, cs]

    def own(item):
        if item == 0:
            return in_ref.at[mp]
        if item == 1:
            return out_ref
        return spot(item, z, x, core)

    def copy(item, zs, xs, target, send, recv, source=None):
        return pltpu.make_async_remote_copy(
            spot(item, zs, xs, core) if source is None else source, spot(item, zs, xs, core),
            send, recv, device_id=target, device_id_type=MESH_ID)

    def right_copy(item, zs, source=None):
        return copy(item, zs, x, device_at(right, x, core), right_send.at[zs, item], z_recv.at[zs, item], source)

    def left_copy(item, zs, source=None):
        return copy(item, zs, x, device_at(left, x, core), left_send.at[zs, item], z_recv.at[zs, item], source)

    def x_copy(item, zs, source=None):
        return copy(item, zs, x, device_at(z, 1 - x, core), x_send.at[zs, item], x_recv.at[zs, item], source)

    def core_copy(item, zs, xs, source=None):
        return copy(item, zs, xs, device_at(z, x, 1 - core), core_send.at[zs, xs, item], core_recv.at[zs, xs, item], source)

    y_copies = [
        pltpu.make_async_remote_copy(
            in_ref.at[1 - mp], all_in.at[:, z, x, core, mp], y_send.at[0], y_recv.at[0],
            device_id=(dp, 1 - mp), device_id_type=MESH_ID),
        pltpu.make_async_remote_copy(
            small_ref, all_small.at[z, x, core, mp], y_send.at[1], y_recv.at[1],
            device_id=(dp, 1 - mp), device_id_type=MESH_ID),
    ]
    locals_ = [
        pltpu.make_async_copy(in_ref.at[mp], spot(0, z, x, core), local_sem.at[0]),
        pltpu.make_async_copy(out_ref, spot(1, z, x, core), local_sem.at[1]),
        pltpu.make_async_copy(small_ref, all_small.at[z, x, core, mp], local_sem.at[2]),
    ]
    cot_lanes = pl.ds(pl.multiple_of(mp * cot_ref.shape[1], 128), cot_ref.shape[1])
    cot_local = pltpu.make_async_copy(cot_ref, cot_full.at[:, cot_lanes], local_sem.at[3])
    cot_copy = pltpu.make_async_remote_copy(
        cot_ref, cot_full.at[:, cot_lanes], y_send.at[2], y_recv.at[2],
        device_id=(dp, 1 - mp), device_id_type=MESH_ID)
    for one in y_copies:
        one.start()
    locals_[2].start()

    for item in range(ITEMS):
        if item == 2:
            y_copies[0].wait_recv()
        if item == 3:
            y_copies[1].wait_recv()
            locals_[2].wait()
        source = own(item)

        @pl.when(z < DEPTH - 1)
        def _():
            right_copy(item, z, source).start()

        @pl.when(z > 0)
        def _():
            left_copy(item, z, source).start()

        x_copy(item, z, source).start()
        core_copy(item, z, x, source).start()
    locals_[0].start()
    locals_[1].start()
    cot_copy.start()
    cot_local.start()
    glu_low[0:2] = glu_in_ref[...].astype(BF)
    for tile in range(glu_out_ref.shape[0] // 128):
        lanes = slice(128 * tile, 128 * tile + 128)
        glu_low[2, :, lanes] = glu_out_ref[lanes, :].T.astype(BF)

    def from_x(item, zs):
        pltpu.make_async_remote_copy(
            spot(item, zs, 1 - x, core), spot(item, zs, 1 - x, core), x_send.at[zs, item],
            x_recv.at[zs, item], device_id=device_at(z, 1 - x, core), device_id_type=MESH_ID).wait_recv()
        core_copy(item, zs, 1 - x).start()

    for hop in range(1, DEPTH + 1):
        for item in range(ITEMS):
            if hop < DEPTH:
                @pl.when(z >= hop)
                def _():
                    zs = z - hop
                    right_copy(item, zs).wait_recv()

                    @pl.when(z < DEPTH - 1)
                    def _():
                        right_copy(item, zs).start()

                    x_copy(item, zs).start()
                    core_copy(item, zs, x).start()

                @pl.when(z + hop < DEPTH)
                def _():
                    zs = z + hop
                    left_copy(item, zs).wait_recv()

                    @pl.when(z > 0)
                    def _():
                        left_copy(item, zs).start()

                    x_copy(item, zs).start()
                    core_copy(item, zs, x).start()
            if hop == 1:
                from_x(item, z)
            else:
                @pl.when(z >= hop - 1)
                def _():
                    from_x(item, z - (hop - 1))

                @pl.when(z + hop - 1 < DEPTH)
                def _():
                    from_x(item, z + (hop - 1))

    for item in range(ITEMS):
        for zs in range(DEPTH):
            @pl.when((z >= zs) & (z < DEPTH - 1))
            def _():
                right_copy(item, zs).wait_send()

            @pl.when((z <= zs) & (z > 0))
            def _():
                left_copy(item, zs).wait_send()

            x_copy(item, zs).wait_send()
            for xs in range(2):
                core_copy(item, zs, xs).wait()
    for one in y_copies:
        one.wait_send()
    locals_[0].wait()
    locals_[1].wait()
    cot_local.wait()
    cot_copy.wait_send()
    pltpu.make_async_remote_copy(
        cot_ref, cot_full.at[:, pl.ds(pl.multiple_of((1 - mp) * cot_ref.shape[1], 128), cot_ref.shape[1])],
        y_send.at[2], y_recv.at[2], device_id=(dp, 1 - mp), device_id_type=MESH_ID).wait_recv()


def gather_call(mixer, gain, lengths, domains, glu_in, glu_out, cot, collective):
    _, own_rows, full = mixer.shape
    channels = full // 2
    dma = pltpu.SemaphoreType.DMA
    any_space = pl.BlockSpec(memory_space=pl.ANY)
    in_vmem = pl.BlockSpec(memory_space=pltpu.VMEM)
    _, glu_rows, hidden = glu_in.shape
    return pl.pallas_call(
        gather_kernel,
        in_specs=[in_vmem] * 6 + [any_space],
        out_specs=[any_space] * 4 + [in_vmem],
        out_shape=[
            jax.ShapeDtypeStruct((3, DEPTH, 2, 2, 2, own_rows, channels), BF),
            jax.ShapeDtypeStruct((DEPTH, 2, 2, own_rows, full), BF),
            jax.ShapeDtypeStruct((DEPTH, 2, 2, 2, 8, 128), F32),
            jax.ShapeDtypeStruct((cot.shape[0], 2 * cot.shape[1]), BF),
            jax.ShapeDtypeStruct((3, glu_rows, hidden), BF),
        ],
        scratch_shapes=[
            pltpu.VMEM((2, 3, own_rows, channels), BF),
            pltpu.VMEM((own_rows, full), BF),
            pltpu.VMEM((8, 128), F32),
            dma((DEPTH, ITEMS)), dma((DEPTH, ITEMS)), dma((DEPTH, ITEMS)), dma((DEPTH, ITEMS)),
            dma((DEPTH, ITEMS)), dma((DEPTH, 2, ITEMS)), dma((DEPTH, 2, ITEMS)), dma((3,)), dma((3,)), dma((4,)),
        ],
        compiler_params=pltpu.CompilerParams(
            collective_id=collective, has_side_effects=True, vmem_limit_bytes=VMEM_LIMIT),
        cost_estimate=pl.CostEstimate(flops=0, bytes_accessed=300_000_000, transcendentals=0),
    )(mixer, gain, lengths, domains, glu_in, glu_out, cot)


def shards(
    tokens,
    cotangent,
    lengths,
    domains,
    lower_bound,
    mixer_master,
    mixer_first,
    mixer_second,
    glu_in_master,
    glu_in_first,
    glu_in_second,
    glu_out_master,
    glu_out_first,
    glu_out_second,
    gain_master,
    gain_first,
    gain_second,
):
    batches, _, length, full = tokens.shape
    rows = batches * length
    groups = lax.axis_size("dp")
    narrow = lax.axis_size("mp")
    place = lax.axis_index("mp")
    own_rows = mixer_master.shape[1]
    channels = groups * own_rows
    part = full // narrow
    quick = groups == 16 and narrow == 2 and own_rows == 64

    domain_ids = jnp.arange(NDOM, dtype=jnp.int32)
    member = (domains[..., 0][..., None] == domain_ids).astype(F32)
    cot_part = cotangent.reshape(rows, part)
    if quick:
        mixer_in, mixer_out, small, cot_full, glu_low = gather_call(
            mixer_master, gain_master, lengths, domains[..., 0], glu_in_master, glu_out_master, cot_part, 2
        )
        mixer_in = mixer_in.reshape(3, full, channels)
        mixer_out = mixer_out.reshape(channels, full)
        small = small.reshape(groups, narrow, 8, 128)
        gain_full = small[:, :, :3, :own_rows].transpose(2, 0, 1, 3).reshape(3, full)
        counts = jnp.sum(small[:, 0, 3, :NDOM], axis=0)
    else:
        gain_full = lax.all_gather(
            gain_master.astype(BF), ("dp", "mp"), axis=1, tiled=True
        ).astype(F32)
        mixer_low = mixer_master.astype(BF)
        in_blocks = mixer_low[:3].reshape(3, own_rows, groups, narrow, own_rows)
        in_blocks = in_blocks.transpose(3, 0, 1, 2, 4).reshape(narrow, 3, own_rows, channels)
        in_rows = mp_swap(in_blocks).transpose(1, 0, 2, 3).reshape(3, narrow * own_rows, channels)
        mixer_in = lax.all_gather(in_rows, "dp", axis=1, tiled=True)
        mixer_out = lax.all_gather(mixer_low[3], "dp", axis=0, tiled=True)
        counts = lax.psum(jnp.sum(member * lengths.astype(F32)[..., None], axis=(0, 1)), "dp")
        cot_full = mp_gather(cot_part)
        glu_low = jnp.concatenate([glu_in_master.astype(BF), glu_out_master.astype(BF).T[None]])
    glu = lax.all_gather(glu_low, "dp", axis=1, tiled=True)

    seq_weight = jnp.sum(counts) / (NDOM * jnp.sum(member * counts, axis=-1))
    positions = jnp.arange(length, dtype=jnp.int32)
    token_weight = jnp.where(positions[None, :] < lengths[:, :1], seq_weight[:, :1], 0.0)
    token_weight = token_weight.reshape(rows, 1)

    own_channels = lambda v: lax.dynamic_index_in_dim(
        v.reshape(groups, narrow, own_rows), place, 1, keepdims=False
    ).reshape(channels)
    bound = own_channels(lower_bound)
    state_gain = own_channels(gain_full[1])

    token_rows = tokens.reshape(rows, full)
    seq_in = token_rows.astype(F32)
    inverse_in = inverse_rms(seq_in)
    unit_in = seq_in * inverse_in
    normed_in = (unit_in * gain_full[0]).astype(BF)
    pre = jnp.einsum("td,kde->kte", normed_in, mixer_in, preferred_element_type=F32)
    pre = pre.reshape(3, batches, length, channels)
    states, raw, square = scan_forward(pre, bound, state_gain)
    square = mp_sum_wide(square.reshape(rows, 1))
    inverse_state = lax.rsqrt(square / full + EPSILON)
    mixed = jnp.dot(raw.reshape(rows, channels), mixer_out, preferred_element_type=F32)
    back_low = (cot_full.astype(F32) * token_weight).astype(BF)
    if quick:
        mixed = mixed.astype(BF)
        came, left_back, left_in = lax.optimization_barrier(
            (partner_swap(mixed), back_low.T, normed_in.T)
        )
        mixed = mixed.astype(F32) + came.astype(F32)
    else:
        mixed = mp_sum(mixed)
    branch_mix = inverse_state * mixed
    middle = seq_in + branch_mix
    inverse_mid = inverse_rms(middle)
    unit_mid = middle * inverse_mid
    normed_mid = (unit_mid * gain_full[2]).astype(BF)

    across = (((1,), (1,)), ((), ()))
    down = (((0,), (0,)), ((), ()))
    dot = functools.partial(lax.dot_general, preferred_element_type=F32)
    if quick:
        glu_sums, glu_tail, sum_own, sum_came, half_own, half_send = glu_call(normed_mid, back_low, left_back, glu, 0)
        half_came = partner_swap(half_send)
        glu_tail = lax.psum_scatter(glu_tail, "dp", scatter_dimension=1, tiled=True)
    else:
        pre_act = jnp.dot(normed_mid, glu[0], preferred_element_type=F32)
        pre_up = jnp.dot(normed_mid, glu[1], preferred_element_type=F32)
        grad_hidden = jnp.dot(back_low, glu[2], preferred_element_type=F32)
        act_part = jax.nn.silu(pre_act)
        hidden = (act_part * pre_up).astype(BF)
        grad_act = (grad_hidden * pre_up * silu_slope(pre_act)).astype(BF)
        grad_up = (grad_hidden * act_part).astype(BF)
        grad_normed = mp_sum(dot(grad_act, glu[0], across) + dot(grad_up, glu[1], across))
        glu_grad = jnp.stack(
            [dot(normed_mid, grad_act, down), dot(normed_mid, grad_up, down), dot(back_low, hidden, down)]
        ).astype(BF)
        glu_own = lax.psum_scatter(glu_grad, "dp", scatter_dimension=1, tiled=True).astype(F32)
        branch = mp_scatter(dot(hidden, glu[2], across))
    scale = 1.0 / (batches * groups * tokens.shape[1])
    own_features = lambda v: lax.dynamic_slice_in_dim(v, place * part, part, v.ndim - 1)
    if quick:
        grad_middle_own, middle_low, state_mean, grad_gated, gain_mid = middle_back(
            sum_own, sum_came, middle, cot_full, token_rows, token_weight, gain_full[2], mixer_out
        )
        gain_mid = gain_mid[0]
    else:
        inverse_mid = inverse_rms(middle)
        unit_mid = middle * inverse_mid
        gain_mid = jnp.sum(grad_normed * unit_mid, axis=0)
        scaled_mid = grad_normed * gain_full[2]
        back = cot_full.astype(F32) * token_weight
        grad_middle = back + inverse_mid * (
            scaled_mid - unit_mid * jnp.mean(scaled_mid * unit_mid, axis=-1, keepdims=True)
        )
        grad_middle_own = own_features(grad_middle)
        middle_low = grad_middle.astype(BF)
        state_mean = jnp.mean(middle_low.astype(F32) * branch_mix, axis=-1, keepdims=True)
        grad_gated = dot(middle_low, mixer_out, across)
    by_batch = lambda v: v.reshape(batches, length, v.shape[-1])
    grad_pre, gated_out, gain_state, pre_dot = scan_backward(
        pre, states, by_batch(grad_gated), by_batch(inverse_state), by_batch(state_mean), bound, state_gain
    )
    if quick:
        scattered = glu_in_master.shape[2] // LANES - TAIL
        glu_ins = (glu_in_master, glu_in_first, glu_in_second)
        glu_downs = (glu_out_master, glu_out_first, glu_out_second)
        glu_new = glu_update(
            glu_sums, lambda kind, q: (3 * q + kind, 0, 0), 0, scattered, glu_ins, glu_downs, scale
        )
        half_came, grad_pre, glu_new = lax.optimization_barrier((half_came, grad_pre, glu_new))
        branch = half_own.astype(F32) + half_came.astype(F32)
    grad_pre = grad_pre.reshape(3, rows, channels)
    gated_out = gated_out.reshape(rows, channels)
    gain_state = jnp.sum(gain_state, axis=0).reshape(groups, 1, own_rows)
    gain_state = lax.dynamic_update_slice_in_dim(
        jnp.zeros((groups, narrow, own_rows), F32), gain_state, place, 1
    )
    device = lax.axis_index("dp") * narrow + place
    if quick:
        gain_parts = jnp.stack(
            [
                jnp.zeros((groups, narrow * own_rows), F32),
                gain_state.reshape(groups, narrow * own_rows),
                0.5 * gain_mid.reshape(groups, narrow * own_rows),
            ],
            axis=1,
        )
        gain_parts = jnp.pad(gain_parts, ((0, 0), (0, 5), (0, 0)))
        pre_dot = pre_dot.reshape(-1, 128)
        mixer_own, gain_own, grad_normed_in, dot_came = mixer_call(
            left_in, grad_pre, gated_out.T, middle_low, gain_parts, token_rows, inverse_in, mixer_in, pre_dot, 1
        )
        in_mean = (pre_dot + dot_came).reshape(rows, 1) / full
        gain_own = lax.dynamic_slice_in_dim(gain_own[:3], place * own_rows, own_rows, 1)
    else:
        grad_mix_out = dot(gated_out, middle_low, down).astype(BF)
        grad_mix_in = jnp.einsum("td,kte->kde", normed_in, grad_pre, preferred_element_type=F32)
        in_own = lax.psum_scatter(grad_mix_in.astype(BF), "dp", scatter_dimension=1, tiled=True)
        out_own = lax.psum_scatter(grad_mix_out, "dp", scatter_dimension=0, tiled=True)
        in_own = mp_swap(in_own.reshape(3, narrow, own_rows, channels).transpose(1, 0, 2, 3))
        in_own = in_own.reshape(narrow, 3, own_rows, groups, own_rows).transpose(1, 2, 3, 0, 4)
        grad_normed_in = jnp.einsum("kte,kde->td", grad_pre, mixer_in, preferred_element_type=F32)
        gain_in = jnp.sum(grad_normed_in * unit_in, axis=0)
        grad_normed_in = mp_scatter(grad_normed_in)
        gain_rows = jnp.stack([gain_in, gain_state.reshape(full), gain_mid / narrow])
        gain_total = lax.psum(gain_rows, ("dp", "mp"))
        gain_own = lax.dynamic_slice_in_dim(gain_total, device * own_rows, own_rows, 1)
        in_mean = mp_sum_wide(pre_dot.reshape(rows, 1)) / full
        in_own = in_own.reshape(3, own_rows, full)
        mixer_own = jnp.concatenate([in_own, out_own[None]]).astype(F32)
    unit_in_own = own_features(token_rows).astype(F32) * inverse_in
    grad_seq = grad_middle_own + inverse_in * (
        grad_normed_in * own_features(gain_full[0]) - unit_in_own * in_mean
    )
    grad_tokens = grad_seq.astype(BF)
    layer_out = (own_features(middle) + branch).astype(BF)

    update = functools.partial(adamw_update, count=STEP_NUMBER)
    mixer_new = update(
        mixer_master, mixer_first, mixer_second, mixer_own * scale, rate=MATRIX_RATE, decay=DECAY_RATE
    )
    gain_new = update(
        gain_master, gain_first, gain_second, gain_own * scale, rate=GAIN_RATE, decay=0.0
    )
    if quick:
        glu_new = glu_update(
            glu_tail, lambda kind, q: (kind, 0, q), scattered, TAIL, glu_ins, glu_downs, scale, glu_new
        )
    else:
        glu_in_new = update(
            glu_in_master, glu_in_first, glu_in_second, glu_own[:2] * scale,
            rate=MATRIX_RATE, decay=DECAY_RATE,
        )
        glu_out_new = update(
            glu_out_master, glu_out_first, glu_out_second, glu_own[2].T * scale,
            rate=MATRIX_RATE, decay=DECAY_RATE,
        )
        glu_new = (*glu_in_new, *glu_out_new)
    return (
        layer_out.reshape(batches, 1, length, part),
        grad_tokens.reshape(batches, 1, length, part),
        *mixer_new,
        *glu_new,
        *gain_new,
    )


def solution(mesh):
    weights = (
        [P(None, ("dp", "mp"), None)] * 3
        + [P(None, "dp", "mp")] * 3
        + [P("mp", "dp")] * 3
        + [P(None, ("dp", "mp"))] * 3
    )
    in_specs = (
        P(None, "dp", None, None),
        P(None, "dp", None, "mp"),
        P(None, "dp"),
        P(None, "dp", None),
        P(),
        *weights,
    )
    out_specs = (P(None, "dp", None, "mp"), P(None, "dp", None, "mp"), *weights)
    return jax.shard_map(shards, mesh=mesh, in_specs=in_specs, out_specs=out_specs, check_vma=False)
```

```python
import functools

import jax
import jax.numpy as jnp
from jax import lax
from jax.experimental import pallas as pl
from jax.experimental.pallas import tpu as pltpu
from jax.sharding import PartitionSpec as P

NDOM = 8

EPSILON = 1e-06
BETA_ONE = 0.9
BETA_TWO = 0.95
ADAM_EPSILON = 1e-08
DECAY_RATE = 0.1
MATRIX_RATE = 0.06
GAIN_RATE = 0.5
STEP_NUMBER = 3.0

BF = jnp.bfloat16
F32 = jnp.float32
VMEM_LIMIT = 56 * 1024 * 1024


def inverse_rms(values):
    return lax.rsqrt(jnp.mean(values * values, axis=-1, keepdims=True) + EPSILON)


def silu_slope(values):
    sigma = jax.nn.sigmoid(values)
    return sigma * (1.0 + values * (1.0 - sigma))


def adamw_update(master, first, second, gradient, count, rate, decay):
    first_new = BETA_ONE * first + (1.0 - BETA_ONE) * gradient
    second_new = BETA_TWO * second + (1.0 - BETA_TWO) * gradient * gradient
    first_hat = first_new / (1.0 - BETA_ONE**count)
    second_hat = second_new / (1.0 - BETA_TWO**count)
    master_new = master - rate * (
        first_hat / (jnp.sqrt(second_hat) + ADAM_EPSILON) + decay * master
    )
    return (master_new, first_new, second_new)


def partner_swap(value):
    return lax.ppermute(value, "mp", [(0, 1), (1, 0)])


def mp_sum(part):
    low = part.astype(BF)
    if lax.axis_size("mp") == 2:
        return low.astype(F32) + partner_swap(low).astype(F32)
    return lax.psum(low.astype(F32), "mp")


def mp_sum_wide(part):
    if lax.axis_size("mp") == 2:
        return part + partner_swap(part)
    return lax.psum(part, "mp")


def mp_scatter(part):
    if lax.axis_size("mp") == 2:
        half = part.shape[1] // 2
        place = lax.axis_index("mp")
        own = lax.dynamic_slice_in_dim(part, place * half, half, 1)
        other = lax.dynamic_slice_in_dim(part, (1 - place) * half, half, 1)
        return own.astype(BF).astype(F32) + partner_swap(other.astype(BF)).astype(F32)
    return lax.psum_scatter(part.astype(BF), "mp", scatter_dimension=1, tiled=True).astype(F32)


def mp_swap(pieces):
    if lax.axis_size("mp") == 2:
        place = lax.axis_index("mp")
        own = lax.dynamic_index_in_dim(pieces, place, 0, keepdims=False)
        came = partner_swap(lax.dynamic_index_in_dim(pieces, 1 - place, 0, keepdims=False))
        first = place == 0
        return jnp.stack([jnp.where(first, own, came), jnp.where(first, came, own)])
    return lax.all_to_all(pieces, "mp", 0, 0, tiled=False)


def mp_gather(part):
    if lax.axis_size("mp") == 2:
        place = lax.axis_index("mp")
        came = partner_swap(part)
        first = place == 0
        return jnp.concatenate([jnp.where(first, part, came), jnp.where(first, came, part)], axis=1)
    return lax.all_gather(part, "mp", axis=1, tiled=True)


SUB_ROWS = 8
TILE_ROWS = 64


def channel_block(width):
    return 512 if width % 512 == 0 else width


def scan_rows(total, decay, carry):
    row = lax.broadcasted_iota(jnp.int32, total.shape, 0)
    shift = 1
    while shift < SUB_ROWS:
        keep = row >= shift
        total = total + decay * jnp.where(keep, pltpu.roll(total, shift, 0), 0.0)
        decay = decay * jnp.where(keep, pltpu.roll(decay, shift, 0), 1.0)
        shift *= 2
    return total + decay * carry


def scan_rows_back(total, decay, carry):
    row = lax.broadcasted_iota(jnp.int32, total.shape, 0)
    shift = 1
    while shift < SUB_ROWS:
        keep = row < SUB_ROWS - shift
        total = total + decay * jnp.where(keep, pltpu.roll(total, SUB_ROWS - shift, 0), 0.0)
        decay = decay * jnp.where(keep, pltpu.roll(decay, SUB_ROWS - shift, 0), 1.0)
        shift *= 2
    return total + decay * carry


def scan_forward_kernel(pre_ref, bound_ref, gain_ref, states_ref, raw_ref, square_ref):
    length, width = states_ref.shape[1], states_ref.shape[2]
    bound = bound_ref[...]
    gain = gain_ref[...]
    first_block = pl.program_id(1) == 0

    def step(index, carry):
        rows = pl.ds(pl.multiple_of(index * TILE_ROWS, TILE_ROWS), TILE_ROWS)
        forget = bound + (1.0 - bound) * jax.nn.sigmoid(pre_ref[1, 0, rows, :])
        total = (1.0 - forget) * jax.nn.silu(pre_ref[0, 0, rows, :])
        parts = []
        for low in range(0, TILE_ROWS, SUB_ROWS):
            part = scan_rows(total[low : low + SUB_ROWS], forget[low : low + SUB_ROWS], carry)
            carry = part[SUB_ROWS - 1 : SUB_ROWS]
            parts.append(part)
        states = jnp.concatenate(parts)
        states_ref[0, rows, :] = states
        raw = states * gain * jax.nn.silu(pre_ref[2, 0, rows, :])
        raw_ref[0, rows, :] = raw.astype(raw_ref.dtype)
        square = jnp.sum(states * states, axis=-1, keepdims=True)
        square_ref[0, rows, :] = square + jnp.where(first_block, 0.0, square_ref[0, rows, :])
        return carry

    lax.fori_loop(0, length // TILE_ROWS, step, jnp.zeros((1, width), F32))


def scan_forward(pre, bound, gain):
    _, batches, length, width = pre.shape
    block = channel_block(width)
    return pl.pallas_call(
        scan_forward_kernel,
        grid=(batches, width // block),
        in_specs=[
            pl.BlockSpec((3, 1, length, block), lambda b, c: (0, b, 0, c)),
            pl.BlockSpec((1, block), lambda b, c: (0, c)),
            pl.BlockSpec((1, block), lambda b, c: (0, c)),
        ],
        out_specs=[
            pl.BlockSpec((1, length, block), lambda b, c: (b, 0, c)),
            pl.BlockSpec((1, length, block), lambda b, c: (b, 0, c)),
            pl.BlockSpec((1, length, 1), lambda b, c: (b, 0, 0)),
        ],
        out_shape=[
            jax.ShapeDtypeStruct((batches, length, width), F32),
            jax.ShapeDtypeStruct((batches, length, width), BF),
            jax.ShapeDtypeStruct((batches, length, 1), F32),
        ],
        compiler_params=pltpu.CompilerParams(vmem_limit_bytes=VMEM_LIMIT),
        cost_estimate=pl.CostEstimate(
            flops=batches * length * width * 40,
            bytes_accessed=batches * length * width * 18,
            transcendentals=batches * length * width * 3,
        ),
    )(pre, bound[None], gain[None])


def scan_backward_kernel(
    pre_ref, states_ref, gated_ref, inverse_ref, mean_ref, bound_ref, gain_ref,
    grad_ref, gain_grad_ref, dot_ref,
):
    length, width = states_ref.shape[1], states_ref.shape[2]
    bound = bound_ref[...]
    gain = gain_ref[...]
    first_block = pl.program_id(1) == 0
    row = lax.broadcasted_iota(jnp.int32, (TILE_ROWS, width), 0)
    tiles = length // TILE_ROWS

    def step(index, carry):
        carried_next, forget_next, gain_sum = carry
        place = tiles - 1 - index
        rows = pl.ds(pl.multiple_of(place * TILE_ROWS, TILE_ROWS), TILE_ROWS)
        pre_input = pre_ref[0, 0, rows, :]
        pre_forget = pre_ref[1, 0, rows, :]
        pre_gate = pre_ref[2, 0, rows, :]
        states = states_ref[0, rows, :]
        inverse = inverse_ref[0, rows, :]
        grad_gated = gated_ref[0, rows, :]
        unit = states * inverse
        gate_sig = jax.nn.sigmoid(pre_gate)
        gate = pre_gate * gate_sig
        gain_sum = gain_sum + grad_gated * unit * gate
        scaled = grad_gated * gain
        grad_gate = (scaled * unit * (gate_sig * (1.0 + pre_gate * (1.0 - gate_sig)))).astype(BF)
        grad_ref[2, 0, rows, :] = grad_gate
        total = inverse * (scaled * gate - unit * mean_ref[0, rows, :])
        sigma = jax.nn.sigmoid(pre_forget)
        forget = bound + (1.0 - bound) * sigma
        decay = jnp.where(row == TILE_ROWS - 1, forget_next, pltpu.roll(forget, TILE_ROWS - 1, 0))
        parts = []
        for low in range(TILE_ROWS - SUB_ROWS, -1, -SUB_ROWS):
            part = scan_rows_back(
                total[low : low + SUB_ROWS], decay[low : low + SUB_ROWS], carried_next
            )
            carried_next = part[0:1]
            parts.insert(0, part)
        carried = jnp.concatenate(parts)
        before_rows = pl.ds(
            pl.multiple_of(jnp.maximum(place - 1, 0) * TILE_ROWS, TILE_ROWS), TILE_ROWS
        )
        before = states_ref[0, before_rows, :][TILE_ROWS - 1 : TILE_ROWS, :]
        before = jnp.where(place == 0, 0.0, before)
        earlier = jnp.where(row == 0, before, pltpu.roll(states, 1, 0))
        input_sig = jax.nn.sigmoid(pre_input)
        fresh = pre_input * input_sig
        slope = input_sig * (1.0 + pre_input * (1.0 - input_sig))
        grad_input = (carried * (1.0 - forget) * slope).astype(BF)
        grad_forget = (
            carried * (earlier - fresh) * (1.0 - bound) * sigma * (1.0 - sigma)
        ).astype(BF)
        grad_ref[0, 0, rows, :] = grad_input
        grad_ref[1, 0, rows, :] = grad_forget
        dots = (
            grad_input.astype(F32) * pre_input
            + grad_forget.astype(F32) * pre_forget
            + grad_gate.astype(F32) * pre_gate
        )
        dot = jnp.sum(dots, axis=-1, keepdims=True)
        dot_ref[0, rows, :] = dot + jnp.where(first_block, 0.0, dot_ref[0, rows, :])
        return carried_next, forget[0:1, :], gain_sum

    zero = jnp.zeros((1, width), F32)
    _, _, gain_sum = lax.fori_loop(
        0, tiles, step, (zero, zero, jnp.zeros((TILE_ROWS, width), F32))
    )
    gain_grad_ref[0] = jnp.sum(gain_sum, axis=0, keepdims=True)


def scan_backward(pre, states, grad_gated, inverse, mean, bound, gain):
    _, batches, length, width = pre.shape
    block = channel_block(width)
    whole = pl.BlockSpec((1, length, block), lambda b, c: (b, 0, c))
    column = pl.BlockSpec((1, length, 1), lambda b, c: (b, 0, 0))
    line = pl.BlockSpec((1, block), lambda b, c: (0, c))
    three = pl.BlockSpec((3, 1, length, block), lambda b, c: (0, b, 0, c))
    return pl.pallas_call(
        scan_backward_kernel,
        grid=(batches, width // block),
        in_specs=[three, whole, whole, column, column, line, line],
        out_specs=[
            three,
            pl.BlockSpec((1, 1, block), lambda b, c: (b, 0, c)),
            column,
        ],
        out_shape=[
            jax.ShapeDtypeStruct((3, batches, length, width), BF),
            jax.ShapeDtypeStruct((batches, 1, width), F32),
            jax.ShapeDtypeStruct((batches, length, 1), F32),
        ],
        compiler_params=pltpu.CompilerParams(vmem_limit_bytes=VMEM_LIMIT),
        cost_estimate=pl.CostEstimate(
            flops=batches * length * width * 80,
            bytes_accessed=batches * length * width * 28,
            transcendentals=batches * length * width * 3,
        ),
    )(pre, states, grad_gated, inverse, mean, bound[None], gain[None])


MESH_ID = pl.DeviceIdType.MESH
DEPTH = 4
LANES = 256
X_LAG = 4
Z_LAG = X_LAG + 2
SWAP_LAG = 2
TAIL = 2


def device_place():
    dp = lax.axis_index("dp")
    return dp // 4, lax.rem(dp // 2, 2), lax.rem(dp, 2)


def device_at(z, x, core):
    return (z * 4 + x * 2 + core, lax.axis_index("mp"))


def greet(z, x, core):
    barrier = pltpu.get_barrier_semaphore()
    targets = [device_at(z, x, 1 - core), device_at(z, 1 - x, core)]
    targets += [device_at(lax.rem(z + hop, DEPTH), x, core) for hop in range(1, DEPTH)]
    targets.append((lax.axis_index("dp"), 1 - lax.axis_index("mp")))
    for target in targets:
        pl.semaphore_signal(barrier, 1, device_id=target, device_id_type=MESH_ID)


def await_partners():
    pl.semaphore_wait(pltpu.get_barrier_semaphore(), DEPTH + 2)


def scatter_step(step, chunks, compute, finish, scratch, small_last=False):
    (own, core_out, core_in, keep, x_out, x_in, sums, mine, z_out, z_in,
     core_send, core_recv, x_send, x_recv, z_send, z_recv) = scratch
    z, x, core = device_place()

    def core_copy(p, cut=()):
        return pltpu.make_async_remote_copy(
            core_out.at[(lax.rem(p, 2), *cut)], core_in.at[(lax.rem(p, 4), *cut)],
            core_send.at[lax.rem(p, 2)], core_recv.at[lax.rem(p, 4)],
            device_id=device_at(z, x, 1 - core), device_id_type=MESH_ID)

    def x_copy(p, cut=()):
        return pltpu.make_async_remote_copy(
            x_out.at[(lax.rem(p, X_LAG), *cut)], x_in.at[(lax.rem(p, 2 * X_LAG), *cut)],
            x_send.at[lax.rem(p, X_LAG)], x_recv.at[lax.rem(p, 2 * X_LAG)],
            device_id=device_at(z, 1 - x, core), device_id_type=MESH_ID)

    def z_copy(p, hop, cut=()):
        return pltpu.make_async_remote_copy(
            z_out.at[(lax.rem(p, 4), hop - 1, *cut)], z_in.at[(lax.rem(p, 8), hop - 1, *cut)],
            z_send.at[lax.rem(p, 4), hop - 1], z_recv.at[lax.rem(p, 8), hop - 1],
            device_id=device_at(lax.rem(z + hop, DEPTH), x, core), device_id_type=MESH_ID)

    corner = (slice(0, 16), slice(0, 128))
    every = slice(None)

    def go(copy, lead, p, act):
        if not small_last:
            act(copy(p))
            return
        pl.when(p < chunks - 1)(lambda: act(copy(p)))
        pl.when(p == chunks - 1)(lambda: act(copy(p, (*(every,) * lead, *corner))))

    def core_go(p, act):
        go(core_copy, 2, p, act)

    def x_go(p, act):
        go(x_copy, 1, p, act)

    def z_go(p, hop, act):
        go(lambda p, cut=(): z_copy(p, hop, cut), 0, p, act)

    start, wait_recv, wait_send = (
        lambda copy: copy.start(), lambda copy: copy.wait_recv(), lambda copy: copy.wait_send())

    @pl.when(step < chunks)
    def _():
        @pl.when(step >= 2)
        def _():
            core_go(step - 2, wait_send)

        def to_partner(value):
            core_out[lax.rem(step, 2)] = value.astype(BF)

        def to_own(value):
            own[lax.rem(step, 2)] = value

        compute(step, 1 - core, to_partner)
        core_go(step, start)
        compute(step, core, to_own)

    @pl.when((step >= 1) & (step < chunks + 1))
    def _():
        p = step - 1
        core_go(p, wait_recv)

        @pl.when(p >= X_LAG)
        def _():
            x_go(p - X_LAG, wait_send)

        two, four, slot = lax.rem(p, 2), lax.rem(p, 4), lax.rem(p, X_LAG)
        x_out[slot] = (own[two, :, 1 - x] + core_in[four, :, 1 - x].astype(F32)).astype(BF)
        x_go(p, start)
        keep[slot] = own[two, :, x] + core_in[four, :, x].astype(F32)

    @pl.when((step >= X_LAG) & (step < chunks + X_LAG))
    def _():
        p = step - X_LAG
        x_go(p, wait_recv)
        four = lax.rem(p, 4)
        sums[...] = keep[lax.rem(p, X_LAG)] + x_in[lax.rem(p, 2 * X_LAG)].astype(F32)
        for hop in range(1, DEPTH):
            @pl.when(p >= 4)
            def _():
                z_go(p - 4, hop, wait_send)

            z_out[four, hop - 1] = sums[lax.rem(z + hop, DEPTH)].astype(BF)
            z_go(p, hop, start)
        mine[four] = sums[z]

    @pl.when((step >= Z_LAG) & (step < chunks + Z_LAG))
    def _():
        p = step - Z_LAG
        for hop in range(1, DEPTH):
            z_go(p, hop, wait_recv)
        got = z_in.at[lax.rem(p, 8)]
        finish(p, mine[lax.rem(p, 4)] + got[0].astype(F32) + got[1].astype(F32) + got[2].astype(F32))

    @pl.when(step == chunks + Z_LAG - 1)
    def _():
        for p in range(chunks - 2, chunks):
            core_go(jnp.int32(p), wait_send)
        for p in range(chunks - X_LAG, chunks):
            x_go(jnp.int32(p), wait_send)
        for p in range(chunks - 4, chunks):
            for hop in range(1, DEPTH):
                z_go(jnp.int32(p), hop, wait_send)


def scatter_scratch(rows, lanes):
    quad = (DEPTH, 2, rows, lanes)
    line = (DEPTH, rows, lanes)
    dma = pltpu.SemaphoreType.DMA
    return [
        pltpu.VMEM((2, *quad), F32),
        pltpu.VMEM((2, *quad), BF),
        pltpu.VMEM((4, *quad), BF),
        pltpu.VMEM((X_LAG, *line), F32),
        pltpu.VMEM((X_LAG, *line), BF),
        pltpu.VMEM((2 * X_LAG, *line), BF),
        pltpu.VMEM(line, F32),
        pltpu.VMEM((4, rows, lanes), F32),
        pltpu.VMEM((4, DEPTH - 1, rows, lanes), BF),
        pltpu.VMEM((8, DEPTH - 1, rows, lanes), BF),
        dma((2,)), dma((4,)), dma((X_LAG,)), dma((2 * X_LAG,)), dma((4, DEPTH - 1)), dma((8, DEPTH - 1)),
    ]


def scatter_out(chunks, rows, lanes):
    spec = pl.BlockSpec((1, rows, lanes), lambda q: (jnp.maximum(q - Z_LAG, 0), 0, 0))
    return spec, jax.ShapeDtypeStruct((chunks, rows, lanes), F32)


def fixed(shape):
    return pl.BlockSpec(shape, lambda q: (0,) * len(shape), pipeline_mode=pl.Buffered(1))


def glu_kernel(
    hidden_blocks, full_blocks, normed_ref, back_ref, left_ref, left_back_ref, glu_ref,
    out_ref, sum_own, sum_came, half_own, half_send, tail_ref,
    tail_stage, tail_sem, left, left_back, left_sem, acts, weights_in, weights_back, sum_stage, half_stage,
    in_sem, back_sem, stage_sem, sum_send, sum_recv, *scratch,
):
    z, x, core = device_place()
    dp, mp = lax.axis_index("dp"), lax.axis_index("mp")
    step = pl.program_id(0)
    scattered = hidden_blocks - TAIL
    chunks = 3 * scattered
    rows = normed_ref.shape[0]
    row_block = rows // 2
    half_blocks = full_blocks // 2
    across = (((1,), (1,)), ((), ()))
    spread = min(hidden_blocks + hidden_blocks // 2, 16)
    second = step - spread

    def first_tasks(at):
        return at * hidden_blocks // spread

    def second_task(at):
        return 2 * at // 3

    def has_second(at):
        return (at == 0) | (
            (at > 0) & (second_task(at) > second_task(at - 1)) & (second_task(at) < full_blocks))

    unit_block = first_tasks(step)

    def lane_block(index):
        return pl.ds(pl.multiple_of(index * LANES, LANES), LANES)

    def load_in(index):
        return pltpu.make_async_copy(glu_ref.at[:, :, lane_block(index)], weights_in, in_sem)

    def load_back(index):
        return pltpu.make_async_copy(glu_ref.at[:, lane_block(index), :], weights_back, back_sem)

    def stage(index, kind, target):
        source = (sum_stage, half_stage)[kind].at[lax.rem(index, 2)]
        return pltpu.make_async_copy(source, target, stage_sem.at[lax.rem(index, 2), kind])

    def half_spot(index):
        return lax.rem(index, half_blocks)

    def sum_copy(index):
        return pltpu.make_async_remote_copy(
            sum_own.at[:, lane_block(index)], sum_came.at[:, lane_block(index)],
            sum_send.at[index], sum_recv.at[index], device_id=(dp, 1 - mp), device_id_type=MESH_ID)

    left_loads = (
        pltpu.make_async_copy(left_ref, left, left_sem.at[0]),
        pltpu.make_async_copy(left_back_ref, left_back, left_sem.at[1]),
    )

    @pl.when(step == 0)
    def _():
        greet(z, x, core)
        for one in (load_in(0), *left_loads, load_back(0)):
            one.start()

    @pl.when((step < spread) & ((step == 0) | (unit_block > first_tasks(step - 1))))
    def _():
        load_in(unit_block).wait()
        lanes = lane_block(unit_block)

        def part(index, _):
            part_rows = pl.ds(pl.multiple_of(index * row_block, row_block), row_block)
            normed = normed_ref[part_rows, :]
            pre_act = jnp.dot(normed, weights_in[0], preferred_element_type=F32)
            pre_up = jnp.dot(normed, weights_in[1], preferred_element_type=F32)
            grad_hidden = jnp.dot(back_ref[part_rows, :], weights_in[2], preferred_element_type=F32)
            sigma = jax.nn.sigmoid(pre_act)
            act_part = pre_act * sigma
            acts[0, part_rows, lanes] = (
                grad_hidden * pre_up * (sigma * (1.0 + pre_act * (1.0 - sigma)))).astype(BF)
            acts[1, part_rows, lanes] = (grad_hidden * act_part).astype(BF)
            acts[2, part_rows, lanes] = (act_part * pre_up).astype(BF)
            return 0

        lax.fori_loop(0, rows // row_block, part, 0)

        @pl.when(unit_block + 1 < hidden_blocks)
        def _():
            load_in(unit_block + 1).start()

    @pl.when(step == 0)
    def _():
        await_partners()

    @pl.when(has_second(second - 1))
    def _():
        index = second_task(second - 1)
        stage(index, 0, sum_own.at[:, lane_block(index)]).wait()
        sum_copy(index).start()
        spot = half_spot(index)
        stage(index, 1, half_own.at[:, lane_block(spot)]).wait()

    @pl.when(has_second(second))
    def _():
        index = second_task(second)
        load_back(index).wait()
        slot = lax.rem(index, 2)

        def part(at, _):
            part_rows = pl.ds(pl.multiple_of(at * row_block, row_block), row_block)
            dot = functools.partial(
                lax.dot_general, dimension_numbers=across, preferred_element_type=F32)
            grad_normed = dot(acts[0, part_rows, :], weights_back[0])
            grad_normed += dot(acts[1, part_rows, :], weights_back[1])
            sum_stage[slot, part_rows, :] = grad_normed.astype(BF)
            half_stage[slot, part_rows, :] = dot(acts[2, part_rows, :], weights_back[2]).astype(BF)
            return 0

        lax.fori_loop(0, rows // row_block, part, 0)

        @pl.when(index + 1 < full_blocks)
        def _():
            load_back(index + 1).start()

        stage(index, 0, sum_own.at[:, lane_block(index)]).start()
        spot = half_spot(index)

        @pl.when(index // half_blocks == mp)
        def _():
            stage(index, 1, half_own.at[:, lane_block(spot)]).start()

        @pl.when(index // half_blocks != mp)
        def _():
            stage(index, 1, half_send.at[:, lane_block(spot)]).start()

    def compute(q, core_side, store):
        kind = lax.rem(q, 3)
        side_rows = left.shape[3]

        def product(side_ref):
            side = side_ref[:, :, core_side].reshape(DEPTH * 2 * side_rows, rows)
            right = acts[kind, :, lane_block(q // 3)]
            store(jnp.dot(side, right, preferred_element_type=F32).reshape(
                DEPTH, 2, side_rows, LANES))

        pl.when(kind < 2)(lambda: product(left))
        pl.when(kind == 2)(lambda: product(left_back))

    @pl.when(step == 0)
    def _():
        for one in left_loads:
            one.wait()

    def finish(p, value):
        out_ref[0] = value

    scatter_step(step, chunks, compute, finish, scratch)

    def tail_copy(index):
        spot = tail_ref.at[lax.rem(index, 3), :, :, :, :, lane_block(index // 3)]
        return pltpu.make_async_copy(
            tail_stage.at[lax.rem(index, 2)], spot, tail_sem.at[lax.rem(index, 2)])

    tail_start = chunks + Z_LAG - 3 * TAIL

    @pl.when(step >= tail_start)
    def _():
        index = step - tail_start

        @pl.when(index >= 2)
        def _():
            tail_copy(index - 2).wait()

        for side in (0, 1):
            def to_stage(value):
                tail_stage[lax.rem(index, 2), :, :, side] = value.astype(BF)

            compute(chunks + index, side, to_stage)
        tail_copy(index).start()

    @pl.when(step == chunks + Z_LAG - 1)
    def _():
        for index in range(3 * TAIL - 2, 3 * TAIL):
            tail_copy(jnp.int32(index)).wait()
        for index in range(full_blocks):
            sum_copy(index).wait()


def glu_call(normed, back_low, left_back, glu, collective):
    rows, full = normed.shape
    hidden = glu.shape[2]
    hidden_blocks, full_blocks = hidden // LANES, full // LANES
    block = full // 16
    chunks = 3 * (hidden_blocks - TAIL)
    left_shape = (DEPTH, 2, 2, block, rows)
    any_space = pl.BlockSpec(memory_space=pl.ANY)
    out_spec, out_shape = scatter_out(chunks, block, LANES)
    dma = pltpu.SemaphoreType.DMA
    wide = jax.ShapeDtypeStruct((rows, full), BF)
    half = jax.ShapeDtypeStruct((rows, full // 2), BF)
    out, sum_own, sum_came, half_own, half_send, tail = pl.pallas_call(
        functools.partial(glu_kernel, hidden_blocks, full_blocks),
        grid=(chunks + Z_LAG,),
        in_specs=[fixed(normed.shape), fixed(back_low.shape)] + [any_space] * 3,
        out_specs=[out_spec] + [any_space] * 5,
        out_shape=[
            out_shape, wide, wide, half, half,
            jax.ShapeDtypeStruct((3, DEPTH, 2, 2, block, TAIL * LANES), BF),
        ],
        scratch_shapes=[
            pltpu.VMEM((2, DEPTH, 2, 2, block, LANES), BF),
            dma((2,)),
            pltpu.VMEM(left_shape, BF),
            pltpu.VMEM(left_shape, BF),
            dma((2,)),
            pltpu.VMEM((3, rows, hidden), BF),
            pltpu.VMEM((3, full, LANES), BF),
            pltpu.VMEM((3, LANES, hidden), BF),
            pltpu.VMEM((2, rows, LANES), BF),
            pltpu.VMEM((2, rows, LANES), BF),
            dma(()), dma(()), dma((2, 2)),
            dma((full_blocks,)), dma((full_blocks,)),
            *scatter_scratch(block, LANES),
        ],
        compiler_params=pltpu.CompilerParams(
            collective_id=collective, has_side_effects=True, vmem_limit_bytes=62 * 1024 * 1024),
        cost_estimate=pl.CostEstimate(
            flops=18 * rows * full * hidden, bytes_accessed=6 * full * hidden * 2,
            transcendentals=rows * hidden),
    )(normed, back_low, owner_rows(normed), left_back, glu)
    return out, tail.reshape(3, full, TAIL * LANES), sum_own, sum_came, half_own, half_send


def mixer_kernel(
    full_blocks, left_hbm, grad_hbm, left_out_ref, right_out_ref, gain_ref, tokens_ref, inverse_ref,
    weights_ref, dot_ref, out_ref, gain_out, half_own, half_send, half_came, dot_came,
    left_ref, grad_ref, big_sem, weights, token_block, gain_sum, gain_chunk, total, swap_out, swap_in, half_stage,
    load_sem, stage_sem, half_send_sem, half_recv, swap_send, swap_recv, dot_sem, *scratch,
):
    z, x, core = device_place()
    dp, mp = lax.axis_index("dp"), lax.axis_index("mp")
    step = pl.program_id(0)
    tokens, channels = grad_ref.shape[1], grad_ref.shape[2]
    block, half = left_ref.shape[3], left_out_ref.shape[3]
    outer = full_blocks // 2
    across = channels // LANES
    gains = outer + 3 * across
    chunks = gains + 1
    half_blocks = full_blocks // 2
    row_block = tokens // 2
    partner = (dp, 1 - mp)

    def lane_block(index):
        return pl.ds(pl.multiple_of(index * LANES, LANES), LANES)

    def loads(index):
        return (
            pltpu.make_async_copy(weights_ref.at[:, lane_block(index), :], weights, load_sem.at[0]),
            pltpu.make_async_copy(tokens_ref.at[:, lane_block(index)], token_block, load_sem.at[1]),
        )

    def stage(index, target):
        return pltpu.make_async_copy(
            half_stage.at[lax.rem(index, 2)], target, stage_sem.at[lax.rem(index, 2)])

    def half_copy(spot):
        return pltpu.make_async_remote_copy(
            half_send.at[:, lane_block(spot)], half_came.at[:, lane_block(spot)],
            half_send_sem.at[spot], half_recv.at[spot], device_id=partner, device_id_type=MESH_ID)

    def swap_copy(index):
        return pltpu.make_async_remote_copy(
            swap_out.at[lax.rem(index, 2)], swap_in.at[lax.rem(index, 8)],
            swap_send.at[lax.rem(index, 2)], swap_recv.at[lax.rem(index, 8)],
            device_id=partner, device_id_type=MESH_ID)

    big_loads = (
        pltpu.make_async_copy(grad_hbm, grad_ref, big_sem.at[0]),
        pltpu.make_async_copy(left_hbm, left_ref, big_sem.at[1]),
    )
    dot_copy = pltpu.make_async_remote_copy(
        dot_ref, dot_came, dot_sem.at[0], dot_sem.at[1], device_id=partner, device_id_type=MESH_ID)

    @pl.when(step == 0)
    def _():
        greet(z, x, core)
        for one in (*big_loads, *loads(0)):
            one.start()
        gain_chunk[...] = jnp.zeros_like(gain_chunk)
        gain_sum[...] = jnp.zeros_like(gain_sum)
        await_partners()
        dot_copy.start()

    @pl.when(step == 1)
    def _():
        for one in big_loads:
            one.wait()

    task = (step - 1) // 2

    @pl.when((step >= 2) & (step <= 2 * full_blocks) & (lax.rem(step, 2) == 0))
    def _():
        index = task
        spot = lax.rem(index, half_blocks)
        stage(index, half_own.at[:, lane_block(spot)]).wait()

        @pl.when(index // half_blocks != mp)
        def _():
            half_copy(spot).start()

    @pl.when((step < 2 * full_blocks) & (lax.rem(step, 2) == 1))
    def _():
        for one in loads(task):
            one.wait()
        slot = lax.rem(task, 2)
        spot = lax.rem(task, half_blocks)

        def part(at, gain_in):
            part_rows = pl.ds(pl.multiple_of(at * row_block, row_block), row_block)
            dot = functools.partial(
                lax.dot_general, dimension_numbers=(((1,), (1,)), ((), ())), preferred_element_type=F32)
            grad = dot(grad_ref[0, part_rows, :], weights[0])
            grad += dot(grad_ref[1, part_rows, :], weights[1])
            grad += dot(grad_ref[2, part_rows, :], weights[2])
            half_stage[slot, part_rows, :] = grad.astype(BF)
            unit = token_block[part_rows, :].astype(F32) * inverse_ref[part_rows, :]
            return gain_in + jnp.sum(grad * unit, axis=0, keepdims=True)

        gain_in = lax.fori_loop(0, tokens // row_block, part, jnp.zeros((1, LANES), F32))
        gain_sum[2 * task, 0:1, :] = gain_in[:, :128]
        gain_sum[2 * task + 1, 0:1, :] = gain_in[:, 128:]

        @pl.when(task + 1 < full_blocks)
        def _():
            for one in loads(task + 1):
                one.start()

        @pl.when(task // half_blocks == mp)
        def _():
            stage(task, half_own.at[:, lane_block(spot)]).start()

        @pl.when(task // half_blocks != mp)
        def _():
            stage(task, half_send.at[:, lane_block(spot)]).start()

    def compute(q, core_side, store):
        @pl.when(q < outer)
        def _():
            side = left_out_ref[:, :, core_side].reshape(channels // 2, tokens)
            parts = [
                jnp.dot(side, right_out_ref[:, lane_block(2 * q + at)], preferred_element_type=F32)
                for at in (0, 1)
            ]
            parts = [part.reshape(DEPTH, 2, half, LANES) for part in parts]
            store(jnp.concatenate(parts, axis=2))

        @pl.when((q >= outer) & (q < gains))
        def _():
            at = q - outer
            side = left_ref[:, :, core_side].reshape(DEPTH * 2 * block, tokens)
            right = grad_ref[at // across, :, lane_block(lax.rem(at, across))]
            store(jnp.dot(side, right, preferred_element_type=F32).reshape(DEPTH, 2, block, LANES))

        @pl.when(q == gains)
        def _():
            for owner in range(2 * DEPTH):
                line = 2 * owner + core_side
                gain_chunk[owner // 2, owner % 2, 0:8, 0:128] = gain_ref[line] + gain_sum[line]
            store(gain_chunk[...])

    def finish(p, value):
        total[lax.rem(p, 4)] = value

        @pl.when(p >= outer)
        def _():
            index = p - outer

            @pl.when(index >= 2)
            def _():
                swap_copy(index - 2).wait_send()

            first = jnp.where(p == gains, 0, 1 - mp) * half
            rows = pl.ds(pl.multiple_of(first, half), half)
            swap_out[lax.rem(index, 2)] = total[lax.rem(p, 4), rows, :].astype(BF)
            swap_copy(index).start()

    scatter_step(step, chunks, compute, finish, scratch, small_last=True)

    @pl.when((step >= Z_LAG + SWAP_LAG) & (step < chunks + Z_LAG + SWAP_LAG))
    def _():
        p = step - Z_LAG - SWAP_LAG
        slot = lax.rem(p, 4)

        @pl.when(p < outer)
        def _():
            out_ref[0, :, :LANES] = total[slot, :half, :]
            out_ref[0, :, LANES:] = total[slot, half:, :]

        @pl.when(p >= outer)
        def _():
            swap_copy(p - outer).wait_recv()
            came = swap_in[lax.rem(p - outer, 8)].astype(F32)

            @pl.when(p < gains)
            def _():
                own = total[slot, pl.ds(pl.multiple_of(mp * half, half), half), :]
                first = jnp.where(mp == 0, own, came)
                second = jnp.where(mp == 0, came, own)
                for tile in (0, 1):
                    lanes = slice(128 * tile, 128 * tile + 128)
                    left, right = split_lanes(first[:, lanes], second[:, lanes])
                    out_ref[0, :, 256 * tile : 256 * tile + 128] = left
                    out_ref[0, :, 256 * tile + 128 : 256 * tile + 256] = right

            @pl.when(p == gains)
            def _():
                gain_out[...] = total[slot, 0:8, 0:128] + came[0:8, 0:128]

    @pl.when(step == chunks + Z_LAG + SWAP_LAG - 1)
    def _():
        for spot in range(half_blocks):
            half_copy(spot).wait()
        for index in range(gains - outer - 1, gains - outer + 1):
            swap_copy(index).wait_send()
        dot_copy.wait()


def mixer_call(
    left_in, grad_pre, left_out, right_out, gain_parts, tokens, inverse, weights, dots, collective
):
    _, rows, channels = grad_pre.shape
    full = right_out.shape[1]
    block, half = full // 16, channels // 16
    full_blocks, across = full // LANES, channels // LANES
    outer, inner = full_blocks // 2, 3 * across
    chunks = outer + inner + 1
    any_space = pl.BlockSpec(memory_space=pl.ANY)
    dma = pltpu.SemaphoreType.DMA
    part = jax.ShapeDtypeStruct((rows, full // 2), BF)

    def out_place(q):
        p = jnp.clip(q - Z_LAG - SWAP_LAG, 0, outer + inner - 1)
        inside = jnp.maximum(p - outer, 0)
        return (
            jnp.where(p < outer, 3, inside // across), 0, jnp.where(p < outer, p, lax.rem(inside, across)))

    out, gains, half_own, _, half_came, dot_came = pl.pallas_call(
        functools.partial(mixer_kernel, full_blocks),
        grid=(chunks + Z_LAG + SWAP_LAG,),
        in_specs=[
            any_space, any_space,
            fixed((DEPTH, 2, 2, half, rows)), fixed(right_out.shape), fixed(gain_parts.shape),
            any_space, fixed(inverse.shape), any_space, any_space,
        ],
        out_specs=[
            pl.BlockSpec((1, half, 2 * LANES), out_place),
            pl.BlockSpec((8, 128), lambda q: (0, 0)),
        ] + [any_space] * 4,
        out_shape=[
            jax.ShapeDtypeStruct((4, half, full), F32), jax.ShapeDtypeStruct((8, 128), F32),
            part, part, part, jax.ShapeDtypeStruct(dots.shape, F32),
        ],
        scratch_shapes=[
            pltpu.VMEM((DEPTH, 2, 2, block, rows), BF),
            pltpu.VMEM(grad_pre.shape, BF),
            dma((2,)),
            pltpu.VMEM((3, LANES, channels), BF),
            pltpu.VMEM((rows, LANES), BF),
            pltpu.VMEM((16, 8, 128), F32),
            pltpu.VMEM((DEPTH, 2, block, LANES), F32),
            pltpu.VMEM((4, block, LANES), F32),
            pltpu.VMEM((2, half, LANES), BF),
            pltpu.VMEM((8, half, LANES), BF),
            pltpu.VMEM((2, rows, LANES), BF),
            dma((2,)), dma((2,)), dma((full_blocks // 2,)), dma((full_blocks // 2,)),
            dma((2,)), dma((8,)), dma((2,)),
            *scatter_scratch(block, LANES),
        ],
        compiler_params=pltpu.CompilerParams(
            collective_id=collective, has_side_effects=True, vmem_limit_bytes=VMEM_LIMIT),
        cost_estimate=pl.CostEstimate(
            flops=14 * full * rows * channels, bytes_accessed=16 * full * channels, transcendentals=0),
    )(
        left_in, grad_pre, left_out, right_out, gain_parts, tokens, inverse, weights, dots,
    )
    return out, gains, half_own.astype(F32) + half_came.astype(F32), dot_came


def transpose_kernel(in_ref, out_ref):
    turned = in_ref[...].T
    out_ref[...] = turned.reshape(out_ref.shape)


def owner_rows(value, owners=2):
    rows, width = value.shape
    block = width // 16
    return pl.pallas_call(
        transpose_kernel,
        grid=(2 * DEPTH,),
        in_specs=[pl.BlockSpec((rows, owners * block), lambda q: (0, q))],
        out_specs=pl.BlockSpec((1, 1, owners, block, rows), lambda q: (q // 2, lax.rem(q, 2), 0, 0, 0)),
        out_shape=jax.ShapeDtypeStruct((DEPTH, 2, owners, block, rows), value.dtype),
        compiler_params=pltpu.CompilerParams(vmem_limit_bytes=VMEM_LIMIT),
        cost_estimate=pl.CostEstimate(flops=0, bytes_accessed=4 * rows * width, transcendentals=0),
    )(value)


def middle_back_kernel(
    sum_own_ref, sum_came_ref, middle_ref, cot_ref, tokens_ref, weight_ref, gain_ref, mixer_ref,
    grad_own_ref, low_ref, mean_ref, gated_ref, gain_grad_ref,
):
    rows, full = middle_ref.shape
    part = full // 2
    middle = middle_ref[...]
    inverse = lax.rsqrt(jnp.mean(middle * middle, axis=-1, keepdims=True) + EPSILON)
    unit = middle * inverse
    grad_normed = sum_own_ref[...].astype(F32) + sum_came_ref[...].astype(F32)
    product = grad_normed * unit
    before = jnp.where(pl.program_id(0) == 0, 0.0, gain_grad_ref[...])
    gain_grad_ref[...] = before + jnp.sum(product, axis=0, keepdims=True)
    dots = jnp.mean(product * gain_ref[...], axis=-1, keepdims=True)
    back = cot_ref[...].astype(F32) * weight_ref[...]
    grad = back + inverse * (grad_normed * gain_ref[...] - unit * dots)
    first = lax.axis_index("mp") == 0
    grad_own_ref[...] = jnp.where(first, grad[:, :part], grad[:, part:])
    low = grad.astype(BF)
    low_ref[...] = low
    branch = middle - tokens_ref[...].astype(F32)
    mean_ref[...] = jnp.mean(low.astype(F32) * branch, axis=-1, keepdims=True)
    gated_ref[...] = lax.dot_general(
        low, mixer_ref[...], (((1,), (1,)), ((), ())), preferred_element_type=F32)


def middle_back(sum_own, sum_came, middle, cot, tokens, weight, gain, mixer_out):
    rows, full = middle.shape
    channels = mixer_out.shape[0]
    step = 224 if rows % 224 == 0 else rows
    line = lambda width: pl.BlockSpec((step, width), lambda r: (r, 0))
    shape = jax.ShapeDtypeStruct
    return pl.pallas_call(
        middle_back_kernel,
        grid=(rows // step,),
        in_specs=[line(full)] * 5 + [line(1), fixed((1, full)), fixed(mixer_out.shape)],
        out_specs=[
            line(full // 2), line(full), line(1), line(channels),
            pl.BlockSpec((1, full), lambda r: (0, 0)),
        ],
        out_shape=[
            shape((rows, full // 2), F32), shape((rows, full), BF), shape((rows, 1), F32),
            shape((rows, channels), F32), shape((1, full), F32),
        ],
        compiler_params=pltpu.CompilerParams(vmem_limit_bytes=VMEM_LIMIT),
        cost_estimate=pl.CostEstimate(
            flops=2 * rows * full * channels, bytes_accessed=rows * full * 20, transcendentals=0),
    )(sum_own, sum_came, middle, cot, tokens, weight, gain[None], mixer_out)


def glu_update_kernel(scale, act_ref, up_ref, out_ref, *refs):
    in_refs, down_refs, in_new, down_new = refs[:3], refs[3:6], refs[-6:-3], refs[-3:]
    count = STEP_NUMBER
    for at, grad_ref in ((0, act_ref), (1, up_ref)):
        new = adamw_update(
            *(ref[at] for ref in in_refs), grad_ref[0].astype(F32) * scale, count, MATRIX_RATE, DECAY_RATE)
        for ref, value in zip(in_new, new):
            ref[at] = value
    new = adamw_update(
        *(ref[...] for ref in down_refs), out_ref[0].astype(F32).T * scale, count, MATRIX_RATE, DECAY_RATE)
    for ref, value in zip(down_new, new):
        ref[...] = value


def glu_update(sums, sum_place, first, blocks, ins, downs, scale, earlier=()):
    rows, lanes = ins[0].shape[1], LANES
    sum_spec = lambda kind: pl.BlockSpec((1, rows, lanes), lambda q: sum_place(kind, q))
    in_spec = pl.BlockSpec((2, rows, lanes), lambda q: (0, 0, q + first))
    down_spec = pl.BlockSpec((lanes, rows), lambda q: (q + first, 0))
    new = pl.pallas_call(
        functools.partial(glu_update_kernel, scale),
        grid=(blocks,),
        in_specs=[sum_spec(0), sum_spec(1), sum_spec(2)] + [in_spec] * 3 + [down_spec] * 3
        + [pl.BlockSpec(memory_space=pl.ANY)] * len(earlier),
        out_specs=[in_spec] * 3 + [down_spec] * 3,
        out_shape=[jax.ShapeDtypeStruct(ins[0].shape, F32)] * 3 + [jax.ShapeDtypeStruct(downs[0].shape, F32)] * 3,
        input_output_aliases={9 + at: at for at in range(len(earlier))},
        compiler_params=pltpu.CompilerParams(vmem_limit_bytes=VMEM_LIMIT),
        cost_estimate=pl.CostEstimate(
            flops=60 * rows * lanes * blocks, bytes_accessed=84 * rows * lanes * blocks,
            transcendentals=6 * rows * lanes * blocks),
    )(sums, sums, sums, *ins, *downs, *earlier)
    return tuple(new)


ITEMS = 4


def split_lanes(first, second):
    low = lax.broadcasted_iota(jnp.int32, first.shape, 1) < 64
    return (
        jnp.where(low, first, pltpu.roll(second, 64, 1)),
        jnp.where(low, pltpu.roll(first, 64, 1), second),
    )


def gather_kernel(mixer_ref, gain_ref, lengths_ref, domains_ref, glu_in_ref, glu_out_ref, cot_ref,
                  all_in, all_out, all_small, cot_full, glu_low,
                  in_ref, out_ref, small_ref, right_send, left_send,
                  z_recv, x_send, x_recv, core_send, core_recv, y_send, y_recv, local_sem):
    z, x, core = device_place()
    mp = lax.axis_index("mp")
    barrier = pltpu.get_barrier_semaphore()
    right, left = lax.rem(z + 1, DEPTH), lax.rem(z + DEPTH - 1, DEPTH)
    dp = lax.axis_index("dp")
    for target in (
        device_at(right, x, core), device_at(left, x, core), device_at(z, 1 - x, core),
        device_at(z, x, 1 - core), (dp, 1 - mp),
    ):
        pl.semaphore_signal(barrier, 1, device_id=target, device_id_type=MESH_ID)
    for kind in range(3):
        for tile in range(in_ref.shape[3] // 128):
            first = mixer_ref[kind, :, 256 * tile : 256 * tile + 128]
            second = mixer_ref[kind, :, 256 * tile + 128 : 256 * tile + 256]
            for side, value in enumerate(split_lanes(first, second)):
                in_ref[side, kind, :, 128 * tile : 128 * tile + 128] = value.astype(BF)
    out_ref[...] = mixer_ref[3].astype(BF)
    lane = lax.broadcasted_iota(jnp.int32, (1, 128), 1)
    live = jnp.zeros((1, 128), F32)
    for batch in range(lengths_ref.shape[0]):
        count = lengths_ref[batch : batch + 1, :].astype(F32)
        live = live + jnp.where(lane == domains_ref[batch : batch + 1, :], count, 0.0)
    small_ref[...] = jnp.zeros_like(small_ref)
    small_ref[0:3, 0:64] = gain_ref[...].astype(BF).astype(F32)
    small_ref[3:4, :] = live
    pl.semaphore_wait(barrier, 5)

    def spot(item, zs, xs, cs, side=None):
        if item == 0:
            return all_in.at[:, zs, xs, cs, mp if side is None else side]
        if item == 1:
            return all_out.at[zs, xs, cs]
        if item == 2:
            return all_in.at[:, zs, xs, cs, 1 - mp]
        return all_small.at[zs, xs, cs]

    def own(item):
        if item == 0:
            return in_ref.at[mp]
        if item == 1:
            return out_ref
        return spot(item, z, x, core)

    def copy(item, zs, xs, target, send, recv, source=None):
        return pltpu.make_async_remote_copy(
            spot(item, zs, xs, core) if source is None else source, spot(item, zs, xs, core),
            send, recv, device_id=target, device_id_type=MESH_ID)

    def right_copy(item, zs, source=None):
        return copy(item, zs, x, device_at(right, x, core), right_send.at[zs, item], z_recv.at[zs, item], source)

    def left_copy(item, zs, source=None):
        return copy(item, zs, x, device_at(left, x, core), left_send.at[zs, item], z_recv.at[zs, item], source)

    def x_copy(item, zs, source=None):
        return copy(item, zs, x, device_at(z, 1 - x, core), x_send.at[zs, item], x_recv.at[zs, item], source)

    def core_copy(item, zs, xs, source=None):
        return copy(item, zs, xs, device_at(z, x, 1 - core), core_send.at[zs, xs, item], core_recv.at[zs, xs, item], source)

    y_copies = [
        pltpu.make_async_remote_copy(
            in_ref.at[1 - mp], all_in.at[:, z, x, core, mp], y_send.at[0], y_recv.at[0],
            device_id=(dp, 1 - mp), device_id_type=MESH_ID),
        pltpu.make_async_remote_copy(
            small_ref, all_small.at[z, x, core, mp], y_send.at[1], y_recv.at[1],
            device_id=(dp, 1 - mp), device_id_type=MESH_ID),
    ]
    locals_ = [
        pltpu.make_async_copy(in_ref.at[mp], spot(0, z, x, core), local_sem.at[0]),
        pltpu.make_async_copy(out_ref, spot(1, z, x, core), local_sem.at[1]),
        pltpu.make_async_copy(small_ref, all_small.at[z, x, core, mp], local_sem.at[2]),
    ]
    cot_lanes = pl.ds(pl.multiple_of(mp * cot_ref.shape[1], 128), cot_ref.shape[1])
    cot_local = pltpu.make_async_copy(cot_ref, cot_full.at[:, cot_lanes], local_sem.at[3])
    cot_copy = pltpu.make_async_remote_copy(
        cot_ref, cot_full.at[:, cot_lanes], y_send.at[2], y_recv.at[2],
        device_id=(dp, 1 - mp), device_id_type=MESH_ID)
    for one in y_copies:
        one.start()
    locals_[2].start()

    for item in range(ITEMS):
        if item == 2:
            y_copies[0].wait_recv()
        if item == 3:
            y_copies[1].wait_recv()
            locals_[2].wait()
        source = own(item)

        @pl.when(z < DEPTH - 1)
        def _():
            right_copy(item, z, source).start()

        @pl.when(z > 0)
        def _():
            left_copy(item, z, source).start()

        x_copy(item, z, source).start()
        core_copy(item, z, x, source).start()
    locals_[0].start()
    locals_[1].start()
    cot_copy.start()
    cot_local.start()
    glu_low[0:2] = glu_in_ref[...].astype(BF)
    for tile in range(glu_out_ref.shape[0] // 128):
        lanes = slice(128 * tile, 128 * tile + 128)
        glu_low[2, :, lanes] = glu_out_ref[lanes, :].T.astype(BF)

    def from_x(item, zs):
        pltpu.make_async_remote_copy(
            spot(item, zs, 1 - x, core), spot(item, zs, 1 - x, core), x_send.at[zs, item],
            x_recv.at[zs, item], device_id=device_at(z, 1 - x, core), device_id_type=MESH_ID).wait_recv()
        core_copy(item, zs, 1 - x).start()

    for hop in range(1, DEPTH + 1):
        for item in range(ITEMS):
            if hop < DEPTH:
                @pl.when(z >= hop)
                def _():
                    zs = z - hop
                    right_copy(item, zs).wait_recv()

                    @pl.when(z < DEPTH - 1)
                    def _():
                        right_copy(item, zs).start()

                    x_copy(item, zs).start()
                    core_copy(item, zs, x).start()

                @pl.when(z + hop < DEPTH)
                def _():
                    zs = z + hop
                    left_copy(item, zs).wait_recv()

                    @pl.when(z > 0)
                    def _():
                        left_copy(item, zs).start()

                    x_copy(item, zs).start()
                    core_copy(item, zs, x).start()
            if hop == 1:
                from_x(item, z)
            else:
                @pl.when(z >= hop - 1)
                def _():
                    from_x(item, z - (hop - 1))

                @pl.when(z + hop - 1 < DEPTH)
                def _():
                    from_x(item, z + (hop - 1))

    for item in range(ITEMS):
        for zs in range(DEPTH):
            @pl.when((z >= zs) & (z < DEPTH - 1))
            def _():
                right_copy(item, zs).wait_send()

            @pl.when((z <= zs) & (z > 0))
            def _():
                left_copy(item, zs).wait_send()

            x_copy(item, zs).wait_send()
            for xs in range(2):
                core_copy(item, zs, xs).wait()
    for one in y_copies:
        one.wait_send()
    locals_[0].wait()
    locals_[1].wait()
    cot_local.wait()
    cot_copy.wait_send()
    pltpu.make_async_remote_copy(
        cot_ref, cot_full.at[:, pl.ds(pl.multiple_of((1 - mp) * cot_ref.shape[1], 128), cot_ref.shape[1])],
        y_send.at[2], y_recv.at[2], device_id=(dp, 1 - mp), device_id_type=MESH_ID).wait_recv()


def gather_call(mixer, gain, lengths, domains, glu_in, glu_out, cot, collective):
    _, own_rows, full = mixer.shape
    channels = full // 2
    dma = pltpu.SemaphoreType.DMA
    any_space = pl.BlockSpec(memory_space=pl.ANY)
    in_vmem = pl.BlockSpec(memory_space=pltpu.VMEM)
    _, glu_rows, hidden = glu_in.shape
    return pl.pallas_call(
        gather_kernel,
        in_specs=[in_vmem] * 6 + [any_space],
        out_specs=[any_space] * 4 + [in_vmem],
        out_shape=[
            jax.ShapeDtypeStruct((3, DEPTH, 2, 2, 2, own_rows, channels), BF),
            jax.ShapeDtypeStruct((DEPTH, 2, 2, own_rows, full), BF),
            jax.ShapeDtypeStruct((DEPTH, 2, 2, 2, 8, 128), F32),
            jax.ShapeDtypeStruct((cot.shape[0], 2 * cot.shape[1]), BF),
            jax.ShapeDtypeStruct((3, glu_rows, hidden), BF),
        ],
        scratch_shapes=[
            pltpu.VMEM((2, 3, own_rows, channels), BF),
            pltpu.VMEM((own_rows, full), BF),
            pltpu.VMEM((8, 128), F32),
            dma((DEPTH, ITEMS)), dma((DEPTH, ITEMS)), dma((DEPTH, ITEMS)), dma((DEPTH, ITEMS)),
            dma((DEPTH, ITEMS)), dma((DEPTH, 2, ITEMS)), dma((DEPTH, 2, ITEMS)), dma((3,)), dma((3,)), dma((4,)),
        ],
        compiler_params=pltpu.CompilerParams(
            collective_id=collective, has_side_effects=True, vmem_limit_bytes=VMEM_LIMIT),
        cost_estimate=pl.CostEstimate(flops=0, bytes_accessed=300_000_000, transcendentals=0),
    )(mixer, gain, lengths, domains, glu_in, glu_out, cot)


def shards(
    tokens,
    cotangent,
    lengths,
    domains,
    lower_bound,
    mixer_master,
    mixer_first,
    mixer_second,
    glu_in_master,
    glu_in_first,
    glu_in_second,
    glu_out_master,
    glu_out_first,
    glu_out_second,
    gain_master,
    gain_first,
    gain_second,
):
    batches, _, length, full = tokens.shape
    rows = batches * length
    groups = lax.axis_size("dp")
    narrow = lax.axis_size("mp")
    place = lax.axis_index("mp")
    own_rows = mixer_master.shape[1]
    channels = groups * own_rows
    part = full // narrow
    quick = groups == 16 and narrow == 2 and own_rows == 64

    domain_ids = jnp.arange(NDOM, dtype=jnp.int32)
    member = (domains[..., 0][..., None] == domain_ids).astype(F32)
    cot_part = cotangent.reshape(rows, part)
    if quick:
        mixer_in, mixer_out, small, cot_full, glu_low = gather_call(
            mixer_master, gain_master, lengths, domains[..., 0], glu_in_master, glu_out_master, cot_part, 2
        )
        mixer_in = mixer_in.reshape(3, full, channels)
        mixer_out = mixer_out.reshape(channels, full)
        small = small.reshape(groups, narrow, 8, 128)
        gain_full = small[:, :, :3, :own_rows].transpose(2, 0, 1, 3).reshape(3, full)
        counts = jnp.sum(small[:, 0, 3, :NDOM], axis=0)
    else:
        gain_full = lax.all_gather(
            gain_master.astype(BF), ("dp", "mp"), axis=1, tiled=True
        ).astype(F32)
        mixer_low = mixer_master.astype(BF)
        in_blocks = mixer_low[:3].reshape(3, own_rows, groups, narrow, own_rows)
        in_blocks = in_blocks.transpose(3, 0, 1, 2, 4).reshape(narrow, 3, own_rows, channels)
        in_rows = mp_swap(in_blocks).transpose(1, 0, 2, 3).reshape(3, narrow * own_rows, channels)
        mixer_in = lax.all_gather(in_rows, "dp", axis=1, tiled=True)
        mixer_out = lax.all_gather(mixer_low[3], "dp", axis=0, tiled=True)
        counts = lax.psum(jnp.sum(member * lengths.astype(F32)[..., None], axis=(0, 1)), "dp")
        cot_full = mp_gather(cot_part)
        glu_low = jnp.concatenate([glu_in_master.astype(BF), glu_out_master.astype(BF).T[None]])
    glu = lax.all_gather(glu_low, "dp", axis=1, tiled=True)

    seq_weight = jnp.sum(counts) / (NDOM * jnp.sum(member * counts, axis=-1))
    positions = jnp.arange(length, dtype=jnp.int32)
    token_weight = jnp.where(positions[None, :] < lengths[:, :1], seq_weight[:, :1], 0.0)
    token_weight = token_weight.reshape(rows, 1)

    own_channels = lambda v: lax.dynamic_index_in_dim(
        v.reshape(groups, narrow, own_rows), place, 1, keepdims=False
    ).reshape(channels)
    bound = own_channels(lower_bound)
    state_gain = own_channels(gain_full[1])

    token_rows = tokens.reshape(rows, full)
    seq_in = token_rows.astype(F32)
    inverse_in = inverse_rms(seq_in)
    unit_in = seq_in * inverse_in
    normed_in = (unit_in * gain_full[0]).astype(BF)
    pre = jnp.einsum("td,kde->kte", normed_in, mixer_in, preferred_element_type=F32)
    pre = pre.reshape(3, batches, length, channels)
    states, raw, square = scan_forward(pre, bound, state_gain)
    square = mp_sum_wide(square.reshape(rows, 1))
    inverse_state = lax.rsqrt(square / full + EPSILON)
    mixed = jnp.dot(raw.reshape(rows, channels), mixer_out, preferred_element_type=F32)
    back_low = (cot_full.astype(F32) * token_weight).astype(BF)
    gated_out = (raw.reshape(rows, channels).astype(F32) * inverse_state).astype(BF)
    if quick:
        mixed = mixed.astype(BF)
        came, left_back, left_in, left_out, token_weight, inverse_in = lax.optimization_barrier(
            (
                partner_swap(mixed), owner_rows(back_low), owner_rows(normed_in), owner_rows(gated_out),
                token_weight, inverse_in,
            )
        )
        mixed = mixed.astype(F32) + came.astype(F32)
    else:
        mixed = mp_sum(mixed)
    branch_mix = inverse_state * mixed
    middle = seq_in + branch_mix
    inverse_mid = inverse_rms(middle)
    unit_mid = middle * inverse_mid
    normed_mid = (unit_mid * gain_full[2]).astype(BF)

    across = (((1,), (1,)), ((), ()))
    down = (((0,), (0,)), ((), ()))
    dot = functools.partial(lax.dot_general, preferred_element_type=F32)
    if quick:
        glu_sums, glu_tail, sum_own, sum_came, half_own, half_send = glu_call(normed_mid, back_low, left_back, glu, 0)
        half_came = partner_swap(half_send)
        glu_tail = lax.psum_scatter(glu_tail, "dp", scatter_dimension=1, tiled=True)
    else:
        pre_act = jnp.dot(normed_mid, glu[0], preferred_element_type=F32)
        pre_up = jnp.dot(normed_mid, glu[1], preferred_element_type=F32)
        grad_hidden = jnp.dot(back_low, glu[2], preferred_element_type=F32)
        act_part = jax.nn.silu(pre_act)
        hidden = (act_part * pre_up).astype(BF)
        grad_act = (grad_hidden * pre_up * silu_slope(pre_act)).astype(BF)
        grad_up = (grad_hidden * act_part).astype(BF)
        grad_normed = mp_sum(dot(grad_act, glu[0], across) + dot(grad_up, glu[1], across))
        glu_grad = jnp.stack(
            [dot(normed_mid, grad_act, down), dot(normed_mid, grad_up, down), dot(back_low, hidden, down)]
        ).astype(BF)
        glu_own = lax.psum_scatter(glu_grad, "dp", scatter_dimension=1, tiled=True).astype(F32)
        branch = mp_scatter(dot(hidden, glu[2], across))
    scale = 1.0 / (batches * groups * tokens.shape[1])
    own_features = lambda v: lax.dynamic_slice_in_dim(v, place * part, part, v.ndim - 1)
    if quick:
        grad_middle_own, middle_low, state_mean, grad_gated, gain_mid = middle_back(
            sum_own, sum_came, middle, cot_full, token_rows, token_weight, gain_full[2], mixer_out
        )
        gain_mid = gain_mid[0]
    else:
        inverse_mid = inverse_rms(middle)
        unit_mid = middle * inverse_mid
        gain_mid = jnp.sum(grad_normed * unit_mid, axis=0)
        scaled_mid = grad_normed * gain_full[2]
        back = cot_full.astype(F32) * token_weight
        grad_middle = back + inverse_mid * (
            scaled_mid - unit_mid * jnp.mean(scaled_mid * unit_mid, axis=-1, keepdims=True)
        )
        grad_middle_own = own_features(grad_middle)
        middle_low = grad_middle.astype(BF)
        state_mean = jnp.mean(middle_low.astype(F32) * branch_mix, axis=-1, keepdims=True)
        grad_gated = dot(middle_low, mixer_out, across)
    by_batch = lambda v: v.reshape(batches, length, v.shape[-1])
    grad_pre, gain_state, pre_dot = scan_backward(
        pre, states, by_batch(grad_gated), by_batch(inverse_state), by_batch(state_mean), bound, state_gain
    )
    if quick:
        scattered = glu_in_master.shape[2] // LANES - TAIL
        glu_ins = (glu_in_master, glu_in_first, glu_in_second)
        glu_downs = (glu_out_master, glu_out_first, glu_out_second)
        glu_new = glu_update(
            glu_sums, lambda kind, q: (3 * q + kind, 0, 0), 0, scattered, glu_ins, glu_downs, scale
        )
        branch = half_own.astype(F32) + half_came.astype(F32)
        layer_out = (own_features(middle) + branch).astype(BF)
        layer_out, grad_pre, glu_new = lax.optimization_barrier((layer_out, grad_pre, glu_new))
    grad_pre = grad_pre.reshape(3, rows, channels)
    gain_state = jnp.sum(gain_state, axis=0).reshape(groups, 1, own_rows)
    gain_state = lax.dynamic_update_slice_in_dim(
        jnp.zeros((groups, narrow, own_rows), F32), gain_state, place, 1
    )
    device = lax.axis_index("dp") * narrow + place
    if quick:
        gain_parts = jnp.stack(
            [
                jnp.zeros((groups, narrow * own_rows), F32),
                gain_state.reshape(groups, narrow * own_rows),
                0.5 * gain_mid.reshape(groups, narrow * own_rows),
            ],
            axis=1,
        )
        gain_parts = jnp.pad(gain_parts, ((0, 0), (0, 5), (0, 0)))
        pre_dot = pre_dot.reshape(-1, 128)
        mixer_own, gain_own, grad_normed_in, dot_came = mixer_call(
            left_in, grad_pre, left_out, middle_low, gain_parts, token_rows, inverse_in, mixer_in, pre_dot, 1
        )
        in_mean = (pre_dot + dot_came).reshape(rows, 1) / full
        gain_own = lax.dynamic_slice_in_dim(gain_own[:3], place * own_rows, own_rows, 1)
    else:
        grad_mix_out = dot(gated_out, middle_low, down).astype(BF)
        grad_mix_in = jnp.einsum("td,kte->kde", normed_in, grad_pre, preferred_element_type=F32)
        in_own = lax.psum_scatter(grad_mix_in.astype(BF), "dp", scatter_dimension=1, tiled=True)
        out_own = lax.psum_scatter(grad_mix_out, "dp", scatter_dimension=0, tiled=True)
        in_own = mp_swap(in_own.reshape(3, narrow, own_rows, channels).transpose(1, 0, 2, 3))
        in_own = in_own.reshape(narrow, 3, own_rows, groups, own_rows).transpose(1, 2, 3, 0, 4)
        grad_normed_in = jnp.einsum("kte,kde->td", grad_pre, mixer_in, preferred_element_type=F32)
        gain_in = jnp.sum(grad_normed_in * unit_in, axis=0)
        grad_normed_in = mp_scatter(grad_normed_in)
        gain_rows = jnp.stack([gain_in, gain_state.reshape(full), gain_mid / narrow])
        gain_total = lax.psum(gain_rows, ("dp", "mp"))
        gain_own = lax.dynamic_slice_in_dim(gain_total, device * own_rows, own_rows, 1)
        in_mean = mp_sum_wide(pre_dot.reshape(rows, 1)) / full
        in_own = in_own.reshape(3, own_rows, full)
        mixer_own = jnp.concatenate([in_own, out_own[None]]).astype(F32)
    unit_in_own = own_features(token_rows).astype(F32) * inverse_in
    grad_seq = grad_middle_own + inverse_in * (
        grad_normed_in * own_features(gain_full[0]) - unit_in_own * in_mean
    )
    grad_tokens = grad_seq.astype(BF)
    if not quick:
        layer_out = (own_features(middle) + branch).astype(BF)

    update = functools.partial(adamw_update, count=STEP_NUMBER)
    mixer_new = update(
        mixer_master, mixer_first, mixer_second, mixer_own * scale, rate=MATRIX_RATE, decay=DECAY_RATE
    )
    gain_new = update(
        gain_master, gain_first, gain_second, gain_own * scale, rate=GAIN_RATE, decay=0.0
    )
    if quick:
        glu_new = glu_update(
            glu_tail, lambda kind, q: (kind, 0, q), scattered, TAIL, glu_ins, glu_downs, scale, glu_new
        )
    else:
        glu_in_new = update(
            glu_in_master, glu_in_first, glu_in_second, glu_own[:2] * scale,
            rate=MATRIX_RATE, decay=DECAY_RATE,
        )
        glu_out_new = update(
            glu_out_master, glu_out_first, glu_out_second, glu_own[2].T * scale,
            rate=MATRIX_RATE, decay=DECAY_RATE,
        )
        glu_new = (*glu_in_new, *glu_out_new)
    return (
        layer_out.reshape(batches, 1, length, part),
        grad_tokens.reshape(batches, 1, length, part),
        *mixer_new,
        *glu_new,
        *gain_new,
    )


def solution(mesh):
    weights = (
        [P(None, ("dp", "mp"), None)] * 3
        + [P(None, "dp", "mp")] * 3
        + [P("mp", "dp")] * 3
        + [P(None, ("dp", "mp"))] * 3
    )
    in_specs = (
        P(None, "dp", None, None),
        P(None, "dp", None, "mp"),
        P(None, "dp"),
        P(None, "dp", None),
        P(),
        *weights,
    )
    out_specs = (P(None, "dp", None, "mp"), P(None, "dp", None, "mp"), *weights)
    return jax.shard_map(shards, mesh=mesh, in_specs=in_specs, out_specs=out_specs, check_vma=False)
```

```python
import functools

import jax
import jax.numpy as jnp
from jax import lax
from jax.experimental import pallas as pl
from jax.experimental.pallas import tpu as pltpu
from jax.sharding import PartitionSpec as P

NDOM = 8

EPSILON = 1e-06
BETA_ONE = 0.9
BETA_TWO = 0.95
ADAM_EPSILON = 1e-08
DECAY_RATE = 0.1
MATRIX_RATE = 0.06
GAIN_RATE = 0.5
STEP_NUMBER = 3.0

BF = jnp.bfloat16
F32 = jnp.float32
VMEM_LIMIT = 56 * 1024 * 1024


def inverse_rms(values):
    return lax.rsqrt(jnp.mean(values * values, axis=-1, keepdims=True) + EPSILON)


def silu_slope(values):
    sigma = jax.nn.sigmoid(values)
    return sigma * (1.0 + values * (1.0 - sigma))


def adamw_update(master, first, second, gradient, count, rate, decay):
    first_new = BETA_ONE * first + (1.0 - BETA_ONE) * gradient
    second_new = BETA_TWO * second + (1.0 - BETA_TWO) * gradient * gradient
    first_hat = first_new / (1.0 - BETA_ONE**count)
    second_hat = second_new / (1.0 - BETA_TWO**count)
    master_new = master - rate * (
        first_hat / (jnp.sqrt(second_hat) + ADAM_EPSILON) + decay * master
    )
    return (master_new, first_new, second_new)


def partner_swap(value):
    return lax.ppermute(value, "mp", [(0, 1), (1, 0)])


def mp_sum(part):
    low = part.astype(BF)
    if lax.axis_size("mp") == 2:
        return low.astype(F32) + partner_swap(low).astype(F32)
    return lax.psum(low.astype(F32), "mp")


def mp_sum_wide(part):
    if lax.axis_size("mp") == 2:
        return part + partner_swap(part)
    return lax.psum(part, "mp")


def mp_scatter(part):
    if lax.axis_size("mp") == 2:
        half = part.shape[1] // 2
        place = lax.axis_index("mp")
        own = lax.dynamic_slice_in_dim(part, place * half, half, 1)
        other = lax.dynamic_slice_in_dim(part, (1 - place) * half, half, 1)
        return own.astype(BF).astype(F32) + partner_swap(other.astype(BF)).astype(F32)
    return lax.psum_scatter(part.astype(BF), "mp", scatter_dimension=1, tiled=True).astype(F32)


def mp_swap(pieces):
    if lax.axis_size("mp") == 2:
        place = lax.axis_index("mp")
        own = lax.dynamic_index_in_dim(pieces, place, 0, keepdims=False)
        came = partner_swap(lax.dynamic_index_in_dim(pieces, 1 - place, 0, keepdims=False))
        first = place == 0
        return jnp.stack([jnp.where(first, own, came), jnp.where(first, came, own)])
    return lax.all_to_all(pieces, "mp", 0, 0, tiled=False)


def mp_gather(part):
    if lax.axis_size("mp") == 2:
        place = lax.axis_index("mp")
        came = partner_swap(part)
        first = place == 0
        return jnp.concatenate([jnp.where(first, part, came), jnp.where(first, came, part)], axis=1)
    return lax.all_gather(part, "mp", axis=1, tiled=True)


SUB_ROWS = 8
TILE_ROWS = 64


def channel_block(width):
    return 512 if width % 512 == 0 else width


def scan_rows(total, decay, carry):
    row = lax.broadcasted_iota(jnp.int32, total.shape, 0)
    shift = 1
    while shift < SUB_ROWS:
        keep = row >= shift
        total = total + decay * jnp.where(keep, pltpu.roll(total, shift, 0), 0.0)
        decay = decay * jnp.where(keep, pltpu.roll(decay, shift, 0), 1.0)
        shift *= 2
    return total + decay * carry


def scan_rows_back(total, decay, carry):
    row = lax.broadcasted_iota(jnp.int32, total.shape, 0)
    shift = 1
    while shift < SUB_ROWS:
        keep = row < SUB_ROWS - shift
        total = total + decay * jnp.where(keep, pltpu.roll(total, SUB_ROWS - shift, 0), 0.0)
        decay = decay * jnp.where(keep, pltpu.roll(decay, SUB_ROWS - shift, 0), 1.0)
        shift *= 2
    return total + decay * carry


def scan_forward_kernel(pre_ref, bound_ref, gain_ref, states_ref, raw_ref, square_ref):
    length, width = states_ref.shape[1], states_ref.shape[2]
    bound = bound_ref[...]
    gain = gain_ref[...]
    first_block = pl.program_id(1) == 0

    def step(index, carry):
        rows = pl.ds(pl.multiple_of(index * TILE_ROWS, TILE_ROWS), TILE_ROWS)
        forget = bound + (1.0 - bound) * jax.nn.sigmoid(pre_ref[1, 0, rows, :])
        total = (1.0 - forget) * jax.nn.silu(pre_ref[0, 0, rows, :])
        parts = []
        for low in range(0, TILE_ROWS, SUB_ROWS):
            part = scan_rows(total[low : low + SUB_ROWS], forget[low : low + SUB_ROWS], carry)
            carry = part[SUB_ROWS - 1 : SUB_ROWS]
            parts.append(part)
        states = jnp.concatenate(parts)
        states_ref[0, rows, :] = states
        raw = states * gain * jax.nn.silu(pre_ref[2, 0, rows, :])
        raw_ref[0, rows, :] = raw.astype(raw_ref.dtype)
        square = jnp.sum(states * states, axis=-1, keepdims=True)
        square_ref[0, rows, :] = square + jnp.where(first_block, 0.0, square_ref[0, rows, :])
        return carry

    lax.fori_loop(0, length // TILE_ROWS, step, jnp.zeros((1, width), F32))


def scan_forward(pre, bound, gain):
    _, batches, length, width = pre.shape
    block = channel_block(width)
    return pl.pallas_call(
        scan_forward_kernel,
        grid=(batches, width // block),
        in_specs=[
            pl.BlockSpec((3, 1, length, block), lambda b, c: (0, b, 0, c)),
            pl.BlockSpec((1, block), lambda b, c: (0, c)),
            pl.BlockSpec((1, block), lambda b, c: (0, c)),
        ],
        out_specs=[
            pl.BlockSpec((1, length, block), lambda b, c: (b, 0, c)),
            pl.BlockSpec((1, length, block), lambda b, c: (b, 0, c)),
            pl.BlockSpec((1, length, 1), lambda b, c: (b, 0, 0)),
        ],
        out_shape=[
            jax.ShapeDtypeStruct((batches, length, width), F32),
            jax.ShapeDtypeStruct((batches, length, width), BF),
            jax.ShapeDtypeStruct((batches, length, 1), F32),
        ],
        compiler_params=pltpu.CompilerParams(vmem_limit_bytes=VMEM_LIMIT),
        cost_estimate=pl.CostEstimate(
            flops=batches * length * width * 40,
            bytes_accessed=batches * length * width * 18,
            transcendentals=batches * length * width * 3,
        ),
    )(pre, bound[None], gain[None])


def scan_backward_kernel(
    pre_ref, states_ref, gated_ref, inverse_ref, mean_ref, bound_ref, gain_ref,
    grad_ref, gain_grad_ref, dot_ref,
):
    length, width = states_ref.shape[1], states_ref.shape[2]
    bound = bound_ref[...]
    gain = gain_ref[...]
    first_block = pl.program_id(1) == 0
    row = lax.broadcasted_iota(jnp.int32, (TILE_ROWS, width), 0)
    tiles = length // TILE_ROWS

    def step(index, carry):
        carried_next, forget_next, gain_sum = carry
        place = tiles - 1 - index
        rows = pl.ds(pl.multiple_of(place * TILE_ROWS, TILE_ROWS), TILE_ROWS)
        pre_input = pre_ref[0, 0, rows, :]
        pre_forget = pre_ref[1, 0, rows, :]
        pre_gate = pre_ref[2, 0, rows, :]
        states = states_ref[0, rows, :]
        inverse = inverse_ref[0, rows, :]
        grad_gated = gated_ref[0, rows, :]
        unit = states * inverse
        gate_sig = jax.nn.sigmoid(pre_gate)
        gate = pre_gate * gate_sig
        gain_sum = gain_sum + grad_gated * unit * gate
        scaled = grad_gated * gain
        grad_gate = (scaled * unit * (gate_sig * (1.0 + pre_gate * (1.0 - gate_sig)))).astype(BF)
        grad_ref[2, 0, rows, :] = grad_gate
        total = inverse * (scaled * gate - unit * mean_ref[0, rows, :])
        sigma = jax.nn.sigmoid(pre_forget)
        forget = bound + (1.0 - bound) * sigma
        decay = jnp.where(row == TILE_ROWS - 1, forget_next, pltpu.roll(forget, TILE_ROWS - 1, 0))
        parts = []
        for low in range(TILE_ROWS - SUB_ROWS, -1, -SUB_ROWS):
            part = scan_rows_back(
                total[low : low + SUB_ROWS], decay[low : low + SUB_ROWS], carried_next
            )
            carried_next = part[0:1]
            parts.insert(0, part)
        carried = jnp.concatenate(parts)
        before_rows = pl.ds(
            pl.multiple_of(jnp.maximum(place - 1, 0) * TILE_ROWS, TILE_ROWS), TILE_ROWS
        )
        before = states_ref[0, before_rows, :][TILE_ROWS - 1 : TILE_ROWS, :]
        before = jnp.where(place == 0, 0.0, before)
        earlier = jnp.where(row == 0, before, pltpu.roll(states, 1, 0))
        input_sig = jax.nn.sigmoid(pre_input)
        fresh = pre_input * input_sig
        slope = input_sig * (1.0 + pre_input * (1.0 - input_sig))
        grad_input = (carried * (1.0 - forget) * slope).astype(BF)
        grad_forget = (
            carried * (earlier - fresh) * (1.0 - bound) * sigma * (1.0 - sigma)
        ).astype(BF)
        grad_ref[0, 0, rows, :] = grad_input
        grad_ref[1, 0, rows, :] = grad_forget
        dots = (
            grad_input.astype(F32) * pre_input
            + grad_forget.astype(F32) * pre_forget
            + grad_gate.astype(F32) * pre_gate
        )
        dot = jnp.sum(dots, axis=-1, keepdims=True)
        dot_ref[0, rows, :] = dot + jnp.where(first_block, 0.0, dot_ref[0, rows, :])
        return carried_next, forget[0:1, :], gain_sum

    zero = jnp.zeros((1, width), F32)
    _, _, gain_sum = lax.fori_loop(
        0, tiles, step, (zero, zero, jnp.zeros((TILE_ROWS, width), F32))
    )
    gain_grad_ref[0] = jnp.sum(gain_sum, axis=0, keepdims=True)


def scan_backward(pre, states, grad_gated, inverse, mean, bound, gain):
    _, batches, length, width = pre.shape
    block = channel_block(width)
    whole = pl.BlockSpec((1, length, block), lambda b, c: (b, 0, c))
    column = pl.BlockSpec((1, length, 1), lambda b, c: (b, 0, 0))
    line = pl.BlockSpec((1, block), lambda b, c: (0, c))
    three = pl.BlockSpec((3, 1, length, block), lambda b, c: (0, b, 0, c))
    return pl.pallas_call(
        scan_backward_kernel,
        grid=(batches, width // block),
        in_specs=[three, whole, whole, column, column, line, line],
        out_specs=[
            three,
            pl.BlockSpec((1, 1, block), lambda b, c: (b, 0, c)),
            column,
        ],
        out_shape=[
            jax.ShapeDtypeStruct((3, batches, length, width), BF),
            jax.ShapeDtypeStruct((batches, 1, width), F32),
            jax.ShapeDtypeStruct((batches, length, 1), F32),
        ],
        compiler_params=pltpu.CompilerParams(vmem_limit_bytes=VMEM_LIMIT),
        cost_estimate=pl.CostEstimate(
            flops=batches * length * width * 80,
            bytes_accessed=batches * length * width * 28,
            transcendentals=batches * length * width * 3,
        ),
    )(pre, states, grad_gated, inverse, mean, bound[None], gain[None])


MESH_ID = pl.DeviceIdType.MESH
DEPTH = 4
LANES = 256
X_LAG = 4
Z_LAG = X_LAG + 2
SWAP_LAG = 2
TAIL = 2


def device_place():
    dp = lax.axis_index("dp")
    return dp // 4, lax.rem(dp // 2, 2), lax.rem(dp, 2)


def device_at(z, x, core):
    return (z * 4 + x * 2 + core, lax.axis_index("mp"))


def greet(z, x, core):
    barrier = pltpu.get_barrier_semaphore()
    targets = [device_at(z, x, 1 - core), device_at(z, 1 - x, core)]
    targets += [device_at(lax.rem(z + hop, DEPTH), x, core) for hop in range(1, DEPTH)]
    targets.append((lax.axis_index("dp"), 1 - lax.axis_index("mp")))
    for target in targets:
        pl.semaphore_signal(barrier, 1, device_id=target, device_id_type=MESH_ID)


def await_partners():
    pl.semaphore_wait(pltpu.get_barrier_semaphore(), DEPTH + 2)


def scatter_step(step, chunks, compute, finish, scratch, small_last=False):
    (own, core_out, core_in, keep, x_out, x_in, sums, mine, z_out, z_in,
     core_send, core_recv, x_send, x_recv, z_send, z_recv) = scratch
    z, x, core = device_place()

    def core_copy(p, cut=()):
        return pltpu.make_async_remote_copy(
            core_out.at[(lax.rem(p, 2), *cut)], core_in.at[(lax.rem(p, 4), *cut)],
            core_send.at[lax.rem(p, 2)], core_recv.at[lax.rem(p, 4)],
            device_id=device_at(z, x, 1 - core), device_id_type=MESH_ID)

    def x_copy(p, cut=()):
        return pltpu.make_async_remote_copy(
            x_out.at[(lax.rem(p, X_LAG), *cut)], x_in.at[(lax.rem(p, 2 * X_LAG), *cut)],
            x_send.at[lax.rem(p, X_LAG)], x_recv.at[lax.rem(p, 2 * X_LAG)],
            device_id=device_at(z, 1 - x, core), device_id_type=MESH_ID)

    def z_copy(p, hop, cut=()):
        return pltpu.make_async_remote_copy(
            z_out.at[(lax.rem(p, 4), hop - 1, *cut)], z_in.at[(lax.rem(p, 8), hop - 1, *cut)],
            z_send.at[lax.rem(p, 4), hop - 1], z_recv.at[lax.rem(p, 8), hop - 1],
            device_id=device_at(lax.rem(z + hop, DEPTH), x, core), device_id_type=MESH_ID)

    corner = (slice(0, 16), slice(0, 128))
    every = slice(None)

    def go(copy, lead, p, act):
        if not small_last:
            act(copy(p))
            return
        pl.when(p < chunks - 1)(lambda: act(copy(p)))
        pl.when(p == chunks - 1)(lambda: act(copy(p, (*(every,) * lead, *corner))))

    def core_go(p, act):
        go(core_copy, 2, p, act)

    def x_go(p, act):
        go(x_copy, 1, p, act)

    def z_go(p, hop, act):
        go(lambda p, cut=(): z_copy(p, hop, cut), 0, p, act)

    start, wait_recv, wait_send = (
        lambda copy: copy.start(), lambda copy: copy.wait_recv(), lambda copy: copy.wait_send())

    @pl.when(step < chunks)
    def _():
        @pl.when(step >= 2)
        def _():
            core_go(step - 2, wait_send)

        def to_partner(value):
            core_out[lax.rem(step, 2)] = value.astype(BF)

        def to_own(value):
            own[lax.rem(step, 2)] = value

        compute(step, 1 - core, to_partner)
        core_go(step, start)
        compute(step, core, to_own)

    @pl.when((step >= 1) & (step < chunks + 1))
    def _():
        p = step - 1
        core_go(p, wait_recv)

        @pl.when(p >= X_LAG)
        def _():
            x_go(p - X_LAG, wait_send)

        two, four, slot = lax.rem(p, 2), lax.rem(p, 4), lax.rem(p, X_LAG)
        x_out[slot] = (own[two, :, 1 - x] + core_in[four, :, 1 - x].astype(F32)).astype(BF)
        x_go(p, start)
        keep[slot] = own[two, :, x] + core_in[four, :, x].astype(F32)

    @pl.when((step >= X_LAG) & (step < chunks + X_LAG))
    def _():
        p = step - X_LAG
        x_go(p, wait_recv)
        four = lax.rem(p, 4)
        sums[...] = keep[lax.rem(p, X_LAG)] + x_in[lax.rem(p, 2 * X_LAG)].astype(F32)
        for hop in range(1, DEPTH):
            @pl.when(p >= 4)
            def _():
                z_go(p - 4, hop, wait_send)

            z_out[four, hop - 1] = sums[lax.rem(z + hop, DEPTH)].astype(BF)
            z_go(p, hop, start)
        mine[four] = sums[z]

    @pl.when((step >= Z_LAG) & (step < chunks + Z_LAG))
    def _():
        p = step - Z_LAG
        for hop in range(1, DEPTH):
            z_go(p, hop, wait_recv)
        got = z_in.at[lax.rem(p, 8)]
        finish(p, mine[lax.rem(p, 4)] + got[0].astype(F32) + got[1].astype(F32) + got[2].astype(F32))

    @pl.when(step == chunks + Z_LAG - 1)
    def _():
        for p in range(chunks - 2, chunks):
            core_go(jnp.int32(p), wait_send)
        for p in range(chunks - X_LAG, chunks):
            x_go(jnp.int32(p), wait_send)
        for p in range(chunks - 4, chunks):
            for hop in range(1, DEPTH):
                z_go(jnp.int32(p), hop, wait_send)


def scatter_scratch(rows, lanes):
    quad = (DEPTH, 2, rows, lanes)
    line = (DEPTH, rows, lanes)
    dma = pltpu.SemaphoreType.DMA
    return [
        pltpu.VMEM((2, *quad), F32),
        pltpu.VMEM((2, *quad), BF),
        pltpu.VMEM((4, *quad), BF),
        pltpu.VMEM((X_LAG, *line), F32),
        pltpu.VMEM((X_LAG, *line), BF),
        pltpu.VMEM((2 * X_LAG, *line), BF),
        pltpu.VMEM(line, F32),
        pltpu.VMEM((4, rows, lanes), F32),
        pltpu.VMEM((4, DEPTH - 1, rows, lanes), BF),
        pltpu.VMEM((8, DEPTH - 1, rows, lanes), BF),
        dma((2,)), dma((4,)), dma((X_LAG,)), dma((2 * X_LAG,)), dma((4, DEPTH - 1)), dma((8, DEPTH - 1)),
    ]


def scatter_out(chunks, rows, lanes):
    spec = pl.BlockSpec((1, rows, lanes), lambda q: (jnp.maximum(q - Z_LAG, 0), 0, 0))
    return spec, jax.ShapeDtypeStruct((chunks, rows, lanes), F32)


def fixed(shape):
    return pl.BlockSpec(shape, lambda q: (0,) * len(shape), pipeline_mode=pl.Buffered(1))


def glu_kernel(
    hidden_blocks, full_blocks, normed_ref, back_ref, left_ref, left_back_ref, glu_ref,
    out_ref, sum_own, sum_came, half_own, half_send, tail_ref,
    tail_stage, tail_sem, left, left_back, left_sem, acts, weights_in, weights_back, sum_stage, half_stage,
    in_sem, back_sem, stage_sem, sum_send, sum_recv, *scratch,
):
    z, x, core = device_place()
    dp, mp = lax.axis_index("dp"), lax.axis_index("mp")
    step = pl.program_id(0)
    scattered = hidden_blocks - TAIL
    chunks = 3 * scattered
    rows = normed_ref.shape[0]
    row_block = rows // 2
    half_blocks = full_blocks // 2
    across = (((1,), (1,)), ((), ()))
    spread = min(hidden_blocks + hidden_blocks // 2, 16)
    second = step - spread

    def first_tasks(at):
        return at * hidden_blocks // spread

    def second_task(at):
        return 2 * at // 3

    def has_second(at):
        return (at == 0) | (
            (at > 0) & (second_task(at) > second_task(at - 1)) & (second_task(at) < full_blocks))

    unit_block = first_tasks(step)

    def lane_block(index):
        return pl.ds(pl.multiple_of(index * LANES, LANES), LANES)

    def load_in(index):
        return pltpu.make_async_copy(glu_ref.at[:, :, lane_block(index)], weights_in, in_sem)

    def load_back(index):
        return pltpu.make_async_copy(glu_ref.at[:, lane_block(index), :], weights_back, back_sem)

    def stage(index, kind, target):
        source = (sum_stage, half_stage)[kind].at[lax.rem(index, 2)]
        return pltpu.make_async_copy(source, target, stage_sem.at[lax.rem(index, 2), kind])

    def half_spot(index):
        return lax.rem(index, half_blocks)

    def sum_copy(index):
        return pltpu.make_async_remote_copy(
            sum_own.at[:, lane_block(index)], sum_came.at[:, lane_block(index)],
            sum_send.at[index], sum_recv.at[index], device_id=(dp, 1 - mp), device_id_type=MESH_ID)

    left_loads = (
        pltpu.make_async_copy(left_ref, left, left_sem.at[0]),
        pltpu.make_async_copy(left_back_ref, left_back, left_sem.at[1]),
    )

    @pl.when(step == 0)
    def _():
        greet(z, x, core)
        for one in (load_in(0), *left_loads, load_back(0)):
            one.start()

    @pl.when((step < spread) & ((step == 0) | (unit_block > first_tasks(step - 1))))
    def _():
        load_in(unit_block).wait()
        lanes = lane_block(unit_block)

        def part(index, _):
            part_rows = pl.ds(pl.multiple_of(index * row_block, row_block), row_block)
            normed = normed_ref[part_rows, :]
            pre_act = jnp.dot(normed, weights_in[0], preferred_element_type=F32)
            pre_up = jnp.dot(normed, weights_in[1], preferred_element_type=F32)
            grad_hidden = jnp.dot(back_ref[part_rows, :], weights_in[2], preferred_element_type=F32)
            sigma = jax.nn.sigmoid(pre_act)
            act_part = pre_act * sigma
            acts[0, part_rows, lanes] = (
                grad_hidden * pre_up * (sigma * (1.0 + pre_act * (1.0 - sigma)))).astype(BF)
            acts[1, part_rows, lanes] = (grad_hidden * act_part).astype(BF)
            acts[2, part_rows, lanes] = (act_part * pre_up).astype(BF)
            return 0

        lax.fori_loop(0, rows // row_block, part, 0)

        @pl.when(unit_block + 1 < hidden_blocks)
        def _():
            load_in(unit_block + 1).start()

    @pl.when(step == 0)
    def _():
        await_partners()

    @pl.when(has_second(second - 1))
    def _():
        index = second_task(second - 1)
        stage(index, 0, sum_own.at[:, lane_block(index)]).wait()
        sum_copy(index).start()
        spot = half_spot(index)
        stage(index, 1, half_own.at[:, lane_block(spot)]).wait()

    @pl.when(has_second(second))
    def _():
        index = second_task(second)
        load_back(index).wait()
        slot = lax.rem(index, 2)

        def part(at, _):
            part_rows = pl.ds(pl.multiple_of(at * row_block, row_block), row_block)
            dot = functools.partial(
                lax.dot_general, dimension_numbers=across, preferred_element_type=F32)
            grad_normed = dot(acts[0, part_rows, :], weights_back[0])
            grad_normed += dot(acts[1, part_rows, :], weights_back[1])
            sum_stage[slot, part_rows, :] = grad_normed.astype(BF)
            half_stage[slot, part_rows, :] = dot(acts[2, part_rows, :], weights_back[2]).astype(BF)
            return 0

        lax.fori_loop(0, rows // row_block, part, 0)

        @pl.when(index + 1 < full_blocks)
        def _():
            load_back(index + 1).start()

        stage(index, 0, sum_own.at[:, lane_block(index)]).start()
        spot = half_spot(index)

        @pl.when(index // half_blocks == mp)
        def _():
            stage(index, 1, half_own.at[:, lane_block(spot)]).start()

        @pl.when(index // half_blocks != mp)
        def _():
            stage(index, 1, half_send.at[:, lane_block(spot)]).start()

    def compute(q, core_side, store):
        kind = lax.rem(q, 3)
        side_rows = left.shape[3]

        def product(side_ref):
            side = side_ref[:, :, core_side].reshape(DEPTH * 2 * side_rows, rows)
            right = acts[kind, :, lane_block(q // 3)]
            store(jnp.dot(side, right, preferred_element_type=F32).reshape(
                DEPTH, 2, side_rows, LANES))

        pl.when(kind < 2)(lambda: product(left))
        pl.when(kind == 2)(lambda: product(left_back))

    @pl.when(step == 0)
    def _():
        for one in left_loads:
            one.wait()

    def finish(p, value):
        out_ref[0] = value

    scatter_step(step, chunks, compute, finish, scratch)

    def tail_copy(index):
        spot = tail_ref.at[lax.rem(index, 3), :, :, :, :, lane_block(index // 3)]
        return pltpu.make_async_copy(
            tail_stage.at[lax.rem(index, 2)], spot, tail_sem.at[lax.rem(index, 2)])

    tail_start = chunks + Z_LAG - 3 * TAIL

    @pl.when(step >= tail_start)
    def _():
        index = step - tail_start

        @pl.when(index >= 2)
        def _():
            tail_copy(index - 2).wait()

        for side in (0, 1):
            def to_stage(value):
                tail_stage[lax.rem(index, 2), :, :, side] = value.astype(BF)

            compute(chunks + index, side, to_stage)
        tail_copy(index).start()

    @pl.when(step == chunks + Z_LAG - 1)
    def _():
        for index in range(3 * TAIL - 2, 3 * TAIL):
            tail_copy(jnp.int32(index)).wait()
        for index in range(full_blocks):
            sum_copy(index).wait()


def glu_call(normed, back_low, left_back, glu, collective):
    rows, full = normed.shape
    hidden = glu.shape[2]
    hidden_blocks, full_blocks = hidden // LANES, full // LANES
    block = full // 16
    chunks = 3 * (hidden_blocks - TAIL)
    left_shape = (DEPTH, 2, 2, block, rows)
    any_space = pl.BlockSpec(memory_space=pl.ANY)
    out_spec, out_shape = scatter_out(chunks, block, LANES)
    dma = pltpu.SemaphoreType.DMA
    wide = jax.ShapeDtypeStruct((rows, full), BF)
    half = jax.ShapeDtypeStruct((rows, full // 2), BF)
    out, sum_own, sum_came, half_own, half_send, tail = pl.pallas_call(
        functools.partial(glu_kernel, hidden_blocks, full_blocks),
        grid=(chunks + Z_LAG,),
        in_specs=[fixed(normed.shape), fixed(back_low.shape)] + [any_space] * 3,
        out_specs=[out_spec] + [any_space] * 5,
        out_shape=[
            out_shape, wide, wide, half, half,
            jax.ShapeDtypeStruct((3, DEPTH, 2, 2, block, TAIL * LANES), BF),
        ],
        scratch_shapes=[
            pltpu.VMEM((2, DEPTH, 2, 2, block, LANES), BF),
            dma((2,)),
            pltpu.VMEM(left_shape, BF),
            pltpu.VMEM(left_shape, BF),
            dma((2,)),
            pltpu.VMEM((3, rows, hidden), BF),
            pltpu.VMEM((3, full, LANES), BF),
            pltpu.VMEM((3, LANES, hidden), BF),
            pltpu.VMEM((2, rows, LANES), BF),
            pltpu.VMEM((2, rows, LANES), BF),
            dma(()), dma(()), dma((2, 2)),
            dma((full_blocks,)), dma((full_blocks,)),
            *scatter_scratch(block, LANES),
        ],
        compiler_params=pltpu.CompilerParams(
            collective_id=collective, has_side_effects=True, vmem_limit_bytes=62 * 1024 * 1024),
        cost_estimate=pl.CostEstimate(
            flops=18 * rows * full * hidden, bytes_accessed=6 * full * hidden * 2,
            transcendentals=rows * hidden),
    )(normed, back_low, owner_rows(normed), left_back, glu)
    return out, tail.reshape(3, full, TAIL * LANES), sum_own, sum_came, half_own, half_send


def mixer_kernel(
    full_blocks, left_hbm, grad_hbm, left_out_ref, right_out_ref, gain_ref, tokens_ref, inverse_ref,
    weights_ref, dot_ref, out_ref, gain_out, half_own, half_send, half_came, dot_came,
    left_ref, grad_ref, big_sem, weights, token_block, gain_sum, gain_chunk, total, swap_out, swap_in, half_stage,
    load_sem, stage_sem, half_send_sem, half_recv, swap_send, swap_recv, dot_sem, *scratch,
):
    z, x, core = device_place()
    dp, mp = lax.axis_index("dp"), lax.axis_index("mp")
    step = pl.program_id(0)
    tokens, channels = grad_ref.shape[1], grad_ref.shape[2]
    block, half = left_ref.shape[3], left_out_ref.shape[3]
    outer = full_blocks // 2
    across = channels // LANES
    gains = outer + 3 * across
    chunks = gains + 1
    half_blocks = full_blocks // 2
    row_block = tokens // 2
    partner = (dp, 1 - mp)

    def lane_block(index):
        return pl.ds(pl.multiple_of(index * LANES, LANES), LANES)

    def loads(index):
        return (
            pltpu.make_async_copy(weights_ref.at[:, lane_block(index), :], weights, load_sem.at[0]),
            pltpu.make_async_copy(tokens_ref.at[:, lane_block(index)], token_block, load_sem.at[1]),
        )

    def stage(index, target):
        return pltpu.make_async_copy(
            half_stage.at[lax.rem(index, 2)], target, stage_sem.at[lax.rem(index, 2)])

    def half_copy(spot):
        return pltpu.make_async_remote_copy(
            half_send.at[:, lane_block(spot)], half_came.at[:, lane_block(spot)],
            half_send_sem.at[spot], half_recv.at[spot], device_id=partner, device_id_type=MESH_ID)

    def swap_copy(index):
        return pltpu.make_async_remote_copy(
            swap_out.at[lax.rem(index, 2)], swap_in.at[lax.rem(index, 8)],
            swap_send.at[lax.rem(index, 2)], swap_recv.at[lax.rem(index, 8)],
            device_id=partner, device_id_type=MESH_ID)

    big_loads = (
        pltpu.make_async_copy(grad_hbm, grad_ref, big_sem.at[0]),
        pltpu.make_async_copy(left_hbm, left_ref, big_sem.at[1]),
    )
    dot_copy = pltpu.make_async_remote_copy(
        dot_ref, dot_came, dot_sem.at[0], dot_sem.at[1], device_id=partner, device_id_type=MESH_ID)

    @pl.when(step == 0)
    def _():
        greet(z, x, core)
        for one in (*big_loads, *loads(0)):
            one.start()
        gain_chunk[...] = jnp.zeros_like(gain_chunk)
        gain_sum[...] = jnp.zeros_like(gain_sum)
        await_partners()
        dot_copy.start()

    @pl.when(step == 1)
    def _():
        for one in big_loads:
            one.wait()

    task = (step - 1) // 2

    @pl.when((step >= 2) & (step <= 2 * full_blocks) & (lax.rem(step, 2) == 0))
    def _():
        index = task
        spot = lax.rem(index, half_blocks)
        stage(index, half_own.at[:, lane_block(spot)]).wait()

        @pl.when(index // half_blocks != mp)
        def _():
            half_copy(spot).start()

    @pl.when((step < 2 * full_blocks) & (lax.rem(step, 2) == 1))
    def _():
        for one in loads(task):
            one.wait()
        slot = lax.rem(task, 2)
        spot = lax.rem(task, half_blocks)

        def part(at, gain_in):
            part_rows = pl.ds(pl.multiple_of(at * row_block, row_block), row_block)
            dot = functools.partial(
                lax.dot_general, dimension_numbers=(((1,), (1,)), ((), ())), preferred_element_type=F32)
            grad = dot(grad_ref[0, part_rows, :], weights[0])
            grad += dot(grad_ref[1, part_rows, :], weights[1])
            grad += dot(grad_ref[2, part_rows, :], weights[2])
            half_stage[slot, part_rows, :] = grad.astype(BF)
            unit = token_block[part_rows, :].astype(F32) * inverse_ref[part_rows, :]
            return gain_in + jnp.sum(grad * unit, axis=0, keepdims=True)

        gain_in = lax.fori_loop(0, tokens // row_block, part, jnp.zeros((1, LANES), F32))
        gain_sum[2 * task, 0:1, :] = gain_in[:, :128]
        gain_sum[2 * task + 1, 0:1, :] = gain_in[:, 128:]

        @pl.when(task + 1 < full_blocks)
        def _():
            for one in loads(task + 1):
                one.start()

        @pl.when(task // half_blocks == mp)
        def _():
            stage(task, half_own.at[:, lane_block(spot)]).start()

        @pl.when(task // half_blocks != mp)
        def _():
            stage(task, half_send.at[:, lane_block(spot)]).start()

    def compute(q, core_side, store):
        @pl.when(q < outer)
        def _():
            side = left_out_ref[:, :, core_side].reshape(channels // 2, tokens)
            parts = [
                jnp.dot(side, right_out_ref[:, lane_block(2 * q + at)], preferred_element_type=F32)
                for at in (0, 1)
            ]
            parts = [part.reshape(DEPTH, 2, half, LANES) for part in parts]
            store(jnp.concatenate(parts, axis=2))

        @pl.when((q >= outer) & (q < gains))
        def _():
            at = q - outer
            side = left_ref[:, :, core_side].reshape(DEPTH * 2 * block, tokens)
            right = grad_ref[at // across, :, lane_block(lax.rem(at, across))]
            store(jnp.dot(side, right, preferred_element_type=F32).reshape(DEPTH, 2, block, LANES))

        @pl.when(q == gains)
        def _():
            for owner in range(2 * DEPTH):
                line = 2 * owner + core_side
                gain_chunk[owner // 2, owner % 2, 0:8, 0:128] = gain_ref[line] + gain_sum[line]
            store(gain_chunk[...])

    def finish(p, value):
        total[lax.rem(p, 4)] = value

        @pl.when(p >= outer)
        def _():
            index = p - outer

            @pl.when(index >= 2)
            def _():
                swap_copy(index - 2).wait_send()

            first = jnp.where(p == gains, 0, 1 - mp) * half
            rows = pl.ds(pl.multiple_of(first, half), half)
            swap_out[lax.rem(index, 2)] = total[lax.rem(p, 4), rows, :].astype(BF)
            swap_copy(index).start()

    scatter_step(step, chunks, compute, finish, scratch, small_last=True)

    @pl.when((step >= Z_LAG + SWAP_LAG) & (step < chunks + Z_LAG + SWAP_LAG))
    def _():
        p = step - Z_LAG - SWAP_LAG
        slot = lax.rem(p, 4)

        @pl.when(p < outer)
        def _():
            out_ref[0, :, :LANES] = total[slot, :half, :]
            out_ref[0, :, LANES:] = total[slot, half:, :]

        @pl.when(p >= outer)
        def _():
            swap_copy(p - outer).wait_recv()
            came = swap_in[lax.rem(p - outer, 8)].astype(F32)

            @pl.when(p < gains)
            def _():
                own = total[slot, pl.ds(pl.multiple_of(mp * half, half), half), :]
                first = jnp.where(mp == 0, own, came)
                second = jnp.where(mp == 0, came, own)
                for tile in (0, 1):
                    lanes = slice(128 * tile, 128 * tile + 128)
                    left, right = split_lanes(first[:, lanes], second[:, lanes])
                    out_ref[0, :, 256 * tile : 256 * tile + 128] = left
                    out_ref[0, :, 256 * tile + 128 : 256 * tile + 256] = right

            @pl.when(p == gains)
            def _():
                gain_out[...] = total[slot, 0:8, 0:128] + came[0:8, 0:128]

    @pl.when(step == chunks + Z_LAG + SWAP_LAG - 1)
    def _():
        for spot in range(half_blocks):
            half_copy(spot).wait()
        for index in range(gains - outer - 1, gains - outer + 1):
            swap_copy(index).wait_send()
        dot_copy.wait()


def mixer_call(
    left_in, grad_pre, left_out, right_out, gain_parts, tokens, inverse, weights, dots, collective
):
    _, rows, channels = grad_pre.shape
    full = right_out.shape[1]
    block, half = full // 16, channels // 16
    full_blocks, across = full // LANES, channels // LANES
    outer, inner = full_blocks // 2, 3 * across
    chunks = outer + inner + 1
    any_space = pl.BlockSpec(memory_space=pl.ANY)
    dma = pltpu.SemaphoreType.DMA
    part = jax.ShapeDtypeStruct((rows, full // 2), BF)

    def out_place(q):
        p = jnp.clip(q - Z_LAG - SWAP_LAG, 0, outer + inner - 1)
        inside = jnp.maximum(p - outer, 0)
        return (
            jnp.where(p < outer, 3, inside // across), 0, jnp.where(p < outer, p, lax.rem(inside, across)))

    out, gains, half_own, _, half_came, dot_came = pl.pallas_call(
        functools.partial(mixer_kernel, full_blocks),
        grid=(chunks + Z_LAG + SWAP_LAG,),
        in_specs=[
            any_space, any_space,
            fixed((DEPTH, 2, 2, half, rows)), fixed(right_out.shape), fixed(gain_parts.shape),
            any_space, fixed(inverse.shape), any_space, any_space,
        ],
        out_specs=[
            pl.BlockSpec((1, half, 2 * LANES), out_place),
            pl.BlockSpec((8, 128), lambda q: (0, 0)),
        ] + [any_space] * 4,
        out_shape=[
            jax.ShapeDtypeStruct((4, half, full), F32), jax.ShapeDtypeStruct((8, 128), F32),
            part, part, part, jax.ShapeDtypeStruct(dots.shape, F32),
        ],
        scratch_shapes=[
            pltpu.VMEM((DEPTH, 2, 2, block, rows), BF),
            pltpu.VMEM(grad_pre.shape, BF),
            dma((2,)),
            pltpu.VMEM((3, LANES, channels), BF),
            pltpu.VMEM((rows, LANES), BF),
            pltpu.VMEM((16, 8, 128), F32),
            pltpu.VMEM((DEPTH, 2, block, LANES), F32),
            pltpu.VMEM((4, block, LANES), F32),
            pltpu.VMEM((2, half, LANES), BF),
            pltpu.VMEM((8, half, LANES), BF),
            pltpu.VMEM((2, rows, LANES), BF),
            dma((2,)), dma((2,)), dma((full_blocks // 2,)), dma((full_blocks // 2,)),
            dma((2,)), dma((8,)), dma((2,)),
            *scatter_scratch(block, LANES),
        ],
        compiler_params=pltpu.CompilerParams(
            collective_id=collective, has_side_effects=True, vmem_limit_bytes=VMEM_LIMIT),
        cost_estimate=pl.CostEstimate(
            flops=14 * full * rows * channels, bytes_accessed=16 * full * channels, transcendentals=0),
    )(
        left_in, grad_pre, left_out, right_out, gain_parts, tokens, inverse, weights, dots,
    )
    return out, gains, half_own.astype(F32) + half_came.astype(F32), dot_came


def transpose_kernel(in_ref, out_ref):
    turned = in_ref[...].T
    out_ref[...] = turned.reshape(out_ref.shape)


def owner_rows(value, owners=2):
    rows, width = value.shape
    block = width // 16
    return pl.pallas_call(
        transpose_kernel,
        grid=(2 * DEPTH,),
        in_specs=[pl.BlockSpec((rows, owners * block), lambda q: (0, q))],
        out_specs=pl.BlockSpec((1, 1, owners, block, rows), lambda q: (q // 2, lax.rem(q, 2), 0, 0, 0)),
        out_shape=jax.ShapeDtypeStruct((DEPTH, 2, owners, block, rows), value.dtype),
        compiler_params=pltpu.CompilerParams(vmem_limit_bytes=VMEM_LIMIT),
        cost_estimate=pl.CostEstimate(flops=0, bytes_accessed=4 * rows * width, transcendentals=0),
    )(value)


def middle_back_kernel(
    sum_own_ref, sum_came_ref, middle_ref, cot_ref, tokens_ref, weight_ref, gain_ref, mixer_ref,
    grad_own_ref, low_ref, mean_ref, gated_ref, gain_grad_ref,
):
    rows, full = middle_ref.shape
    part = full // 2
    middle = middle_ref[...]
    inverse = lax.rsqrt(jnp.mean(middle * middle, axis=-1, keepdims=True) + EPSILON)
    unit = middle * inverse
    grad_normed = sum_own_ref[...].astype(F32) + sum_came_ref[...].astype(F32)
    product = grad_normed * unit
    before = jnp.where(pl.program_id(0) == 0, 0.0, gain_grad_ref[...])
    gain_grad_ref[...] = before + jnp.sum(product, axis=0, keepdims=True)
    dots = jnp.mean(product * gain_ref[...], axis=-1, keepdims=True)
    back = cot_ref[...].astype(F32) * weight_ref[...]
    grad = back + inverse * (grad_normed * gain_ref[...] - unit * dots)
    first = lax.axis_index("mp") == 0
    grad_own_ref[...] = jnp.where(first, grad[:, :part], grad[:, part:])
    low = grad.astype(BF)
    low_ref[...] = low
    branch = middle - tokens_ref[...].astype(F32)
    mean_ref[...] = jnp.mean(low.astype(F32) * branch, axis=-1, keepdims=True)
    gated_ref[...] = lax.dot_general(
        low, mixer_ref[...], (((1,), (1,)), ((), ())), preferred_element_type=F32)


def middle_back(sum_own, sum_came, middle, cot, tokens, weight, gain, mixer_out):
    rows, full = middle.shape
    channels = mixer_out.shape[0]
    step = 224 if rows % 224 == 0 else rows
    line = lambda width: pl.BlockSpec((step, width), lambda r: (r, 0))
    shape = jax.ShapeDtypeStruct
    return pl.pallas_call(
        middle_back_kernel,
        grid=(rows // step,),
        in_specs=[line(full)] * 5 + [line(1), fixed((1, full)), fixed(mixer_out.shape)],
        out_specs=[
            line(full // 2), line(full), line(1), line(channels),
            pl.BlockSpec((1, full), lambda r: (0, 0)),
        ],
        out_shape=[
            shape((rows, full // 2), F32), shape((rows, full), BF), shape((rows, 1), F32),
            shape((rows, channels), F32), shape((1, full), F32),
        ],
        compiler_params=pltpu.CompilerParams(vmem_limit_bytes=VMEM_LIMIT),
        cost_estimate=pl.CostEstimate(
            flops=2 * rows * full * channels, bytes_accessed=rows * full * 20, transcendentals=0),
    )(sum_own, sum_came, middle, cot, tokens, weight, gain[None], mixer_out)


def glu_update_kernel(scale, act_ref, up_ref, out_ref, *refs):
    in_refs, down_refs, in_new, down_new = refs[:3], refs[3:6], refs[-6:-3], refs[-3:]
    count = STEP_NUMBER
    for at, grad_ref in ((0, act_ref), (1, up_ref)):
        new = adamw_update(
            *(ref[at] for ref in in_refs), grad_ref[0].astype(F32) * scale, count, MATRIX_RATE, DECAY_RATE)
        for ref, value in zip(in_new, new):
            ref[at] = value
    new = adamw_update(
        *(ref[...] for ref in down_refs), out_ref[0].astype(F32).T * scale, count, MATRIX_RATE, DECAY_RATE)
    for ref, value in zip(down_new, new):
        ref[...] = value


def glu_update(sums, sum_place, first, blocks, ins, downs, scale, earlier=()):
    rows, lanes = ins[0].shape[1], LANES
    sum_spec = lambda kind: pl.BlockSpec((1, rows, lanes), lambda q: sum_place(kind, q))
    in_spec = pl.BlockSpec((2, rows, lanes), lambda q: (0, 0, q + first))
    down_spec = pl.BlockSpec((lanes, rows), lambda q: (q + first, 0))
    new = pl.pallas_call(
        functools.partial(glu_update_kernel, scale),
        grid=(blocks,),
        in_specs=[sum_spec(0), sum_spec(1), sum_spec(2)] + [in_spec] * 3 + [down_spec] * 3
        + [pl.BlockSpec(memory_space=pl.ANY)] * len(earlier),
        out_specs=[in_spec] * 3 + [down_spec] * 3,
        out_shape=[jax.ShapeDtypeStruct(ins[0].shape, F32)] * 3 + [jax.ShapeDtypeStruct(downs[0].shape, F32)] * 3,
        input_output_aliases={9 + at: at for at in range(len(earlier))},
        compiler_params=pltpu.CompilerParams(vmem_limit_bytes=VMEM_LIMIT),
        cost_estimate=pl.CostEstimate(
            flops=60 * rows * lanes * blocks, bytes_accessed=84 * rows * lanes * blocks,
            transcendentals=6 * rows * lanes * blocks),
    )(sums, sums, sums, *ins, *downs, *earlier)
    return tuple(new)


ITEMS = 6
ALONG_Z = (0, 5, 2, 3)


def split_lanes(first, second):
    low = lax.broadcasted_iota(jnp.int32, first.shape, 1) < 64
    return (
        jnp.where(low, first, pltpu.roll(second, 64, 1)),
        jnp.where(low, pltpu.roll(first, 64, 1), second),
    )


def gather_kernel(mixer_ref, gain_ref, lengths_ref, domains_ref, glu_in_ref, glu_out_ref, cot_ref,
                  all_in, all_out, all_small, cot_full, glu_low,
                  in_ref, out_ref, small_ref, right_send, left_send,
                  z_recv, x_send, x_recv, core_send, core_recv, y_send, y_recv, local_sem):
    z, x, core = device_place()
    mp = lax.axis_index("mp")
    barrier = pltpu.get_barrier_semaphore()
    right, left = lax.rem(z + 1, DEPTH), lax.rem(z + DEPTH - 1, DEPTH)
    dp = lax.axis_index("dp")
    for target in (
        device_at(right, x, core), device_at(left, x, core), device_at(z, 1 - x, core),
        device_at(z, x, 1 - core), (dp, 1 - mp),
    ):
        pl.semaphore_signal(barrier, 1, device_id=target, device_id_type=MESH_ID)
    for kind in range(3):
        for tile in range(in_ref.shape[3] // 128):
            first = mixer_ref[kind, :, 256 * tile : 256 * tile + 128]
            second = mixer_ref[kind, :, 256 * tile + 128 : 256 * tile + 256]
            for side, value in enumerate(split_lanes(first, second)):
                in_ref[side, kind, :, 128 * tile : 128 * tile + 128] = value.astype(BF)
    out_ref[...] = mixer_ref[3].astype(BF)
    lane = lax.broadcasted_iota(jnp.int32, (1, 128), 1)
    live = jnp.zeros((1, 128), F32)
    for batch in range(lengths_ref.shape[0]):
        count = lengths_ref[batch : batch + 1, :].astype(F32)
        live = live + jnp.where(lane == domains_ref[batch : batch + 1, :], count, 0.0)
    small_ref[...] = jnp.zeros_like(small_ref)
    small_ref[0:3, 0:64] = gain_ref[...].astype(BF).astype(F32)
    small_ref[3:4, :] = live
    pl.semaphore_wait(barrier, 5)

    def spot(item, zs, xs, cs, side=None):
        if item == 0:
            return all_in.at[:, zs, xs, cs, mp if side is None else side]
        if item in (1, 4, 5):
            rows = out_ref.shape[0] // 2
            return all_out.at[zs, xs, cs, slice(rows, None) if item == 5 else slice(0, rows)]
        if item == 2:
            return all_in.at[:, zs, xs, cs, 1 - mp]
        return all_small.at[zs, xs, cs]

    def own(item):
        if item == 0:
            return in_ref.at[mp]
        if item in (1, 5):
            rows = out_ref.shape[0] // 2
            return out_ref.at[slice(rows, None) if item == 5 else slice(0, rows)]
        return spot(item, z, x, core)

    def copy(item, zs, xs, target, send, recv, source=None):
        return pltpu.make_async_remote_copy(
            spot(item, zs, xs, core) if source is None else source, spot(item, zs, xs, core),
            send, recv, device_id=target, device_id_type=MESH_ID)

    def column(item):
        return 1 - x if item == 4 else x

    def right_copy(item, zs, source=None):
        return copy(item, zs, column(item), device_at(right, x, core), right_send.at[zs, item], z_recv.at[zs, item], source)

    def left_copy(item, zs, source=None):
        return copy(item, zs, column(item), device_at(left, x, core), left_send.at[zs, item], z_recv.at[zs, item], source)

    def x_copy(item, zs, source=None):
        return copy(item, zs, x, device_at(z, 1 - x, core), x_send.at[zs, item], x_recv.at[zs, item], source)

    def core_copy(item, zs, xs, source=None):
        return copy(item, zs, xs, device_at(z, x, 1 - core), core_send.at[zs, xs, item], core_recv.at[zs, xs, item], source)

    y_copies = [
        pltpu.make_async_remote_copy(
            in_ref.at[1 - mp], all_in.at[:, z, x, core, mp], y_send.at[0], y_recv.at[0],
            device_id=(dp, 1 - mp), device_id_type=MESH_ID),
        pltpu.make_async_remote_copy(
            small_ref, all_small.at[z, x, core, mp], y_send.at[1], y_recv.at[1],
            device_id=(dp, 1 - mp), device_id_type=MESH_ID),
    ]
    locals_ = [
        pltpu.make_async_copy(in_ref.at[mp], spot(0, z, x, core), local_sem.at[0]),
        pltpu.make_async_copy(out_ref, all_out.at[z, x, core], local_sem.at[1]),
        pltpu.make_async_copy(small_ref, all_small.at[z, x, core, mp], local_sem.at[2]),
    ]
    cot_lanes = pl.ds(pl.multiple_of(mp * cot_ref.shape[1], 128), cot_ref.shape[1])
    cot_local = pltpu.make_async_copy(cot_ref, cot_full.at[:, cot_lanes], local_sem.at[3])
    cot_copy = pltpu.make_async_remote_copy(
        cot_ref, cot_full.at[:, cot_lanes], y_send.at[2], y_recv.at[2],
        device_id=(dp, 1 - mp), device_id_type=MESH_ID)
    for one in y_copies:
        one.start()
    locals_[2].start()

    def both_ways(item, source=None):
        @pl.when(z < DEPTH - 1)
        def _():
            right_copy(item, z, source).start()

        @pl.when(z > 0)
        def _():
            left_copy(item, z, source).start()

    for item in (1, *ALONG_Z):
        if item == 2:
            y_copies[0].wait_recv()
        if item == 3:
            y_copies[1].wait_recv()
            locals_[2].wait()
        source = own(item)
        both_ways(item, source)
        x_copy(item, z, source).start()
        core_copy(item, z, x, source).start()
    locals_[0].start()
    locals_[1].start()
    cot_copy.start()
    cot_local.start()
    glu_low[0:2] = glu_in_ref[...].astype(BF)
    for tile in range(glu_out_ref.shape[0] // 128):
        lanes = slice(128 * tile, 128 * tile + 128)
        glu_low[2, :, lanes] = glu_out_ref[lanes, :].T.astype(BF)

    def from_x(item, zs):
        pltpu.make_async_remote_copy(
            spot(item, zs, 1 - x, core), spot(item, zs, 1 - x, core), x_send.at[zs, item],
            x_recv.at[zs, item], device_id=device_at(z, 1 - x, core), device_id_type=MESH_ID).wait_recv()
        core_copy(item, zs, 1 - x).start()

    def arrived(item, hop):
        sent = 1 if item == 4 else item

        @pl.when(z >= hop)
        def _():
            zs = z - hop
            right_copy(item, zs).wait_recv()

            @pl.when(z < DEPTH - 1)
            def _():
                right_copy(item, zs).start()

            if item in ALONG_Z:
                x_copy(item, zs).start()
            core_copy(sent, zs, column(item)).start()

        @pl.when(z + hop < DEPTH)
        def _():
            zs = z + hop
            left_copy(item, zs).wait_recv()

            @pl.when(z > 0)
            def _():
                left_copy(item, zs).start()

            if item in ALONG_Z:
                x_copy(item, zs).start()
            core_copy(sent, zs, column(item)).start()

    for hop in range(1, DEPTH + 1):
        if hop == 1:
            from_x(1, z)
            both_ways(4)
        if hop < DEPTH:
            arrived(1, hop)
        for item in ALONG_Z:
            if hop < DEPTH:
                arrived(item, hop)
            if hop == 1:
                from_x(item, z)
            else:
                @pl.when(z >= hop - 1)
                def _():
                    from_x(item, z - (hop - 1))

                @pl.when(z + hop - 1 < DEPTH)
                def _():
                    from_x(item, z + (hop - 1))
        if hop < DEPTH:
            arrived(4, hop)

    for item in range(ITEMS):
        for zs in range(DEPTH):
            @pl.when((z >= zs) & (z < DEPTH - 1))
            def _():
                right_copy(item, zs).wait_send()

            @pl.when((z <= zs) & (z > 0))
            def _():
                left_copy(item, zs).wait_send()

            if item in ALONG_Z:
                x_copy(item, zs).wait_send()
            if item == 4:
                continue
            for xs in range(2):
                core_copy(item, zs, xs).wait()
    x_copy(1, z).wait_send()
    for one in y_copies:
        one.wait_send()
    locals_[0].wait()
    locals_[1].wait()
    cot_local.wait()
    cot_copy.wait_send()
    pltpu.make_async_remote_copy(
        cot_ref, cot_full.at[:, pl.ds(pl.multiple_of((1 - mp) * cot_ref.shape[1], 128), cot_ref.shape[1])],
        y_send.at[2], y_recv.at[2], device_id=(dp, 1 - mp), device_id_type=MESH_ID).wait_recv()


def gather_call(mixer, gain, lengths, domains, glu_in, glu_out, cot, collective):
    _, own_rows, full = mixer.shape
    channels = full // 2
    dma = pltpu.SemaphoreType.DMA
    any_space = pl.BlockSpec(memory_space=pl.ANY)
    in_vmem = pl.BlockSpec(memory_space=pltpu.VMEM)
    _, glu_rows, hidden = glu_in.shape
    return pl.pallas_call(
        gather_kernel,
        in_specs=[in_vmem] * 6 + [any_space],
        out_specs=[any_space] * 4 + [in_vmem],
        out_shape=[
            jax.ShapeDtypeStruct((3, DEPTH, 2, 2, 2, own_rows, channels), BF),
            jax.ShapeDtypeStruct((DEPTH, 2, 2, own_rows, full), BF),
            jax.ShapeDtypeStruct((DEPTH, 2, 2, 2, 8, 128), F32),
            jax.ShapeDtypeStruct((cot.shape[0], 2 * cot.shape[1]), BF),
            jax.ShapeDtypeStruct((3, glu_rows, hidden), BF),
        ],
        scratch_shapes=[
            pltpu.VMEM((2, 3, own_rows, channels), BF),
            pltpu.VMEM((own_rows, full), BF),
            pltpu.VMEM((8, 128), F32),
            dma((DEPTH, ITEMS)), dma((DEPTH, ITEMS)), dma((DEPTH, ITEMS)), dma((DEPTH, ITEMS)),
            dma((DEPTH, ITEMS)), dma((DEPTH, 2, ITEMS)), dma((DEPTH, 2, ITEMS)), dma((3,)), dma((3,)), dma((4,)),
        ],
        compiler_params=pltpu.CompilerParams(
            collective_id=collective, has_side_effects=True, vmem_limit_bytes=VMEM_LIMIT),
        cost_estimate=pl.CostEstimate(flops=0, bytes_accessed=300_000_000, transcendentals=0),
    )(mixer, gain, lengths, domains, glu_in, glu_out, cot)


def shards(
    tokens,
    cotangent,
    lengths,
    domains,
    lower_bound,
    mixer_master,
    mixer_first,
    mixer_second,
    glu_in_master,
    glu_in_first,
    glu_in_second,
    glu_out_master,
    glu_out_first,
    glu_out_second,
    gain_master,
    gain_first,
    gain_second,
):
    batches, _, length, full = tokens.shape
    rows = batches * length
    groups = lax.axis_size("dp")
    narrow = lax.axis_size("mp")
    place = lax.axis_index("mp")
    own_rows = mixer_master.shape[1]
    channels = groups * own_rows
    part = full // narrow
    quick = groups == 16 and narrow == 2 and own_rows == 64

    domain_ids = jnp.arange(NDOM, dtype=jnp.int32)
    member = (domains[..., 0][..., None] == domain_ids).astype(F32)
    cot_part = cotangent.reshape(rows, part)
    if quick:
        mixer_in, mixer_out, small, cot_full, glu_low = gather_call(
            mixer_master, gain_master, lengths, domains[..., 0], glu_in_master, glu_out_master, cot_part, 2
        )
        mixer_in = mixer_in.reshape(3, full, channels)
        mixer_out = mixer_out.reshape(channels, full)
        small = small.reshape(groups, narrow, 8, 128)
        gain_full = small[:, :, :3, :own_rows].transpose(2, 0, 1, 3).reshape(3, full)
        counts = jnp.sum(small[:, 0, 3, :NDOM], axis=0)
    else:
        gain_full = lax.all_gather(
            gain_master.astype(BF), ("dp", "mp"), axis=1, tiled=True
        ).astype(F32)
        mixer_low = mixer_master.astype(BF)
        in_blocks = mixer_low[:3].reshape(3, own_rows, groups, narrow, own_rows)
        in_blocks = in_blocks.transpose(3, 0, 1, 2, 4).reshape(narrow, 3, own_rows, channels)
        in_rows = mp_swap(in_blocks).transpose(1, 0, 2, 3).reshape(3, narrow * own_rows, channels)
        mixer_in = lax.all_gather(in_rows, "dp", axis=1, tiled=True)
        mixer_out = lax.all_gather(mixer_low[3], "dp", axis=0, tiled=True)
        counts = lax.psum(jnp.sum(member * lengths.astype(F32)[..., None], axis=(0, 1)), "dp")
        cot_full = mp_gather(cot_part)
        glu_low = jnp.concatenate([glu_in_master.astype(BF), glu_out_master.astype(BF).T[None]])
    glu = lax.all_gather(glu_low, "dp", axis=1, tiled=True)

    seq_weight = jnp.sum(counts) / (NDOM * jnp.sum(member * counts, axis=-1))
    positions = jnp.arange(length, dtype=jnp.int32)
    token_weight = jnp.where(positions[None, :] < lengths[:, :1], seq_weight[:, :1], 0.0)
    token_weight = token_weight.reshape(rows, 1)

    own_channels = lambda v: lax.dynamic_index_in_dim(
        v.reshape(groups, narrow, own_rows), place, 1, keepdims=False
    ).reshape(channels)
    bound = own_channels(lower_bound)
    state_gain = own_channels(gain_full[1])

    token_rows = tokens.reshape(rows, full)
    seq_in = token_rows.astype(F32)
    inverse_in = inverse_rms(seq_in)
    unit_in = seq_in * inverse_in
    normed_in = (unit_in * gain_full[0]).astype(BF)
    pre = jnp.einsum("td,kde->kte", normed_in, mixer_in, preferred_element_type=F32)
    pre = pre.reshape(3, batches, length, channels)
    states, raw, square = scan_forward(pre, bound, state_gain)
    square = mp_sum_wide(square.reshape(rows, 1))
    inverse_state = lax.rsqrt(square / full + EPSILON)
    mixed = jnp.dot(raw.reshape(rows, channels), mixer_out, preferred_element_type=F32)
    back_low = (cot_full.astype(F32) * token_weight).astype(BF)
    gated_out = (raw.reshape(rows, channels).astype(F32) * inverse_state).astype(BF)
    if quick:
        mixed = mixed.astype(BF)
        came, left_back, left_in, left_out, token_weight, inverse_in = lax.optimization_barrier(
            (
                partner_swap(mixed), owner_rows(back_low), owner_rows(normed_in), owner_rows(gated_out),
                token_weight, inverse_in,
            )
        )
        mixed = mixed.astype(F32) + came.astype(F32)
    else:
        mixed = mp_sum(mixed)
    branch_mix = inverse_state * mixed
    middle = seq_in + branch_mix
    inverse_mid = inverse_rms(middle)
    unit_mid = middle * inverse_mid
    normed_mid = (unit_mid * gain_full[2]).astype(BF)

    across = (((1,), (1,)), ((), ()))
    down = (((0,), (0,)), ((), ()))
    dot = functools.partial(lax.dot_general, preferred_element_type=F32)
    if quick:
        glu_sums, glu_tail, sum_own, sum_came, half_own, half_send = glu_call(normed_mid, back_low, left_back, glu, 0)
        half_came = partner_swap(half_send)
        glu_tail = lax.psum_scatter(glu_tail, "dp", scatter_dimension=1, tiled=True)
    else:
        pre_act = jnp.dot(normed_mid, glu[0], preferred_element_type=F32)
        pre_up = jnp.dot(normed_mid, glu[1], preferred_element_type=F32)
        grad_hidden = jnp.dot(back_low, glu[2], preferred_element_type=F32)
        act_part = jax.nn.silu(pre_act)
        hidden = (act_part * pre_up).astype(BF)
        grad_act = (grad_hidden * pre_up * silu_slope(pre_act)).astype(BF)
        grad_up = (grad_hidden * act_part).astype(BF)
        grad_normed = mp_sum(dot(grad_act, glu[0], across) + dot(grad_up, glu[1], across))
        glu_grad = jnp.stack(
            [dot(normed_mid, grad_act, down), dot(normed_mid, grad_up, down), dot(back_low, hidden, down)]
        ).astype(BF)
        glu_own = lax.psum_scatter(glu_grad, "dp", scatter_dimension=1, tiled=True).astype(F32)
        branch = mp_scatter(dot(hidden, glu[2], across))
    scale = 1.0 / (batches * groups * tokens.shape[1])
    own_features = lambda v: lax.dynamic_slice_in_dim(v, place * part, part, v.ndim - 1)
    if quick:
        grad_middle_own, middle_low, state_mean, grad_gated, gain_mid = middle_back(
            sum_own, sum_came, middle, cot_full, token_rows, token_weight, gain_full[2], mixer_out
        )
        gain_mid = gain_mid[0]
    else:
        inverse_mid = inverse_rms(middle)
        unit_mid = middle * inverse_mid
        gain_mid = jnp.sum(grad_normed * unit_mid, axis=0)
        scaled_mid = grad_normed * gain_full[2]
        back = cot_full.astype(F32) * token_weight
        grad_middle = back + inverse_mid * (
            scaled_mid - unit_mid * jnp.mean(scaled_mid * unit_mid, axis=-1, keepdims=True)
        )
        grad_middle_own = own_features(grad_middle)
        middle_low = grad_middle.astype(BF)
        state_mean = jnp.mean(middle_low.astype(F32) * branch_mix, axis=-1, keepdims=True)
        grad_gated = dot(middle_low, mixer_out, across)
    by_batch = lambda v: v.reshape(batches, length, v.shape[-1])
    grad_pre, gain_state, pre_dot = scan_backward(
        pre, states, by_batch(grad_gated), by_batch(inverse_state), by_batch(state_mean), bound, state_gain
    )
    if quick:
        scattered = glu_in_master.shape[2] // LANES - TAIL
        glu_ins = (glu_in_master, glu_in_first, glu_in_second)
        glu_downs = (glu_out_master, glu_out_first, glu_out_second)
        glu_new = glu_update(
            glu_sums, lambda kind, q: (3 * q + kind, 0, 0), 0, scattered, glu_ins, glu_downs, scale
        )
        branch = half_own.astype(F32) + half_came.astype(F32)
        layer_out = (own_features(middle) + branch).astype(BF)
        layer_out, grad_pre, glu_new = lax.optimization_barrier((layer_out, grad_pre, glu_new))
    grad_pre = grad_pre.reshape(3, rows, channels)
    gain_state = jnp.sum(gain_state, axis=0).reshape(groups, 1, own_rows)
    gain_state = lax.dynamic_update_slice_in_dim(
        jnp.zeros((groups, narrow, own_rows), F32), gain_state, place, 1
    )
    device = lax.axis_index("dp") * narrow + place
    if quick:
        gain_parts = jnp.stack(
            [
                jnp.zeros((groups, narrow * own_rows), F32),
                gain_state.reshape(groups, narrow * own_rows),
                0.5 * gain_mid.reshape(groups, narrow * own_rows),
            ],
            axis=1,
        )
        gain_parts = jnp.pad(gain_parts, ((0, 0), (0, 5), (0, 0)))
        pre_dot = pre_dot.reshape(-1, 128)
        mixer_own, gain_own, grad_normed_in, dot_came = mixer_call(
            left_in, grad_pre, left_out, middle_low, gain_parts, token_rows, inverse_in, mixer_in, pre_dot, 1
        )
        in_mean = (pre_dot + dot_came).reshape(rows, 1) / full
        gain_own = lax.dynamic_slice_in_dim(gain_own[:3], place * own_rows, own_rows, 1)
    else:
        grad_mix_out = dot(gated_out, middle_low, down).astype(BF)
        grad_mix_in = jnp.einsum("td,kte->kde", normed_in, grad_pre, preferred_element_type=F32)
        in_own = lax.psum_scatter(grad_mix_in.astype(BF), "dp", scatter_dimension=1, tiled=True)
        out_own = lax.psum_scatter(grad_mix_out, "dp", scatter_dimension=0, tiled=True)
        in_own = mp_swap(in_own.reshape(3, narrow, own_rows, channels).transpose(1, 0, 2, 3))
        in_own = in_own.reshape(narrow, 3, own_rows, groups, own_rows).transpose(1, 2, 3, 0, 4)
        grad_normed_in = jnp.einsum("kte,kde->td", grad_pre, mixer_in, preferred_element_type=F32)
        gain_in = jnp.sum(grad_normed_in * unit_in, axis=0)
        grad_normed_in = mp_scatter(grad_normed_in)
        gain_rows = jnp.stack([gain_in, gain_state.reshape(full), gain_mid / narrow])
        gain_total = lax.psum(gain_rows, ("dp", "mp"))
        gain_own = lax.dynamic_slice_in_dim(gain_total, device * own_rows, own_rows, 1)
        in_mean = mp_sum_wide(pre_dot.reshape(rows, 1)) / full
        in_own = in_own.reshape(3, own_rows, full)
        mixer_own = jnp.concatenate([in_own, out_own[None]]).astype(F32)
    unit_in_own = own_features(token_rows).astype(F32) * inverse_in
    grad_seq = grad_middle_own + inverse_in * (
        grad_normed_in * own_features(gain_full[0]) - unit_in_own * in_mean
    )
    grad_tokens = grad_seq.astype(BF)
    if not quick:
        layer_out = (own_features(middle) + branch).astype(BF)

    update = functools.partial(adamw_update, count=STEP_NUMBER)
    mixer_new = update(
        mixer_master, mixer_first, mixer_second, mixer_own * scale, rate=MATRIX_RATE, decay=DECAY_RATE
    )
    gain_new = update(
        gain_master, gain_first, gain_second, gain_own * scale, rate=GAIN_RATE, decay=0.0
    )
    if quick:
        glu_new = glu_update(
            glu_tail, lambda kind, q: (kind, 0, q), scattered, TAIL, glu_ins, glu_downs, scale, glu_new
        )
    else:
        glu_in_new = update(
            glu_in_master, glu_in_first, glu_in_second, glu_own[:2] * scale,
            rate=MATRIX_RATE, decay=DECAY_RATE,
        )
        glu_out_new = update(
            glu_out_master, glu_out_first, glu_out_second, glu_own[2].T * scale,
            rate=MATRIX_RATE, decay=DECAY_RATE,
        )
        glu_new = (*glu_in_new, *glu_out_new)
    return (
        layer_out.reshape(batches, 1, length, part),
        grad_tokens.reshape(batches, 1, length, part),
        *mixer_new,
        *glu_new,
        *gain_new,
    )


def solution(mesh):
    weights = (
        [P(None, ("dp", "mp"), None)] * 3
        + [P(None, "dp", "mp")] * 3
        + [P("mp", "dp")] * 3
        + [P(None, ("dp", "mp"))] * 3
    )
    in_specs = (
        P(None, "dp", None, None),
        P(None, "dp", None, "mp"),
        P(None, "dp"),
        P(None, "dp", None),
        P(),
        *weights,
    )
    out_specs = (P(None, "dp", None, "mp"), P(None, "dp", None, "mp"), *weights)
    return jax.shard_map(shards, mesh=mesh, in_specs=in_specs, out_specs=out_specs, check_vma=False)
```

```python
import functools

import jax
import jax.numpy as jnp
from jax import lax
from jax.experimental import pallas as pl
from jax.experimental.pallas import tpu as pltpu
from jax.sharding import PartitionSpec as P

NDOM = 8

EPSILON = 1e-06
BETA_ONE = 0.9
BETA_TWO = 0.95
ADAM_EPSILON = 1e-08
DECAY_RATE = 0.1
MATRIX_RATE = 0.06
GAIN_RATE = 0.5
STEP_NUMBER = 3.0

BF = jnp.bfloat16
F32 = jnp.float32
VMEM_LIMIT = 56 * 1024 * 1024


def inverse_rms(values):
    return lax.rsqrt(jnp.mean(values * values, axis=-1, keepdims=True) + EPSILON)


def silu_slope(values):
    sigma = jax.nn.sigmoid(values)
    return sigma * (1.0 + values * (1.0 - sigma))


def adamw_update(master, first, second, gradient, count, rate, decay):
    first_new = BETA_ONE * first + (1.0 - BETA_ONE) * gradient
    second_new = BETA_TWO * second + (1.0 - BETA_TWO) * gradient * gradient
    first_hat = first_new / (1.0 - BETA_ONE**count)
    second_hat = second_new / (1.0 - BETA_TWO**count)
    master_new = master - rate * (
        first_hat / (jnp.sqrt(second_hat) + ADAM_EPSILON) + decay * master
    )
    return (master_new, first_new, second_new)


def partner_swap(value):
    return lax.ppermute(value, "mp", [(0, 1), (1, 0)])


def mp_sum(part):
    low = part.astype(BF)
    if lax.axis_size("mp") == 2:
        return low.astype(F32) + partner_swap(low).astype(F32)
    return lax.psum(low.astype(F32), "mp")


def mp_sum_wide(part):
    if lax.axis_size("mp") == 2:
        return part + partner_swap(part)
    return lax.psum(part, "mp")


def mp_scatter(part):
    if lax.axis_size("mp") == 2:
        half = part.shape[1] // 2
        place = lax.axis_index("mp")
        own = lax.dynamic_slice_in_dim(part, place * half, half, 1)
        other = lax.dynamic_slice_in_dim(part, (1 - place) * half, half, 1)
        return own.astype(BF).astype(F32) + partner_swap(other.astype(BF)).astype(F32)
    return lax.psum_scatter(part.astype(BF), "mp", scatter_dimension=1, tiled=True).astype(F32)


def mp_swap(pieces):
    if lax.axis_size("mp") == 2:
        place = lax.axis_index("mp")
        own = lax.dynamic_index_in_dim(pieces, place, 0, keepdims=False)
        came = partner_swap(lax.dynamic_index_in_dim(pieces, 1 - place, 0, keepdims=False))
        first = place == 0
        return jnp.stack([jnp.where(first, own, came), jnp.where(first, came, own)])
    return lax.all_to_all(pieces, "mp", 0, 0, tiled=False)


def mp_gather(part):
    if lax.axis_size("mp") == 2:
        place = lax.axis_index("mp")
        came = partner_swap(part)
        first = place == 0
        return jnp.concatenate([jnp.where(first, part, came), jnp.where(first, came, part)], axis=1)
    return lax.all_gather(part, "mp", axis=1, tiled=True)


SUB_ROWS = 8
TILE_ROWS = 64


def channel_block(width):
    return 512 if width % 512 == 0 else width


def scan_rows(total, decay, carry):
    row = lax.broadcasted_iota(jnp.int32, total.shape, 0)
    shift = 1
    while shift < SUB_ROWS:
        keep = row >= shift
        total = total + decay * jnp.where(keep, pltpu.roll(total, shift, 0), 0.0)
        decay = decay * jnp.where(keep, pltpu.roll(decay, shift, 0), 1.0)
        shift *= 2
    return total + decay * carry


def scan_rows_back(total, decay, carry):
    row = lax.broadcasted_iota(jnp.int32, total.shape, 0)
    shift = 1
    while shift < SUB_ROWS:
        keep = row < SUB_ROWS - shift
        total = total + decay * jnp.where(keep, pltpu.roll(total, SUB_ROWS - shift, 0), 0.0)
        decay = decay * jnp.where(keep, pltpu.roll(decay, SUB_ROWS - shift, 0), 1.0)
        shift *= 2
    return total + decay * carry


def scan_forward_kernel(pre_ref, bound_ref, gain_ref, states_ref, raw_ref, square_ref):
    length, width = states_ref.shape[1], states_ref.shape[2]
    bound = bound_ref[...]
    gain = gain_ref[...]
    first_block = pl.program_id(1) == 0

    def step(index, carry):
        rows = pl.ds(pl.multiple_of(index * TILE_ROWS, TILE_ROWS), TILE_ROWS)
        forget = bound + (1.0 - bound) * jax.nn.sigmoid(pre_ref[1, 0, rows, :])
        total = (1.0 - forget) * jax.nn.silu(pre_ref[0, 0, rows, :])
        parts = []
        for low in range(0, TILE_ROWS, SUB_ROWS):
            part = scan_rows(total[low : low + SUB_ROWS], forget[low : low + SUB_ROWS], carry)
            carry = part[SUB_ROWS - 1 : SUB_ROWS]
            parts.append(part)
        states = jnp.concatenate(parts)
        states_ref[0, rows, :] = states
        raw = states * gain * jax.nn.silu(pre_ref[2, 0, rows, :])
        raw_ref[0, rows, :] = raw.astype(raw_ref.dtype)
        square = jnp.sum(states * states, axis=-1, keepdims=True)
        square_ref[0, rows, :] = square + jnp.where(first_block, 0.0, square_ref[0, rows, :])
        return carry

    lax.fori_loop(0, length // TILE_ROWS, step, jnp.zeros((1, width), F32))


def scan_forward(pre, bound, gain):
    _, batches, length, width = pre.shape
    block = channel_block(width)
    return pl.pallas_call(
        scan_forward_kernel,
        grid=(batches, width // block),
        in_specs=[
            pl.BlockSpec((3, 1, length, block), lambda b, c: (0, b, 0, c)),
            pl.BlockSpec((1, block), lambda b, c: (0, c)),
            pl.BlockSpec((1, block), lambda b, c: (0, c)),
        ],
        out_specs=[
            pl.BlockSpec((1, length, block), lambda b, c: (b, 0, c)),
            pl.BlockSpec((1, length, block), lambda b, c: (b, 0, c)),
            pl.BlockSpec((1, length, 1), lambda b, c: (b, 0, 0)),
        ],
        out_shape=[
            jax.ShapeDtypeStruct((batches, length, width), F32),
            jax.ShapeDtypeStruct((batches, length, width), BF),
            jax.ShapeDtypeStruct((batches, length, 1), F32),
        ],
        compiler_params=pltpu.CompilerParams(vmem_limit_bytes=VMEM_LIMIT),
        cost_estimate=pl.CostEstimate(
            flops=batches * length * width * 40,
            bytes_accessed=batches * length * width * 18,
            transcendentals=batches * length * width * 3,
        ),
    )(pre, bound[None], gain[None])


def scan_backward_kernel(
    pre_ref, states_ref, gated_ref, inverse_ref, mean_ref, bound_ref, gain_ref,
    grad_ref, gain_grad_ref, dot_ref,
):
    length, width = states_ref.shape[1], states_ref.shape[2]
    bound = bound_ref[...]
    gain = gain_ref[...]
    first_block = pl.program_id(1) == 0
    row = lax.broadcasted_iota(jnp.int32, (TILE_ROWS, width), 0)
    tiles = length // TILE_ROWS

    def step(index, carry):
        carried_next, forget_next, gain_sum = carry
        place = tiles - 1 - index
        rows = pl.ds(pl.multiple_of(place * TILE_ROWS, TILE_ROWS), TILE_ROWS)
        pre_input = pre_ref[0, 0, rows, :]
        pre_forget = pre_ref[1, 0, rows, :]
        pre_gate = pre_ref[2, 0, rows, :]
        states = states_ref[0, rows, :]
        inverse = inverse_ref[0, rows, :]
        grad_gated = gated_ref[0, rows, :]
        unit = states * inverse
        gate_sig = jax.nn.sigmoid(pre_gate)
        gate = pre_gate * gate_sig
        gain_sum = gain_sum + grad_gated * unit * gate
        scaled = grad_gated * gain
        grad_gate = (scaled * unit * (gate_sig * (1.0 + pre_gate * (1.0 - gate_sig)))).astype(BF)
        grad_ref[2, 0, rows, :] = grad_gate
        total = inverse * (scaled * gate - unit * mean_ref[0, rows, :])
        sigma = jax.nn.sigmoid(pre_forget)
        forget = bound + (1.0 - bound) * sigma
        decay = jnp.where(row == TILE_ROWS - 1, forget_next, pltpu.roll(forget, TILE_ROWS - 1, 0))
        parts = []
        for low in range(TILE_ROWS - SUB_ROWS, -1, -SUB_ROWS):
            part = scan_rows_back(
                total[low : low + SUB_ROWS], decay[low : low + SUB_ROWS], carried_next
            )
            carried_next = part[0:1]
            parts.insert(0, part)
        carried = jnp.concatenate(parts)
        before_rows = pl.ds(
            pl.multiple_of(jnp.maximum(place - 1, 0) * TILE_ROWS, TILE_ROWS), TILE_ROWS
        )
        before = states_ref[0, before_rows, :][TILE_ROWS - 1 : TILE_ROWS, :]
        before = jnp.where(place == 0, 0.0, before)
        earlier = jnp.where(row == 0, before, pltpu.roll(states, 1, 0))
        input_sig = jax.nn.sigmoid(pre_input)
        fresh = pre_input * input_sig
        slope = input_sig * (1.0 + pre_input * (1.0 - input_sig))
        grad_input = (carried * (1.0 - forget) * slope).astype(BF)
        grad_forget = (
            carried * (earlier - fresh) * (1.0 - bound) * sigma * (1.0 - sigma)
        ).astype(BF)
        grad_ref[0, 0, rows, :] = grad_input
        grad_ref[1, 0, rows, :] = grad_forget
        dots = (
            grad_input.astype(F32) * pre_input
            + grad_forget.astype(F32) * pre_forget
            + grad_gate.astype(F32) * pre_gate
        )
        dot = jnp.sum(dots, axis=-1, keepdims=True)
        dot_ref[0, rows, :] = dot + jnp.where(first_block, 0.0, dot_ref[0, rows, :])
        return carried_next, forget[0:1, :], gain_sum

    zero = jnp.zeros((1, width), F32)
    _, _, gain_sum = lax.fori_loop(
        0, tiles, step, (zero, zero, jnp.zeros((TILE_ROWS, width), F32))
    )
    gain_grad_ref[0] = jnp.sum(gain_sum, axis=0, keepdims=True)


def scan_backward(pre, states, grad_gated, inverse, mean, bound, gain):
    _, batches, length, width = pre.shape
    block = channel_block(width)
    whole = pl.BlockSpec((1, length, block), lambda b, c: (b, 0, c))
    column = pl.BlockSpec((1, length, 1), lambda b, c: (b, 0, 0))
    line = pl.BlockSpec((1, block), lambda b, c: (0, c))
    three = pl.BlockSpec((3, 1, length, block), lambda b, c: (0, b, 0, c))
    return pl.pallas_call(
        scan_backward_kernel,
        grid=(batches, width // block),
        in_specs=[three, whole, whole, column, column, line, line],
        out_specs=[
            three,
            pl.BlockSpec((1, 1, block), lambda b, c: (b, 0, c)),
            column,
        ],
        out_shape=[
            jax.ShapeDtypeStruct((3, batches, length, width), BF),
            jax.ShapeDtypeStruct((batches, 1, width), F32),
            jax.ShapeDtypeStruct((batches, length, 1), F32),
        ],
        compiler_params=pltpu.CompilerParams(vmem_limit_bytes=VMEM_LIMIT),
        cost_estimate=pl.CostEstimate(
            flops=batches * length * width * 80,
            bytes_accessed=batches * length * width * 28,
            transcendentals=batches * length * width * 3,
        ),
    )(pre, states, grad_gated, inverse, mean, bound[None], gain[None])


MESH_ID = pl.DeviceIdType.MESH
DEPTH = 4
LANES = 256
X_LAG = 4
Z_LAG = X_LAG + 2
SWAP_LAG = 2
TAIL = 2


def device_place():
    dp = lax.axis_index("dp")
    return dp // 4, lax.rem(dp // 2, 2), lax.rem(dp, 2)


def device_at(z, x, core):
    return (z * 4 + x * 2 + core, lax.axis_index("mp"))


def greet(z, x, core):
    barrier = pltpu.get_barrier_semaphore()
    targets = [device_at(z, x, 1 - core), device_at(z, 1 - x, core)]
    targets += [device_at(lax.rem(z + hop, DEPTH), x, core) for hop in range(1, DEPTH)]
    targets.append((lax.axis_index("dp"), 1 - lax.axis_index("mp")))
    for target in targets:
        pl.semaphore_signal(barrier, 1, device_id=target, device_id_type=MESH_ID)


def await_partners():
    pl.semaphore_wait(pltpu.get_barrier_semaphore(), DEPTH + 2)


def scatter_step(step, chunks, compute, finish, scratch, small_last=False):
    (own, core_out, core_in, keep, x_out, x_in, sums, mine, z_out, z_in,
     core_send, core_recv, x_send, x_recv, z_send, z_recv) = scratch
    z, x, core = device_place()

    def core_copy(p, cut=()):
        return pltpu.make_async_remote_copy(
            core_out.at[(lax.rem(p, 2), *cut)], core_in.at[(lax.rem(p, 4), *cut)],
            core_send.at[lax.rem(p, 2)], core_recv.at[lax.rem(p, 4)],
            device_id=device_at(z, x, 1 - core), device_id_type=MESH_ID)

    def x_copy(p, cut=()):
        return pltpu.make_async_remote_copy(
            x_out.at[(lax.rem(p, X_LAG), *cut)], x_in.at[(lax.rem(p, 2 * X_LAG), *cut)],
            x_send.at[lax.rem(p, X_LAG)], x_recv.at[lax.rem(p, 2 * X_LAG)],
            device_id=device_at(z, 1 - x, core), device_id_type=MESH_ID)

    def z_copy(p, hop, cut=()):
        return pltpu.make_async_remote_copy(
            z_out.at[(lax.rem(p, 4), hop - 1, *cut)], z_in.at[(lax.rem(p, 8), hop - 1, *cut)],
            z_send.at[lax.rem(p, 4), hop - 1], z_recv.at[lax.rem(p, 8), hop - 1],
            device_id=device_at(lax.rem(z + hop, DEPTH), x, core), device_id_type=MESH_ID)

    corner = (slice(0, 16), slice(0, 128))
    every = slice(None)

    def go(copy, lead, p, act):
        if not small_last:
            act(copy(p))
            return
        pl.when(p < chunks - 1)(lambda: act(copy(p)))
        pl.when(p == chunks - 1)(lambda: act(copy(p, (*(every,) * lead, *corner))))

    def core_go(p, act):
        go(core_copy, 2, p, act)

    def x_go(p, act):
        go(x_copy, 1, p, act)

    def z_go(p, hop, act):
        go(lambda p, cut=(): z_copy(p, hop, cut), 0, p, act)

    start, wait_recv, wait_send = (
        lambda copy: copy.start(), lambda copy: copy.wait_recv(), lambda copy: copy.wait_send())

    @pl.when(step < chunks)
    def _():
        @pl.when(step >= 2)
        def _():
            core_go(step - 2, wait_send)

        def to_partner(value):
            core_out[lax.rem(step, 2)] = value.astype(BF)

        def to_own(value):
            own[lax.rem(step, 2)] = value

        compute(step, 1 - core, to_partner)
        core_go(step, start)
        compute(step, core, to_own)

    @pl.when((step >= 1) & (step < chunks + 1))
    def _():
        p = step - 1
        core_go(p, wait_recv)

        @pl.when(p >= X_LAG)
        def _():
            x_go(p - X_LAG, wait_send)

        two, four, slot = lax.rem(p, 2), lax.rem(p, 4), lax.rem(p, X_LAG)
        x_out[slot] = (own[two, :, 1 - x] + core_in[four, :, 1 - x].astype(F32)).astype(BF)
        x_go(p, start)
        keep[slot] = own[two, :, x] + core_in[four, :, x].astype(F32)

    @pl.when((step >= X_LAG) & (step < chunks + X_LAG))
    def _():
        p = step - X_LAG
        x_go(p, wait_recv)
        four = lax.rem(p, 4)
        sums[...] = keep[lax.rem(p, X_LAG)] + x_in[lax.rem(p, 2 * X_LAG)].astype(F32)
        for hop in range(1, DEPTH):
            @pl.when(p >= 4)
            def _():
                z_go(p - 4, hop, wait_send)

            z_out[four, hop - 1] = sums[lax.rem(z + hop, DEPTH)].astype(BF)
            z_go(p, hop, start)
        mine[four] = sums[z]

    @pl.when((step >= Z_LAG) & (step < chunks + Z_LAG))
    def _():
        p = step - Z_LAG
        for hop in range(1, DEPTH):
            z_go(p, hop, wait_recv)
        got = z_in.at[lax.rem(p, 8)]
        finish(p, mine[lax.rem(p, 4)] + got[0].astype(F32) + got[1].astype(F32) + got[2].astype(F32))

    @pl.when(step == chunks + Z_LAG - 1)
    def _():
        for p in range(chunks - 2, chunks):
            core_go(jnp.int32(p), wait_send)
        for p in range(chunks - X_LAG, chunks):
            x_go(jnp.int32(p), wait_send)
        for p in range(chunks - 4, chunks):
            for hop in range(1, DEPTH):
                z_go(jnp.int32(p), hop, wait_send)


def scatter_scratch(rows, lanes):
    quad = (DEPTH, 2, rows, lanes)
    line = (DEPTH, rows, lanes)
    dma = pltpu.SemaphoreType.DMA
    return [
        pltpu.VMEM((2, *quad), F32),
        pltpu.VMEM((2, *quad), BF),
        pltpu.VMEM((4, *quad), BF),
        pltpu.VMEM((X_LAG, *line), F32),
        pltpu.VMEM((X_LAG, *line), BF),
        pltpu.VMEM((2 * X_LAG, *line), BF),
        pltpu.VMEM(line, F32),
        pltpu.VMEM((4, rows, lanes), F32),
        pltpu.VMEM((4, DEPTH - 1, rows, lanes), BF),
        pltpu.VMEM((8, DEPTH - 1, rows, lanes), BF),
        dma((2,)), dma((4,)), dma((X_LAG,)), dma((2 * X_LAG,)), dma((4, DEPTH - 1)), dma((8, DEPTH - 1)),
    ]


def scatter_out(chunks, rows, lanes):
    spec = pl.BlockSpec((1, rows, lanes), lambda q: (jnp.maximum(q - Z_LAG, 0), 0, 0))
    return spec, jax.ShapeDtypeStruct((chunks, rows, lanes), F32)


def fixed(shape):
    return pl.BlockSpec(shape, lambda q: (0,) * len(shape), pipeline_mode=pl.Buffered(1))


def glu_kernel(
    hidden_blocks, full_blocks, normed_ref, back_ref, left_ref, left_back_ref, glu_ref,
    out_ref, sum_own, sum_came, half_own, half_send, tail_ref,
    tail_stage, tail_sem, left, left_back, left_sem, acts, weights_in, weights_back, sum_stage, half_stage,
    in_sem, back_sem, stage_sem, sum_send, sum_recv, *scratch,
):
    z, x, core = device_place()
    dp, mp = lax.axis_index("dp"), lax.axis_index("mp")
    step = pl.program_id(0)
    scattered = hidden_blocks - TAIL
    chunks = 3 * scattered
    rows = normed_ref.shape[0]
    row_block = rows // 2
    half_blocks = full_blocks // 2
    across = (((1,), (1,)), ((), ()))
    spread = min(hidden_blocks + hidden_blocks // 2, 16)
    second = step - spread

    def first_tasks(at):
        return at * hidden_blocks // spread

    def second_task(at):
        return 2 * at // 3

    def has_second(at):
        return (at == 0) | (
            (at > 0) & (second_task(at) > second_task(at - 1)) & (second_task(at) < full_blocks))

    unit_block = first_tasks(step)

    def lane_block(index):
        return pl.ds(pl.multiple_of(index * LANES, LANES), LANES)

    def load_in(index):
        return pltpu.make_async_copy(glu_ref.at[:, :, lane_block(index)], weights_in, in_sem)

    def load_back(index):
        return pltpu.make_async_copy(glu_ref.at[:, lane_block(index), :], weights_back, back_sem)

    def stage(index, kind, target):
        source = (sum_stage, half_stage)[kind].at[lax.rem(index, 2)]
        return pltpu.make_async_copy(source, target, stage_sem.at[lax.rem(index, 2), kind])

    def half_spot(index):
        return lax.rem(index, half_blocks)

    def sum_copy(index):
        return pltpu.make_async_remote_copy(
            sum_own.at[:, lane_block(index)], sum_came.at[:, lane_block(index)],
            sum_send.at[index], sum_recv.at[index], device_id=(dp, 1 - mp), device_id_type=MESH_ID)

    left_loads = (
        pltpu.make_async_copy(left_ref, left, left_sem.at[0]),
        pltpu.make_async_copy(left_back_ref, left_back, left_sem.at[1]),
    )

    @pl.when(step == 0)
    def _():
        greet(z, x, core)
        for one in (load_in(0), *left_loads, load_back(0)):
            one.start()

    @pl.when((step < spread) & ((step == 0) | (unit_block > first_tasks(step - 1))))
    def _():
        load_in(unit_block).wait()
        lanes = lane_block(unit_block)

        def part(index, _):
            part_rows = pl.ds(pl.multiple_of(index * row_block, row_block), row_block)
            normed = normed_ref[part_rows, :]
            pre_act = jnp.dot(normed, weights_in[0], preferred_element_type=F32)
            pre_up = jnp.dot(normed, weights_in[1], preferred_element_type=F32)
            grad_hidden = jnp.dot(back_ref[part_rows, :], weights_in[2], preferred_element_type=F32)
            sigma = jax.nn.sigmoid(pre_act)
            act_part = pre_act * sigma
            acts[0, part_rows, lanes] = (
                grad_hidden * pre_up * (sigma * (1.0 + pre_act * (1.0 - sigma)))).astype(BF)
            acts[1, part_rows, lanes] = (grad_hidden * act_part).astype(BF)
            acts[2, part_rows, lanes] = (act_part * pre_up).astype(BF)
            return 0

        lax.fori_loop(0, rows // row_block, part, 0)

        @pl.when(unit_block + 1 < hidden_blocks)
        def _():
            load_in(unit_block + 1).start()

    @pl.when(step == 0)
    def _():
        await_partners()

    @pl.when(has_second(second - 1))
    def _():
        index = second_task(second - 1)
        stage(index, 0, sum_own.at[:, lane_block(index)]).wait()
        sum_copy(index).start()
        spot = half_spot(index)
        stage(index, 1, half_own.at[:, lane_block(spot)]).wait()

    @pl.when(has_second(second))
    def _():
        index = second_task(second)
        load_back(index).wait()
        slot = lax.rem(index, 2)

        def part(at, _):
            part_rows = pl.ds(pl.multiple_of(at * row_block, row_block), row_block)
            dot = functools.partial(
                lax.dot_general, dimension_numbers=across, preferred_element_type=F32)
            grad_normed = dot(acts[0, part_rows, :], weights_back[0])
            grad_normed += dot(acts[1, part_rows, :], weights_back[1])
            sum_stage[slot, part_rows, :] = grad_normed.astype(BF)
            half_stage[slot, part_rows, :] = dot(acts[2, part_rows, :], weights_back[2]).astype(BF)
            return 0

        lax.fori_loop(0, rows // row_block, part, 0)

        @pl.when(index + 1 < full_blocks)
        def _():
            load_back(index + 1).start()

        stage(index, 0, sum_own.at[:, lane_block(index)]).start()
        spot = half_spot(index)

        @pl.when(index // half_blocks == mp)
        def _():
            stage(index, 1, half_own.at[:, lane_block(spot)]).start()

        @pl.when(index // half_blocks != mp)
        def _():
            stage(index, 1, half_send.at[:, lane_block(spot)]).start()

    def compute(q, core_side, store):
        kind = lax.rem(q, 3)
        side_rows = left.shape[3]

        def product(side_ref):
            side = side_ref[:, :, core_side].reshape(DEPTH * 2 * side_rows, rows)
            right = acts[kind, :, lane_block(q // 3)]
            store(jnp.dot(side, right, preferred_element_type=F32).reshape(
                DEPTH, 2, side_rows, LANES))

        pl.when(kind < 2)(lambda: product(left))
        pl.when(kind == 2)(lambda: product(left_back))

    @pl.when(step == 0)
    def _():
        for one in left_loads:
            one.wait()

    def finish(p, value):
        out_ref[0] = value

    scatter_step(step, chunks, compute, finish, scratch)

    def tail_copy(index):
        spot = tail_ref.at[lax.rem(index, 3), :, :, :, :, lane_block(index // 3)]
        return pltpu.make_async_copy(
            tail_stage.at[lax.rem(index, 2)], spot, tail_sem.at[lax.rem(index, 2)])

    tail_start = chunks + Z_LAG - 3 * TAIL

    @pl.when(step >= tail_start)
    def _():
        index = step - tail_start

        @pl.when(index >= 2)
        def _():
            tail_copy(index - 2).wait()

        for side in (0, 1):
            def to_stage(value):
                tail_stage[lax.rem(index, 2), :, :, side] = value.astype(BF)

            compute(chunks + index, side, to_stage)
        tail_copy(index).start()

    @pl.when(step == chunks + Z_LAG - 1)
    def _():
        for index in range(3 * TAIL - 2, 3 * TAIL):
            tail_copy(jnp.int32(index)).wait()
        for index in range(full_blocks):
            sum_copy(index).wait()


def glu_call(normed, back_low, left_back, glu, collective):
    rows, full = normed.shape
    hidden = glu.shape[2]
    hidden_blocks, full_blocks = hidden // LANES, full // LANES
    block = full // 16
    chunks = 3 * (hidden_blocks - TAIL)
    left_shape = (DEPTH, 2, 2, block, rows)
    any_space = pl.BlockSpec(memory_space=pl.ANY)
    out_spec, out_shape = scatter_out(chunks, block, LANES)
    dma = pltpu.SemaphoreType.DMA
    wide = jax.ShapeDtypeStruct((rows, full), BF)
    half = jax.ShapeDtypeStruct((rows, full // 2), BF)
    out, sum_own, sum_came, half_own, half_send, tail = pl.pallas_call(
        functools.partial(glu_kernel, hidden_blocks, full_blocks),
        grid=(chunks + Z_LAG,),
        in_specs=[fixed(normed.shape), fixed(back_low.shape)] + [any_space] * 3,
        out_specs=[out_spec] + [any_space] * 5,
        out_shape=[
            out_shape, wide, wide, half, half,
            jax.ShapeDtypeStruct((3, DEPTH, 2, 2, block, TAIL * LANES), BF),
        ],
        scratch_shapes=[
            pltpu.VMEM((2, DEPTH, 2, 2, block, LANES), BF),
            dma((2,)),
            pltpu.VMEM(left_shape, BF),
            pltpu.VMEM(left_shape, BF),
            dma((2,)),
            pltpu.VMEM((3, rows, hidden), BF),
            pltpu.VMEM((3, full, LANES), BF),
            pltpu.VMEM((3, LANES, hidden), BF),
            pltpu.VMEM((2, rows, LANES), BF),
            pltpu.VMEM((2, rows, LANES), BF),
            dma(()), dma(()), dma((2, 2)),
            dma((full_blocks,)), dma((full_blocks,)),
            *scatter_scratch(block, LANES),
        ],
        compiler_params=pltpu.CompilerParams(
            collective_id=collective, has_side_effects=True, vmem_limit_bytes=62 * 1024 * 1024),
        cost_estimate=pl.CostEstimate(
            flops=18 * rows * full * hidden, bytes_accessed=6 * full * hidden * 2,
            transcendentals=rows * hidden),
    )(normed, back_low, owner_rows(normed), left_back, glu)
    return out, tail.reshape(3, full, TAIL * LANES), sum_own, sum_came, half_own, half_send


def mixer_kernel(
    full_blocks, left_hbm, grad_hbm, left_out_ref, right_out_ref, gain_ref, tokens_ref, inverse_ref,
    weights_ref, dot_ref, out_ref, gain_out, half_own, half_send, half_came, dot_came,
    left_ref, grad_ref, big_sem, weights, token_block, gain_sum, gain_chunk, total, swap_out, swap_in, half_stage,
    load_sem, stage_sem, half_send_sem, half_recv, swap_send, swap_recv, dot_sem, *scratch,
):
    z, x, core = device_place()
    dp, mp = lax.axis_index("dp"), lax.axis_index("mp")
    step = pl.program_id(0)
    tokens, channels = grad_ref.shape[1], grad_ref.shape[2]
    block, half = left_ref.shape[3], left_out_ref.shape[3]
    outer = full_blocks // 2
    across = channels // LANES
    gains = outer + 3 * across
    chunks = gains + 1
    half_blocks = full_blocks // 2
    row_block = tokens // 2
    partner = (dp, 1 - mp)

    def lane_block(index):
        return pl.ds(pl.multiple_of(index * LANES, LANES), LANES)

    def loads(index):
        return (
            pltpu.make_async_copy(weights_ref.at[:, lane_block(index), :], weights, load_sem.at[0]),
            pltpu.make_async_copy(tokens_ref.at[:, lane_block(index)], token_block, load_sem.at[1]),
        )

    def stage(index, target):
        return pltpu.make_async_copy(
            half_stage.at[lax.rem(index, 2)], target, stage_sem.at[lax.rem(index, 2)])

    def half_copy(spot):
        return pltpu.make_async_remote_copy(
            half_send.at[:, lane_block(spot)], half_came.at[:, lane_block(spot)],
            half_send_sem.at[spot], half_recv.at[spot], device_id=partner, device_id_type=MESH_ID)

    def swap_copy(index):
        return pltpu.make_async_remote_copy(
            swap_out.at[lax.rem(index, 2)], swap_in.at[lax.rem(index, 8)],
            swap_send.at[lax.rem(index, 2)], swap_recv.at[lax.rem(index, 8)],
            device_id=partner, device_id_type=MESH_ID)

    big_loads = (
        pltpu.make_async_copy(grad_hbm, grad_ref, big_sem.at[0]),
        pltpu.make_async_copy(left_hbm, left_ref, big_sem.at[1]),
    )
    dot_copy = pltpu.make_async_remote_copy(
        dot_ref, dot_came, dot_sem.at[0], dot_sem.at[1], device_id=partner, device_id_type=MESH_ID)

    @pl.when(step == 0)
    def _():
        greet(z, x, core)
        for one in (*big_loads, *loads(0)):
            one.start()
        gain_chunk[...] = jnp.zeros_like(gain_chunk)
        gain_sum[...] = jnp.zeros_like(gain_sum)
        await_partners()
        dot_copy.start()

    @pl.when(step == 1)
    def _():
        for one in big_loads:
            one.wait()

    task = (step - 1) // 2

    @pl.when((step >= 2) & (step <= 2 * full_blocks) & (lax.rem(step, 2) == 0))
    def _():
        index = task
        spot = lax.rem(index, half_blocks)
        stage(index, half_own.at[:, lane_block(spot)]).wait()

        @pl.when(index // half_blocks != mp)
        def _():
            half_copy(spot).start()

    @pl.when((step < 2 * full_blocks) & (lax.rem(step, 2) == 1))
    def _():
        for one in loads(task):
            one.wait()
        slot = lax.rem(task, 2)
        spot = lax.rem(task, half_blocks)

        def part(at, gain_in):
            part_rows = pl.ds(pl.multiple_of(at * row_block, row_block), row_block)
            dot = functools.partial(
                lax.dot_general, dimension_numbers=(((1,), (1,)), ((), ())), preferred_element_type=F32)
            grad = dot(grad_ref[0, part_rows, :], weights[0])
            grad += dot(grad_ref[1, part_rows, :], weights[1])
            grad += dot(grad_ref[2, part_rows, :], weights[2])
            half_stage[slot, part_rows, :] = grad.astype(BF)
            unit = token_block[part_rows, :].astype(F32) * inverse_ref[part_rows, :]
            return gain_in + jnp.sum(grad * unit, axis=0, keepdims=True)

        gain_in = lax.fori_loop(0, tokens // row_block, part, jnp.zeros((1, LANES), F32))
        gain_sum[2 * task, 0:1, :] = gain_in[:, :128]
        gain_sum[2 * task + 1, 0:1, :] = gain_in[:, 128:]

        @pl.when(task + 1 < full_blocks)
        def _():
            for one in loads(task + 1):
                one.start()

        @pl.when(task // half_blocks == mp)
        def _():
            stage(task, half_own.at[:, lane_block(spot)]).start()

        @pl.when(task // half_blocks != mp)
        def _():
            stage(task, half_send.at[:, lane_block(spot)]).start()

    def compute(q, core_side, store):
        @pl.when(q < outer)
        def _():
            side = left_out_ref[:, :, core_side].reshape(channels // 2, tokens)
            parts = [
                jnp.dot(side, right_out_ref[:, lane_block(2 * q + at)], preferred_element_type=F32)
                for at in (0, 1)
            ]
            parts = [part.reshape(DEPTH, 2, half, LANES) for part in parts]
            store(jnp.concatenate(parts, axis=2))

        @pl.when((q >= outer) & (q < gains))
        def _():
            at = q - outer
            side = left_ref[:, :, core_side].reshape(DEPTH * 2 * block, tokens)
            right = grad_ref[at // across, :, lane_block(lax.rem(at, across))]
            store(jnp.dot(side, right, preferred_element_type=F32).reshape(DEPTH, 2, block, LANES))

        @pl.when(q == gains)
        def _():
            for owner in range(2 * DEPTH):
                line = 2 * owner + core_side
                gain_chunk[owner // 2, owner % 2, 0:8, 0:128] = gain_ref[line] + gain_sum[line]
            store(gain_chunk[...])

    def finish(p, value):
        total[lax.rem(p, 4)] = value

        @pl.when(p >= outer)
        def _():
            index = p - outer

            @pl.when(index >= 2)
            def _():
                swap_copy(index - 2).wait_send()

            first = jnp.where(p == gains, 0, 1 - mp) * half
            rows = pl.ds(pl.multiple_of(first, half), half)
            swap_out[lax.rem(index, 2)] = total[lax.rem(p, 4), rows, :].astype(BF)
            swap_copy(index).start()

    scatter_step(step, chunks, compute, finish, scratch, small_last=True)

    @pl.when((step >= Z_LAG + SWAP_LAG) & (step < chunks + Z_LAG + SWAP_LAG))
    def _():
        p = step - Z_LAG - SWAP_LAG
        slot = lax.rem(p, 4)

        @pl.when(p < outer)
        def _():
            out_ref[0, :, :LANES] = total[slot, :half, :]
            out_ref[0, :, LANES:] = total[slot, half:, :]

        @pl.when(p >= outer)
        def _():
            swap_copy(p - outer).wait_recv()
            came = swap_in[lax.rem(p - outer, 8)].astype(F32)

            @pl.when(p < gains)
            def _():
                own = total[slot, pl.ds(pl.multiple_of(mp * half, half), half), :]
                first = jnp.where(mp == 0, own, came)
                second = jnp.where(mp == 0, came, own)
                for tile in (0, 1):
                    lanes = slice(128 * tile, 128 * tile + 128)
                    left, right = split_lanes(first[:, lanes], second[:, lanes])
                    out_ref[0, :, 256 * tile : 256 * tile + 128] = left
                    out_ref[0, :, 256 * tile + 128 : 256 * tile + 256] = right

            @pl.when(p == gains)
            def _():
                gain_out[...] = total[slot, 0:8, 0:128] + came[0:8, 0:128]

    @pl.when(step == chunks + Z_LAG + SWAP_LAG - 1)
    def _():
        for spot in range(half_blocks):
            half_copy(spot).wait()
        for index in range(gains - outer - 1, gains - outer + 1):
            swap_copy(index).wait_send()
        dot_copy.wait()


def mixer_call(
    left_in, grad_pre, left_out, right_out, gain_parts, tokens, inverse, weights, dots, collective
):
    _, rows, channels = grad_pre.shape
    full = right_out.shape[1]
    block, half = full // 16, channels // 16
    full_blocks, across = full // LANES, channels // LANES
    outer, inner = full_blocks // 2, 3 * across
    chunks = outer + inner + 1
    any_space = pl.BlockSpec(memory_space=pl.ANY)
    dma = pltpu.SemaphoreType.DMA
    part = jax.ShapeDtypeStruct((rows, full // 2), BF)

    def out_place(q):
        p = jnp.clip(q - Z_LAG - SWAP_LAG, 0, outer + inner - 1)
        inside = jnp.maximum(p - outer, 0)
        return (
            jnp.where(p < outer, 3, inside // across), 0, jnp.where(p < outer, p, lax.rem(inside, across)))

    out, gains, half_own, _, half_came, dot_came = pl.pallas_call(
        functools.partial(mixer_kernel, full_blocks),
        grid=(chunks + Z_LAG + SWAP_LAG,),
        in_specs=[
            any_space, any_space,
            fixed((DEPTH, 2, 2, half, rows)), fixed(right_out.shape), fixed(gain_parts.shape),
            any_space, fixed(inverse.shape), any_space, any_space,
        ],
        out_specs=[
            pl.BlockSpec((1, half, 2 * LANES), out_place),
            pl.BlockSpec((8, 128), lambda q: (0, 0)),
        ] + [any_space] * 4,
        out_shape=[
            jax.ShapeDtypeStruct((4, half, full), F32), jax.ShapeDtypeStruct((8, 128), F32),
            part, part, part, jax.ShapeDtypeStruct(dots.shape, F32),
        ],
        scratch_shapes=[
            pltpu.VMEM((DEPTH, 2, 2, block, rows), BF),
            pltpu.VMEM(grad_pre.shape, BF),
            dma((2,)),
            pltpu.VMEM((3, LANES, channels), BF),
            pltpu.VMEM((rows, LANES), BF),
            pltpu.VMEM((16, 8, 128), F32),
            pltpu.VMEM((DEPTH, 2, block, LANES), F32),
            pltpu.VMEM((4, block, LANES), F32),
            pltpu.VMEM((2, half, LANES), BF),
            pltpu.VMEM((8, half, LANES), BF),
            pltpu.VMEM((2, rows, LANES), BF),
            dma((2,)), dma((2,)), dma((full_blocks // 2,)), dma((full_blocks // 2,)),
            dma((2,)), dma((8,)), dma((2,)),
            *scatter_scratch(block, LANES),
        ],
        compiler_params=pltpu.CompilerParams(
            collective_id=collective, has_side_effects=True, vmem_limit_bytes=VMEM_LIMIT),
        cost_estimate=pl.CostEstimate(
            flops=14 * full * rows * channels, bytes_accessed=16 * full * channels, transcendentals=0),
    )(
        left_in, grad_pre, left_out, right_out, gain_parts, tokens, inverse, weights, dots,
    )
    return out, gains, half_own.astype(F32) + half_came.astype(F32), dot_came


def transpose_kernel(in_ref, out_ref):
    turned = in_ref[...].T
    out_ref[...] = turned.reshape(out_ref.shape)


def owner_rows(value, owners=2):
    rows, width = value.shape
    block = width // 16
    return pl.pallas_call(
        transpose_kernel,
        grid=(2 * DEPTH,),
        in_specs=[pl.BlockSpec((rows, owners * block), lambda q: (0, q))],
        out_specs=pl.BlockSpec((1, 1, owners, block, rows), lambda q: (q // 2, lax.rem(q, 2), 0, 0, 0)),
        out_shape=jax.ShapeDtypeStruct((DEPTH, 2, owners, block, rows), value.dtype),
        compiler_params=pltpu.CompilerParams(vmem_limit_bytes=VMEM_LIMIT),
        cost_estimate=pl.CostEstimate(flops=0, bytes_accessed=4 * rows * width, transcendentals=0),
    )(value)


def middle_back_kernel(
    sum_own_ref, sum_came_ref, middle_ref, cot_ref, tokens_ref, weight_ref, gain_ref, mixer_ref,
    grad_own_ref, low_ref, mean_ref, gated_ref, gain_grad_ref,
):
    rows, full = middle_ref.shape
    part = full // 2
    middle = middle_ref[...]
    inverse = lax.rsqrt(jnp.mean(middle * middle, axis=-1, keepdims=True) + EPSILON)
    unit = middle * inverse
    grad_normed = sum_own_ref[...].astype(F32) + sum_came_ref[...].astype(F32)
    product = grad_normed * unit
    before = jnp.where(pl.program_id(0) == 0, 0.0, gain_grad_ref[...])
    gain_grad_ref[...] = before + jnp.sum(product, axis=0, keepdims=True)
    dots = jnp.mean(product * gain_ref[...], axis=-1, keepdims=True)
    back = cot_ref[...].astype(F32) * weight_ref[...]
    grad = back + inverse * (grad_normed * gain_ref[...] - unit * dots)
    first = lax.axis_index("mp") == 0
    grad_own_ref[...] = jnp.where(first, grad[:, :part], grad[:, part:])
    low = grad.astype(BF)
    low_ref[...] = low
    branch = middle - tokens_ref[...].astype(F32)
    mean_ref[...] = jnp.mean(low.astype(F32) * branch, axis=-1, keepdims=True)
    gated_ref[...] = lax.dot_general(
        low, mixer_ref[...], (((1,), (1,)), ((), ())), preferred_element_type=F32)


def middle_back(sum_own, sum_came, middle, cot, tokens, weight, gain, mixer_out):
    rows, full = middle.shape
    channels = mixer_out.shape[0]
    step = 224 if rows % 224 == 0 else rows
    line = lambda width: pl.BlockSpec((step, width), lambda r: (r, 0))
    shape = jax.ShapeDtypeStruct
    return pl.pallas_call(
        middle_back_kernel,
        grid=(rows // step,),
        in_specs=[line(full)] * 5 + [line(1), fixed((1, full)), fixed(mixer_out.shape)],
        out_specs=[
            line(full // 2), line(full), line(1), line(channels),
            pl.BlockSpec((1, full), lambda r: (0, 0)),
        ],
        out_shape=[
            shape((rows, full // 2), F32), shape((rows, full), BF), shape((rows, 1), F32),
            shape((rows, channels), F32), shape((1, full), F32),
        ],
        compiler_params=pltpu.CompilerParams(vmem_limit_bytes=VMEM_LIMIT),
        cost_estimate=pl.CostEstimate(
            flops=2 * rows * full * channels, bytes_accessed=rows * full * 20, transcendentals=0),
    )(sum_own, sum_came, middle, cot, tokens, weight, gain[None], mixer_out)


def glu_update_kernel(scale, act_ref, up_ref, out_ref, *refs):
    in_refs, down_refs, in_new, down_new = refs[:3], refs[3:6], refs[-6:-3], refs[-3:]
    count = STEP_NUMBER
    for at, grad_ref in ((0, act_ref), (1, up_ref)):
        new = adamw_update(
            *(ref[at] for ref in in_refs), grad_ref[0].astype(F32) * scale, count, MATRIX_RATE, DECAY_RATE)
        for ref, value in zip(in_new, new):
            ref[at] = value
    new = adamw_update(
        *(ref[...] for ref in down_refs), out_ref[0].astype(F32).T * scale, count, MATRIX_RATE, DECAY_RATE)
    for ref, value in zip(down_new, new):
        ref[...] = value


def glu_update(sums, sum_place, first, blocks, ins, downs, scale, earlier=()):
    rows, lanes = ins[0].shape[1], LANES
    sum_spec = lambda kind: pl.BlockSpec((1, rows, lanes), lambda q: sum_place(kind, q))
    in_spec = pl.BlockSpec((2, rows, lanes), lambda q: (0, 0, q + first))
    down_spec = pl.BlockSpec((lanes, rows), lambda q: (q + first, 0))
    new = pl.pallas_call(
        functools.partial(glu_update_kernel, scale),
        grid=(blocks,),
        in_specs=[sum_spec(0), sum_spec(1), sum_spec(2)] + [in_spec] * 3 + [down_spec] * 3
        + [pl.BlockSpec(memory_space=pl.ANY)] * len(earlier),
        out_specs=[in_spec] * 3 + [down_spec] * 3,
        out_shape=[jax.ShapeDtypeStruct(ins[0].shape, F32)] * 3 + [jax.ShapeDtypeStruct(downs[0].shape, F32)] * 3,
        input_output_aliases={9 + at: at for at in range(len(earlier))},
        compiler_params=pltpu.CompilerParams(vmem_limit_bytes=VMEM_LIMIT),
        cost_estimate=pl.CostEstimate(
            flops=60 * rows * lanes * blocks, bytes_accessed=84 * rows * lanes * blocks,
            transcendentals=6 * rows * lanes * blocks),
    )(sums, sums, sums, *ins, *downs, *earlier)
    return tuple(new)


ITEMS = 6
ALONG_Z = (0, 5, 2, 3)


def split_lanes(first, second):
    low = lax.broadcasted_iota(jnp.int32, first.shape, 1) < 64
    return (
        jnp.where(low, first, pltpu.roll(second, 64, 1)),
        jnp.where(low, pltpu.roll(first, 64, 1), second),
    )


def gather_kernel(mixer_ref, gain_ref, lengths_ref, domains_ref, glu_in_hbm, glu_out_hbm, cot_ref,
                  all_in, all_out, all_small, cot_full, glu_low,
                  glu_in_ref, glu_out_ref, glu_sem, in_ref, out_ref, small_ref, right_send, left_send,
                  z_recv, x_send, x_recv, core_send, core_recv, y_send, y_recv, local_sem):
    z, x, core = device_place()
    mp = lax.axis_index("mp")
    glu_loads = (
        pltpu.make_async_copy(glu_in_hbm, glu_in_ref, glu_sem.at[0]),
        pltpu.make_async_copy(glu_out_hbm, glu_out_ref, glu_sem.at[1]),
    )
    for one in glu_loads:
        one.start()
    barrier = pltpu.get_barrier_semaphore()
    right, left = lax.rem(z + 1, DEPTH), lax.rem(z + DEPTH - 1, DEPTH)
    dp = lax.axis_index("dp")
    for target in (
        device_at(right, x, core), device_at(left, x, core), device_at(z, 1 - x, core),
        device_at(z, x, 1 - core), (dp, 1 - mp),
    ):
        pl.semaphore_signal(barrier, 1, device_id=target, device_id_type=MESH_ID)
    for kind in range(3):
        for tile in range(in_ref.shape[3] // 128):
            first = mixer_ref[kind, :, 256 * tile : 256 * tile + 128]
            second = mixer_ref[kind, :, 256 * tile + 128 : 256 * tile + 256]
            for side, value in enumerate(split_lanes(first, second)):
                in_ref[side, kind, :, 128 * tile : 128 * tile + 128] = value.astype(BF)
    out_ref[...] = mixer_ref[3].astype(BF)
    lane = lax.broadcasted_iota(jnp.int32, (1, 128), 1)
    live = jnp.zeros((1, 128), F32)
    for batch in range(lengths_ref.shape[0]):
        count = lengths_ref[batch : batch + 1, :].astype(F32)
        live = live + jnp.where(lane == domains_ref[batch : batch + 1, :], count, 0.0)
    small_ref[...] = jnp.zeros_like(small_ref)
    small_ref[0:3, 0:64] = gain_ref[...].astype(BF).astype(F32)
    small_ref[3:4, :] = live
    pl.semaphore_wait(barrier, 5)

    def spot(item, zs, xs, cs, side=None):
        if item == 0:
            return all_in.at[:, zs, xs, cs, mp if side is None else side]
        if item in (1, 4, 5):
            rows = out_ref.shape[0] // 2
            return all_out.at[zs, xs, cs, slice(rows, None) if item == 5 else slice(0, rows)]
        if item == 2:
            return all_in.at[:, zs, xs, cs, 1 - mp]
        return all_small.at[zs, xs, cs]

    def own(item):
        if item == 0:
            return in_ref.at[mp]
        if item in (1, 5):
            rows = out_ref.shape[0] // 2
            return out_ref.at[slice(rows, None) if item == 5 else slice(0, rows)]
        return spot(item, z, x, core)

    def copy(item, zs, xs, target, send, recv, source=None):
        return pltpu.make_async_remote_copy(
            spot(item, zs, xs, core) if source is None else source, spot(item, zs, xs, core),
            send, recv, device_id=target, device_id_type=MESH_ID)

    def column(item):
        return 1 - x if item == 4 else x

    def right_copy(item, zs, source=None):
        return copy(item, zs, column(item), device_at(right, x, core), right_send.at[zs, item], z_recv.at[zs, item], source)

    def left_copy(item, zs, source=None):
        return copy(item, zs, column(item), device_at(left, x, core), left_send.at[zs, item], z_recv.at[zs, item], source)

    def x_copy(item, zs, source=None):
        return copy(item, zs, x, device_at(z, 1 - x, core), x_send.at[zs, item], x_recv.at[zs, item], source)

    def core_copy(item, zs, xs, source=None):
        return copy(item, zs, xs, device_at(z, x, 1 - core), core_send.at[zs, xs, item], core_recv.at[zs, xs, item], source)

    y_copies = [
        pltpu.make_async_remote_copy(
            in_ref.at[1 - mp], all_in.at[:, z, x, core, mp], y_send.at[0], y_recv.at[0],
            device_id=(dp, 1 - mp), device_id_type=MESH_ID),
        pltpu.make_async_remote_copy(
            small_ref, all_small.at[z, x, core, mp], y_send.at[1], y_recv.at[1],
            device_id=(dp, 1 - mp), device_id_type=MESH_ID),
    ]
    locals_ = [
        pltpu.make_async_copy(in_ref.at[mp], spot(0, z, x, core), local_sem.at[0]),
        pltpu.make_async_copy(out_ref, all_out.at[z, x, core], local_sem.at[1]),
        pltpu.make_async_copy(small_ref, all_small.at[z, x, core, mp], local_sem.at[2]),
    ]
    cot_lanes = pl.ds(pl.multiple_of(mp * cot_ref.shape[1], 128), cot_ref.shape[1])
    cot_local = pltpu.make_async_copy(cot_ref, cot_full.at[:, cot_lanes], local_sem.at[3])
    cot_copy = pltpu.make_async_remote_copy(
        cot_ref, cot_full.at[:, cot_lanes], y_send.at[2], y_recv.at[2],
        device_id=(dp, 1 - mp), device_id_type=MESH_ID)
    for one in y_copies:
        one.start()
    locals_[2].start()

    def both_ways(item, source=None):
        @pl.when(z < DEPTH - 1)
        def _():
            right_copy(item, z, source).start()

        @pl.when(z > 0)
        def _():
            left_copy(item, z, source).start()

    for item in (1, *ALONG_Z):
        if item == 2:
            y_copies[0].wait_recv()
        if item == 3:
            y_copies[1].wait_recv()
            locals_[2].wait()
        source = own(item)
        both_ways(item, source)
        x_copy(item, z, source).start()
        core_copy(item, z, x, source).start()
    locals_[0].start()
    locals_[1].start()
    cot_copy.start()
    cot_local.start()
    for one in glu_loads:
        one.wait()
    glu_low[0:2] = glu_in_ref[...].astype(BF)
    for tile in range(glu_out_ref.shape[0] // 128):
        lanes = slice(128 * tile, 128 * tile + 128)
        glu_low[2, :, lanes] = glu_out_ref[lanes, :].T.astype(BF)

    def from_x(item, zs):
        pltpu.make_async_remote_copy(
            spot(item, zs, 1 - x, core), spot(item, zs, 1 - x, core), x_send.at[zs, item],
            x_recv.at[zs, item], device_id=device_at(z, 1 - x, core), device_id_type=MESH_ID).wait_recv()
        core_copy(item, zs, 1 - x).start()

    def arrived(item, hop):
        sent = 1 if item == 4 else item

        @pl.when(z >= hop)
        def _():
            zs = z - hop
            right_copy(item, zs).wait_recv()

            @pl.when(z < DEPTH - 1)
            def _():
                right_copy(item, zs).start()

            if item in ALONG_Z:
                x_copy(item, zs).start()
            core_copy(sent, zs, column(item)).start()

        @pl.when(z + hop < DEPTH)
        def _():
            zs = z + hop
            left_copy(item, zs).wait_recv()

            @pl.when(z > 0)
            def _():
                left_copy(item, zs).start()

            if item in ALONG_Z:
                x_copy(item, zs).start()
            core_copy(sent, zs, column(item)).start()

    for hop in range(1, DEPTH + 1):
        if hop == 1:
            from_x(1, z)
            both_ways(4)
        if hop < DEPTH:
            arrived(1, hop)
        for item in ALONG_Z:
            if hop < DEPTH:
                arrived(item, hop)
            if hop == 1:
                from_x(item, z)
            else:
                @pl.when(z >= hop - 1)
                def _():
                    from_x(item, z - (hop - 1))

                @pl.when(z + hop - 1 < DEPTH)
                def _():
                    from_x(item, z + (hop - 1))
        if hop < DEPTH:
            arrived(4, hop)

    for item in range(ITEMS):
        for zs in range(DEPTH):
            @pl.when((z >= zs) & (z < DEPTH - 1))
            def _():
                right_copy(item, zs).wait_send()

            @pl.when((z <= zs) & (z > 0))
            def _():
                left_copy(item, zs).wait_send()

            if item in ALONG_Z:
                x_copy(item, zs).wait_send()
            if item == 4:
                continue
            for xs in range(2):
                core_copy(item, zs, xs).wait()
    x_copy(1, z).wait_send()
    for one in y_copies:
        one.wait_send()
    locals_[0].wait()
    locals_[1].wait()
    cot_local.wait()
    cot_copy.wait_send()
    pltpu.make_async_remote_copy(
        cot_ref, cot_full.at[:, pl.ds(pl.multiple_of((1 - mp) * cot_ref.shape[1], 128), cot_ref.shape[1])],
        y_send.at[2], y_recv.at[2], device_id=(dp, 1 - mp), device_id_type=MESH_ID).wait_recv()


def gather_call(mixer, gain, lengths, domains, glu_in, glu_out, cot, collective):
    _, own_rows, full = mixer.shape
    channels = full // 2
    dma = pltpu.SemaphoreType.DMA
    any_space = pl.BlockSpec(memory_space=pl.ANY)
    in_vmem = pl.BlockSpec(memory_space=pltpu.VMEM)
    _, glu_rows, hidden = glu_in.shape
    return pl.pallas_call(
        gather_kernel,
        in_specs=[in_vmem] * 4 + [any_space] * 3,
        out_specs=[any_space] * 4 + [in_vmem],
        out_shape=[
            jax.ShapeDtypeStruct((3, DEPTH, 2, 2, 2, own_rows, channels), BF),
            jax.ShapeDtypeStruct((DEPTH, 2, 2, own_rows, full), BF),
            jax.ShapeDtypeStruct((DEPTH, 2, 2, 2, 8, 128), F32),
            jax.ShapeDtypeStruct((cot.shape[0], 2 * cot.shape[1]), BF),
            jax.ShapeDtypeStruct((3, glu_rows, hidden), BF),
        ],
        scratch_shapes=[
            pltpu.VMEM(glu_in.shape, F32),
            pltpu.VMEM(glu_out.shape, F32),
            dma((2,)),
            pltpu.VMEM((2, 3, own_rows, channels), BF),
            pltpu.VMEM((own_rows, full), BF),
            pltpu.VMEM((8, 128), F32),
            dma((DEPTH, ITEMS)), dma((DEPTH, ITEMS)), dma((DEPTH, ITEMS)), dma((DEPTH, ITEMS)),
            dma((DEPTH, ITEMS)), dma((DEPTH, 2, ITEMS)), dma((DEPTH, 2, ITEMS)), dma((3,)), dma((3,)), dma((4,)),
        ],
        compiler_params=pltpu.CompilerParams(
            collective_id=collective, has_side_effects=True, vmem_limit_bytes=VMEM_LIMIT),
        cost_estimate=pl.CostEstimate(flops=0, bytes_accessed=300_000_000, transcendentals=0),
    )(mixer, gain, lengths, domains, glu_in, glu_out, cot)


def shards(
    tokens,
    cotangent,
    lengths,
    domains,
    lower_bound,
    mixer_master,
    mixer_first,
    mixer_second,
    glu_in_master,
    glu_in_first,
    glu_in_second,
    glu_out_master,
    glu_out_first,
    glu_out_second,
    gain_master,
    gain_first,
    gain_second,
):
    batches, _, length, full = tokens.shape
    rows = batches * length
    groups = lax.axis_size("dp")
    narrow = lax.axis_size("mp")
    place = lax.axis_index("mp")
    own_rows = mixer_master.shape[1]
    channels = groups * own_rows
    part = full // narrow
    quick = groups == 16 and narrow == 2 and own_rows == 64

    domain_ids = jnp.arange(NDOM, dtype=jnp.int32)
    member = (domains[..., 0][..., None] == domain_ids).astype(F32)
    cot_part = cotangent.reshape(rows, part)
    if quick:
        mixer_in, mixer_out, small, cot_full, glu_low = gather_call(
            mixer_master, gain_master, lengths, domains[..., 0], glu_in_master, glu_out_master, cot_part, 2
        )
        mixer_in = mixer_in.reshape(3, full, channels)
        mixer_out = mixer_out.reshape(channels, full)
        small = small.reshape(groups, narrow, 8, 128)
        gain_full = small[:, :, :3, :own_rows].transpose(2, 0, 1, 3).reshape(3, full)
        counts = jnp.sum(small[:, 0, 3, :NDOM], axis=0)
    else:
        gain_full = lax.all_gather(
            gain_master.astype(BF), ("dp", "mp"), axis=1, tiled=True
        ).astype(F32)
        mixer_low = mixer_master.astype(BF)
        in_blocks = mixer_low[:3].reshape(3, own_rows, groups, narrow, own_rows)
        in_blocks = in_blocks.transpose(3, 0, 1, 2, 4).reshape(narrow, 3, own_rows, channels)
        in_rows = mp_swap(in_blocks).transpose(1, 0, 2, 3).reshape(3, narrow * own_rows, channels)
        mixer_in = lax.all_gather(in_rows, "dp", axis=1, tiled=True)
        mixer_out = lax.all_gather(mixer_low[3], "dp", axis=0, tiled=True)
        counts = lax.psum(jnp.sum(member * lengths.astype(F32)[..., None], axis=(0, 1)), "dp")
        cot_full = mp_gather(cot_part)
        glu_low = jnp.concatenate([glu_in_master.astype(BF), glu_out_master.astype(BF).T[None]])
    glu = lax.all_gather(glu_low, "dp", axis=1, tiled=True)

    seq_weight = jnp.sum(counts) / (NDOM * jnp.sum(member * counts, axis=-1))
    positions = jnp.arange(length, dtype=jnp.int32)
    token_weight = jnp.where(positions[None, :] < lengths[:, :1], seq_weight[:, :1], 0.0)
    token_weight = token_weight.reshape(rows, 1)

    own_channels = lambda v: lax.dynamic_index_in_dim(
        v.reshape(groups, narrow, own_rows), place, 1, keepdims=False
    ).reshape(channels)
    bound = own_channels(lower_bound)
    state_gain = own_channels(gain_full[1])

    token_rows = tokens.reshape(rows, full)
    seq_in = token_rows.astype(F32)
    inverse_in = inverse_rms(seq_in)
    unit_in = seq_in * inverse_in
    normed_in = (unit_in * gain_full[0]).astype(BF)
    pre = jnp.einsum("td,kde->kte", normed_in, mixer_in, preferred_element_type=F32)
    pre = pre.reshape(3, batches, length, channels)
    states, raw, square = scan_forward(pre, bound, state_gain)
    square = mp_sum_wide(square.reshape(rows, 1))
    inverse_state = lax.rsqrt(square / full + EPSILON)
    mixed = jnp.dot(raw.reshape(rows, channels), mixer_out, preferred_element_type=F32)
    back_low = (cot_full.astype(F32) * token_weight).astype(BF)
    gated_out = (raw.reshape(rows, channels).astype(F32) * inverse_state).astype(BF)
    if quick:
        mixed = mixed.astype(BF)
        came, left_back, left_in, left_out, token_weight, inverse_in = lax.optimization_barrier(
            (
                partner_swap(mixed), owner_rows(back_low), owner_rows(normed_in), owner_rows(gated_out),
                token_weight, inverse_in,
            )
        )
        mixed = mixed.astype(F32) + came.astype(F32)
    else:
        mixed = mp_sum(mixed)
    branch_mix = inverse_state * mixed
    middle = seq_in + branch_mix
    inverse_mid = inverse_rms(middle)
    unit_mid = middle * inverse_mid
    normed_mid = (unit_mid * gain_full[2]).astype(BF)

    across = (((1,), (1,)), ((), ()))
    down = (((0,), (0,)), ((), ()))
    dot = functools.partial(lax.dot_general, preferred_element_type=F32)
    if quick:
        glu_sums, glu_tail, sum_own, sum_came, half_own, half_send = glu_call(normed_mid, back_low, left_back, glu, 0)
        half_came = partner_swap(half_send)
        glu_tail = lax.psum_scatter(glu_tail, "dp", scatter_dimension=1, tiled=True)
    else:
        pre_act = jnp.dot(normed_mid, glu[0], preferred_element_type=F32)
        pre_up = jnp.dot(normed_mid, glu[1], preferred_element_type=F32)
        grad_hidden = jnp.dot(back_low, glu[2], preferred_element_type=F32)
        act_part = jax.nn.silu(pre_act)
        hidden = (act_part * pre_up).astype(BF)
        grad_act = (grad_hidden * pre_up * silu_slope(pre_act)).astype(BF)
        grad_up = (grad_hidden * act_part).astype(BF)
        grad_normed = mp_sum(dot(grad_act, glu[0], across) + dot(grad_up, glu[1], across))
        glu_grad = jnp.stack(
            [dot(normed_mid, grad_act, down), dot(normed_mid, grad_up, down), dot(back_low, hidden, down)]
        ).astype(BF)
        glu_own = lax.psum_scatter(glu_grad, "dp", scatter_dimension=1, tiled=True).astype(F32)
        branch = mp_scatter(dot(hidden, glu[2], across))
    scale = 1.0 / (batches * groups * tokens.shape[1])
    own_features = lambda v: lax.dynamic_slice_in_dim(v, place * part, part, v.ndim - 1)
    if quick:
        grad_middle_own, middle_low, state_mean, grad_gated, gain_mid = middle_back(
            sum_own, sum_came, middle, cot_full, token_rows, token_weight, gain_full[2], mixer_out
        )
        gain_mid = gain_mid[0]
    else:
        inverse_mid = inverse_rms(middle)
        unit_mid = middle * inverse_mid
        gain_mid = jnp.sum(grad_normed * unit_mid, axis=0)
        scaled_mid = grad_normed * gain_full[2]
        back = cot_full.astype(F32) * token_weight
        grad_middle = back + inverse_mid * (
            scaled_mid - unit_mid * jnp.mean(scaled_mid * unit_mid, axis=-1, keepdims=True)
        )
        grad_middle_own = own_features(grad_middle)
        middle_low = grad_middle.astype(BF)
        state_mean = jnp.mean(middle_low.astype(F32) * branch_mix, axis=-1, keepdims=True)
        grad_gated = dot(middle_low, mixer_out, across)
    by_batch = lambda v: v.reshape(batches, length, v.shape[-1])
    grad_pre, gain_state, pre_dot = scan_backward(
        pre, states, by_batch(grad_gated), by_batch(inverse_state), by_batch(state_mean), bound, state_gain
    )
    if quick:
        scattered = glu_in_master.shape[2] // LANES - TAIL
        glu_ins = (glu_in_master, glu_in_first, glu_in_second)
        glu_downs = (glu_out_master, glu_out_first, glu_out_second)
        glu_new = glu_update(
            glu_sums, lambda kind, q: (3 * q + kind, 0, 0), 0, scattered, glu_ins, glu_downs, scale
        )
        branch = half_own.astype(F32) + half_came.astype(F32)
        layer_out = (own_features(middle) + branch).astype(BF)
        layer_out, grad_pre, glu_new = lax.optimization_barrier((layer_out, grad_pre, glu_new))
    grad_pre = grad_pre.reshape(3, rows, channels)
    gain_state = jnp.sum(gain_state, axis=0).reshape(groups, 1, own_rows)
    gain_state = lax.dynamic_update_slice_in_dim(
        jnp.zeros((groups, narrow, own_rows), F32), gain_state, place, 1
    )
    device = lax.axis_index("dp") * narrow + place
    if quick:
        gain_parts = jnp.stack(
            [
                jnp.zeros((groups, narrow * own_rows), F32),
                gain_state.reshape(groups, narrow * own_rows),
                0.5 * gain_mid.reshape(groups, narrow * own_rows),
            ],
            axis=1,
        )
        gain_parts = jnp.pad(gain_parts, ((0, 0), (0, 5), (0, 0)))
        pre_dot = pre_dot.reshape(-1, 128)
        mixer_own, gain_own, grad_normed_in, dot_came = mixer_call(
            left_in, grad_pre, left_out, middle_low, gain_parts, token_rows, inverse_in, mixer_in, pre_dot, 1
        )
        in_mean = (pre_dot + dot_came).reshape(rows, 1) / full
        gain_own = lax.dynamic_slice_in_dim(gain_own[:3], place * own_rows, own_rows, 1)
    else:
        grad_mix_out = dot(gated_out, middle_low, down).astype(BF)
        grad_mix_in = jnp.einsum("td,kte->kde", normed_in, grad_pre, preferred_element_type=F32)
        in_own = lax.psum_scatter(grad_mix_in.astype(BF), "dp", scatter_dimension=1, tiled=True)
        out_own = lax.psum_scatter(grad_mix_out, "dp", scatter_dimension=0, tiled=True)
        in_own = mp_swap(in_own.reshape(3, narrow, own_rows, channels).transpose(1, 0, 2, 3))
        in_own = in_own.reshape(narrow, 3, own_rows, groups, own_rows).transpose(1, 2, 3, 0, 4)
        grad_normed_in = jnp.einsum("kte,kde->td", grad_pre, mixer_in, preferred_element_type=F32)
        gain_in = jnp.sum(grad_normed_in * unit_in, axis=0)
        grad_normed_in = mp_scatter(grad_normed_in)
        gain_rows = jnp.stack([gain_in, gain_state.reshape(full), gain_mid / narrow])
        gain_total = lax.psum(gain_rows, ("dp", "mp"))
        gain_own = lax.dynamic_slice_in_dim(gain_total, device * own_rows, own_rows, 1)
        in_mean = mp_sum_wide(pre_dot.reshape(rows, 1)) / full
        in_own = in_own.reshape(3, own_rows, full)
        mixer_own = jnp.concatenate([in_own, out_own[None]]).astype(F32)
    unit_in_own = own_features(token_rows).astype(F32) * inverse_in
    grad_seq = grad_middle_own + inverse_in * (
        grad_normed_in * own_features(gain_full[0]) - unit_in_own * in_mean
    )
    grad_tokens = grad_seq.astype(BF)
    if not quick:
        layer_out = (own_features(middle) + branch).astype(BF)

    update = functools.partial(adamw_update, count=STEP_NUMBER)
    mixer_new = update(
        mixer_master, mixer_first, mixer_second, mixer_own * scale, rate=MATRIX_RATE, decay=DECAY_RATE
    )
    gain_new = update(
        gain_master, gain_first, gain_second, gain_own * scale, rate=GAIN_RATE, decay=0.0
    )
    if quick:
        glu_new = glu_update(
            glu_tail, lambda kind, q: (kind, 0, q), scattered, TAIL, glu_ins, glu_downs, scale, glu_new
        )
    else:
        glu_in_new = update(
            glu_in_master, glu_in_first, glu_in_second, glu_own[:2] * scale,
            rate=MATRIX_RATE, decay=DECAY_RATE,
        )
        glu_out_new = update(
            glu_out_master, glu_out_first, glu_out_second, glu_own[2].T * scale,
            rate=MATRIX_RATE, decay=DECAY_RATE,
        )
        glu_new = (*glu_in_new, *glu_out_new)
    return (
        layer_out.reshape(batches, 1, length, part),
        grad_tokens.reshape(batches, 1, length, part),
        *mixer_new,
        *glu_new,
        *gain_new,
    )


def solution(mesh):
    weights = (
        [P(None, ("dp", "mp"), None)] * 3
        + [P(None, "dp", "mp")] * 3
        + [P("mp", "dp")] * 3
        + [P(None, ("dp", "mp"))] * 3
    )
    in_specs = (
        P(None, "dp", None, None),
        P(None, "dp", None, "mp"),
        P(None, "dp"),
        P(None, "dp", None),
        P(),
        *weights,
    )
    out_specs = (P(None, "dp", None, "mp"), P(None, "dp", None, "mp"), *weights)
    return jax.shard_map(shards, mesh=mesh, in_specs=in_specs, out_specs=out_specs, check_vma=False)
```
